32 devices in a mesh: dp: 4 (over y, x), ctx: 8 (over z, core).
Axes of the slice: x: 2, y: 2, z: 4, core: 2. Of those that a mesh axis runs over, the one named last changes fastest.
Arguments:
- inputs: bfloat16 [8192, 8192], P(('dp', 'ctx')), parts along dimension 0, may hold values from -6 to 6
- key_query: bfloat16 [8192, 2048], P(('dp', 'ctx')), parts along dimension 0, may hold values from -3 to 3
- conv_inputs: float32 [4, 8192], replicated, may hold values from -3 to 3
- conv_kq: float32 [4, 2048], replicated, may hold values from -3 to 3
- step_size: float32 [8192, 128], P(('dp', 'ctx')), parts along dimension 0, may hold values from 0.1 to 1
- decay_log: float32 [8192, 128], P(('dp', 'ctx')), parts along dimension 0, may hold values from -1 to 0, as said below
- skip_gain: float32 [128], replicated, may hold values from 0.5 to 1.5
- norm_gain: float32 [8192], replicated, may hold values from 0.5 to 1.5
Outputs:
- mixed: bfloat16 [8192, 8192], P('dp', 'ctx'), parts along dimension 0
The draws below stay inside these ranges and needn't reach their ends.
There are 4 independent parts, one for each index of `dp`. The reference program is written for one: setup_inputs(seed, part) draws one part's arguments, and reference() takes and returns one part's arrays. A program takes and returns all parts, laid end to end along the dimension named above; an argument that names none is the same for every part. Nothing has to cross between parts.
Inputs may be any that keep to these rules, and one draw needn't show every extreme that they name: `decay_log`: log decay factors, all negative.
All inputs are finite; a program needn't handle non-finite values.
Results may differ from the reference program's by a relative error of at most 0.0085.
Values may be sent and summed in bfloat16 or wider, within the bound.
No kernel may reach another device: no remote copies, remote signals or barrier semaphores. Data moves between devices by JAX's collectives and lax.ppermute only.
A program may use at most 448 MiB of HBM per device.

```python
import math
import jax
import jax.numpy as jnp
from jax import lax

HEADS = 128
HEAD_DIM = 64
STATE = 128
GROUPS = 8
KW = 4
BLOCK = 128
TOK_DEV = 256
TOKEN_COUNT = 2048
HP = 8192


def draw_decay_log(key, part):
    sampler_seeds = jax.random.split(jax.random.fold_in(key, 17), 10)
    order = jax.random.permutation(sampler_seeds[0], HEADS)
    mixed_count = HEADS // 2
    mixed = (order < mixed_count).astype(jnp.float32)
    pieces = TOKEN_COUNT // TOK_DEV
    fast_piece = jax.random.randint(sampler_seeds[1], (pieces, 1, HEADS), 0, 2).astype(jnp.float32) * mixed[None, None, :]
    steady_rate = jnp.exp(jax.random.uniform(sampler_seeds[2], (HEADS,), jnp.float32, math.log(0.1), math.log(0.5))) / TOKEN_COUNT
    fast_rate = jnp.exp(jax.random.uniform(sampler_seeds[3], (HEADS,), jnp.float32, math.log(1.0 / 50.0), math.log(1.0 / 20.0)))
    rough = jnp.exp(jax.random.uniform(sampler_seeds[4], (pieces, TOK_DEV, HEADS), jnp.float32, math.log(0.5), math.log(2.0)))
    factor = jnp.exp(jax.random.uniform(sampler_seeds[5], (pieces, 1, HEADS), jnp.float32, math.log(0.5), math.log(2.0)))
    drawn_flags = (jax.random.randint(sampler_seeds[6], (pieces, TOK_DEV, HEADS), 0, 20) < 8).astype(jnp.float32)
    drawn_on = drawn_flags * mixed[None, None, :] * (1.0 - fast_piece)
    drawn_size = jnp.exp(jax.random.uniform(sampler_seeds[7], (pieces, TOK_DEV, HEADS), jnp.float32, math.log(0.003), math.log(0.009)))
    base = fast_piece * fast_rate[None, None, :] * rough + (1.0 - fast_piece) * steady_rate[None, None, :] * rough
    rate = (base + drawn_on * drawn_size) * factor
    starting_shift = -rate.reshape(TOKEN_COUNT, HEADS)
    spike_location = jax.random.randint(sampler_seeds[8], (3,), 0, TOKEN_COUNT)
    slot_numbers = jnp.arange(TOKEN_COUNT, dtype=jnp.int32)
    spiked_flags = jnp.any(slot_numbers[:, None] == spike_location[None, :], axis=1)
    objective_scalar = jax.random.uniform(sampler_seeds[9], (TOKEN_COUNT, HEADS), jnp.float32, 0.2, 0.4)
    spike_entries = jnp.where(spiked_flags[:, None], jnp.log(1.0 - objective_scalar), 0.0)
    return (starting_shift + spike_entries).astype(jnp.float32)


def levels(own_key, dims, cuts, low, top_value):
    def one(dim, parts):
        steps = jax.random.uniform(jax.random.fold_in(jax.random.fold_in(own_key, 6), dim), (parts,), jnp.float32, low / len(cuts), top_value / len(cuts))
        return jnp.repeat(jnp.exp(steps), dims[dim] // parts).reshape((-1,) + (1,) * (len(dims) - dim - 1))

    loudness = one(*cuts[0])
    for cut in cuts[1:]:
        loudness = loudness * one(*cut)
    return loudness


def normal_values(key, shape, scale, bound, shards=(), held_as=jnp.bfloat16):
    level = levels(key, shape, shards, -0.22, 0.18) if shards else 1.0
    values = jax.random.normal(key, shape, jnp.float32) * scale * level
    return jnp.minimum(jnp.maximum(values, -bound), bound).astype(held_as)


def setup_inputs(seed: int = 0, part: int = 0) -> dict:
    seeds = jax.random.split(jax.random.key(seed), 9)
    part_splits = jax.random.split(jax.random.fold_in(seeds[8], part), 9)
    inputs = normal_values(part_splits[0], (TOKEN_COUNT, HP), 1.0, 6.0, ((0, 8),))
    key_query = normal_values(part_splits[1], (TOKEN_COUNT, 2 * GROUPS * STATE), 0.5, 3.0, ((0, 8),))
    conv_inputs = normal_values(seeds[2], (KW, HP), KW ** -0.5, 3.0, (), jnp.float32)
    conv_kq = normal_values(seeds[3], (KW, 2 * GROUPS * STATE), KW ** -0.5, 3.0, (), jnp.float32)
    step_size = jnp.clip(jnp.exp(math.log(1.0) - 2.3025851 * jax.random.uniform(part_splits[4], (TOKEN_COUNT, HEADS), jnp.float32) ** levels(part_splits[4], (TOKEN_COUNT, HEADS), ((0, 8),), -0.2, 0.2)), 0.1, 1.0)
    decay_log = draw_decay_log(jax.random.fold_in(jax.random.fold_in(seeds[8], part), 71), part)
    skip_gain = jnp.clip(jax.random.uniform(seeds[6], (HEADS,), jnp.float32, 0.5, 1.5), 0.5, 1.5)
    norm_gain = jnp.clip(1.0 + 0.1 * jax.random.normal(seeds[7], (HP,), jnp.float32), 0.5, 1.5)
    return {"inputs": inputs, "key_query": key_query, "conv_inputs": conv_inputs, "conv_kq": conv_kq, "step_size": step_size, "decay_log": decay_log, "skip_gain": skip_gain, "norm_gain": norm_gain}


def convolve(values, weight):
    length = values.shape[0]
    padded = jnp.concatenate([jnp.zeros((KW - 1, values.shape[1]), jnp.float32), values.astype(jnp.float32)], axis=0)
    summed = jnp.zeros(values.shape, jnp.float32)
    for offset in range(KW):
        summed = summed + weight[offset][None, :] * padded[offset:offset + length]
    return jax.nn.silu(summed).astype(jnp.bfloat16)

def block_terms(scaled, b_part, c_part, decays):
    per_group = HEADS // GROUPS
    cumul = jnp.cumsum(decays, axis=0)
    upper = cumul.T
    slot_numbers = lax.broadcasted_iota(jnp.int32, (BLOCK, BLOCK), 0)
    sources = lax.broadcasted_iota(jnp.int32, (BLOCK, BLOCK), 1)
    spread = jnp.where((slot_numbers >= sources)[None], upper[:, :, None] - upper[:, None, :], -jnp.inf)
    decay_mat = jnp.exp(spread).reshape(GROUPS, per_group, BLOCK, BLOCK)
    scores = jnp.einsum('tgn,sgn->gts', c_part.astype(jnp.float32), b_part.astype(jnp.float32))
    weights = (scores[:, None] * decay_mat).astype(jnp.bfloat16)
    intra = jnp.einsum('ghts,sghp->tghp', weights.astype(jnp.float32), scaled.astype(jnp.float32))
    last = cumul[-1]
    fade = jnp.exp(last[None, :] - cumul).reshape(BLOCK, GROUPS, per_group)
    keyed = (b_part[:, :, None, :].astype(jnp.float32) * fade[:, :, :, None]).astype(jnp.bfloat16)
    state = jnp.einsum('sghn,sghp->ghnp', keyed.astype(jnp.float32), scaled.astype(jnp.float32))
    return (intra, state.reshape(HEADS, STATE, HEAD_DIM), last, cumul)

def carried(c_part, incoming, cumul):
    per_group = HEADS // GROUPS
    held = incoming.astype(jnp.bfloat16).reshape(GROUPS, per_group, STATE, HEAD_DIM)
    term = jnp.einsum('tgn,ghnp->tghp', c_part.astype(jnp.float32), held.astype(jnp.float32))
    return term * jnp.exp(cumul).reshape(BLOCK, GROUPS, per_group)[:, :, :, None]

def finish(intra, inter, x_block, skip_gain, norm_gain):
    per_group = HEADS // GROUPS
    skipped = skip_gain.reshape(GROUPS, per_group)[None, :, :, None] * x_block.reshape(BLOCK, GROUPS, per_group, HEAD_DIM).astype(jnp.float32)
    summed = (intra + inter + skipped).reshape(BLOCK, GROUPS, per_group * HEAD_DIM)
    power = lax.optimization_barrier(jnp.mean(summed * summed, axis=-1, keepdims=True))
    normed = summed * lax.rsqrt(power + 1e-05) * norm_gain.reshape(GROUPS, per_group * HEAD_DIM)[None]
    return normed.reshape(BLOCK, HEADS * HEAD_DIM).astype(jnp.bfloat16)

def reference(inputs, key_query, conv_inputs, conv_kq, step_size, decay_log, skip_gain, norm_gain):
    per_group = HEADS // GROUPS
    width = GROUPS * STATE
    x_conv = convolve(inputs, conv_inputs)
    kq_conv = convolve(key_query, conv_kq)
    length = x_conv.shape[0]
    scaled = (x_conv.reshape(length, HEADS, HEAD_DIM).astype(jnp.float32) * step_size[:, :, None]).astype(jnp.bfloat16)
    count = length // BLOCK
    x_blocks = x_conv.reshape(count, BLOCK, HEADS * HEAD_DIM)
    s_blocks = scaled.reshape(count, BLOCK, GROUPS, per_group, HEAD_DIM)
    b_blocks = kq_conv[:, :width].reshape(count, BLOCK, GROUPS, STATE)
    c_blocks = kq_conv[:, width:].reshape(count, BLOCK, GROUPS, STATE)
    d_blocks = decay_log.reshape(count, BLOCK, HEADS)

    def advance(carry, piece):
        x_block, s_block, b_block, c_block, d_block = piece
        intra, state, last, cumul = block_terms(s_block, b_block, c_block, d_block)
        inter = carried(c_block, carry, cumul)
        normed = finish(intra, inter, x_block, skip_gain, norm_gain)
        return (jnp.exp(last)[:, None, None] * carry + state, normed)
    start = jnp.zeros((HEADS, STATE, HEAD_DIM), jnp.float32)
    _, outputs = lax.scan(advance, start, (x_blocks, s_blocks, b_blocks, c_blocks, d_blocks))
    return outputs.reshape(length, HEADS * HEAD_DIM)
```

```python
import functools

import jax
import jax.numpy as jnp
from jax import lax
from jax.experimental import pallas as pl
from jax.experimental.pallas import tpu as pltpu
from jax.sharding import PartitionSpec as P

HEADS = 128
HEAD_DIM = 64
STATE = 128
GROUPS = 8
KW = 4
BLOCK = 128
GROUP_WIDTH = HEADS * HEAD_DIM // GROUPS
EPS = 1e-05
HALO = 8
TILE = 256


def contract(a, b, dims):
    return lax.dot_general(a, b, (dims, ((), ())), preferred_element_type=jnp.float32)


def contract_exact(a, b, dims):
    return lax.dot_general(
        a,
        b,
        (dims, ((), ())),
        preferred_element_type=jnp.float32,
        precision=lax.Precision.HIGHEST,
    )


def mixer_kernel(peers, whole_group, *refs):
    me_ref = refs[0]
    parts = refs[1 : 1 + peers]
    auxes = refs[1 + peers : 1 + 2 * peers]
    taps_ref, skip_ref, gain_ref = refs[1 + 2 * peers : 4 + 2 * peers]
    outs = refs[4 + 2 * peers : 5 + 2 * peers + (0 if whole_group else 1)]
    raw, aux, wide, carry, total_ref, sems = refs[-6:]
    step = pl.program_id(0)
    me = me_ref[0]
    rows = raw.shape[1]
    width = outs[0].shape[1]
    heads = width // HEAD_DIM

    @pl.when(step == 0)
    def _():
        for k in range(peers):
            source = lax.rem(me + (peers - k), peers)
            pltpu.make_async_copy(parts[k], raw.at[source], sems.at[0, source]).start()
            pltpu.make_async_copy(auxes[k], aux.at[source], sems.at[1, source]).start()
        carry[...] = jnp.zeros_like(carry)
        wide[rows : rows + HALO] = jnp.zeros((HALO, wide.shape[1]), jnp.float32)

    pltpu.make_async_copy(parts[0], raw.at[step], sems.at[0, step]).wait()
    pltpu.make_async_copy(auxes[0], aux.at[step], sems.at[1, step]).wait()

    wide[0:HALO] = wide[rows : rows + HALO]
    wide[HALO : HALO + rows] = raw[step].astype(jnp.float32)

    row = lax.broadcasted_iota(jnp.int32, (BLOCK, BLOCK), 0)
    col = lax.broadcasted_iota(jnp.int32, (BLOCK, BLOCK), 1)
    lower = row >= col
    tril = jnp.where(lower, 1.0, 0.0).astype(jnp.float32)
    eye = jnp.where(row == col, 1.0, 0.0).astype(jnp.float32)
    head_of = lax.broadcasted_iota(jnp.int32, (2 * heads, width), 1) // HEAD_DIM
    head_row = lax.rem(lax.broadcasted_iota(jnp.int32, (2 * heads, width), 0), heads)
    spread = jnp.where(head_of == head_row, 1.0, 0.0).astype(jnp.bfloat16)

    def halves(v):
        high = v.astype(jnp.bfloat16)
        low = (v - high.astype(jnp.float32)).astype(jnp.bfloat16)
        return jnp.concatenate([high, low], axis=1)

    def activated(start, lo, hi):
        summed = taps_ref[0:1, lo:hi] * wide[pl.ds(start, BLOCK), lo:hi]
        for k in range(1, KW):
            summed = summed + taps_ref[k : k + 1, lo:hi] * wide[pl.ds(start + k, BLOCK), lo:hi]
        return (summed / (1.0 + jnp.exp(-summed))).astype(jnp.bfloat16)

    for block in range(rows // BLOCK):
        top = block * BLOCK
        start = top + HALO - KW + 1
        decays = aux[step, 0:heads, top : top + BLOCK]
        steps = aux[step, heads : 2 * heads, top : top + BLOCK]
        cumul = contract_exact(tril, decays, ((1,), (1,)))
        steps = contract_exact(eye, steps, ((1,), (1,)))
        middle = cumul[BLOCK // 2 - 1 : BLOCK // 2]
        inward = halves(steps * jnp.exp(middle - cumul))
        outward = halves(
            jnp.concatenate(
                [jnp.exp(cumul - middle), jnp.broadcast_to(jnp.exp(middle), (16, heads))], axis=0
            )
        )
        b_part = activated(start, width, width + STATE)
        c_part = activated(start, width + STATE, width + 2 * STATE)
        scores = contract(c_part, b_part, ((1,), (1,)))
        scores = jnp.where(lower, scores, 0.0).astype(jnp.bfloat16)
        left = jnp.concatenate([scores, c_part], axis=1)
        power = jnp.zeros((BLOCK, 1), jnp.float32)
        for lo in range(0, width, TILE):
            hi = lo + TILE
            x_conv = activated(start, lo, hi).astype(jnp.float32)
            scaled = (x_conv * contract(inward, spread[:, lo:hi], ((1,), (0,)))).astype(
                jnp.bfloat16
            )
            out_scale = contract(outward, spread[:, lo:hi], ((1,), (0,)))
            held = carry[:, lo:hi] * out_scale[BLOCK : BLOCK + 1]
            right = jnp.concatenate([scaled, held.astype(jnp.bfloat16)], axis=0)
            mixed = contract(left, right, ((1,), (0,)))
            total = mixed * out_scale[:BLOCK] + skip_ref[0:1, lo:hi] * x_conv
            total_ref[:, lo:hi] = total
            power = power + jnp.sum(total * total, axis=1, keepdims=True)
            added = contract(b_part, scaled, ((0,), (0,)))
            carry[:, lo:hi] = (held + added) * out_scale[BLOCK - 1 : BLOCK]
        if whole_group:
            norm = lax.rsqrt(power * (1.0 / GROUP_WIDTH) + EPS)
            for lo in range(0, width, TILE):
                hi = lo + TILE
                outs[0][top : top + BLOCK, lo:hi] = (
                    total_ref[:, lo:hi] * norm * gain_ref[0:1, lo:hi]
                ).astype(jnp.bfloat16)
        else:
            outs[0][top : top + BLOCK, :] = total_ref[...]
            outs[1][top : top + BLOCK, :] = jnp.broadcast_to(power, (BLOCK, 128))


def per_device(inputs, key_query, conv_inputs, conv_kq, step_size, decay_log, skip_gain, norm_gain):
    peers = lax.axis_size("ctx")
    me = lax.axis_index("ctx")
    rows = inputs.shape[0]
    width = HEADS * HEAD_DIM // peers
    heads = HEADS // peers
    span = GROUP_WIDTH // width
    scalars = jnp.concatenate(
        [
            decay_log.T.reshape(peers, heads, rows),
            step_size.T.reshape(peers, heads, rows),
        ],
        axis=1,
    )

    def columns(a, first, size):
        return lax.dynamic_slice_in_dim(a, first, size, axis=1)

    def message(x, kq, owner):
        group = owner // span
        return jnp.concatenate(
            [
                columns(x, owner * width, width),
                columns(kq, group * STATE, STATE),
                columns(kq, (GROUPS + group) * STATE, STATE),
            ],
            axis=1,
        )

    parts = []
    auxes = []
    for k in range(peers):
        owner = lax.rem(me + k, peers)
        part = message(inputs, key_query, owner)
        scalar = lax.dynamic_index_in_dim(scalars, owner, 0, False)
        if k:
            pairs = [(i, (i + k) % peers) for i in range(peers)]
            part = lax.ppermute(part, "ctx", pairs)
            scalar = lax.ppermute(scalar, "ctx", pairs)
        parts.append(part)
        auxes.append(scalar)

    taps = message(conv_inputs, conv_kq, me)
    skip = columns(jnp.repeat(skip_gain, HEAD_DIM)[None], me * width, width)
    gain = columns(norm_gain[None], me * width, width)

    whole_group = span == 1
    total_rows = peers * rows
    out_shape = [
        jax.ShapeDtypeStruct((total_rows, width), jnp.bfloat16 if whole_group else jnp.float32)
    ]
    out_specs = [pl.BlockSpec((rows, width), lambda i: (i, 0))]
    if not whole_group:
        out_shape.append(jax.ShapeDtypeStruct((total_rows, 128), jnp.float32))
        out_specs.append(pl.BlockSpec((rows, 128), lambda i: (i, 0)))
    any_spec = pl.BlockSpec(memory_space=pl.ANY)
    full = width + 2 * STATE
    outs = pl.pallas_call(
        functools.partial(mixer_kernel, peers, whole_group),
        grid=(peers,),
        in_specs=[pl.BlockSpec(memory_space=pltpu.SMEM)]
        + [any_spec] * (2 * peers)
        + [
            pl.BlockSpec((KW, full), lambda i: (0, 0)),
            pl.BlockSpec((1, width), lambda i: (0, 0)),
            pl.BlockSpec((1, width), lambda i: (0, 0)),
        ],
        out_specs=out_specs,
        out_shape=out_shape,
        scratch_shapes=[
            pltpu.VMEM((peers, rows, full), jnp.bfloat16),
            pltpu.VMEM((peers, 2 * heads, rows), jnp.float32),
            pltpu.VMEM((rows + HALO, full), jnp.float32),
            pltpu.VMEM((STATE, width), jnp.float32),
            pltpu.VMEM((BLOCK, width), jnp.float32),
            pltpu.SemaphoreType.DMA((2, peers)),
        ],
        compiler_params=pltpu.CompilerParams(vmem_limit_bytes=40 * 1024 * 1024),
        cost_estimate=pl.CostEstimate(
            flops=2 * total_rows * width * 450,
            bytes_accessed=total_rows * (2 * full + 2 * width),
            transcendentals=total_rows * full,
        ),
        name="mixer",
    )(me.reshape(1).astype(jnp.int32), *parts, *auxes, taps, skip, gain)
    if whole_group:
        return outs[0]
    total, power = outs
    sharers = [list(range(i, i + span)) for i in range(0, peers, span)]
    power = lax.psum(power[:, :1], "ctx", axis_index_groups=sharers)
    return (total * lax.rsqrt(power * (1.0 / GROUP_WIDTH) + EPS) * gain).astype(jnp.bfloat16)


def solution(mesh):
    in_specs = (
        P(("dp", "ctx"), None),
        P(("dp", "ctx"), None),
        P(),
        P(),
        P(("dp", "ctx"), None),
        P(("dp", "ctx"), None),
        P(),
        P(),
    )
    out_specs = P("dp", "ctx")
    return jax.shard_map(
        per_device, mesh=mesh, in_specs=in_specs, out_specs=out_specs, check_vma=False
    )
```

```python
import functools

import jax
import jax.numpy as jnp
from jax import lax
from jax.experimental import pallas as pl
from jax.experimental.pallas import tpu as pltpu
from jax.sharding import PartitionSpec as P

HEADS = 128
HEAD_DIM = 64
STATE = 128
GROUPS = 8
KW = 4
BLOCK = 128
GROUP_WIDTH = HEADS * HEAD_DIM // GROUPS
EPS = 1e-05
HALO = 8
LANES = 128
FIELDS = 5
SPLIT = (0.5, 0.5)
ORDER = (4, 3, 5, 2, 6, 1, 7)
VMEM_LIMIT = 48 * 1024 * 1024


def contract(a, b, dims):
    return lax.dot_general(a, b, (dims, ((), ())), preferred_element_type=jnp.float32)


def as_parts(v, count):
    parts = []
    for _ in range(count):
        part = v.astype(jnp.bfloat16)
        parts.append(part)
        v = v - part.astype(jnp.float32)
    return parts


def pack_kernel(peers, span, offset, width, heads, first, *refs):
    me = refs[0][0]
    x_ref = refs[1]
    if first:
        kq_ref, decay_ref, step_ref = refs[2:5]
        outs = refs[5 : 5 + peers]
        scalars, sems = refs[-2:]
    else:
        outs = refs[2 : 2 + peers]
        sems = refs[-1]
    rows = x_ref.shape[0]
    owned = HEADS * HEAD_DIM // peers
    copies = []
    for k in range(peers):
        owner = lax.rem(me + k, peers)
        column = pl.multiple_of(owner * owned + offset, LANES)
        copies.append(
            pltpu.make_async_copy(
                x_ref.at[:, pl.ds(column, width)],
                outs[k].at[0:rows, 0:width],
                sems.at[0, k],
            )
        )
        if first:
            group = owner // span
            for j in range(2):
                column = pl.multiple_of((j * GROUPS + group) * STATE, LANES)
                copies.append(
                    pltpu.make_async_copy(
                        kq_ref.at[:, pl.ds(column, STATE)],
                        outs[k].at[0:rows, width + j * STATE : width + (j + 1) * STATE],
                        sems.at[1 + j, k],
                    )
                )
    for copy in copies:
        copy.start()
    if first:
        scalars[...] = jnp.zeros_like(scalars)
        fields = as_parts(decay_ref[...].T, 3) + as_parts(step_ref[...].T, 2)
        across = scalars.shape[2] // rows
        for owner in range(peers):
            for p, field in enumerate(fields):
                top = p // across * heads
                left = p % across * rows
                scalars[owner, top : top + heads, left : left + rows] = field[
                    owner * heads : (owner + 1) * heads
                ]
        for k in range(peers):
            owner = lax.rem(me + k, peers)
            copy = pltpu.make_async_copy(
                scalars.at[owner], outs[k].at[rows:], sems.at[3, k]
            )
            copy.start()
            copies.append(copy)
    for copy in copies:
        copy.wait()


def mixer_kernel(peers, rows, heads, chunk, widths, whole_group, *refs):
    refs = list(refs)

    def take(count):
        taken = refs[:count]
        del refs[:count]
        return taken

    first = chunk == 0
    final = chunk == len(widths) - 1 and whole_group
    later = range(1, len(widths)) if first else ()
    width = widths[chunk]
    (me_ref,) = take(1)
    parts = take(peers)
    taps_ref, skip_ref = take(2)
    if not first:
        left_ref, b_ref, inward_ref, outward_ref, power_ref = take(5)
    if final:
        (gain_ref,) = take(1)
        earlier = take(chunk)
        (out_ref,) = take(1)
    else:
        total_ref, sums_ref = take(2)
    if first and later:
        left_ref, b_ref = take(2)
        inward_refs = take(len(later))
        outward_refs = take(len(later))
    raw, wide, carry, sems = take(4)
    if final:
        (total_ref,) = take(1)
    blocks = rows // BLOCK
    step = pl.program_id(0)
    me = me_ref[0]

    @pl.when(step == 0)
    def _():
        for k in range(peers):
            source = lax.rem(me + (peers - k), peers)
            pltpu.make_async_copy(parts[k], raw.at[source], sems.at[source]).start()
        carry[...] = jnp.zeros_like(carry)
        wide[rows : rows + HALO] = jnp.zeros((HALO, wide.shape[1]), jnp.float32)

    pltpu.make_async_copy(parts[0], raw.at[step], sems.at[step]).wait()

    wide[0:HALO] = wide[rows : rows + HALO]
    wide[HALO : HALO + rows] = raw[step, 0:rows].astype(jnp.float32)

    def spread(count):
        head_of = lax.broadcasted_iota(jnp.int32, (2 * count, count * HEAD_DIM), 1) // HEAD_DIM
        row = lax.rem(
            lax.broadcasted_iota(jnp.int32, (2 * count, count * HEAD_DIM), 0), count
        )
        return jnp.where(head_of == row, 1.0, 0.0).astype(jnp.bfloat16)

    def activated(start, size, lo, hi):
        summed = taps_ref[0:1, lo:hi] * wide[pl.ds(start, size), lo:hi]
        for k in range(1, KW):
            summed = summed + taps_ref[k : k + 1, lo:hi] * wide[pl.ds(start + k, size), lo:hi]
        return summed * pltpu.reciprocal(1.0 + jnp.exp(-summed), approx=True)

    top_shift = HALO - KW + 1
    if first:
        full = width + 2 * STATE
        across = full // rows
        row = lax.broadcasted_iota(jnp.int32, (rows, rows), 0)
        col = lax.broadcasted_iota(jnp.int32, (rows, rows), 1)
        lower = (row >= col) & (row // BLOCK == col // BLOCK)
        ones = jnp.where(lower, 1.0, 0.0).astype(jnp.bfloat16)
        eye = jnp.where(row == col, 1.0, 0.0).astype(jnp.bfloat16)

        def field(p):
            top = rows + p // across * heads
            lane = p % across * rows
            return raw[step, top : top + heads, lane : lane + rows]

        def by_rows(matrix, numbers):
            return sum(contract(matrix, field(p), ((1,), (1,))) for p in numbers)

        cumul = by_rows(ones, (0, 1, 2))
        steps = by_rows(eye, (3, 4))
        middles = [
            cumul[b * BLOCK + BLOCK // 2 - 1 : b * BLOCK + BLOCK // 2] for b in range(blocks)
        ]
        middle = jnp.concatenate([jnp.broadcast_to(m, (BLOCK, heads)) for m in middles], axis=0)
        inward = as_parts(steps * jnp.exp(middle - cumul), 2)
        outward = as_parts(
            jnp.concatenate(
                [jnp.exp(cumul - middle)]
                + [jnp.broadcast_to(jnp.exp(m), (16, heads)) for m in middles],
                axis=0,
            ),
            2,
        )

        def chosen(halves, index):
            begin = sum(widths[:index]) // HEAD_DIM
            end = begin + widths[index] // HEAD_DIM
            return jnp.concatenate([half[:, begin:end] for half in halves], axis=1)

        bc = activated(top_shift, rows, width, full).astype(jnp.bfloat16)
        b_part, c_part = bc[:, :STATE], bc[:, STATE:]
        scores = contract(c_part, b_part, ((1,), (1,)))
        scores = jnp.where(lower, scores, 0.0).astype(jnp.bfloat16)
        lefts = [
            jnp.concatenate(
                [
                    scores[b * BLOCK : (b + 1) * BLOCK, b * BLOCK : (b + 1) * BLOCK],
                    c_part[b * BLOCK : (b + 1) * BLOCK],
                ],
                axis=1,
            )
            for b in range(blocks)
        ]
        for index in later:
            inward_refs[index - 1][...] = chosen(inward, index)
            outward_refs[index - 1][...] = chosen(outward, index)
        if later:
            b_ref[...] = b_part
            for b in range(blocks):
                left_ref[b * BLOCK : (b + 1) * BLOCK] = lefts[b]
        inward = chosen(inward, 0)
        outward = chosen(outward, 0)
    else:
        inward = inward_ref[...]
        outward = outward_ref[...]
        b_part = b_ref[...]
        lefts = [left_ref[b * BLOCK : (b + 1) * BLOCK] for b in range(blocks)]

    tile = min(2 * LANES, width)
    expand = spread(width // HEAD_DIM)
    for b in range(blocks):
        top = b * BLOCK
        extra = rows + 16 * b
        power = jnp.zeros((BLOCK, LANES), jnp.float32)
        if not first:
            power = power_ref[top : top + BLOCK]
        for lo in range(0, width, tile):
            hi = lo + tile
            x_conv = activated(top + top_shift, BLOCK, lo, hi)
            in_scale = contract(inward[top : top + BLOCK], expand[:, lo:hi], ((1,), (0,)))
            out_scale = contract(outward[top : top + BLOCK], expand[:, lo:hi], ((1,), (0,)))
            mid_scale = contract(outward[extra : extra + 16], expand[:, lo:hi], ((1,), (0,)))
            scaled = (x_conv * in_scale).astype(jnp.bfloat16)
            held = carry[:, lo:hi] * mid_scale[0:1]
            right = jnp.concatenate([scaled, held.astype(jnp.bfloat16)], axis=0)
            mixed = contract(lefts[b], right, ((1,), (0,)))
            total = mixed * out_scale + skip_ref[0:1, lo:hi] * x_conv
            total_ref[top : top + BLOCK, lo:hi] = total
            squares = total * total
            for lane in range(0, tile, LANES):
                power = power + squares[:, lane : lane + LANES]
            added = contract(b_part[top : top + BLOCK], scaled, ((0,), (0,)))
            carry[:, lo:hi] = (held + added) * out_scale[BLOCK - 1 : BLOCK]
        if final:
            summed = jnp.sum(power, axis=1, keepdims=True)
            norm = lax.rsqrt(summed * (1.0 / GROUP_WIDTH) + EPS)
            sources = list(earlier) + [total_ref]
            column = 0
            for source, size in zip(sources, widths):
                out_ref[top : top + BLOCK, column : column + size] = (
                    source[top : top + BLOCK] * norm * gain_ref[0:1, column : column + size]
                ).astype(jnp.bfloat16)
                column += size
        else:
            sums_ref[top : top + BLOCK] = power


def per_device(inputs, key_query, conv_inputs, conv_kq, step_size, decay_log, skip_gain, norm_gain):
    peers = lax.axis_size("ctx")
    me = lax.axis_index("ctx")
    place = me.reshape(1).astype(jnp.int32)
    rows = inputs.shape[0]
    owned = HEADS * HEAD_DIM // peers
    heads = HEADS // peers
    span = GROUP_WIDTH // owned
    whole_group = span == 1
    total_rows = peers * rows
    blocks = rows // BLOCK
    widths = [int(owned * part) // LANES * LANES for part in SPLIT]
    offsets = [sum(widths[:i]) for i in range(len(widths))]
    order = ORDER if peers == len(ORDER) + 1 else tuple(range(1, peers))

    smem = pl.BlockSpec(memory_space=pltpu.SMEM)
    anywhere = pl.BlockSpec(memory_space=pl.ANY)
    vmem = pl.BlockSpec(memory_space=pltpu.VMEM)
    params = pltpu.CompilerParams(vmem_limit_bytes=VMEM_LIMIT)

    def columns(a, first, size):
        return lax.dynamic_slice_in_dim(a, first, size, axis=1)

    def pack(chunk):
        width = widths[chunk]
        first = chunk == 0
        cols = width + (2 * STATE if first else 0)
        extra = 0
        if first:
            lines = -(-FIELDS // (cols // rows)) * heads
            extra = -(-lines // 16) * 16
        shape = jax.ShapeDtypeStruct((rows + extra, cols), jnp.bfloat16)
        operands = [place, inputs]
        in_specs = [smem, anywhere]
        scratch = []
        if first:
            operands += [key_query, decay_log, step_size]
            in_specs += [anywhere, vmem, vmem]
            scratch.append(pltpu.VMEM((peers, extra, cols), jnp.bfloat16))
        scratch.append(pltpu.SemaphoreType.DMA((4, peers)))
        return pl.pallas_call(
            functools.partial(pack_kernel, peers, span, offsets[chunk], width, heads, first),
            in_specs=in_specs,
            out_specs=[anywhere] * peers,
            out_shape=[shape] * peers,
            scratch_shapes=scratch,
            compiler_params=params,
            cost_estimate=pl.CostEstimate(
                flops=0, bytes_accessed=4 * peers * rows * cols, transcendentals=0
            ),
            name=f"pack{chunk}",
        )(*operands)

    def exchange(messages):
        received = list(messages)
        for k in order:
            pairs = [(i, (i + k) % peers) for i in range(peers)]
            received[k] = lax.ppermute(messages[k], "ctx", pairs)
        return received

    received = [exchange(pack(chunk)) for chunk in range(len(widths))]

    taps_x = columns(conv_inputs, me * owned, owned)
    group = me // span
    taps_kq = jnp.concatenate(
        [
            columns(conv_kq, group * STATE, STATE),
            columns(conv_kq, (GROUPS + group) * STATE, STATE),
        ],
        axis=1,
    )
    skip = jnp.repeat(lax.dynamic_slice_in_dim(skip_gain, me * heads, heads), HEAD_DIM)[None]
    gain = columns(norm_gain[None], me * owned, owned)

    def by_source(count, lanes, dtype):
        spec = pl.BlockSpec((count, lanes), lambda i: (i, 0))
        return spec, jax.ShapeDtypeStruct((peers * count, lanes), dtype)

    def fixed(count, lanes):
        return pl.BlockSpec((count, lanes), lambda i: (0, 0))

    totals = []
    power = None
    shared = None
    for chunk, width in enumerate(widths):
        first = chunk == 0
        final = chunk == len(widths) - 1 and whole_group
        taps = taps_x[:, offsets[chunk] : offsets[chunk] + width]
        if first:
            taps = jnp.concatenate([taps, taps_kq], axis=1)
        cols = taps.shape[1]
        operands = [place, *received[chunk], taps, skip[:, offsets[chunk] : offsets[chunk] + width]]
        in_specs = [smem] + [anywhere] * peers + [fixed(KW, cols), fixed(1, width)]
        out = []
        scale_rows = rows + 16 * blocks
        if not first:
            left, b_part, inward, outward = shared
            small = 2 * width // HEAD_DIM
            operands += [left, b_part, inward[chunk - 1], outward[chunk - 1], power]
            in_specs += [
                by_source(rows, 2 * STATE, jnp.bfloat16)[0],
                by_source(rows, STATE, jnp.bfloat16)[0],
                by_source(rows, small, jnp.bfloat16)[0],
                by_source(scale_rows, small, jnp.bfloat16)[0],
                by_source(rows, LANES, jnp.float32)[0],
            ]
        if final:
            operands += [gain, *totals]
            in_specs += [fixed(1, owned)]
            in_specs += [by_source(rows, size, jnp.float32)[0] for size in widths[:chunk]]
            out.append(by_source(rows, owned, jnp.bfloat16))
        else:
            out.append(by_source(rows, width, jnp.float32))
            out.append(by_source(rows, LANES, jnp.float32))
        if first and len(widths) > 1:
            out.append(by_source(rows, 2 * STATE, jnp.bfloat16))
            out.append(by_source(rows, STATE, jnp.bfloat16))
            for count in (rows, scale_rows):
                for size in widths[1:]:
                    out.append(by_source(count, 2 * size // HEAD_DIM, jnp.bfloat16))
        scratch = [
            pltpu.VMEM((peers,) + received[chunk][0].shape, jnp.bfloat16),
            pltpu.VMEM((rows + HALO, cols), jnp.float32),
            pltpu.VMEM((STATE, width), jnp.float32),
            pltpu.SemaphoreType.DMA((peers,)),
        ]
        if final:
            scratch.append(pltpu.VMEM((rows, width), jnp.float32))
        results = pl.pallas_call(
            functools.partial(mixer_kernel, peers, rows, heads, chunk, widths, whole_group),
            grid=(peers,),
            in_specs=in_specs,
            out_specs=[spec for spec, _ in out],
            out_shape=[shape for _, shape in out],
            scratch_shapes=scratch,
            compiler_params=params,
            cost_estimate=pl.CostEstimate(
                flops=2 * total_rows * width * 450,
                bytes_accessed=total_rows * (2 * cols + 8 * width),
                transcendentals=total_rows * cols,
            ),
            name=f"mixer{chunk}",
        )(*operands)
        if final:
            return results[0]
        totals.append(results[0])
        power = results[1]
        if first and len(widths) > 1:
            rest = results[4:]
            shared = (results[2], results[3], rest[: len(rest) // 2], rest[len(rest) // 2 :])
    sharers = [list(range(i, i + span)) for i in range(0, peers, span)]
    summed = jnp.sum(power, axis=1, keepdims=True)
    summed = lax.psum(summed, "ctx", axis_index_groups=sharers)
    total = jnp.concatenate(totals, axis=1)
    return (total * lax.rsqrt(summed * (1.0 / GROUP_WIDTH) + EPS) * gain).astype(jnp.bfloat16)


def solution(mesh):
    in_specs = (
        P(("dp", "ctx"), None),
        P(("dp", "ctx"), None),
        P(),
        P(),
        P(("dp", "ctx"), None),
        P(("dp", "ctx"), None),
        P(),
        P(),
    )
    out_specs = P("dp", "ctx")
    return jax.shard_map(
        per_device, mesh=mesh, in_specs=in_specs, out_specs=out_specs, check_vma=False
    )
```

```python
import functools

import jax
import jax.numpy as jnp
from jax import lax
from jax.experimental import pallas as pl
from jax.experimental.pallas import tpu as pltpu
from jax.sharding import PartitionSpec as P

HEADS = 128
HEAD_DIM = 64
STATE = 128
GROUPS = 8
KW = 4
BLOCK = 128
GROUP_WIDTH = HEADS * HEAD_DIM // GROUPS
EPS = 1e-05
HALO = 8
LANES = 128
FIELDS = 4
STRIP = 64
PACK_VMEM = 58 * 1024 * 1024
VMEM_LIMIT = 32 * 1024 * 1024


def contract(a, b, dims):
    return lax.dot_general(a, b, (dims, ((), ())), preferred_element_type=jnp.float32)


def as_parts(v, count):
    parts = []
    for _ in range(count):
        part = v.astype(jnp.bfloat16)
        parts.append(part)
        v = v - part.astype(jnp.float32)
    return parts


def pack_kernel(peers, span, offset, width, heads, first, codes, *refs):
    refs = list(refs)
    me = refs.pop(0)[0]
    x_ref = refs.pop(0)
    if first:
        kq_ref, decay_ref, step_ref = refs[:3]
        del refs[:3]
    outs = refs[: len(codes)]
    del refs[: len(codes)]
    if first:
        raw_scalars, scalars, kq_near = refs[:3]
    sems = refs[-1]
    rows = x_ref.shape[0]
    owned = HEADS * HEAD_DIM // peers
    copies = []
    if first:
        loads = [
            pltpu.make_async_copy(ref, raw_scalars.at[i], sems.at[3, i])
            for i, ref in enumerate((decay_ref, step_ref))
        ]
        loads.append(pltpu.make_async_copy(kq_ref, kq_near, sems.at[3, 2]))
        for load in loads:
            load.start()
    for i, code in enumerate(codes):
        owner = me ^ code
        column = pl.multiple_of(owner * owned + offset, LANES)
        copies.append(
            pltpu.make_async_copy(
                x_ref.at[:, pl.ds(column, width)],
                outs[i].at[0:rows, 0:width],
                sems.at[0, i],
            )
        )
    for copy in copies:
        copy.start()
    if first:
        for load in loads:
            load.wait()
        fields = as_parts(raw_scalars[0].T, 2) + as_parts(raw_scalars[1].T, 2)
        for p, field in enumerate(fields):
            field = field.astype(jnp.float32)
            for owner in range(peers):
                scalars[p, owner] = field[owner * heads : (owner + 1) * heads]
        across = outs[0].shape[1] // rows
        for i, code in enumerate(codes):
            owner = me ^ code
            outs[i][rows:] = jnp.zeros((outs[i].shape[0] - rows, outs[i].shape[1]), jnp.bfloat16)
            for p in range(FIELDS):
                top = rows + p // across * heads
                left = p % across * rows
                outs[i][top : top + heads, left : left + rows] = scalars[p, owner].astype(
                    jnp.bfloat16
                )
            for j in range(2):
                column = pl.multiple_of((j * GROUPS + owner // span) * STATE, LANES)
                left = width + j * STATE
                outs[i][0:rows, left : left + STATE] = kq_near[:, pl.ds(column, STATE)]
    for copy in copies:
        copy.wait()


def mixer_kernel(peers, rows, heads, chunk, widths, whole_group, *refs):
    refs = list(refs)

    def take(count):
        taken = refs[:count]
        del refs[:count]
        return taken

    first = chunk == 0
    final = chunk == len(widths) - 1 and whole_group
    later = range(1, len(widths)) if first else ()
    width = widths[chunk]
    (me_ref,) = take(1)
    parts = take(peers)
    taps_ref, skip_ref = take(2)
    if not first:
        left_ref, b_ref, inward_ref, outward_ref, power_ref = take(5)
    if final:
        (gain_ref,) = take(1)
        earlier = take(chunk)
        (out_ref,) = take(1)
    else:
        total_ref, sums_ref = take(2)
    if first and later:
        left_ref, b_ref = take(2)
        inward_refs = take(len(later))
        outward_refs = take(len(later))
    wide, carry = take(2)
    if final:
        (total_ref,) = take(1)
    if first:
        (scalars,) = take(1)
    blocks = rows // BLOCK
    step = pl.program_id(0)
    me = me_ref[0]
    scale_rows = rows + 16 * blocks
    base = pl.multiple_of(step * rows, rows)
    scale_base = pl.multiple_of(step * scale_rows, 32)

    @pl.when(step == 0)
    def _():
        carry[...] = jnp.zeros_like(carry)
        wide[rows : rows + HALO] = jnp.zeros((HALO, wide.shape[1]), jnp.float32)

    wide[0:HALO] = wide[rows : rows + HALO]
    slot = me ^ step
    for k in range(peers):

        @pl.when(slot == k)
        def _():
            wide[HALO : HALO + rows] = parts[k][0:rows].astype(jnp.float32)
            if first:
                scalars[...] = parts[k][rows:]

    def spread(count):
        head_of = lax.broadcasted_iota(jnp.int32, (2 * count, count * HEAD_DIM), 1) // HEAD_DIM
        row = lax.rem(
            lax.broadcasted_iota(jnp.int32, (2 * count, count * HEAD_DIM), 0), count
        )
        return jnp.where(head_of == row, 1.0, 0.0).astype(jnp.bfloat16)

    def activated(top, size, lo, hi):
        rows_out = []
        for r in range(top, top + size, STRIP):
            lanes_out = []
            for lane in range(lo, hi, LANES):
                tap = [taps_ref[k : k + 1, lane : lane + LANES] for k in range(KW)]
                now = wide[r : r + STRIP + HALO, lane : lane + LANES]
                before = pltpu.roll(now, 1, 0)
                older = pltpu.roll(tap[0] * before + tap[1] * now, 2, 0)
                summed = (older + (tap[2] * before + tap[3] * now))[HALO:]
                lanes_out.append(
                    summed * pltpu.reciprocal(1.0 + jnp.exp(-summed), approx=True)
                )
            rows_out.append(jnp.concatenate(lanes_out, axis=1))
        return jnp.concatenate(rows_out, axis=0)

    if first:
        full = width + 2 * STATE
        across = full // rows
        row = lax.broadcasted_iota(jnp.int32, (rows, rows), 0)
        col = lax.broadcasted_iota(jnp.int32, (rows, rows), 1)
        lower = (row >= col) & (row // BLOCK == col // BLOCK)
        ones = jnp.where(lower, 1.0, 0.0).astype(jnp.bfloat16)
        eye = jnp.where(row == col, 1.0, 0.0).astype(jnp.bfloat16)

        def field(p):
            top = p // across * heads
            lane = p % across * rows
            return scalars[top : top + heads, lane : lane + rows]

        def by_rows(matrix, numbers):
            return sum(contract(matrix, field(p), ((1,), (1,))) for p in numbers)

        cumul = by_rows(ones, (0, 1))
        steps = by_rows(eye, (2, 3))
        middles = [
            cumul[b * BLOCK + BLOCK // 2 - 1 : b * BLOCK + BLOCK // 2] for b in range(blocks)
        ]
        middle = jnp.concatenate([jnp.broadcast_to(m, (BLOCK, heads)) for m in middles], axis=0)
        inward = as_parts(steps * jnp.exp(middle - cumul), 2)
        outward = as_parts(
            jnp.concatenate(
                [jnp.exp(cumul - middle)]
                + [jnp.broadcast_to(jnp.exp(m), (16, heads)) for m in middles],
                axis=0,
            ),
            2,
        )

        def chosen(halves, index):
            begin = sum(widths[:index]) // HEAD_DIM
            end = begin + widths[index] // HEAD_DIM
            return jnp.concatenate([half[:, begin:end] for half in halves], axis=1)

        bc = activated(0, rows, width, full).astype(jnp.bfloat16)
        b_part, c_part = bc[:, :STATE], bc[:, STATE:]
        scores = contract(c_part, b_part, ((1,), (1,)))
        scores = jnp.where(lower, scores, 0.0).astype(jnp.bfloat16)
        lefts = [
            jnp.concatenate(
                [
                    scores[b * BLOCK : (b + 1) * BLOCK, b * BLOCK : (b + 1) * BLOCK],
                    c_part[b * BLOCK : (b + 1) * BLOCK],
                ],
                axis=1,
            )
            for b in range(blocks)
        ]
        for index in later:
            inward_refs[index - 1][pl.ds(base, rows)] = chosen(inward, index)
            outward_refs[index - 1][pl.ds(scale_base, scale_rows)] = chosen(outward, index)
        if later:
            b_ref[pl.ds(base, rows)] = b_part
            for b in range(blocks):
                left_ref[pl.ds(base + b * BLOCK, BLOCK)] = lefts[b]
        inward = chosen(inward, 0)
        outward = chosen(outward, 0)
    else:
        inward = inward_ref[pl.ds(base, rows)]
        outward = outward_ref[pl.ds(scale_base, scale_rows)]
        b_part = b_ref[pl.ds(base, rows)]
        lefts = [left_ref[pl.ds(base + b * BLOCK, BLOCK)] for b in range(blocks)]

    tile = 2 * LANES if width % (2 * LANES) == 0 else LANES
    expand = spread(width // HEAD_DIM)
    for b in range(blocks):
        top = b * BLOCK
        extra = rows + 16 * b
        power = jnp.zeros((BLOCK, LANES), jnp.float32)
        if not first:
            power = power_ref[pl.ds(base + top, BLOCK)]
        for lo in range(0, width, tile):
            hi = lo + tile
            x_conv = activated(top, BLOCK, lo, hi)
            in_scale = contract(inward[top : top + BLOCK], expand[:, lo:hi], ((1,), (0,)))
            out_scale = contract(outward[top : top + BLOCK], expand[:, lo:hi], ((1,), (0,)))
            mid_scale = contract(outward[extra : extra + 16], expand[:, lo:hi], ((1,), (0,)))
            scaled = (x_conv * in_scale).astype(jnp.bfloat16)
            held = carry[:, lo:hi] * mid_scale[0:1]
            right = jnp.concatenate([scaled, held.astype(jnp.bfloat16)], axis=0)
            mixed = contract(lefts[b], right, ((1,), (0,)))
            total = mixed * out_scale + skip_ref[0:1, lo:hi] * x_conv
            if final:
                total_ref[top : top + BLOCK, lo:hi] = total
            else:
                total_ref[pl.ds(base + top, BLOCK), lo:hi] = total.astype(jnp.bfloat16)
            squares = total * total
            for lane in range(0, tile, LANES):
                power = power + squares[:, lane : lane + LANES]
            added = contract(b_part[top : top + BLOCK], scaled, ((0,), (0,)))
            carry[:, lo:hi] = (held + added) * out_scale[BLOCK - 1 : BLOCK]
        if final:
            summed = jnp.sum(power, axis=1, keepdims=True)
            norm = lax.rsqrt(summed * (1.0 / GROUP_WIDTH) + EPS)
            column = 0
            for index, size in enumerate(widths):
                if index < chunk:
                    block = earlier[index][pl.ds(base + top, BLOCK)].astype(jnp.float32)
                else:
                    block = total_ref[top : top + BLOCK]
                out_ref[top : top + BLOCK, column : column + size] = (
                    block * norm * gain_ref[0:1, column : column + size]
                ).astype(jnp.bfloat16)
                column += size
        else:
            sums_ref[pl.ds(base + top, BLOCK)] = power


def per_device(inputs, key_query, conv_inputs, conv_kq, step_size, decay_log, skip_gain, norm_gain):
    peers = lax.axis_size("ctx")
    me = lax.axis_index("ctx")
    place = me.reshape(1).astype(jnp.int32)
    rows = inputs.shape[0]
    owned = HEADS * HEAD_DIM // peers
    heads = HEADS // peers
    span = GROUP_WIDTH // owned
    whole_group = span == 1
    total_rows = peers * rows
    blocks = rows // BLOCK
    tiles = owned // LANES
    last = max(1, tiles // 4)
    widths = [(tiles - last) * LANES, last * LANES]
    offsets = [0, widths[0]]

    smem = pl.BlockSpec(memory_space=pltpu.SMEM)
    hbm = pl.BlockSpec(memory_space=pltpu.HBM)
    vmem = pl.BlockSpec(memory_space=pltpu.VMEM)
    params = pltpu.CompilerParams(vmem_limit_bytes=VMEM_LIMIT)

    def columns(a, first, size):
        return lax.dynamic_slice_in_dim(a, first, size, axis=1)

    def pack(place, chunk, codes):
        width = widths[chunk]
        first = chunk == 0
        cols = width + (2 * STATE if first else 0)
        extra = 0
        if first:
            lines = -(-FIELDS // (cols // rows)) * heads
            extra = -(-lines // 16) * 16
        shape = jax.ShapeDtypeStruct((rows + extra, cols), jnp.bfloat16)
        operands = [place, inputs]
        in_specs = [smem, hbm]
        scratch = []
        if first:
            operands += [key_query, decay_log, step_size]
            in_specs += [hbm] * 3
            scratch.append(pltpu.VMEM((2, rows, HEADS), jnp.float32))
            scratch.append(pltpu.VMEM((FIELDS, peers, heads, rows), jnp.float32))
            scratch.append(pltpu.VMEM(key_query.shape, jnp.bfloat16))
        scratch.append(pltpu.SemaphoreType.DMA((4, peers)))
        return pl.pallas_call(
            functools.partial(
                pack_kernel, peers, span, offsets[chunk], width, heads, first, codes
            ),
            in_specs=in_specs,
            out_specs=[vmem] * len(codes),
            out_shape=[shape] * len(codes),
            scratch_shapes=scratch,
            compiler_params=pltpu.CompilerParams(vmem_limit_bytes=PACK_VMEM),
            cost_estimate=pl.CostEstimate(
                flops=0, bytes_accessed=4 * len(codes) * rows * cols, transcendentals=0
            ),
            name=f"pack{chunk}",
        )(*operands)

    def send(message, code, after):
        if after is not None:
            message, _ = lax.optimization_barrier((message, after))
        pairs = [(i, i ^ code) for i in range(peers)]
        return lax.ppermute(message, "ctx", pairs)

    far = list(range(peers - 1, peers // 2 - 1, -1))
    near = list(range(peers // 2 - 1, 0, -1))
    messages = {}
    for chunk, codes in ((0, far), (0, near + [0]), (1, far + near + [0])):
        packed = list(pack(place, chunk, tuple(codes)))
        packed[0], place = lax.optimization_barrier((packed[0], place))
        for code, message in zip(codes, packed):
            messages[chunk, code] = message
    received = [[messages[chunk, code] for code in range(peers)] for chunk in range(2)]
    for chunk in range(2):
        for code in far + near:
            after = received[0][code] if chunk else None
            received[chunk][code] = send(messages[chunk, code], code, after)

    taps_x = columns(conv_inputs, me * owned, owned)
    group = me // span
    taps_kq = jnp.concatenate(
        [
            columns(conv_kq, group * STATE, STATE),
            columns(conv_kq, (GROUPS + group) * STATE, STATE),
        ],
        axis=1,
    )
    skip = jnp.repeat(lax.dynamic_slice_in_dim(skip_gain, me * heads, heads), HEAD_DIM)[None]
    gain = columns(norm_gain[None], me * owned, owned)

    def by_source(count, lanes, dtype):
        spec = pl.BlockSpec((count, lanes), lambda i: (i, 0))
        return spec, jax.ShapeDtypeStruct((peers * count, lanes), dtype)

    def whole(count, lanes, dtype):
        return vmem, jax.ShapeDtypeStruct((peers * count, lanes), dtype)

    totals = []
    power = None
    shared = None
    for chunk, width in enumerate(widths):
        first = chunk == 0
        final = chunk == len(widths) - 1 and whole_group
        taps = taps_x[:, offsets[chunk] : offsets[chunk] + width]
        if first:
            taps = jnp.concatenate([taps, taps_kq], axis=1)
        cols = taps.shape[1]
        operands = [place, *received[chunk], taps, skip[:, offsets[chunk] : offsets[chunk] + width]]
        if not first:
            left, b_part, inward, outward = shared
            operands += [left, b_part, inward[chunk - 1], outward[chunk - 1], power]
        if final:
            operands += [gain, *totals]
        out = []
        if final:
            out.append(by_source(rows, owned, jnp.bfloat16))
        else:
            out.append(whole(rows, width, jnp.bfloat16))
            out.append(whole(rows, LANES, jnp.float32))
        if first:
            out.append(whole(rows, 2 * STATE, jnp.bfloat16))
            out.append(whole(rows, STATE, jnp.bfloat16))
            for count in (rows, rows + 16 * blocks):
                for size in widths[1:]:
                    out.append(whole(count, 2 * size // HEAD_DIM, jnp.bfloat16))
        scratch = [
            pltpu.VMEM((rows + HALO, cols), jnp.float32),
            pltpu.VMEM((STATE, width), jnp.float32),
        ]
        if final:
            scratch.append(pltpu.VMEM((rows, width), jnp.float32))
        if first:
            scratch.append(pltpu.VMEM((received[0][0].shape[0] - rows, cols), jnp.bfloat16))
        results = pl.pallas_call(
            functools.partial(mixer_kernel, peers, rows, heads, chunk, widths, whole_group),
            grid=(peers,),
            in_specs=[smem] + [vmem] * (len(operands) - 1),
            out_specs=[spec for spec, _ in out],
            out_shape=[shape for _, shape in out],
            scratch_shapes=scratch,
            compiler_params=params,
            cost_estimate=pl.CostEstimate(
                flops=2 * total_rows * width * 450,
                bytes_accessed=total_rows * (2 * cols + 8 * width),
                transcendentals=total_rows * cols,
            ),
            name=f"mixer{chunk}",
        )(*operands)
        if final:
            return results[0]
        totals.append(results[0])
        power = results[1]
        if first:
            rest = results[4:]
            shared = (results[2], results[3], rest[: len(rest) // 2], rest[len(rest) // 2 :])
    sharers = [list(range(i, i + span)) for i in range(0, peers, span)]
    summed = jnp.sum(power, axis=1, keepdims=True)
    summed = lax.psum(summed, "ctx", axis_index_groups=sharers)
    total = jnp.concatenate(totals, axis=1)
    return (total * lax.rsqrt(summed * (1.0 / GROUP_WIDTH) + EPS) * gain).astype(jnp.bfloat16)


def solution(mesh):
    in_specs = (
        P(("dp", "ctx"), None),
        P(("dp", "ctx"), None),
        P(),
        P(),
        P(("dp", "ctx"), None),
        P(("dp", "ctx"), None),
        P(),
        P(),
    )
    out_specs = P("dp", "ctx")
    return jax.shard_map(
        per_device, mesh=mesh, in_specs=in_specs, out_specs=out_specs, check_vma=False
    )
```

```python
import functools

import jax
import jax.numpy as jnp
from jax import lax
from jax.experimental import pallas as pl
from jax.experimental.pallas import tpu as pltpu
from jax.sharding import PartitionSpec as P

HEADS = 128
HEAD_DIM = 64
STATE = 128
GROUPS = 8
KW = 4
BLOCK = 128
GROUP_WIDTH = HEADS * HEAD_DIM // GROUPS
EPS = 1e-05
HALO = 16
LANES = 128
FIELDS = 4
STRIP = 64
PACK_VMEM = 58 * 1024 * 1024
VMEM_LIMIT = 32 * 1024 * 1024


def contract(a, b, dims):
    return lax.dot_general(a, b, (dims, ((), ())), preferred_element_type=jnp.float32)


def as_parts(v, count):
    parts = []
    for _ in range(count):
        part = v.astype(jnp.bfloat16)
        parts.append(part)
        v = v - part.astype(jnp.float32)
    return parts


def pack_kernel(peers, span, offset, width, heads, first, codes, *refs):
    refs = list(refs)
    me = refs.pop(0)[0]
    x_ref = refs.pop(0)
    if first:
        kq_ref, decay_ref, step_ref = refs[:3]
        del refs[:3]
    outs = refs[: len(codes)]
    del refs[: len(codes)]
    if first:
        raw_scalars, scalars, kq_near = refs[:3]
    sems = refs[-1]
    rows = x_ref.shape[0]
    owned = HEADS * HEAD_DIM // peers
    copies = []
    if first:
        loads = [
            pltpu.make_async_copy(ref, raw_scalars.at[i], sems.at[3, i])
            for i, ref in enumerate((decay_ref, step_ref))
        ]
        loads.append(pltpu.make_async_copy(kq_ref, kq_near, sems.at[3, 2]))
        for load in loads:
            load.start()
    for i, code in enumerate(codes):
        owner = me ^ code
        column = pl.multiple_of(owner * owned + offset, LANES)
        copies.append(
            pltpu.make_async_copy(
                x_ref.at[:, pl.ds(column, width)],
                outs[i].at[0:rows, 0:width],
                sems.at[0, i],
            )
        )
    for copy in copies:
        copy.start()
    if first:
        for load in loads:
            load.wait()
        fields = as_parts(raw_scalars[0].T, 2) + as_parts(raw_scalars[1].T, 2)
        for p, field in enumerate(fields):
            field = field.astype(jnp.float32)
            for owner in range(peers):
                scalars[p, owner] = field[owner * heads : (owner + 1) * heads]
        across = outs[0].shape[1] // rows
        for i, code in enumerate(codes):
            owner = me ^ code
            outs[i][rows:] = jnp.zeros((outs[i].shape[0] - rows, outs[i].shape[1]), jnp.bfloat16)
            for p in range(FIELDS):
                top = rows + p // across * heads
                left = p % across * rows
                outs[i][top : top + heads, left : left + rows] = scalars[p, owner].astype(
                    jnp.bfloat16
                )
            for j in range(2):
                column = pl.multiple_of((j * GROUPS + owner // span) * STATE, LANES)
                left = width + j * STATE
                outs[i][0:rows, left : left + STATE] = kq_near[:, pl.ds(column, STATE)]
    for copy in copies:
        copy.wait()


def mixer_kernel(peers, rows, heads, chunk, widths, whole_group, *refs):
    refs = list(refs)

    def take(count):
        taken = refs[:count]
        del refs[:count]
        return taken

    first = chunk == 0
    final = chunk == len(widths) - 1 and whole_group
    later = range(1, len(widths)) if first else ()
    width = widths[chunk]
    (me_ref,) = take(1)
    parts = take(peers)
    taps_ref, skip_ref = take(2)
    if not first:
        left_ref, b_ref, inward_ref, outward_ref, power_ref = take(5)
    if final:
        (gain_ref,) = take(1)
        earlier = take(chunk)
        (out_ref,) = take(1)
    else:
        total_ref, sums_ref = take(2)
    if first and later:
        left_ref, b_ref = take(2)
        inward_refs = take(len(later))
        outward_refs = take(len(later))
    wide, carry = take(2)
    if final:
        (total_ref,) = take(1)
    if first:
        (scalars,) = take(1)
    blocks = rows // BLOCK
    step = pl.program_id(0)
    me = me_ref[0]
    scale_rows = rows + 16 * blocks
    base = pl.multiple_of(step * rows, rows)
    scale_base = pl.multiple_of(step * scale_rows, 32)

    @pl.when(step == 0)
    def _():
        carry[...] = jnp.zeros_like(carry)
        wide[rows : rows + HALO] = jnp.zeros((HALO, wide.shape[1]), jnp.bfloat16)

    wide[0:HALO] = wide[rows : rows + HALO]
    slot = me ^ step
    for k in range(peers):

        @pl.when(slot == k)
        def _():
            wide[HALO : HALO + rows] = parts[k][0:rows]
            if first:
                scalars[...] = parts[k][rows:]

    def spread(count):
        head_of = lax.broadcasted_iota(jnp.int32, (2 * count, count * HEAD_DIM), 1) // HEAD_DIM
        row = lax.rem(
            lax.broadcasted_iota(jnp.int32, (2 * count, count * HEAD_DIM), 0), count
        )
        return jnp.where(head_of == row, 1.0, 0.0).astype(jnp.bfloat16)

    def activated(top, size, lo, hi):
        rows_out = []
        for r in range(top, top + size, STRIP):
            lanes_out = []
            for lane in range(lo, hi, LANES):
                tap = [taps_ref[k : k + 1, lane : lane + LANES] for k in range(KW)]
                now = wide[r : r + STRIP + HALO, lane : lane + LANES].astype(jnp.float32)[HALO // 2 :]
                before = pltpu.roll(now, 1, 0)
                older = pltpu.roll(tap[0] * before + tap[1] * now, 2, 0)
                summed = (older + (tap[2] * before + tap[3] * now))[HALO // 2 :]
                lanes_out.append(
                    summed * pltpu.reciprocal(1.0 + jnp.exp(-summed), approx=True)
                )
            rows_out.append(jnp.concatenate(lanes_out, axis=1))
        return jnp.concatenate(rows_out, axis=0)

    if first:
        full = width + 2 * STATE
        across = full // rows
        row = lax.broadcasted_iota(jnp.int32, (rows, rows), 0)
        col = lax.broadcasted_iota(jnp.int32, (rows, rows), 1)
        lower = (row >= col) & (row // BLOCK == col // BLOCK)
        ones = jnp.where(lower, 1.0, 0.0).astype(jnp.bfloat16)
        eye = jnp.where(row == col, 1.0, 0.0).astype(jnp.bfloat16)

        def field(p):
            top = p // across * heads
            lane = p % across * rows
            return scalars[top : top + heads, lane : lane + rows]

        def by_rows(matrix, numbers):
            return sum(contract(matrix, field(p), ((1,), (1,))) for p in numbers)

        cumul = by_rows(ones, (0, 1))
        steps = by_rows(eye, (2, 3))
        middles = [
            cumul[b * BLOCK + BLOCK // 2 - 1 : b * BLOCK + BLOCK // 2] for b in range(blocks)
        ]
        middle = jnp.concatenate([jnp.broadcast_to(m, (BLOCK, heads)) for m in middles], axis=0)
        inward = as_parts(steps * jnp.exp(middle - cumul), 2)
        outward = as_parts(
            jnp.concatenate(
                [jnp.exp(cumul - middle)]
                + [jnp.broadcast_to(jnp.exp(m), (16, heads)) for m in middles],
                axis=0,
            ),
            2,
        )

        def chosen(halves, index):
            begin = sum(widths[:index]) // HEAD_DIM
            end = begin + widths[index] // HEAD_DIM
            return jnp.concatenate([half[:, begin:end] for half in halves], axis=1)

        bc = activated(0, rows, width, full).astype(jnp.bfloat16)
        b_part, c_part = bc[:, :STATE], bc[:, STATE:]
        scores = contract(c_part, b_part, ((1,), (1,)))
        scores = jnp.where(lower, scores, 0.0).astype(jnp.bfloat16)
        lefts = [
            jnp.concatenate(
                [
                    scores[b * BLOCK : (b + 1) * BLOCK, b * BLOCK : (b + 1) * BLOCK],
                    c_part[b * BLOCK : (b + 1) * BLOCK],
                ],
                axis=1,
            )
            for b in range(blocks)
        ]
        for index in later:
            inward_refs[index - 1][pl.ds(base, rows)] = chosen(inward, index)
            outward_refs[index - 1][pl.ds(scale_base, scale_rows)] = chosen(outward, index)
        if later:
            b_ref[pl.ds(base, rows)] = b_part
            for b in range(blocks):
                left_ref[pl.ds(base + b * BLOCK, BLOCK)] = lefts[b]
        inward = chosen(inward, 0)
        outward = chosen(outward, 0)
    else:
        inward = inward_ref[pl.ds(base, rows)]
        outward = outward_ref[pl.ds(scale_base, scale_rows)]
        b_part = b_ref[pl.ds(base, rows)]
        lefts = [left_ref[pl.ds(base + b * BLOCK, BLOCK)] for b in range(blocks)]

    tile = 2 * LANES if width % (2 * LANES) == 0 else LANES
    expand = spread(width // HEAD_DIM)
    compact = [
        jnp.concatenate(
            [
                inward[b * BLOCK : (b + 1) * BLOCK],
                outward[b * BLOCK : (b + 1) * BLOCK],
                outward[rows + 16 * b : rows + 16 * (b + 1)],
            ],
            axis=0,
        )
        for b in range(blocks)
    ]
    for b in range(blocks):
        top = b * BLOCK
        power = jnp.zeros((BLOCK, LANES), jnp.float32)
        if not first:
            power = power_ref[pl.ds(base + top, BLOCK)]
        for lo in range(0, width, tile):
            hi = lo + tile
            x_conv = activated(top, BLOCK, lo, hi)
            scales = contract(compact[b], expand[:, lo:hi], ((1,), (0,)))
            in_scale = scales[:BLOCK]
            out_scale = scales[BLOCK : 2 * BLOCK]
            mid_scale = scales[2 * BLOCK :]
            scaled = (x_conv * in_scale).astype(jnp.bfloat16)
            held = carry[:, lo:hi] * mid_scale[0:1]
            right = jnp.concatenate([scaled, held.astype(jnp.bfloat16)], axis=0)
            mixed = contract(lefts[b], right, ((1,), (0,)))
            total = mixed * out_scale + skip_ref[0:1, lo:hi] * x_conv
            if final:
                total_ref[top : top + BLOCK, lo:hi] = total
            else:
                total_ref[pl.ds(base + top, BLOCK), lo:hi] = total.astype(jnp.bfloat16)
            squares = total * total
            for lane in range(0, tile, LANES):
                power = power + squares[:, lane : lane + LANES]
            added = contract(b_part[top : top + BLOCK], scaled, ((0,), (0,)))
            carry[:, lo:hi] = (held + added) * out_scale[BLOCK - 1 : BLOCK]
        if final:
            summed = jnp.sum(power, axis=1, keepdims=True)
            norm = lax.rsqrt(summed * (1.0 / GROUP_WIDTH) + EPS)
            column = 0
            for index, size in enumerate(widths):
                if index < chunk:
                    block = earlier[index][pl.ds(base + top, BLOCK)].astype(jnp.float32)
                else:
                    block = total_ref[top : top + BLOCK]
                out_ref[top : top + BLOCK, column : column + size] = (
                    block * norm * gain_ref[0:1, column : column + size]
                ).astype(jnp.bfloat16)
                column += size
        else:
            sums_ref[pl.ds(base + top, BLOCK)] = power


def per_device(inputs, key_query, conv_inputs, conv_kq, step_size, decay_log, skip_gain, norm_gain):
    peers = lax.axis_size("ctx")
    me = lax.axis_index("ctx")
    place = me.reshape(1).astype(jnp.int32)
    rows = inputs.shape[0]
    owned = HEADS * HEAD_DIM // peers
    heads = HEADS // peers
    span = GROUP_WIDTH // owned
    whole_group = span == 1
    total_rows = peers * rows
    blocks = rows // BLOCK
    tiles = owned // LANES
    last = max(1, tiles // 4)
    widths = [(tiles - last) * LANES, last * LANES]
    offsets = [0, widths[0]]

    smem = pl.BlockSpec(memory_space=pltpu.SMEM)
    hbm = pl.BlockSpec(memory_space=pltpu.HBM)
    vmem = pl.BlockSpec(memory_space=pltpu.VMEM)
    params = pltpu.CompilerParams(vmem_limit_bytes=VMEM_LIMIT)

    def columns(a, first, size):
        return lax.dynamic_slice_in_dim(a, first, size, axis=1)

    def pack(place, chunk, codes):
        width = widths[chunk]
        first = chunk == 0
        cols = width + (2 * STATE if first else 0)
        extra = 0
        if first:
            lines = -(-FIELDS // (cols // rows)) * heads
            extra = -(-lines // 16) * 16
        shape = jax.ShapeDtypeStruct((rows + extra, cols), jnp.bfloat16)
        operands = [place, inputs]
        in_specs = [smem, hbm]
        scratch = []
        if first:
            operands += [key_query, decay_log, step_size]
            in_specs += [hbm] * 3
            scratch.append(pltpu.VMEM((2, rows, HEADS), jnp.float32))
            scratch.append(pltpu.VMEM((FIELDS, peers, heads, rows), jnp.float32))
            scratch.append(pltpu.VMEM(key_query.shape, jnp.bfloat16))
        scratch.append(pltpu.SemaphoreType.DMA((4, peers)))
        return pl.pallas_call(
            functools.partial(
                pack_kernel, peers, span, offsets[chunk], width, heads, first, codes
            ),
            in_specs=in_specs,
            out_specs=[vmem] * len(codes),
            out_shape=[shape] * len(codes),
            scratch_shapes=scratch,
            compiler_params=pltpu.CompilerParams(vmem_limit_bytes=PACK_VMEM),
            cost_estimate=pl.CostEstimate(
                flops=0, bytes_accessed=4 * len(codes) * rows * cols, transcendentals=0
            ),
            name=f"pack{chunk}",
        )(*operands)

    def send(message, code):
        pairs = [(i, i ^ code) for i in range(peers)]
        return lax.ppermute(message, "ctx", pairs)

    far = list(range(peers - 1, peers // 2 - 1, -1))
    near = list(range(peers // 2 - 1, 0, -1))
    received = [{}, {}]

    def exchange(chunk, codes, after):
        token, _ = lax.optimization_barrier((place, after))
        for code, message in zip(codes, pack(token, chunk, tuple(codes))):
            received[chunk][code] = send(message, code) if code else message

    exchange(0, far, ())
    exchange(0, near + [0], [received[0][far[0]]])
    exchange(1, near + [0], [received[0][code] for code in near + far[1:2]])
    exchange(1, far, [received[1][code] for code in near] + [received[0][far[2]]])
    received = [[slots[code] for code in range(peers)] for slots in received]

    taps_x = columns(conv_inputs, me * owned, owned)
    group = me // span
    taps_kq = jnp.concatenate(
        [
            columns(conv_kq, group * STATE, STATE),
            columns(conv_kq, (GROUPS + group) * STATE, STATE),
        ],
        axis=1,
    )
    skip = jnp.repeat(lax.dynamic_slice_in_dim(skip_gain, me * heads, heads), HEAD_DIM)[None]
    gain = columns(norm_gain[None], me * owned, owned)

    def by_source(count, lanes, dtype):
        spec = pl.BlockSpec((count, lanes), lambda i: (i, 0))
        return spec, jax.ShapeDtypeStruct((peers * count, lanes), dtype)

    def whole(count, lanes, dtype):
        return vmem, jax.ShapeDtypeStruct((peers * count, lanes), dtype)

    totals = []
    power = None
    shared = None
    for chunk, width in enumerate(widths):
        first = chunk == 0
        final = chunk == len(widths) - 1 and whole_group
        taps = taps_x[:, offsets[chunk] : offsets[chunk] + width]
        if first:
            taps = jnp.concatenate([taps, taps_kq], axis=1)
        cols = taps.shape[1]
        operands = [place, *received[chunk], taps, skip[:, offsets[chunk] : offsets[chunk] + width]]
        if not first:
            left, b_part, inward, outward = shared
            operands += [left, b_part, inward[chunk - 1], outward[chunk - 1], power]
        if final:
            operands += [gain, *totals]
        out = []
        if final:
            out.append(by_source(rows, owned, jnp.bfloat16))
        else:
            out.append(whole(rows, width, jnp.bfloat16))
            out.append(whole(rows, LANES, jnp.float32))
        if first:
            out.append(whole(rows, 2 * STATE, jnp.bfloat16))
            out.append(whole(rows, STATE, jnp.bfloat16))
            for count in (rows, rows + 16 * blocks):
                for size in widths[1:]:
                    out.append(whole(count, 2 * size // HEAD_DIM, jnp.bfloat16))
        scratch = [
            pltpu.VMEM((rows + HALO, cols), jnp.bfloat16),
            pltpu.VMEM((STATE, width), jnp.float32),
        ]
        if final:
            scratch.append(pltpu.VMEM((rows, width), jnp.float32))
        if first:
            scratch.append(pltpu.VMEM((received[0][0].shape[0] - rows, cols), jnp.bfloat16))
        results = pl.pallas_call(
            functools.partial(mixer_kernel, peers, rows, heads, chunk, widths, whole_group),
            grid=(peers,),
            in_specs=[smem] + [vmem] * (len(operands) - 1),
            out_specs=[spec for spec, _ in out],
            out_shape=[shape for _, shape in out],
            scratch_shapes=scratch,
            compiler_params=params,
            cost_estimate=pl.CostEstimate(
                flops=2 * total_rows * width * 450,
                bytes_accessed=total_rows * (2 * cols + 8 * width),
                transcendentals=total_rows * cols,
            ),
            name=f"mixer{chunk}",
        )(*operands)
        if final:
            return results[0]
        totals.append(results[0])
        power = results[1]
        if first:
            rest = results[4:]
            shared = (results[2], results[3], rest[: len(rest) // 2], rest[len(rest) // 2 :])
    sharers = [list(range(i, i + span)) for i in range(0, peers, span)]
    summed = jnp.sum(power, axis=1, keepdims=True)
    summed = lax.psum(summed, "ctx", axis_index_groups=sharers)
    total = jnp.concatenate(totals, axis=1)
    return (total * lax.rsqrt(summed * (1.0 / GROUP_WIDTH) + EPS) * gain).astype(jnp.bfloat16)


def solution(mesh):
    in_specs = (
        P(("dp", "ctx"), None),
        P(("dp", "ctx"), None),
        P(),
        P(),
        P(("dp", "ctx"), None),
        P(("dp", "ctx"), None),
        P(),
        P(),
    )
    out_specs = P("dp", "ctx")
    return jax.shard_map(
        per_device, mesh=mesh, in_specs=in_specs, out_specs=out_specs, check_vma=False
    )
```

```python
import functools
import math

import jax
import jax.numpy as jnp
from jax import lax
from jax.experimental import pallas as pl
from jax.experimental.pallas import tpu as pltpu
from jax.sharding import PartitionSpec as P

HEADS = 128
HEAD_DIM = 64
STATE = 128
GROUPS = 8
KW = 4
BLOCK = 128
GROUP_WIDTH = HEADS * HEAD_DIM // GROUPS
EPS = 1e-05
HALO = 16
LANES = 128
FIELDS = 3
STRIP = 64
PACK_VMEM = 58 * 1024 * 1024
VMEM_LIMIT = 32 * 1024 * 1024


def contract(a, b, dims):
    return lax.dot_general(a, b, (dims, ((), ())), preferred_element_type=jnp.float32)


def as_parts(v, count):
    parts = []
    for _ in range(count):
        part = v.astype(jnp.bfloat16)
        parts.append(part)
        v = v - part.astype(jnp.float32)
    return parts


def relative(me, ring, code):
    place = lax.rem(me // 2 + code // 2, ring)
    return 2 * place + ((me & 1) ^ (code & 1))


def pack_kernel(peers, span, widths, heads, entries, scalar_rows, *refs):
    refs = list(refs)
    me = refs.pop(0)[0]
    x_ref = refs.pop(0)
    heading = scalar_rows > 0
    if heading:
        kq_ref, decay_ref, step_ref = refs[:3]
        del refs[:3]
    outs = refs[: len(entries)]
    del refs[: len(entries)]
    if heading:
        raw_scalars, scalars, kq_near = refs[:3]
    sems = refs[-1]
    rows = x_ref.shape[0]
    owned = HEADS * HEAD_DIM // peers
    lead = widths[0] + 2 * STATE
    copies = []
    if heading:
        loads = [
            pltpu.make_async_copy(ref, raw_scalars.at[i], sems.at[2, i])
            for i, ref in enumerate((decay_ref, step_ref))
        ]
        loads.append(pltpu.make_async_copy(kq_ref, kq_near, sems.at[2, 2]))
        for load in loads:
            load.start()
    owners = [relative(me, peers // 2, code) for code, _ in entries]
    for i, (owner, (_, kind)) in enumerate(zip(owners, entries)):
        pieces = {
            "full": [(0, 0, 0), (1, widths[0], lead)],
            "lead": [(0, 0, 0)],
            "rest": [(1, widths[0], 0)],
        }[kind]
        for index, offset, left in pieces:
            column = pl.multiple_of(owner * owned + offset, LANES)
            copies.append(
                pltpu.make_async_copy(
                    x_ref.at[:, pl.ds(column, widths[index])],
                    outs[i].at[0:rows, left : left + widths[index]],
                    sems.at[index, i],
                )
            )
    for copy in copies:
        copy.start()
    if heading:
        for load in loads:
            load.wait()
        fields = as_parts(raw_scalars[0].T, 2) + as_parts(raw_scalars[1].T, 1)
        for p, field in enumerate(fields):
            field = field.astype(jnp.float32)
            for owner in range(peers):
                scalars[p, owner] = field[owner * heads : (owner + 1) * heads]
        across = lead // rows
        for i, owner in enumerate(owners):
            outs[i][rows:] = jnp.zeros((scalar_rows, outs[i].shape[1]), jnp.bfloat16)
            for p in range(FIELDS):
                top = rows + p // across * heads
                left = p % across * rows
                outs[i][top : top + heads, left : left + rows] = scalars[p, owner].astype(
                    jnp.bfloat16
                )
            for j in range(2):
                column = pl.multiple_of((j * GROUPS + owner // span) * STATE, LANES)
                left = widths[0] + j * STATE
                outs[i][0:rows, left : left + STATE] = kq_near[:, pl.ds(column, STATE)]
    for copy in copies:
        copy.wait()


def mixer_kernel(peers, rows, heads, chunk, widths, whole_group, *refs):
    refs = list(refs)

    def take(count):
        taken = refs[:count]
        del refs[:count]
        return taken

    first = chunk == 0
    final = chunk == len(widths) - 1 and whole_group
    later = range(1, len(widths)) if first else ()
    width = widths[chunk]
    (me_ref,) = take(1)
    parts = take(peers)
    taps_ref, skip_ref = take(2)
    if not first:
        left_ref, b_ref, inward_ref, outward_ref, power_ref = take(5)
    if final:
        (gain_ref,) = take(1)
        earlier = take(chunk)
        (out_ref,) = take(1)
    else:
        total_ref, sums_ref = take(2)
    if first and later:
        left_ref, b_ref = take(2)
        inward_refs = take(len(later))
        outward_refs = take(len(later))
    wide, carry = take(2)
    if final:
        (total_ref,) = take(1)
    if first:
        (scalars,) = take(1)
    blocks = rows // BLOCK
    step = pl.program_id(0)
    me = me_ref[0]
    scale_rows = rows + 16 * blocks
    base = pl.multiple_of(step * rows, rows)
    scale_base = pl.multiple_of(step * scale_rows, 32)

    @pl.when(step == 0)
    def _():
        carry[...] = jnp.zeros_like(carry)
        wide[rows : rows + HALO] = jnp.zeros((HALO, wide.shape[1]), jnp.bfloat16)

    wide[0:HALO] = wide[rows : rows + HALO]
    ring = peers // 2
    slot = 2 * lax.rem(me // 2 + (ring - step // 2), ring) + ((me ^ step) & 1)
    for k in range(peers):

        @pl.when(slot == k)
        def _():
            if first:
                wide[HALO : HALO + rows] = parts[k][0:rows, 0 : wide.shape[1]]
                scalars[...] = parts[k][rows:, 0 : wide.shape[1]]
            else:
                wide[HALO : HALO + rows] = parts[k][0:rows, parts[k].shape[1] - width :]

    def spread(count):
        head_of = lax.broadcasted_iota(jnp.int32, (2 * count, count * HEAD_DIM), 1) // HEAD_DIM
        row = lax.rem(
            lax.broadcasted_iota(jnp.int32, (2 * count, count * HEAD_DIM), 0), count
        )
        return jnp.where(head_of == row, 1.0, 0.0).astype(jnp.bfloat16)

    def activated(top, size, lo, hi):
        rows_out = []
        for r in range(top, top + size, STRIP):
            lanes_out = []
            for lane in range(lo, hi, LANES):
                tap = [taps_ref[k : k + 1, lane : lane + LANES] for k in range(KW)]
                now = wide[r : r + STRIP + HALO, lane : lane + LANES].astype(jnp.float32)[HALO // 2 :]
                before = pltpu.roll(now, 1, 0)
                older = pltpu.roll(tap[0] * before + tap[1] * now, 2, 0)
                summed = (older + (tap[2] * before + tap[3] * now))[HALO // 2 :]
                lanes_out.append(
                    summed * pltpu.reciprocal(1.0 + jnp.exp(-summed), approx=True)
                )
            rows_out.append(jnp.concatenate(lanes_out, axis=1))
        return jnp.concatenate(rows_out, axis=0)

    if first:
        full = width + 2 * STATE
        across = full // rows
        row = lax.broadcasted_iota(jnp.int32, (rows, rows), 0)
        col = lax.broadcasted_iota(jnp.int32, (rows, rows), 1)
        lower = (row >= col) & (row // BLOCK == col // BLOCK)
        ones = jnp.where(lower, 1.0, 0.0).astype(jnp.bfloat16)
        eye = jnp.where(row == col, 1.0, 0.0).astype(jnp.bfloat16)

        def field(p):
            top = p // across * heads
            lane = p % across * rows
            return scalars[top : top + heads, lane : lane + rows]

        def by_rows(matrix, numbers):
            return sum(contract(matrix, field(p), ((1,), (1,))) for p in numbers)

        cumul = by_rows(ones, (0, 1))
        steps = by_rows(eye, (2,))
        middles = [
            cumul[b * BLOCK + BLOCK // 2 - 1 : b * BLOCK + BLOCK // 2] for b in range(blocks)
        ]
        middle = jnp.concatenate([jnp.broadcast_to(m, (BLOCK, heads)) for m in middles], axis=0)
        inward = as_parts(steps * jnp.exp(middle - cumul), 2)
        outward = as_parts(
            jnp.concatenate(
                [jnp.exp(cumul - middle)]
                + [jnp.broadcast_to(jnp.exp(m), (16, heads)) for m in middles],
                axis=0,
            ),
            2,
        )

        def chosen(halves, index):
            begin = sum(widths[:index]) // HEAD_DIM
            end = begin + widths[index] // HEAD_DIM
            return jnp.concatenate([half[:, begin:end] for half in halves], axis=1)

        bc = activated(0, rows, width, full).astype(jnp.bfloat16)
        b_part, c_part = bc[:, :STATE], bc[:, STATE:]
        scores = contract(c_part, b_part, ((1,), (1,)))
        scores = jnp.where(lower, scores, 0.0).astype(jnp.bfloat16)
        lefts = [
            jnp.concatenate(
                [
                    scores[b * BLOCK : (b + 1) * BLOCK, b * BLOCK : (b + 1) * BLOCK],
                    c_part[b * BLOCK : (b + 1) * BLOCK],
                ],
                axis=1,
            )
            for b in range(blocks)
        ]
        for index in later:
            inward_refs[index - 1][pl.ds(base, rows)] = chosen(inward, index)
            outward_refs[index - 1][pl.ds(scale_base, scale_rows)] = chosen(outward, index)
        if later:
            b_ref[pl.ds(base, rows)] = b_part
            for b in range(blocks):
                left_ref[pl.ds(base + b * BLOCK, BLOCK)] = lefts[b]
        inward = chosen(inward, 0)
        outward = chosen(outward, 0)
    else:
        inward = inward_ref[pl.ds(base, rows)]
        outward = outward_ref[pl.ds(scale_base, scale_rows)]
        b_part = b_ref[pl.ds(base, rows)]
        lefts = [left_ref[pl.ds(base + b * BLOCK, BLOCK)] for b in range(blocks)]

    tile = 2 * LANES if width % (2 * LANES) == 0 else LANES
    expand = spread(width // HEAD_DIM)
    compact = [
        jnp.concatenate(
            [
                inward[b * BLOCK : (b + 1) * BLOCK],
                outward[b * BLOCK : (b + 1) * BLOCK],
                outward[rows + 16 * b : rows + 16 * (b + 1)],
            ],
            axis=0,
        )
        for b in range(blocks)
    ]
    for b in range(blocks):
        top = b * BLOCK
        power = jnp.zeros((BLOCK, LANES), jnp.float32)
        if not first:
            power = power_ref[pl.ds(base + top, BLOCK)]
        for lo in range(0, width, tile):
            hi = lo + tile
            x_conv = activated(top, BLOCK, lo, hi)
            scales = contract(compact[b], expand[:, lo:hi], ((1,), (0,)))
            in_scale = scales[:BLOCK]
            out_scale = scales[BLOCK : 2 * BLOCK]
            mid_scale = scales[2 * BLOCK :]
            scaled = (x_conv * in_scale).astype(jnp.bfloat16)
            held = carry[:, lo:hi] * mid_scale[0:1]
            right = jnp.concatenate([scaled, held.astype(jnp.bfloat16)], axis=0)
            mixed = contract(lefts[b], right, ((1,), (0,)))
            total = mixed * out_scale + skip_ref[0:1, lo:hi] * x_conv
            if final:
                total_ref[top : top + BLOCK, lo:hi] = total
            else:
                total_ref[pl.ds(base + top, BLOCK), lo:hi] = total.astype(jnp.bfloat16)
            squares = total * total
            for lane in range(0, tile, LANES):
                power = power + squares[:, lane : lane + LANES]
            added = contract(b_part[top : top + BLOCK], scaled, ((0,), (0,)))
            carry[:, lo:hi] = (held + added) * out_scale[BLOCK - 1 : BLOCK]
        if final:
            summed = jnp.sum(power, axis=1, keepdims=True)
            norm = lax.rsqrt(summed * (1.0 / GROUP_WIDTH) + EPS)
            column = 0
            for index, size in enumerate(widths):
                if index < chunk:
                    block = earlier[index][pl.ds(base + top, BLOCK)].astype(jnp.float32)
                else:
                    block = total_ref[top : top + BLOCK]
                out_ref[top : top + BLOCK, column : column + size] = (
                    block * norm * gain_ref[0:1, column : column + size]
                ).astype(jnp.bfloat16)
                column += size
        else:
            sums_ref[pl.ds(base + top, BLOCK)] = power


def per_device(inputs, key_query, conv_inputs, conv_kq, step_size, decay_log, skip_gain, norm_gain):
    peers = lax.axis_size("ctx")
    me = lax.axis_index("ctx")
    place = me.reshape(1).astype(jnp.int32)
    rows = inputs.shape[0]
    owned = HEADS * HEAD_DIM // peers
    heads = HEADS // peers
    span = GROUP_WIDTH // owned
    whole_group = span == 1
    total_rows = peers * rows
    blocks = rows // BLOCK
    tiles = owned // LANES
    last = max(1, tiles // 2)
    widths = [(tiles - last) * LANES, last * LANES]
    offsets = [0, widths[0]]

    smem = pl.BlockSpec(memory_space=pltpu.SMEM)
    hbm = pl.BlockSpec(memory_space=pltpu.HBM)
    vmem = pl.BlockSpec(memory_space=pltpu.VMEM)
    params = pltpu.CompilerParams(vmem_limit_bytes=VMEM_LIMIT)

    def columns(a, first, size):
        return lax.dynamic_slice_in_dim(a, first, size, axis=1)

    lead = widths[0] + 2 * STATE
    scalar_rows = -(-(-(-FIELDS // (lead // rows)) * heads) // 16) * 16
    extents = {
        "full": (rows + scalar_rows, lead + widths[1]),
        "lead": (rows + scalar_rows, lead),
        "rest": (rows, widths[1]),
    }

    def pack(entries, after=()):
        token, _ = lax.optimization_barrier((place, after))
        heading = entries[0][1] != "rest"
        shapes = [jax.ShapeDtypeStruct(extents[kind], jnp.bfloat16) for _, kind in entries]
        operands = [token, inputs]
        in_specs = [smem, hbm]
        scratch = []
        if heading:
            operands += [key_query, decay_log, step_size]
            in_specs += [hbm] * 3
            scratch.append(pltpu.VMEM((2, rows, HEADS), jnp.float32))
            scratch.append(pltpu.VMEM((FIELDS, peers, heads, rows), jnp.float32))
            scratch.append(pltpu.VMEM(key_query.shape, jnp.bfloat16))
        scratch.append(pltpu.SemaphoreType.DMA((3, max(3, len(entries)))))
        return pl.pallas_call(
            functools.partial(
                pack_kernel,
                peers,
                span,
                widths,
                heads,
                entries,
                scalar_rows if heading else 0,
            ),
            in_specs=in_specs,
            out_specs=[vmem] * len(entries),
            out_shape=shapes,
            scratch_shapes=scratch,
            compiler_params=pltpu.CompilerParams(vmem_limit_bytes=PACK_VMEM),
            cost_estimate=pl.CostEstimate(
                flops=0,
                bytes_accessed=4 * sum(math.prod(shape.shape) for shape in shapes),
                transcendentals=0,
            ),
            name="pack",
        )(*operands)

    def send(message, code, after=()):
        message, _ = lax.optimization_barrier((message, after))
        pairs = [
            (i, 2 * ((i // 2 + code // 2) % (peers // 2)) + (i % 2 ^ code % 2))
            for i in range(peers)
        ]
        return lax.ppermute(message, "ctx", pairs)

    if peers == 8:
        one, two = pack(((4, "full"), (5, "full")))
        one, two = send(one, 2), send(two, 6)
        leads = pack(
            ((2, "lead"), (6, "lead"), (3, "lead"), (7, "lead"), (1, "full"), (0, "full"))
        )
        rests = pack(((2, "rest"), (6, "rest"), (3, "rest"), (7, "rest")), (one, two))
        lead = {0: leads[5], 1: send(leads[4], 1), 2: send(leads[0], 2), 6: send(leads[1], 6)}
        lead[4] = send(one, 2)
        lead[5] = send(two, 7)
        lead[3] = send(leads[2], 3, lead[2])
        lead[7] = send(leads[3], 7, lead[6])
        rest = {code: lead[code] for code in (0, 1, 4, 5)}
        rest[2] = send(rests[0], 2, lead[2])
        rest[6] = send(rests[1], 6, lead[6])
        rest[3] = send(rests[2], 3, lead[3])
        rest[7] = send(rests[3], 7, lead[7])
    else:
        codes = range(2, peers)
        packed = pack(((0, "full"), (1, "full")) + tuple((code, "lead") for code in codes))
        lead = {code: send(message, code) for code, message in enumerate(packed)}
        packed = pack(tuple((code, "rest") for code in codes), lead[peers - 1])
        rest = {0: lead[0], 1: lead[1]}
        rest.update((code, send(message, code)) for code, message in zip(codes, packed))
    received = [[slots[code] for code in range(peers)] for slots in (lead, rest)]

    taps_x = columns(conv_inputs, me * owned, owned)
    group = me // span
    taps_kq = jnp.concatenate(
        [
            columns(conv_kq, group * STATE, STATE),
            columns(conv_kq, (GROUPS + group) * STATE, STATE),
        ],
        axis=1,
    )
    skip = jnp.repeat(lax.dynamic_slice_in_dim(skip_gain, me * heads, heads), HEAD_DIM)[None]
    gain = columns(norm_gain[None], me * owned, owned)

    def by_source(count, lanes, dtype):
        spec = pl.BlockSpec((count, lanes), lambda i: (i, 0))
        return spec, jax.ShapeDtypeStruct((peers * count, lanes), dtype)

    def whole(count, lanes, dtype):
        return vmem, jax.ShapeDtypeStruct((peers * count, lanes), dtype)

    totals = []
    power = None
    shared = None
    for chunk, width in enumerate(widths):
        first = chunk == 0
        final = chunk == len(widths) - 1 and whole_group
        taps = taps_x[:, offsets[chunk] : offsets[chunk] + width]
        if first:
            taps = jnp.concatenate([taps, taps_kq], axis=1)
        cols = taps.shape[1]
        operands = [place, *received[chunk], taps, skip[:, offsets[chunk] : offsets[chunk] + width]]
        if not first:
            left, b_part, inward, outward = shared
            operands += [left, b_part, inward[chunk - 1], outward[chunk - 1], power]
        if final:
            operands += [gain, *totals]
        out = []
        if final:
            out.append(by_source(rows, owned, jnp.bfloat16))
        else:
            out.append(whole(rows, width, jnp.bfloat16))
            out.append(whole(rows, LANES, jnp.float32))
        if first:
            out.append(whole(rows, 2 * STATE, jnp.bfloat16))
            out.append(whole(rows, STATE, jnp.bfloat16))
            for count in (rows, rows + 16 * blocks):
                for size in widths[1:]:
                    out.append(whole(count, 2 * size // HEAD_DIM, jnp.bfloat16))
        scratch = [
            pltpu.VMEM((rows + HALO, cols), jnp.bfloat16),
            pltpu.VMEM((STATE, width), jnp.float32),
        ]
        if final:
            scratch.append(pltpu.VMEM((rows, width), jnp.float32))
        if first:
            scratch.append(pltpu.VMEM((scalar_rows, cols), jnp.bfloat16))
        results = pl.pallas_call(
            functools.partial(mixer_kernel, peers, rows, heads, chunk, widths, whole_group),
            grid=(peers,),
            in_specs=[smem] + [vmem] * (len(operands) - 1),
            out_specs=[spec for spec, _ in out],
            out_shape=[shape for _, shape in out],
            scratch_shapes=scratch,
            compiler_params=params,
            cost_estimate=pl.CostEstimate(
                flops=2 * total_rows * width * 450,
                bytes_accessed=total_rows * (2 * cols + 8 * width),
                transcendentals=total_rows * cols,
            ),
            name=f"mixer{chunk}",
        )(*operands)
        if final:
            return results[0]
        totals.append(results[0])
        power = results[1]
        if first:
            rest = results[4:]
            shared = (results[2], results[3], rest[: len(rest) // 2], rest[len(rest) // 2 :])
    sharers = [list(range(i, i + span)) for i in range(0, peers, span)]
    summed = jnp.sum(power, axis=1, keepdims=True)
    summed = lax.psum(summed, "ctx", axis_index_groups=sharers)
    total = jnp.concatenate(totals, axis=1)
    return (total * lax.rsqrt(summed * (1.0 / GROUP_WIDTH) + EPS) * gain).astype(jnp.bfloat16)


def solution(mesh):
    in_specs = (
        P(("dp", "ctx"), None),
        P(("dp", "ctx"), None),
        P(),
        P(),
        P(("dp", "ctx"), None),
        P(("dp", "ctx"), None),
        P(),
        P(),
    )
    out_specs = P("dp", "ctx")
    return jax.shard_map(
        per_device, mesh=mesh, in_specs=in_specs, out_specs=out_specs, check_vma=False
    )
```

```python
import functools
import math

import jax
import jax.numpy as jnp
from jax import lax
from jax.experimental import pallas as pl
from jax.experimental.pallas import tpu as pltpu
from jax.sharding import PartitionSpec as P

HEADS = 128
HEAD_DIM = 64
STATE = 128
GROUPS = 8
KW = 4
BLOCK = 128
GROUP_WIDTH = HEADS * HEAD_DIM // GROUPS
EPS = 1e-05
HALO = 16
LANES = 128
FIELDS = 3
STRIP = 64
PACK_VMEM = 58 * 1024 * 1024
VMEM_LIMIT = 32 * 1024 * 1024


def contract(a, b, dims):
    return lax.dot_general(a, b, (dims, ((), ())), preferred_element_type=jnp.float32)


def as_parts(v, count):
    parts = []
    for _ in range(count):
        part = v.astype(jnp.bfloat16)
        parts.append(part)
        v = v - part.astype(jnp.float32)
    return parts


def relative(me, ring, code):
    hops = jnp.where((me & 1) == 0, code // 2, (ring - code // 2) % ring)
    place = lax.rem(me // 2 + hops, ring)
    return 2 * place + ((me & 1) ^ (code & 1))


def pack_kernel(peers, span, widths, heads, entries, scalar_rows, *refs):
    refs = list(refs)
    me = refs.pop(0)[0]
    x_ref = refs.pop(0)
    heading = scalar_rows > 0
    if heading:
        kq_ref, decay_ref, step_ref = refs[:3]
        del refs[:3]
    outs = refs[: len(entries)]
    del refs[: len(entries)]
    if heading:
        raw_scalars, scalars, kq_near = refs[:3]
    sems = refs[-1]
    rows = x_ref.shape[0]
    owned = HEADS * HEAD_DIM // peers
    lead = widths[0] + 2 * STATE
    copies = []
    if heading:
        loads = [
            pltpu.make_async_copy(ref, raw_scalars.at[i], sems.at[2, i])
            for i, ref in enumerate((decay_ref, step_ref))
        ]
        loads.append(pltpu.make_async_copy(kq_ref, kq_near, sems.at[2, 2]))
        for load in loads:
            load.start()
    owners = [relative(me, peers // 2, code) for code, _ in entries]
    for i, (owner, (_, kind)) in enumerate(zip(owners, entries)):
        pieces = {
            "full": [(0, 0, 0), (1, widths[0], lead)],
            "lead": [(0, 0, 0)],
            "rest": [(1, widths[0], 0)],
        }[kind]
        for index, offset, left in pieces:
            column = pl.multiple_of(owner * owned + offset, LANES)
            copies.append(
                pltpu.make_async_copy(
                    x_ref.at[:, pl.ds(column, widths[index])],
                    outs[i].at[0:rows, left : left + widths[index]],
                    sems.at[index, i],
                )
            )
    for copy in copies:
        copy.start()
    if heading:
        for load in loads:
            load.wait()
        fields = as_parts(raw_scalars[0].T, 2) + as_parts(raw_scalars[1].T, 1)
        for p, field in enumerate(fields):
            field = field.astype(jnp.float32)
            for owner in range(peers):
                scalars[p, owner] = field[owner * heads : (owner + 1) * heads]
        across = lead // rows
        for i, owner in enumerate(owners):
            outs[i][rows:] = jnp.zeros((scalar_rows, outs[i].shape[1]), jnp.bfloat16)
            for p in range(FIELDS):
                top = rows + p // across * heads
                left = p % across * rows
                outs[i][top : top + heads, left : left + rows] = scalars[p, owner].astype(
                    jnp.bfloat16
                )
            for j in range(2):
                column = pl.multiple_of((j * GROUPS + owner // span) * STATE, LANES)
                left = widths[0] + j * STATE
                outs[i][0:rows, left : left + STATE] = kq_near[:, pl.ds(column, STATE)]
    for copy in copies:
        copy.wait()


def mixer_kernel(peers, rows, heads, chunk, widths, whole_group, *refs):
    refs = list(refs)

    def take(count):
        taken = refs[:count]
        del refs[:count]
        return taken

    first = chunk == 0
    final = chunk == len(widths) - 1 and whole_group
    later = range(1, len(widths)) if first else ()
    width = widths[chunk]
    (me_ref,) = take(1)
    parts = take(peers)
    taps_ref, skip_ref = take(2)
    if not first:
        left_ref, b_ref, inward_ref, outward_ref, power_ref = take(5)
    if final:
        (gain_ref,) = take(1)
        earlier = take(chunk)
        (out_ref,) = take(1)
    else:
        total_ref, sums_ref = take(2)
    if first and later:
        left_ref, b_ref = take(2)
        inward_refs = take(len(later))
        outward_refs = take(len(later))
    wide, carry = take(2)
    if final:
        (total_ref,) = take(1)
    if first:
        (scalars,) = take(1)
    blocks = rows // BLOCK
    step = pl.program_id(0)
    me = me_ref[0]
    scale_rows = rows + 16 * blocks
    base = pl.multiple_of(step * rows, rows)
    scale_base = pl.multiple_of(step * scale_rows, 32)

    @pl.when(step == 0)
    def _():
        carry[...] = jnp.zeros_like(carry)
        wide[rows : rows + HALO] = jnp.zeros((HALO, wide.shape[1]), jnp.bfloat16)

    wide[0:HALO] = wide[rows : rows + HALO]
    ring = peers // 2
    hops = lax.rem(me // 2 + (ring - step // 2), ring)
    hops = jnp.where((step & 1) == 0, hops, lax.rem(ring - hops, ring))
    slot = 2 * hops + ((me ^ step) & 1)
    for k in range(peers):

        @pl.when(slot == k)
        def _():
            if first:
                wide[HALO : HALO + rows] = parts[k][0:rows, 0 : wide.shape[1]]
                scalars[...] = parts[k][rows:, 0 : wide.shape[1]]
            else:
                wide[HALO : HALO + rows] = parts[k][0:rows, parts[k].shape[1] - width :]

    def spread(count):
        head_of = lax.broadcasted_iota(jnp.int32, (2 * count, count * HEAD_DIM), 1) // HEAD_DIM
        row = lax.rem(
            lax.broadcasted_iota(jnp.int32, (2 * count, count * HEAD_DIM), 0), count
        )
        return jnp.where(head_of == row, 1.0, 0.0).astype(jnp.bfloat16)

    def activated(top, size, lo, hi):
        rows_out = []
        for r in range(top, top + size, STRIP):
            lanes_out = []
            for lane in range(lo, hi, LANES):
                tap = [taps_ref[k : k + 1, lane : lane + LANES] for k in range(KW)]
                now = wide[r : r + STRIP + HALO, lane : lane + LANES].astype(jnp.float32)[HALO // 2 :]
                before = pltpu.roll(now, 1, 0)
                older = pltpu.roll(tap[0] * before + tap[1] * now, 2, 0)
                summed = (older + (tap[2] * before + tap[3] * now))[HALO // 2 :]
                lanes_out.append(
                    summed * pltpu.reciprocal(1.0 + jnp.exp(-summed), approx=True)
                )
            rows_out.append(jnp.concatenate(lanes_out, axis=1))
        return jnp.concatenate(rows_out, axis=0)

    if first:
        full = width + 2 * STATE
        across = full // rows
        row = lax.broadcasted_iota(jnp.int32, (rows, rows), 0)
        col = lax.broadcasted_iota(jnp.int32, (rows, rows), 1)
        lower = (row >= col) & (row // BLOCK == col // BLOCK)
        ones = jnp.where(lower, 1.0, 0.0).astype(jnp.bfloat16)
        eye = jnp.where(row == col, 1.0, 0.0).astype(jnp.bfloat16)

        def field(p):
            top = p // across * heads
            lane = p % across * rows
            return scalars[top : top + heads, lane : lane + rows]

        def by_rows(matrix, numbers):
            return sum(contract(matrix, field(p), ((1,), (1,))) for p in numbers)

        cumul = by_rows(ones, (0, 1))
        steps = by_rows(eye, (2,))
        middles = [
            cumul[b * BLOCK + BLOCK // 2 - 1 : b * BLOCK + BLOCK // 2] for b in range(blocks)
        ]
        middle = jnp.concatenate([jnp.broadcast_to(m, (BLOCK, heads)) for m in middles], axis=0)
        inward = as_parts(steps * jnp.exp(middle - cumul), 2)
        outward = as_parts(
            jnp.concatenate(
                [jnp.exp(cumul - middle)]
                + [jnp.broadcast_to(jnp.exp(m), (16, heads)) for m in middles],
                axis=0,
            ),
            2,
        )

        def chosen(halves, index):
            begin = sum(widths[:index]) // HEAD_DIM
            end = begin + widths[index] // HEAD_DIM
            return jnp.concatenate([half[:, begin:end] for half in halves], axis=1)

        bc = activated(0, rows, width, full).astype(jnp.bfloat16)
        b_part, c_part = bc[:, :STATE], bc[:, STATE:]
        scores = contract(c_part, b_part, ((1,), (1,)))
        scores = jnp.where(lower, scores, 0.0).astype(jnp.bfloat16)
        lefts = [
            jnp.concatenate(
                [
                    scores[b * BLOCK : (b + 1) * BLOCK, b * BLOCK : (b + 1) * BLOCK],
                    c_part[b * BLOCK : (b + 1) * BLOCK],
                ],
                axis=1,
            )
            for b in range(blocks)
        ]
        for index in later:
            inward_refs[index - 1][pl.ds(base, rows)] = chosen(inward, index)
            outward_refs[index - 1][pl.ds(scale_base, scale_rows)] = chosen(outward, index)
        if later:
            b_ref[pl.ds(base, rows)] = b_part
            for b in range(blocks):
                left_ref[pl.ds(base + b * BLOCK, BLOCK)] = lefts[b]
        inward = chosen(inward, 0)
        outward = chosen(outward, 0)
    else:
        inward = inward_ref[pl.ds(base, rows)]
        outward = outward_ref[pl.ds(scale_base, scale_rows)]
        b_part = b_ref[pl.ds(base, rows)]
        lefts = [left_ref[pl.ds(base + b * BLOCK, BLOCK)] for b in range(blocks)]

    tile = 2 * LANES if width % (2 * LANES) == 0 else LANES
    expand = spread(width // HEAD_DIM)
    compact = [
        jnp.concatenate(
            [
                inward[b * BLOCK : (b + 1) * BLOCK],
                outward[b * BLOCK : (b + 1) * BLOCK],
                outward[rows + 16 * b : rows + 16 * (b + 1)],
            ],
            axis=0,
        )
        for b in range(blocks)
    ]
    for b in range(blocks):
        top = b * BLOCK
        power = jnp.zeros((BLOCK, LANES), jnp.float32)
        if not first:
            power = power_ref[pl.ds(base + top, BLOCK)]
        for lo in range(0, width, tile):
            hi = lo + tile
            x_conv = activated(top, BLOCK, lo, hi)
            scales = contract(compact[b], expand[:, lo:hi], ((1,), (0,)))
            in_scale = scales[:BLOCK]
            out_scale = scales[BLOCK : 2 * BLOCK]
            mid_scale = scales[2 * BLOCK :]
            scaled = (x_conv * in_scale).astype(jnp.bfloat16)
            held = carry[:, lo:hi] * mid_scale[0:1]
            right = jnp.concatenate([scaled, held.astype(jnp.bfloat16)], axis=0)
            mixed = contract(lefts[b], right, ((1,), (0,)))
            total = mixed * out_scale + skip_ref[0:1, lo:hi] * x_conv
            if final:
                total_ref[top : top + BLOCK, lo:hi] = total
            else:
                total_ref[pl.ds(base + top, BLOCK), lo:hi] = total.astype(jnp.bfloat16)
            squares = total * total
            for lane in range(0, tile, LANES):
                power = power + squares[:, lane : lane + LANES]
            added = contract(b_part[top : top + BLOCK], scaled, ((0,), (0,)))
            carry[:, lo:hi] = (held + added) * out_scale[BLOCK - 1 : BLOCK]
        if final:
            summed = jnp.sum(power, axis=1, keepdims=True)
            norm = lax.rsqrt(summed * (1.0 / GROUP_WIDTH) + EPS)
            column = 0
            for index, size in enumerate(widths):
                if index < chunk:
                    block = earlier[index][pl.ds(base + top, BLOCK)].astype(jnp.float32)
                else:
                    block = total_ref[top : top + BLOCK]
                out_ref[top : top + BLOCK, column : column + size] = (
                    block * norm * gain_ref[0:1, column : column + size]
                ).astype(jnp.bfloat16)
                column += size
        else:
            sums_ref[pl.ds(base + top, BLOCK)] = power


def per_device(inputs, key_query, conv_inputs, conv_kq, step_size, decay_log, skip_gain, norm_gain):
    peers = lax.axis_size("ctx")
    me = lax.axis_index("ctx")
    place = me.reshape(1).astype(jnp.int32)
    rows = inputs.shape[0]
    owned = HEADS * HEAD_DIM // peers
    heads = HEADS // peers
    span = GROUP_WIDTH // owned
    whole_group = span == 1
    total_rows = peers * rows
    blocks = rows // BLOCK
    tiles = owned // LANES
    last = max(1, tiles // 2)
    widths = [(tiles - last) * LANES, last * LANES]
    offsets = [0, widths[0]]

    smem = pl.BlockSpec(memory_space=pltpu.SMEM)
    hbm = pl.BlockSpec(memory_space=pltpu.HBM)
    vmem = pl.BlockSpec(memory_space=pltpu.VMEM)
    params = pltpu.CompilerParams(vmem_limit_bytes=VMEM_LIMIT)

    def columns(a, first, size):
        return lax.dynamic_slice_in_dim(a, first, size, axis=1)

    lead = widths[0] + 2 * STATE
    scalar_rows = -(-(-(-FIELDS // (lead // rows)) * heads) // 16) * 16
    extents = {
        "full": (rows + scalar_rows, lead + widths[1]),
        "lead": (rows + scalar_rows, lead),
        "rest": (rows, widths[1]),
    }

    def pack(entries, after=()):
        token, _ = lax.optimization_barrier((place, after))
        heading = entries[0][1] != "rest"
        shapes = [jax.ShapeDtypeStruct(extents[kind], jnp.bfloat16) for _, kind in entries]
        operands = [token, inputs]
        in_specs = [smem, hbm]
        scratch = []
        if heading:
            operands += [key_query, decay_log, step_size]
            in_specs += [hbm] * 3
            scratch.append(pltpu.VMEM((2, rows, HEADS), jnp.float32))
            scratch.append(pltpu.VMEM((FIELDS, peers, heads, rows), jnp.float32))
            scratch.append(pltpu.VMEM(key_query.shape, jnp.bfloat16))
        scratch.append(pltpu.SemaphoreType.DMA((3, max(3, len(entries)))))
        return pl.pallas_call(
            functools.partial(
                pack_kernel,
                peers,
                span,
                widths,
                heads,
                entries,
                scalar_rows if heading else 0,
            ),
            in_specs=in_specs,
            out_specs=[vmem] * len(entries),
            out_shape=shapes,
            scratch_shapes=scratch,
            compiler_params=pltpu.CompilerParams(vmem_limit_bytes=PACK_VMEM),
            cost_estimate=pl.CostEstimate(
                flops=0,
                bytes_accessed=4 * sum(math.prod(shape.shape) for shape in shapes),
                transcendentals=0,
            ),
            name="pack",
        )(*operands)

    def send(message, code, after=()):
        message, _ = lax.optimization_barrier((message, after))
        hops = (code // 2, -(code // 2))
        pairs = [
            (i, 2 * ((i // 2 + hops[i % 2]) % (peers // 2)) + (i % 2 ^ code % 2))
            for i in range(peers)
        ]
        return lax.ppermute(message, "ctx", pairs)

    if peers == 8:
        one, two = pack(((4, "full"), (5, "full")))
        one, two = send(one, 2), send(two, 6)
        leads = pack(
            ((2, "lead"), (6, "lead"), (3, "lead"), (7, "lead"), (1, "full"), (0, "full"))
        )
        rests = pack(((2, "rest"), (6, "rest"), (3, "rest"), (7, "rest")), (one, two))
        lead = {0: leads[5], 1: send(leads[4], 1), 2: send(leads[0], 2), 6: send(leads[1], 6)}
        lead[4] = send(one, 2)
        lead[5] = send(two, 7)
        lead[3] = send(leads[2], 3, lead[2])
        lead[7] = send(leads[3], 7, lead[6])
        rest = {code: lead[code] for code in (0, 1, 4, 5)}
        rest[2] = send(rests[0], 2, lead[2])
        rest[6] = send(rests[1], 6, lead[6])
        rest[3] = send(rests[2], 3, lead[3])
        rest[7] = send(rests[3], 7, lead[7])
    else:
        codes = range(2, peers)
        packed = pack(((0, "full"), (1, "full")) + tuple((code, "lead") for code in codes))
        lead = {code: send(message, code) for code, message in enumerate(packed)}
        packed = pack(tuple((code, "rest") for code in codes), lead[peers - 1])
        rest = {0: lead[0], 1: lead[1]}
        rest.update((code, send(message, code)) for code, message in zip(codes, packed))
    received = [[slots[code] for code in range(peers)] for slots in (lead, rest)]

    taps_x = columns(conv_inputs, me * owned, owned)
    group = me // span
    taps_kq = jnp.concatenate(
        [
            columns(conv_kq, group * STATE, STATE),
            columns(conv_kq, (GROUPS + group) * STATE, STATE),
        ],
        axis=1,
    )
    skip = jnp.repeat(lax.dynamic_slice_in_dim(skip_gain, me * heads, heads), HEAD_DIM)[None]
    gain = columns(norm_gain[None], me * owned, owned)

    def by_source(count, lanes, dtype):
        spec = pl.BlockSpec((count, lanes), lambda i: (i, 0))
        return spec, jax.ShapeDtypeStruct((peers * count, lanes), dtype)

    def whole(count, lanes, dtype):
        return vmem, jax.ShapeDtypeStruct((peers * count, lanes), dtype)

    totals = []
    power = None
    shared = None
    for chunk, width in enumerate(widths):
        first = chunk == 0
        final = chunk == len(widths) - 1 and whole_group
        taps = taps_x[:, offsets[chunk] : offsets[chunk] + width]
        if first:
            taps = jnp.concatenate([taps, taps_kq], axis=1)
        cols = taps.shape[1]
        operands = [place, *received[chunk], taps, skip[:, offsets[chunk] : offsets[chunk] + width]]
        if not first:
            left, b_part, inward, outward = shared
            operands += [left, b_part, inward[chunk - 1], outward[chunk - 1], power]
        if final:
            operands += [gain, *totals]
        out = []
        if final:
            out.append(by_source(rows, owned, jnp.bfloat16))
        else:
            out.append(whole(rows, width, jnp.bfloat16))
            out.append(whole(rows, LANES, jnp.float32))
        if first:
            out.append(whole(rows, 2 * STATE, jnp.bfloat16))
            out.append(whole(rows, STATE, jnp.bfloat16))
            for count in (rows, rows + 16 * blocks):
                for size in widths[1:]:
                    out.append(whole(count, 2 * size // HEAD_DIM, jnp.bfloat16))
        scratch = [
            pltpu.VMEM((rows + HALO, cols), jnp.bfloat16),
            pltpu.VMEM((STATE, width), jnp.float32),
        ]
        if final:
            scratch.append(pltpu.VMEM((rows, width), jnp.float32))
        if first:
            scratch.append(pltpu.VMEM((scalar_rows, cols), jnp.bfloat16))
        results = pl.pallas_call(
            functools.partial(mixer_kernel, peers, rows, heads, chunk, widths, whole_group),
            grid=(peers,),
            in_specs=[smem] + [vmem] * (len(operands) - 1),
            out_specs=[spec for spec, _ in out],
            out_shape=[shape for _, shape in out],
            scratch_shapes=scratch,
            compiler_params=params,
            cost_estimate=pl.CostEstimate(
                flops=2 * total_rows * width * 450,
                bytes_accessed=total_rows * (2 * cols + 8 * width),
                transcendentals=total_rows * cols,
            ),
            name=f"mixer{chunk}",
        )(*operands)
        if final:
            return results[0]
        totals.append(results[0])
        power = results[1]
        if first:
            rest = results[4:]
            shared = (results[2], results[3], rest[: len(rest) // 2], rest[len(rest) // 2 :])
    sharers = [list(range(i, i + span)) for i in range(0, peers, span)]
    summed = jnp.sum(power, axis=1, keepdims=True)
    summed = lax.psum(summed, "ctx", axis_index_groups=sharers)
    total = jnp.concatenate(totals, axis=1)
    return (total * lax.rsqrt(summed * (1.0 / GROUP_WIDTH) + EPS) * gain).astype(jnp.bfloat16)


def solution(mesh):
    in_specs = (
        P(("dp", "ctx"), None),
        P(("dp", "ctx"), None),
        P(),
        P(),
        P(("dp", "ctx"), None),
        P(("dp", "ctx"), None),
        P(),
        P(),
    )
    out_specs = P("dp", "ctx")
    return jax.shard_map(
        per_device, mesh=mesh, in_specs=in_specs, out_specs=out_specs, check_vma=False
    )
```

```python
import functools
import math

import jax
import jax.numpy as jnp
from jax import lax
from jax.experimental import pallas as pl
from jax.experimental.pallas import tpu as pltpu
from jax.sharding import PartitionSpec as P

HEADS = 128
HEAD_DIM = 64
STATE = 128
GROUPS = 8
KW = 4
BLOCK = 128
GROUP_WIDTH = HEADS * HEAD_DIM // GROUPS
EPS = 1e-05
HALO = 16
LANES = 128
SUBLANES = 8
FIELDS = 2
STRIP = 64
PACK_VMEM = 58 * 1024 * 1024
VMEM_LIMIT = 32 * 1024 * 1024


def contract(a, b, dims):
    return lax.dot_general(a, b, (dims, ((), ())), preferred_element_type=jnp.float32)


def as_parts(v, count):
    parts = []
    for _ in range(count):
        part = v.astype(jnp.bfloat16)
        parts.append(part)
        v = v - part.astype(jnp.float32)
    return parts


def scalar_units(heads, rows, cols):
    units = []
    for p in range(FIELDS):
        for head in range(0, heads, SUBLANES):
            line, column = divmod(len(units), cols // rows)
            units.append((p, head, min(SUBLANES, heads), line * SUBLANES, column * rows))
    return units


def pack_kernel(peers, span, widths, heads, entries, scalar_rows, *refs):
    refs = list(refs)
    me = refs.pop(0)[0]
    x_ref = refs.pop(0)
    heading = scalar_rows > 0
    if heading:
        kq_ref, decay_ref, step_ref = refs[:3]
        del refs[:3]
    outs = refs[: len(entries)]
    del refs[: len(entries)]
    if heading:
        raw_scalars, scalars, kq_near = refs[:3]
    sems = refs[-1]
    rows = x_ref.shape[0]
    owned = HEADS * HEAD_DIM // peers
    lead = widths[0] + 2 * STATE
    copies = []
    if heading:
        loads = [
            pltpu.make_async_copy(ref, raw_scalars.at[i], sems.at[2, i])
            for i, ref in enumerate((decay_ref, step_ref))
        ]
        loads.append(pltpu.make_async_copy(kq_ref, kq_near, sems.at[2, 2]))
        for load in loads:
            load.start()
    owners = [lax.rem(me + code, peers) for code, _ in entries]
    for i, (owner, (_, kind)) in enumerate(zip(owners, entries)):
        pieces = {
            "full": [(0, 0, 0), (1, widths[0], lead)],
            "lead": [(0, 0, 0)],
            "rest": [(1, widths[0], 0)],
        }[kind]
        for index, offset, left in pieces:
            column = pl.multiple_of(owner * owned + offset, LANES)
            copies.append(
                pltpu.make_async_copy(
                    x_ref.at[:, pl.ds(column, widths[index])],
                    outs[i].at[0:rows, left : left + widths[index]],
                    sems.at[index, i],
                )
            )
    for copy in copies:
        copy.start()
    if heading:
        for load in loads:
            load.wait()
        fields = [raw_scalars[0].T, raw_scalars[1].T]
        for p, field in enumerate(fields):
            for owner in range(peers):
                scalars[p, owner] = field[owner * heads : (owner + 1) * heads]
        for i, owner in enumerate(owners):
            outs[i][rows:] = jnp.zeros((scalar_rows, outs[i].shape[1]), jnp.bfloat16)
            for p, head, count, top, left in scalar_units(heads, rows, lead):
                outs[i][rows + top : rows + top + count, left : left + rows] = scalars[
                    p, owner, head : head + count
                ].astype(jnp.bfloat16)
            for j in range(2):
                column = pl.multiple_of((j * GROUPS + owner // span) * STATE, LANES)
                left = widths[0] + j * STATE
                outs[i][0:rows, left : left + STATE] = kq_near[:, pl.ds(column, STATE)]
    for copy in copies:
        copy.wait()


def mixer_kernel(peers, rows, heads, chunk, widths, whole_group, *refs):
    refs = list(refs)

    def take(count):
        taken = refs[:count]
        del refs[:count]
        return taken

    first = chunk == 0
    final = chunk == len(widths) - 1 and whole_group
    later = range(1, len(widths)) if first else ()
    width = widths[chunk]
    (me_ref,) = take(1)
    parts = take(peers)
    taps_ref, skip_ref = take(2)
    if not first:
        left_ref, b_ref, inward_ref, outward_ref, power_ref = take(5)
    if final:
        (gain_ref,) = take(1)
        earlier = take(chunk)
        (out_ref,) = take(1)
    else:
        total_ref, sums_ref = take(2)
    if first and later:
        left_ref, b_ref = take(2)
        inward_refs = take(len(later))
        outward_refs = take(len(later))
    wide, carry = take(2)
    if final:
        (total_ref,) = take(1)
    if first:
        (scalars,) = take(1)
    blocks = rows // BLOCK
    step = pl.program_id(0)
    me = me_ref[0]
    scale_rows = rows + 16 * blocks
    base = pl.multiple_of(step * rows, rows)
    scale_base = pl.multiple_of(step * scale_rows, 32)

    @pl.when(step == 0)
    def _():
        carry[...] = jnp.zeros_like(carry)
        wide[rows : rows + HALO] = jnp.zeros((HALO, wide.shape[1]), jnp.bfloat16)

    wide[0:HALO] = wide[rows : rows + HALO]
    slot = lax.rem(me + (peers - step), peers)
    for k in range(peers):

        @pl.when(slot == k)
        def _():
            if first:
                wide[HALO : HALO + rows] = parts[k][0:rows, 0 : wide.shape[1]]
                scalars[...] = parts[k][rows:, 0 : wide.shape[1]]
            else:
                wide[HALO : HALO + rows] = parts[k][0:rows, parts[k].shape[1] - width :]

    def spread(count):
        head_of = lax.broadcasted_iota(jnp.int32, (2 * count, count * HEAD_DIM), 1) // HEAD_DIM
        row = lax.rem(
            lax.broadcasted_iota(jnp.int32, (2 * count, count * HEAD_DIM), 0), count
        )
        return jnp.where(head_of == row, 1.0, 0.0).astype(jnp.bfloat16)

    def activated(top, size, lo, hi):
        rows_out = []
        for r in range(top, top + size, STRIP):
            lanes_out = []
            for lane in range(lo, hi, LANES):
                tap = [taps_ref[k : k + 1, lane : lane + LANES] for k in range(KW)]
                now = wide[r : r + STRIP + HALO, lane : lane + LANES].astype(jnp.float32)[HALO // 2 :]
                before = pltpu.roll(now, 1, 0)
                older = pltpu.roll(tap[0] * before + tap[1] * now, 2, 0)
                summed = (older + (tap[2] * before + tap[3] * now))[HALO // 2 :]
                lanes_out.append(
                    summed * pltpu.reciprocal(1.0 + jnp.exp(-summed), approx=True)
                )
            rows_out.append(jnp.concatenate(lanes_out, axis=1))
        return jnp.concatenate(rows_out, axis=0)

    if first:
        full = width + 2 * STATE
        row = lax.broadcasted_iota(jnp.int32, (rows, rows), 0)
        col = lax.broadcasted_iota(jnp.int32, (rows, rows), 1)
        lower = (row >= col) & (row // BLOCK == col // BLOCK)
        ones = jnp.where(lower, 1.0, 0.0).astype(jnp.bfloat16)
        eye = jnp.where(row == col, 1.0, 0.0).astype(jnp.bfloat16)

        def field(p):
            pieces = [
                scalars[top : top + count, left : left + rows].astype(jnp.float32)
                for q, _, count, top, left in scalar_units(heads, rows, full)
                if q == p
            ]
            return jnp.concatenate(pieces, axis=0).astype(jnp.bfloat16)

        cumul = contract(ones, field(0), ((1,), (1,)))
        steps = contract(eye, field(1), ((1,), (1,)))
        middles = [
            cumul[b * BLOCK + BLOCK // 2 - 1 : b * BLOCK + BLOCK // 2] for b in range(blocks)
        ]
        middle = jnp.concatenate([jnp.broadcast_to(m, (BLOCK, heads)) for m in middles], axis=0)
        inward = as_parts(steps * jnp.exp(middle - cumul), 2)
        outward = as_parts(
            jnp.concatenate(
                [jnp.exp(cumul - middle)]
                + [jnp.broadcast_to(jnp.exp(m), (16, heads)) for m in middles],
                axis=0,
            ),
            2,
        )

        def chosen(halves, index):
            begin = sum(widths[:index]) // HEAD_DIM
            end = begin + widths[index] // HEAD_DIM
            return jnp.concatenate([half[:, begin:end] for half in halves], axis=1)

        bc = activated(0, rows, width, full).astype(jnp.bfloat16)
        b_part, c_part = bc[:, :STATE], bc[:, STATE:]
        scores = contract(c_part, b_part, ((1,), (1,)))
        scores = jnp.where(lower, scores, 0.0).astype(jnp.bfloat16)
        lefts = [
            jnp.concatenate(
                [
                    scores[b * BLOCK : (b + 1) * BLOCK, b * BLOCK : (b + 1) * BLOCK],
                    c_part[b * BLOCK : (b + 1) * BLOCK],
                ],
                axis=1,
            )
            for b in range(blocks)
        ]
        for index in later:
            inward_refs[index - 1][pl.ds(base, rows)] = chosen(inward, index)
            outward_refs[index - 1][pl.ds(scale_base, scale_rows)] = chosen(outward, index)
        if later:
            b_ref[pl.ds(base, rows)] = b_part
            for b in range(blocks):
                left_ref[pl.ds(base + b * BLOCK, BLOCK)] = lefts[b]
        inward = chosen(inward, 0)
        outward = chosen(outward, 0)
    else:
        inward = inward_ref[pl.ds(base, rows)]
        outward = outward_ref[pl.ds(scale_base, scale_rows)]
        b_part = b_ref[pl.ds(base, rows)]
        lefts = [left_ref[pl.ds(base + b * BLOCK, BLOCK)] for b in range(blocks)]

    tile = 2 * LANES if width % (2 * LANES) == 0 else LANES
    expand = spread(width // HEAD_DIM)
    compact = [
        jnp.concatenate(
            [
                inward[b * BLOCK : (b + 1) * BLOCK],
                outward[b * BLOCK : (b + 1) * BLOCK],
                outward[rows + 16 * b : rows + 16 * (b + 1)],
            ],
            axis=0,
        )
        for b in range(blocks)
    ]
    for b in range(blocks):
        top = b * BLOCK
        power = jnp.zeros((BLOCK, LANES), jnp.float32)
        if not first:
            power = power_ref[pl.ds(base + top, BLOCK)]
        for lo in range(0, width, tile):
            hi = lo + tile
            x_conv = activated(top, BLOCK, lo, hi)
            scales = contract(compact[b], expand[:, lo:hi], ((1,), (0,)))
            in_scale = scales[:BLOCK]
            out_scale = scales[BLOCK : 2 * BLOCK]
            mid_scale = scales[2 * BLOCK :]
            scaled = (x_conv * in_scale).astype(jnp.bfloat16)
            held = carry[:, lo:hi] * mid_scale[0:1]
            right = jnp.concatenate([scaled, held.astype(jnp.bfloat16)], axis=0)
            mixed = contract(lefts[b], right, ((1,), (0,)))
            total = mixed * out_scale + skip_ref[0:1, lo:hi] * x_conv
            if final:
                total_ref[top : top + BLOCK, lo:hi] = total
            else:
                total_ref[pl.ds(base + top, BLOCK), lo:hi] = total.astype(jnp.bfloat16)
            squares = total * total
            for lane in range(0, tile, LANES):
                power = power + squares[:, lane : lane + LANES]
            added = contract(b_part[top : top + BLOCK], scaled, ((0,), (0,)))
            carry[:, lo:hi] = (held + added) * out_scale[BLOCK - 1 : BLOCK]
        if final:
            summed = jnp.sum(power, axis=1, keepdims=True)
            norm = lax.rsqrt(summed * (1.0 / GROUP_WIDTH) + EPS)
            column = 0
            for index, size in enumerate(widths):
                if index < chunk:
                    block = earlier[index][pl.ds(base + top, BLOCK)].astype(jnp.float32)
                else:
                    block = total_ref[top : top + BLOCK]
                out_ref[top : top + BLOCK, column : column + size] = (
                    block * norm * gain_ref[0:1, column : column + size]
                ).astype(jnp.bfloat16)
                column += size
        else:
            sums_ref[pl.ds(base + top, BLOCK)] = power


def per_device(inputs, key_query, conv_inputs, conv_kq, step_size, decay_log, skip_gain, norm_gain):
    peers = lax.axis_size("ctx")
    me = lax.axis_index("ctx")
    place = me.reshape(1).astype(jnp.int32)
    rows = inputs.shape[0]
    owned = HEADS * HEAD_DIM // peers
    heads = HEADS // peers
    span = GROUP_WIDTH // owned
    whole_group = span == 1
    total_rows = peers * rows
    blocks = rows // BLOCK
    tiles = owned // LANES
    last = max(1, tiles // 4)
    widths = [(tiles - last) * LANES, last * LANES]
    offsets = [0, widths[0]]

    smem = pl.BlockSpec(memory_space=pltpu.SMEM)
    hbm = pl.BlockSpec(memory_space=pltpu.HBM)
    vmem = pl.BlockSpec(memory_space=pltpu.VMEM)
    params = pltpu.CompilerParams(vmem_limit_bytes=VMEM_LIMIT)

    def columns(a, first, size):
        return lax.dynamic_slice_in_dim(a, first, size, axis=1)

    lead_cols = widths[0] + 2 * STATE
    scalar_rows = scalar_units(heads, rows, lead_cols)[-1][3] + SUBLANES
    extents = {
        "full": (rows + scalar_rows, lead_cols + widths[1]),
        "lead": (rows + scalar_rows, lead_cols),
        "rest": (rows, widths[1]),
    }

    def pack(entries, after=()):
        token, _ = lax.optimization_barrier((place, after))
        heading = entries[0][1] != "rest"
        shapes = [jax.ShapeDtypeStruct(extents[kind], jnp.bfloat16) for _, kind in entries]
        operands = [token, inputs]
        in_specs = [smem, hbm]
        scratch = []
        if heading:
            operands += [key_query, decay_log, step_size]
            in_specs += [hbm] * 3
            scratch.append(pltpu.VMEM((2, rows, HEADS), jnp.float32))
            scratch.append(pltpu.VMEM((FIELDS, peers, heads, rows), jnp.float32))
            scratch.append(pltpu.VMEM(key_query.shape, jnp.bfloat16))
        scratch.append(pltpu.SemaphoreType.DMA((3, max(3, len(entries)))))
        return pl.pallas_call(
            functools.partial(
                pack_kernel,
                peers,
                span,
                widths,
                heads,
                entries,
                scalar_rows if heading else 0,
            ),
            in_specs=in_specs,
            out_specs=[vmem] * len(entries),
            out_shape=shapes,
            scratch_shapes=scratch,
            compiler_params=pltpu.CompilerParams(vmem_limit_bytes=PACK_VMEM),
            cost_estimate=pl.CostEstimate(
                flops=0,
                bytes_accessed=4 * sum(math.prod(shape.shape) for shape in shapes),
                transcendentals=0,
            ),
            name="pack",
        )(*operands)

    def send(message, code, after=()):
        message, _ = lax.optimization_barrier((message, after))
        pairs = [(i, (i + code) % peers) for i in range(peers)]
        return lax.ppermute(message, "ctx", pairs)

    far = sorted(range(2, peers - 1), key=lambda code: abs(code - peers // 2))
    near = [1, peers - 1]
    lead = {}
    for code, message in zip(far, pack([(code, "lead") for code in far])):
        lead[code] = send(message, code)
    *packed, lead[0] = pack([(code, "full") for code in near] + [(0, "full")], lead[far[0]])
    for code, message in zip(near, packed):
        lead[code] = send(message, code)
    rest = {code: lead[code] for code in near + [0]}
    packed = pack([(code, "rest") for code in far], lead[far[0]])
    for code, message in zip(far, packed):
        rest[code] = send(message, code, lead[code])
    received = [[slots[code] for code in range(peers)] for slots in (lead, rest)]

    taps_x = columns(conv_inputs, me * owned, owned)
    group = me // span
    taps_kq = jnp.concatenate(
        [
            columns(conv_kq, group * STATE, STATE),
            columns(conv_kq, (GROUPS + group) * STATE, STATE),
        ],
        axis=1,
    )
    skip = jnp.repeat(lax.dynamic_slice_in_dim(skip_gain, me * heads, heads), HEAD_DIM)[None]
    gain = columns(norm_gain[None], me * owned, owned)

    def by_source(count, lanes, dtype):
        spec = pl.BlockSpec((count, lanes), lambda i: (i, 0))
        return spec, jax.ShapeDtypeStruct((peers * count, lanes), dtype)

    def whole(count, lanes, dtype):
        return vmem, jax.ShapeDtypeStruct((peers * count, lanes), dtype)

    totals = []
    power = None
    shared = None
    for chunk, width in enumerate(widths):
        first = chunk == 0
        final = chunk == len(widths) - 1 and whole_group
        taps = taps_x[:, offsets[chunk] : offsets[chunk] + width]
        if first:
            taps = jnp.concatenate([taps, taps_kq], axis=1)
        cols = taps.shape[1]
        operands = [place, *received[chunk], taps, skip[:, offsets[chunk] : offsets[chunk] + width]]
        if not first:
            left, b_part, inward, outward = shared
            operands += [left, b_part, inward[chunk - 1], outward[chunk - 1], power]
        if final:
            operands += [gain, *totals]
        out = []
        if final:
            out.append(by_source(rows, owned, jnp.bfloat16))
        else:
            out.append(whole(rows, width, jnp.bfloat16))
            out.append(whole(rows, LANES, jnp.float32))
        if first:
            out.append(whole(rows, 2 * STATE, jnp.bfloat16))
            out.append(whole(rows, STATE, jnp.bfloat16))
            for count in (rows, rows + 16 * blocks):
                for size in widths[1:]:
                    out.append(whole(count, 2 * size // HEAD_DIM, jnp.bfloat16))
        scratch = [
            pltpu.VMEM((rows + HALO, cols), jnp.bfloat16),
            pltpu.VMEM((STATE, width), jnp.float32),
        ]
        if final:
            scratch.append(pltpu.VMEM((rows, width), jnp.float32))
        if first:
            scratch.append(pltpu.VMEM((scalar_rows, cols), jnp.bfloat16))
        results = pl.pallas_call(
            functools.partial(mixer_kernel, peers, rows, heads, chunk, widths, whole_group),
            grid=(peers,),
            in_specs=[smem] + [vmem] * (len(operands) - 1),
            out_specs=[spec for spec, _ in out],
            out_shape=[shape for _, shape in out],
            scratch_shapes=scratch,
            compiler_params=params,
            cost_estimate=pl.CostEstimate(
                flops=2 * total_rows * width * 450,
                bytes_accessed=total_rows * (2 * cols + 8 * width),
                transcendentals=total_rows * cols,
            ),
            name=f"mixer{chunk}",
        )(*operands)
        if final:
            return results[0]
        totals.append(results[0])
        power = results[1]
        if first:
            rest = results[4:]
            shared = (results[2], results[3], rest[: len(rest) // 2], rest[len(rest) // 2 :])
    sharers = [list(range(i, i + span)) for i in range(0, peers, span)]
    summed = jnp.sum(power, axis=1, keepdims=True)
    summed = lax.psum(summed, "ctx", axis_index_groups=sharers)
    total = jnp.concatenate(totals, axis=1)
    return (total * lax.rsqrt(summed * (1.0 / GROUP_WIDTH) + EPS) * gain).astype(jnp.bfloat16)


def solution(mesh):
    in_specs = (
        P(("dp", "ctx"), None),
        P(("dp", "ctx"), None),
        P(),
        P(),
        P(("dp", "ctx"), None),
        P(("dp", "ctx"), None),
        P(),
        P(),
    )
    out_specs = P("dp", "ctx")
    return jax.shard_map(
        per_device, mesh=mesh, in_specs=in_specs, out_specs=out_specs, check_vma=False
    )
```

```python
import functools
import math

import jax
import jax.numpy as jnp
from jax import lax
from jax.experimental import pallas as pl
from jax.experimental.pallas import tpu as pltpu
from jax.sharding import PartitionSpec as P

HEADS = 128
HEAD_DIM = 64
STATE = 128
GROUPS = 8
KW = 4
BLOCK = 128
GROUP_WIDTH = HEADS * HEAD_DIM // GROUPS
EPS = 1e-05
HALO = 16
LANES = 128
SUBLANES = 8
FIELDS = 2
STRIP = 64
PACK_VMEM = 58 * 1024 * 1024
VMEM_LIMIT = 32 * 1024 * 1024


def contract(a, b, dims):
    return lax.dot_general(a, b, (dims, ((), ())), preferred_element_type=jnp.float32)


def as_parts(v, count):
    parts = []
    for _ in range(count):
        part = v.astype(jnp.bfloat16)
        parts.append(part)
        v = v - part.astype(jnp.float32)
    return parts


def scalar_units(heads, rows, cols):
    units = []
    for p in range(FIELDS):
        for head in range(0, heads, SUBLANES):
            line, column = divmod(len(units), cols // rows)
            units.append((p, head, min(SUBLANES, heads), line * SUBLANES, column * rows))
    return units


def pack_kernel(peers, span, widths, heads, entries, scalar_rows, *refs):
    refs = list(refs)
    me = refs.pop(0)[0]
    x_ref = refs.pop(0)
    heading = scalar_rows > 0
    if heading:
        kq_ref, decay_ref, step_ref = refs[:3]
        del refs[:3]
    outs = refs[: len(entries)]
    del refs[: len(entries)]
    if heading:
        raw_scalars, scalars, kq_near, staged, lines = refs[:5]
    sems = refs[-1]
    rows = x_ref.shape[0]
    owned = HEADS * HEAD_DIM // peers
    lead = widths[0] + 2 * STATE
    copies = []
    if heading:
        loads = [
            pltpu.make_async_copy(ref, raw_scalars.at[i], sems.at[2, i])
            for i, ref in enumerate((decay_ref, step_ref))
        ]
        loads.append(pltpu.make_async_copy(kq_ref, kq_near, sems.at[2, 2]))
        for load in loads:
            load.start()
    owners = [lax.rem(me + code, peers) for code, _ in entries]
    for i, (owner, (_, kind)) in enumerate(zip(owners, entries)):
        pieces = {
            "full": [(0, 0, 0), (1, widths[0], lead)],
            "lead": [(0, 0, 0)],
            "rest": [(1, widths[0], 0)],
        }[kind]
        for index, offset, left in pieces:
            column = pl.multiple_of(owner * owned + offset, LANES)
            copies.append(
                pltpu.make_async_copy(
                    x_ref.at[:, pl.ds(column, widths[index])],
                    outs[i].at[0:rows, left : left + widths[index]],
                    sems.at[index, i],
                )
            )
    for copy in copies:
        copy.start()
    if heading:
        for load in loads:
            load.wait()
        fields = [raw_scalars[0].T, raw_scalars[1].T]
        for p, field in enumerate(fields):
            for owner in range(peers):
                scalars[p, owner] = field[owner * heads : (owner + 1) * heads]
        lines[...] = jnp.zeros_like(lines)
        for i, owner in enumerate(owners):
            for p, head, count, top, left in scalar_units(heads, rows, lead):
                lines[i, top : top + count, left : left + rows] = scalars[
                    p, owner, head : head + count
                ].astype(jnp.bfloat16)
            for j in range(2):
                column = pl.multiple_of((j * GROUPS + owner // span) * STATE, LANES)
                staged[i, :, j * STATE : (j + 1) * STATE] = kq_near[:, pl.ds(column, STATE)]
            late = [
                pltpu.make_async_copy(
                    staged.at[i], outs[i].at[0:rows, widths[0] : lead], sems.at[3, i]
                ),
                pltpu.make_async_copy(
                    lines.at[i], outs[i].at[rows : rows + scalar_rows, 0:lead], sems.at[4, i]
                ),
            ]
            for copy in late:
                copy.start()
            copies += late
    for copy in copies:
        copy.wait()


def mixer_kernel(peers, rows, heads, chunk, widths, whole_group, *refs):
    refs = list(refs)

    def take(count):
        taken = refs[:count]
        del refs[:count]
        return taken

    first = chunk == 0
    final = chunk == len(widths) - 1 and whole_group
    later = range(1, len(widths)) if first else ()
    width = widths[chunk]
    (me_ref,) = take(1)
    parts = take(peers)
    taps_ref, skip_ref = take(2)
    if not first:
        left_ref, b_ref, inward_ref, outward_ref, power_ref = take(5)
    if final:
        (gain_ref,) = take(1)
        earlier = take(chunk)
        (out_ref,) = take(1)
    else:
        total_ref, sums_ref = take(2)
    if first and later:
        left_ref, b_ref = take(2)
        inward_refs = take(len(later))
        outward_refs = take(len(later))
    wide, carry = take(2)
    if final:
        (total_ref,) = take(1)
    if first:
        (scalars,) = take(1)
    blocks = rows // BLOCK
    step = pl.program_id(0)
    me = me_ref[0]
    scale_rows = rows + 16 * blocks
    base = pl.multiple_of(step * rows, rows)
    scale_base = pl.multiple_of(step * scale_rows, 32)

    @pl.when(step == 0)
    def _():
        carry[...] = jnp.zeros_like(carry)
        wide[rows : rows + HALO] = jnp.zeros((HALO, wide.shape[1]), jnp.bfloat16)

    wide[0:HALO] = wide[rows : rows + HALO]
    slot = lax.rem(me + (peers - step), peers)
    for k in range(peers):

        @pl.when(slot == k)
        def _():
            if first:
                wide[HALO : HALO + rows] = parts[k][0:rows, 0 : wide.shape[1]]
                scalars[...] = parts[k][rows:, 0 : wide.shape[1]]
            else:
                wide[HALO : HALO + rows] = parts[k][0:rows, parts[k].shape[1] - width :]

    def spread(count):
        head_of = lax.broadcasted_iota(jnp.int32, (2 * count, count * HEAD_DIM), 1) // HEAD_DIM
        row = lax.rem(
            lax.broadcasted_iota(jnp.int32, (2 * count, count * HEAD_DIM), 0), count
        )
        return jnp.where(head_of == row, 1.0, 0.0).astype(jnp.bfloat16)

    def activated(top, size, lo, hi):
        rows_out = []
        for r in range(top, top + size, STRIP):
            lanes_out = []
            for lane in range(lo, hi, LANES):
                tap = [taps_ref[k : k + 1, lane : lane + LANES] for k in range(KW)]
                now = wide[r : r + STRIP + HALO, lane : lane + LANES].astype(jnp.float32)[HALO // 2 :]
                before = pltpu.roll(now, 1, 0)
                older = pltpu.roll(tap[0] * before + tap[1] * now, 2, 0)
                summed = (older + (tap[2] * before + tap[3] * now))[HALO // 2 :]
                lanes_out.append(
                    summed * pltpu.reciprocal(1.0 + jnp.exp(-summed), approx=True)
                )
            rows_out.append(jnp.concatenate(lanes_out, axis=1))
        return jnp.concatenate(rows_out, axis=0)

    if first:
        full = width + 2 * STATE
        row = lax.broadcasted_iota(jnp.int32, (rows, rows), 0)
        col = lax.broadcasted_iota(jnp.int32, (rows, rows), 1)
        lower = (row >= col) & (row // BLOCK == col // BLOCK)
        ones = jnp.where(lower, 1.0, 0.0).astype(jnp.bfloat16)
        eye = jnp.where(row == col, 1.0, 0.0).astype(jnp.bfloat16)

        def field(p):
            pieces = [
                scalars[top : top + count, left : left + rows].astype(jnp.float32)
                for q, _, count, top, left in scalar_units(heads, rows, full)
                if q == p
            ]
            return jnp.concatenate(pieces, axis=0).astype(jnp.bfloat16)

        cumul = contract(ones, field(0), ((1,), (1,)))
        steps = contract(eye, field(1), ((1,), (1,)))
        middles = [
            cumul[b * BLOCK + BLOCK // 2 - 1 : b * BLOCK + BLOCK // 2] for b in range(blocks)
        ]
        middle = jnp.concatenate([jnp.broadcast_to(m, (BLOCK, heads)) for m in middles], axis=0)
        inward = as_parts(steps * jnp.exp(middle - cumul), 2)
        outward = as_parts(
            jnp.concatenate(
                [jnp.exp(cumul - middle)]
                + [jnp.broadcast_to(jnp.exp(m), (16, heads)) for m in middles],
                axis=0,
            ),
            2,
        )

        def chosen(halves, index):
            begin = sum(widths[:index]) // HEAD_DIM
            end = begin + widths[index] // HEAD_DIM
            return jnp.concatenate([half[:, begin:end] for half in halves], axis=1)

        bc = activated(0, rows, width, full).astype(jnp.bfloat16)
        b_part, c_part = bc[:, :STATE], bc[:, STATE:]
        scores = contract(c_part, b_part, ((1,), (1,)))
        scores = jnp.where(lower, scores, 0.0).astype(jnp.bfloat16)
        lefts = [
            jnp.concatenate(
                [
                    scores[b * BLOCK : (b + 1) * BLOCK, b * BLOCK : (b + 1) * BLOCK],
                    c_part[b * BLOCK : (b + 1) * BLOCK],
                ],
                axis=1,
            )
            for b in range(blocks)
        ]
        for index in later:
            inward_refs[index - 1][pl.ds(base, rows)] = chosen(inward, index)
            outward_refs[index - 1][pl.ds(scale_base, scale_rows)] = chosen(outward, index)
        if later:
            b_ref[pl.ds(base, rows)] = b_part
            for b in range(blocks):
                left_ref[pl.ds(base + b * BLOCK, BLOCK)] = lefts[b]
        inward = chosen(inward, 0)
        outward = chosen(outward, 0)
    else:
        inward = inward_ref[pl.ds(base, rows)]
        outward = outward_ref[pl.ds(scale_base, scale_rows)]
        b_part = b_ref[pl.ds(base, rows)]
        lefts = [left_ref[pl.ds(base + b * BLOCK, BLOCK)] for b in range(blocks)]

    tile = 2 * LANES if width % (2 * LANES) == 0 else LANES
    expand = spread(width // HEAD_DIM)
    compact = [
        jnp.concatenate(
            [
                inward[b * BLOCK : (b + 1) * BLOCK],
                outward[b * BLOCK : (b + 1) * BLOCK],
                outward[rows + 16 * b : rows + 16 * (b + 1)],
            ],
            axis=0,
        )
        for b in range(blocks)
    ]
    for b in range(blocks):
        top = b * BLOCK
        power = jnp.zeros((BLOCK, LANES), jnp.float32)
        if not first:
            power = power_ref[pl.ds(base + top, BLOCK)]
        for lo in range(0, width, tile):
            hi = lo + tile
            x_conv = activated(top, BLOCK, lo, hi)
            scales = contract(compact[b], expand[:, lo:hi], ((1,), (0,)))
            in_scale = scales[:BLOCK]
            out_scale = scales[BLOCK : 2 * BLOCK]
            mid_scale = scales[2 * BLOCK :]
            scaled = (x_conv * in_scale).astype(jnp.bfloat16)
            held = carry[:, lo:hi] * mid_scale[0:1]
            right = jnp.concatenate([scaled, held.astype(jnp.bfloat16)], axis=0)
            mixed = contract(lefts[b], right, ((1,), (0,)))
            total = mixed * out_scale + skip_ref[0:1, lo:hi] * x_conv
            if final:
                total_ref[top : top + BLOCK, lo:hi] = total
            else:
                total_ref[pl.ds(base + top, BLOCK), lo:hi] = total.astype(jnp.bfloat16)
            squares = total * total
            for lane in range(0, tile, LANES):
                power = power + squares[:, lane : lane + LANES]
            added = contract(b_part[top : top + BLOCK], scaled, ((0,), (0,)))
            carry[:, lo:hi] = (held + added) * out_scale[BLOCK - 1 : BLOCK]
        if final:
            summed = jnp.sum(power, axis=1, keepdims=True)
            norm = lax.rsqrt(summed * (1.0 / GROUP_WIDTH) + EPS)
            column = 0
            for index, size in enumerate(widths):
                if index < chunk:
                    block = earlier[index][pl.ds(base + top, BLOCK)].astype(jnp.float32)
                else:
                    block = total_ref[top : top + BLOCK]
                out_ref[top : top + BLOCK, column : column + size] = (
                    block * norm * gain_ref[0:1, column : column + size]
                ).astype(jnp.bfloat16)
                column += size
        else:
            sums_ref[pl.ds(base + top, BLOCK)] = power


def per_device(inputs, key_query, conv_inputs, conv_kq, step_size, decay_log, skip_gain, norm_gain):
    peers = lax.axis_size("ctx")
    me = lax.axis_index("ctx")
    place = me.reshape(1).astype(jnp.int32)
    rows = inputs.shape[0]
    owned = HEADS * HEAD_DIM // peers
    heads = HEADS // peers
    span = GROUP_WIDTH // owned
    whole_group = span == 1
    total_rows = peers * rows
    blocks = rows // BLOCK
    tiles = owned // LANES
    last = max(1, tiles // 4)
    widths = [(tiles - last) * LANES, last * LANES]
    offsets = [0, widths[0]]

    smem = pl.BlockSpec(memory_space=pltpu.SMEM)
    hbm = pl.BlockSpec(memory_space=pltpu.HBM)
    vmem = pl.BlockSpec(memory_space=pltpu.VMEM)
    params = pltpu.CompilerParams(vmem_limit_bytes=VMEM_LIMIT)

    def columns(a, first, size):
        return lax.dynamic_slice_in_dim(a, first, size, axis=1)

    lead_cols = widths[0] + 2 * STATE
    scalar_rows = scalar_units(heads, rows, lead_cols)[-1][3] + SUBLANES
    extents = {
        "full": (rows + scalar_rows, lead_cols + widths[1]),
        "lead": (rows + scalar_rows, lead_cols),
        "rest": (rows, widths[1]),
    }

    def pack(entries, after=()):
        token, _ = lax.optimization_barrier((place, after))
        heading = entries[0][1] != "rest"
        shapes = [jax.ShapeDtypeStruct(extents[kind], jnp.bfloat16) for _, kind in entries]
        operands = [token, inputs]
        in_specs = [smem, hbm]
        scratch = []
        if heading:
            operands += [key_query, decay_log, step_size]
            in_specs += [hbm] * 3
            scratch.append(pltpu.VMEM((2, rows, HEADS), jnp.float32))
            scratch.append(pltpu.VMEM((FIELDS, peers, heads, rows), jnp.float32))
            scratch.append(pltpu.VMEM(key_query.shape, jnp.bfloat16))
            scratch.append(pltpu.VMEM((len(entries), rows, 2 * STATE), jnp.bfloat16))
            scratch.append(pltpu.VMEM((len(entries), scalar_rows, lead_cols), jnp.bfloat16))
        scratch.append(pltpu.SemaphoreType.DMA((5, max(3, len(entries)))))
        return pl.pallas_call(
            functools.partial(
                pack_kernel,
                peers,
                span,
                widths,
                heads,
                entries,
                scalar_rows if heading else 0,
            ),
            in_specs=in_specs,
            out_specs=[hbm] * len(entries),
            out_shape=shapes,
            scratch_shapes=scratch,
            compiler_params=pltpu.CompilerParams(vmem_limit_bytes=PACK_VMEM),
            cost_estimate=pl.CostEstimate(
                flops=0,
                bytes_accessed=4 * sum(math.prod(shape.shape) for shape in shapes),
                transcendentals=0,
            ),
            name="pack",
        )(*operands)

    def send(message, code, after=()):
        message, _ = lax.optimization_barrier((message, after))
        pairs = [(i, (i + code) % peers) for i in range(peers)]
        return lax.ppermute(message, "ctx", pairs)

    far = sorted(range(2, peers - 1), key=lambda code: abs(code - peers // 2))
    near = [1, peers - 1]
    kinds = [(code, "lead") for code in far] + [(code, "full") for code in near + [0]]
    lead = {code: message for (code, _), message in zip(kinds, pack(kinds))}
    rest = {code: lead[code] for code in near + [0]}
    rest.update(zip(far, pack([(code, "rest") for code in far])))
    for code in far + near:
        lead[code] = send(lead[code], code)
    for code in far:
        rest[code] = send(rest[code], code, lead[code])
    for code in near:
        rest[code] = lead[code]
    received = [[slots[code] for code in range(peers)] for slots in (lead, rest)]

    taps_x = columns(conv_inputs, me * owned, owned)
    group = me // span
    taps_kq = jnp.concatenate(
        [
            columns(conv_kq, group * STATE, STATE),
            columns(conv_kq, (GROUPS + group) * STATE, STATE),
        ],
        axis=1,
    )
    skip = jnp.repeat(lax.dynamic_slice_in_dim(skip_gain, me * heads, heads), HEAD_DIM)[None]
    gain = columns(norm_gain[None], me * owned, owned)

    def by_source(count, lanes, dtype):
        spec = pl.BlockSpec((count, lanes), lambda i: (i, 0))
        return spec, jax.ShapeDtypeStruct((peers * count, lanes), dtype)

    def whole(count, lanes, dtype):
        return vmem, jax.ShapeDtypeStruct((peers * count, lanes), dtype)

    totals = []
    power = None
    shared = None
    for chunk, width in enumerate(widths):
        first = chunk == 0
        final = chunk == len(widths) - 1 and whole_group
        taps = taps_x[:, offsets[chunk] : offsets[chunk] + width]
        if first:
            taps = jnp.concatenate([taps, taps_kq], axis=1)
        cols = taps.shape[1]
        operands = [place, *received[chunk], taps, skip[:, offsets[chunk] : offsets[chunk] + width]]
        if not first:
            left, b_part, inward, outward = shared
            operands += [left, b_part, inward[chunk - 1], outward[chunk - 1], power]
        if final:
            operands += [gain, *totals]
        out = []
        if final:
            out.append(by_source(rows, owned, jnp.bfloat16))
        else:
            out.append(whole(rows, width, jnp.bfloat16))
            out.append(whole(rows, LANES, jnp.float32))
        if first:
            out.append(whole(rows, 2 * STATE, jnp.bfloat16))
            out.append(whole(rows, STATE, jnp.bfloat16))
            for count in (rows, rows + 16 * blocks):
                for size in widths[1:]:
                    out.append(whole(count, 2 * size // HEAD_DIM, jnp.bfloat16))
        scratch = [
            pltpu.VMEM((rows + HALO, cols), jnp.bfloat16),
            pltpu.VMEM((STATE, width), jnp.float32),
        ]
        if final:
            scratch.append(pltpu.VMEM((rows, width), jnp.float32))
        if first:
            scratch.append(pltpu.VMEM((scalar_rows, cols), jnp.bfloat16))
        results = pl.pallas_call(
            functools.partial(mixer_kernel, peers, rows, heads, chunk, widths, whole_group),
            grid=(peers,),
            in_specs=[smem] + [vmem] * (len(operands) - 1),
            out_specs=[spec for spec, _ in out],
            out_shape=[shape for _, shape in out],
            scratch_shapes=scratch,
            compiler_params=params,
            cost_estimate=pl.CostEstimate(
                flops=2 * total_rows * width * 450,
                bytes_accessed=total_rows * (2 * cols + 8 * width),
                transcendentals=total_rows * cols,
            ),
            name=f"mixer{chunk}",
        )(*operands)
        if final:
            return results[0]
        totals.append(results[0])
        power = results[1]
        if first:
            rest = results[4:]
            shared = (results[2], results[3], rest[: len(rest) // 2], rest[len(rest) // 2 :])
    sharers = [list(range(i, i + span)) for i in range(0, peers, span)]
    summed = jnp.sum(power, axis=1, keepdims=True)
    summed = lax.psum(summed, "ctx", axis_index_groups=sharers)
    total = jnp.concatenate(totals, axis=1)
    return (total * lax.rsqrt(summed * (1.0 / GROUP_WIDTH) + EPS) * gain).astype(jnp.bfloat16)


def solution(mesh):
    in_specs = (
        P(("dp", "ctx"), None),
        P(("dp", "ctx"), None),
        P(),
        P(),
        P(("dp", "ctx"), None),
        P(("dp", "ctx"), None),
        P(),
        P(),
    )
    out_specs = P("dp", "ctx")
    return jax.shard_map(
        per_device, mesh=mesh, in_specs=in_specs, out_specs=out_specs, check_vma=False
    )
```

```python
import functools
import math

import jax
import jax.numpy as jnp
import numpy as np
from jax import lax
from jax.experimental import pallas as pl
from jax.experimental.pallas import tpu as pltpu
from jax.sharding import PartitionSpec as P

HEADS = 128
HEAD_DIM = 64
STATE = 128
GROUPS = 8
KW = 4
BLOCK = 128
GROUP_WIDTH = HEADS * HEAD_DIM // GROUPS
EPS = 1e-05
HALO = 16
LANES = 128
SUBLANES = 8
FIELDS = 2
ROUND_ORDER = (0, 1, 2, 4, 3, 5, 6, 7)
STRIP = 64
PACK_VMEM = 58 * 1024 * 1024
VMEM_LIMIT = 32 * 1024 * 1024


def contract(a, b, dims):
    return lax.dot_general(a, b, (dims, ((), ())), preferred_element_type=jnp.float32)


def as_parts(v, count):
    parts = []
    for _ in range(count):
        part = v.astype(jnp.bfloat16)
        parts.append(part)
        v = v - part.astype(jnp.float32)
    return parts


def scalar_units(heads, rows, cols):
    units = []
    for p in range(FIELDS):
        for head in range(0, heads, SUBLANES):
            line, column = divmod(len(units), cols // rows)
            units.append((p, head, min(SUBLANES, heads), line * SUBLANES, column * rows))
    return units


def pack_kernel(peers, span, widths, heads, entries, scalar_rows, *refs):
    refs = list(refs)
    owner_ref = refs.pop(0)
    x_ref = refs.pop(0)
    heading = scalar_rows > 0
    if heading:
        kq_ref, decay_ref, step_ref = refs[:3]
        del refs[:3]
    outs = refs[: len(entries)]
    del refs[: len(entries)]
    if heading:
        raw_scalars, scalars, kq_near = refs[:3]
    sems = refs[-1]
    rows = x_ref.shape[0]
    owned = HEADS * HEAD_DIM // peers
    lead = widths[0] + 2 * STATE
    copies = []
    if heading:
        loads = [
            pltpu.make_async_copy(ref, raw_scalars.at[i], sems.at[2, i])
            for i, ref in enumerate((decay_ref, step_ref))
        ]
        loads.append(pltpu.make_async_copy(kq_ref, kq_near, sems.at[2, 2]))
        for load in loads:
            load.start()
    owners = [owner_ref[code] for code, _ in entries]
    for i, (owner, (_, kind)) in enumerate(zip(owners, entries)):
        pieces = {
            "full": [(0, 0, 0), (1, widths[0], lead)],
            "lead": [(0, 0, 0)],
            "rest": [(1, widths[0], 0)],
        }[kind]
        for index, offset, left in pieces:
            column = pl.multiple_of(owner * owned + offset, LANES)
            copies.append(
                pltpu.make_async_copy(
                    x_ref.at[:, pl.ds(column, widths[index])],
                    outs[i].at[0:rows, left : left + widths[index]],
                    sems.at[index, i],
                )
            )
    for copy in copies:
        copy.start()
    if heading:
        for load in loads:
            load.wait()
        fields = [raw_scalars[0].T, raw_scalars[1].T]
        for p, field in enumerate(fields):
            for owner in range(peers):
                scalars[p, owner] = field[owner * heads : (owner + 1) * heads]
        for i, owner in enumerate(owners):
            outs[i][rows:] = jnp.zeros((scalar_rows, outs[i].shape[1]), jnp.bfloat16)
            for p, head, count, top, left in scalar_units(heads, rows, lead):
                outs[i][rows + top : rows + top + count, left : left + rows] = scalars[
                    p, owner, head : head + count
                ].astype(jnp.bfloat16)
            for j in range(2):
                column = pl.multiple_of((j * GROUPS + owner // span) * STATE, LANES)
                left = widths[0] + j * STATE
                outs[i][0:rows, left : left + STATE] = kq_near[:, pl.ds(column, STATE)]
    for copy in copies:
        copy.wait()


def mixer_kernel(peers, rows, heads, chunk, widths, whole_group, *refs):
    refs = list(refs)

    def take(count):
        taken = refs[:count]
        del refs[:count]
        return taken

    first = chunk == 0
    final = chunk == len(widths) - 1 and whole_group
    later = range(1, len(widths)) if first else ()
    width = widths[chunk]
    (slot_ref,) = take(1)
    parts = take(peers)
    taps_ref, skip_ref = take(2)
    if not first:
        left_ref, b_ref, inward_ref, outward_ref, power_ref = take(5)
    if final:
        (gain_ref,) = take(1)
        earlier = take(chunk)
        (out_ref,) = take(1)
    else:
        total_ref, sums_ref = take(2)
    if first and later:
        left_ref, b_ref = take(2)
        inward_refs = take(len(later))
        outward_refs = take(len(later))
    wide, carry = take(2)
    if final:
        (total_ref,) = take(1)
    if first:
        (scalars,) = take(1)
    blocks = rows // BLOCK
    step = pl.program_id(0)
    scale_rows = rows + 16 * blocks
    base = pl.multiple_of(step * rows, rows)
    scale_base = pl.multiple_of(step * scale_rows, 32)

    @pl.when(step == 0)
    def _():
        carry[...] = jnp.zeros_like(carry)
        wide[rows : rows + HALO] = jnp.zeros((HALO, wide.shape[1]), jnp.bfloat16)

    wide[0:HALO] = wide[rows : rows + HALO]
    slot = slot_ref[step]
    for k in range(peers):

        @pl.when(slot == k)
        def _():
            if first:
                wide[HALO : HALO + rows] = parts[k][0:rows, 0 : wide.shape[1]]
                scalars[...] = parts[k][rows:, 0 : wide.shape[1]]
            else:
                wide[HALO : HALO + rows] = parts[k][0:rows, parts[k].shape[1] - width :]

    def spread(count):
        head_of = lax.broadcasted_iota(jnp.int32, (2 * count, count * HEAD_DIM), 1) // HEAD_DIM
        row = lax.rem(
            lax.broadcasted_iota(jnp.int32, (2 * count, count * HEAD_DIM), 0), count
        )
        return jnp.where(head_of == row, 1.0, 0.0).astype(jnp.bfloat16)

    def activated(top, size, lo, hi):
        rows_out = []
        for r in range(top, top + size, STRIP):
            lanes_out = []
            for lane in range(lo, hi, LANES):
                tap = [taps_ref[k : k + 1, lane : lane + LANES] for k in range(KW)]
                now = wide[r : r + STRIP + HALO, lane : lane + LANES].astype(jnp.float32)[HALO // 2 :]
                before = pltpu.roll(now, 1, 0)
                older = pltpu.roll(tap[0] * before + tap[1] * now, 2, 0)
                summed = (older + (tap[2] * before + tap[3] * now))[HALO // 2 :]
                lanes_out.append(
                    summed * pltpu.reciprocal(1.0 + jnp.exp(-summed), approx=True)
                )
            rows_out.append(jnp.concatenate(lanes_out, axis=1))
        return jnp.concatenate(rows_out, axis=0)

    if first:
        full = width + 2 * STATE
        row = lax.broadcasted_iota(jnp.int32, (rows, rows), 0)
        col = lax.broadcasted_iota(jnp.int32, (rows, rows), 1)
        lower = (row >= col) & (row // BLOCK == col // BLOCK)
        ones = jnp.where(lower, 1.0, 0.0).astype(jnp.bfloat16)
        eye = jnp.where(row == col, 1.0, 0.0).astype(jnp.bfloat16)

        def field(p):
            pieces = [
                scalars[top : top + count, left : left + rows].astype(jnp.float32)
                for q, _, count, top, left in scalar_units(heads, rows, full)
                if q == p
            ]
            return jnp.concatenate(pieces, axis=0).astype(jnp.bfloat16)

        cumul = contract(ones, field(0), ((1,), (1,)))
        steps = contract(eye, field(1), ((1,), (1,)))
        middles = [
            cumul[b * BLOCK + BLOCK // 2 - 1 : b * BLOCK + BLOCK // 2] for b in range(blocks)
        ]
        middle = jnp.concatenate([jnp.broadcast_to(m, (BLOCK, heads)) for m in middles], axis=0)
        inward = as_parts(steps * jnp.exp(middle - cumul), 2)
        outward = as_parts(
            jnp.concatenate(
                [jnp.exp(cumul - middle)]
                + [jnp.broadcast_to(jnp.exp(m), (16, heads)) for m in middles],
                axis=0,
            ),
            2,
        )

        def chosen(halves, index):
            begin = sum(widths[:index]) // HEAD_DIM
            end = begin + widths[index] // HEAD_DIM
            return jnp.concatenate([half[:, begin:end] for half in halves], axis=1)

        bc = activated(0, rows, width, full).astype(jnp.bfloat16)
        b_part, c_part = bc[:, :STATE], bc[:, STATE:]
        scores = contract(c_part, b_part, ((1,), (1,)))
        scores = jnp.where(lower, scores, 0.0).astype(jnp.bfloat16)
        lefts = [
            jnp.concatenate(
                [
                    scores[b * BLOCK : (b + 1) * BLOCK, b * BLOCK : (b + 1) * BLOCK],
                    c_part[b * BLOCK : (b + 1) * BLOCK],
                ],
                axis=1,
            )
            for b in range(blocks)
        ]
        for index in later:
            inward_refs[index - 1][pl.ds(base, rows)] = chosen(inward, index)
            outward_refs[index - 1][pl.ds(scale_base, scale_rows)] = chosen(outward, index)
        if later:
            b_ref[pl.ds(base, rows)] = b_part
            for b in range(blocks):
                left_ref[pl.ds(base + b * BLOCK, BLOCK)] = lefts[b]
        inward = chosen(inward, 0)
        outward = chosen(outward, 0)
    else:
        inward = inward_ref[pl.ds(base, rows)]
        outward = outward_ref[pl.ds(scale_base, scale_rows)]
        b_part = b_ref[pl.ds(base, rows)]
        lefts = [left_ref[pl.ds(base + b * BLOCK, BLOCK)] for b in range(blocks)]

    tile = 2 * LANES if width % (2 * LANES) == 0 else LANES
    expand = spread(width // HEAD_DIM)
    compact = [
        jnp.concatenate(
            [
                inward[b * BLOCK : (b + 1) * BLOCK],
                outward[b * BLOCK : (b + 1) * BLOCK],
                outward[rows + 16 * b : rows + 16 * (b + 1)],
            ],
            axis=0,
        )
        for b in range(blocks)
    ]
    for b in range(blocks):
        top = b * BLOCK
        power = jnp.zeros((BLOCK, LANES), jnp.float32)
        if not first:
            power = power_ref[pl.ds(base + top, BLOCK)]
        for lo in range(0, width, tile):
            hi = lo + tile
            x_conv = activated(top, BLOCK, lo, hi)
            scales = contract(compact[b], expand[:, lo:hi], ((1,), (0,)))
            in_scale = scales[:BLOCK]
            out_scale = scales[BLOCK : 2 * BLOCK]
            mid_scale = scales[2 * BLOCK :]
            scaled = (x_conv * in_scale).astype(jnp.bfloat16)
            held = carry[:, lo:hi] * mid_scale[0:1]
            right = jnp.concatenate([scaled, held.astype(jnp.bfloat16)], axis=0)
            mixed = contract(lefts[b], right, ((1,), (0,)))
            total = mixed * out_scale + skip_ref[0:1, lo:hi] * x_conv
            if final:
                total_ref[top : top + BLOCK, lo:hi] = total
            else:
                total_ref[pl.ds(base + top, BLOCK), lo:hi] = total.astype(jnp.bfloat16)
            squares = total * total
            for lane in range(0, tile, LANES):
                power = power + squares[:, lane : lane + LANES]
            added = contract(b_part[top : top + BLOCK], scaled, ((0,), (0,)))
            carry[:, lo:hi] = (held + added) * out_scale[BLOCK - 1 : BLOCK]
        if final:
            summed = jnp.sum(power, axis=1, keepdims=True)
            norm = lax.rsqrt(summed * (1.0 / GROUP_WIDTH) + EPS)
            column = 0
            for index, size in enumerate(widths):
                if index < chunk:
                    block = earlier[index][pl.ds(base + top, BLOCK)].astype(jnp.float32)
                else:
                    block = total_ref[top : top + BLOCK]
                out_ref[top : top + BLOCK, column : column + size] = (
                    block * norm * gain_ref[0:1, column : column + size]
                ).astype(jnp.bfloat16)
                column += size
        else:
            sums_ref[pl.ds(base + top, BLOCK)] = power


def per_device(inputs, key_query, conv_inputs, conv_kq, step_size, decay_log, skip_gain, norm_gain):
    peers = lax.axis_size("ctx")
    me = lax.axis_index("ctx")
    position = np.arange(peers)
    if peers == len(ROUND_ORDER):
        position = np.argsort(ROUND_ORDER)
    steps = np.arange(peers)
    owner_table = np.argsort(position)[(position[:, None] + steps) % peers].astype(np.int32)
    slot_table = ((position[:, None] - position) % peers).astype(np.int32)
    owners = lax.dynamic_index_in_dim(jnp.asarray(owner_table), me, 0, False)
    slots = lax.dynamic_index_in_dim(jnp.asarray(slot_table), me, 0, False)
    rows = inputs.shape[0]
    owned = HEADS * HEAD_DIM // peers
    heads = HEADS // peers
    span = GROUP_WIDTH // owned
    whole_group = span == 1
    total_rows = peers * rows
    blocks = rows // BLOCK
    tiles = owned // LANES
    last = max(1, tiles // 4)
    widths = [(tiles - last) * LANES, last * LANES]
    offsets = [0, widths[0]]

    smem = pl.BlockSpec(memory_space=pltpu.SMEM)
    hbm = pl.BlockSpec(memory_space=pltpu.HBM)
    vmem = pl.BlockSpec(memory_space=pltpu.VMEM)
    params = pltpu.CompilerParams(vmem_limit_bytes=VMEM_LIMIT)

    def columns(a, first, size):
        return lax.dynamic_slice_in_dim(a, first, size, axis=1)

    lead_cols = widths[0] + 2 * STATE
    scalar_rows = scalar_units(heads, rows, lead_cols)[-1][3] + SUBLANES
    extents = {
        "full": (rows + scalar_rows, lead_cols + widths[1]),
        "lead": (rows + scalar_rows, lead_cols),
        "rest": (rows, widths[1]),
    }

    def pack(entries):
        heading = entries[0][1] != "rest"
        shapes = [jax.ShapeDtypeStruct(extents[kind], jnp.bfloat16) for _, kind in entries]
        operands = [owners, inputs]
        in_specs = [smem, hbm]
        scratch = []
        if heading:
            operands += [key_query, decay_log, step_size]
            in_specs += [hbm] * 3
            scratch.append(pltpu.VMEM((2, rows, HEADS), jnp.float32))
            scratch.append(pltpu.VMEM((FIELDS, peers, heads, rows), jnp.float32))
            scratch.append(pltpu.VMEM(key_query.shape, jnp.bfloat16))
        scratch.append(pltpu.SemaphoreType.DMA((3, max(3, len(entries)))))
        return pl.pallas_call(
            functools.partial(
                pack_kernel,
                peers,
                span,
                widths,
                heads,
                entries,
                scalar_rows if heading else 0,
            ),
            in_specs=in_specs,
            out_specs=[vmem] * len(entries),
            out_shape=shapes,
            scratch_shapes=scratch,
            compiler_params=pltpu.CompilerParams(vmem_limit_bytes=PACK_VMEM),
            cost_estimate=pl.CostEstimate(
                flops=0,
                bytes_accessed=4 * sum(math.prod(shape.shape) for shape in shapes),
                transcendentals=0,
            ),
            name="pack",
        )(*operands)

    def send(message, code, after=()):
        message, _ = lax.optimization_barrier((message, after))
        pairs = [(i, int(owner_table[i, code])) for i in range(peers)]
        return lax.ppermute(message, "ctx", pairs)

    far = sorted(range(2, peers - 1), key=lambda code: abs(code - peers // 2))
    near = [1, peers - 1]
    kinds = [(code, "lead") for code in far] + [(code, "full") for code in near + [0]]
    lead = {code: message for (code, _), message in zip(kinds, pack(kinds))}
    rest = {code: lead[code] for code in near + [0]}
    rest.update(zip(far, pack([(code, "rest") for code in far])))
    for code in far + near:
        lead[code] = send(lead[code], code)
    for code in far:
        rest[code] = send(rest[code], code, lead[code])
    for code in near:
        rest[code] = lead[code]
    received = [[parts[code] for code in range(peers)] for parts in (lead, rest)]

    taps_x = columns(conv_inputs, me * owned, owned)
    group = me // span
    taps_kq = jnp.concatenate(
        [
            columns(conv_kq, group * STATE, STATE),
            columns(conv_kq, (GROUPS + group) * STATE, STATE),
        ],
        axis=1,
    )
    skip = jnp.repeat(lax.dynamic_slice_in_dim(skip_gain, me * heads, heads), HEAD_DIM)[None]
    gain = columns(norm_gain[None], me * owned, owned)

    def by_source(count, lanes, dtype):
        spec = pl.BlockSpec((count, lanes), lambda i: (i, 0))
        return spec, jax.ShapeDtypeStruct((peers * count, lanes), dtype)

    def whole(count, lanes, dtype):
        return vmem, jax.ShapeDtypeStruct((peers * count, lanes), dtype)

    totals = []
    power = None
    shared = None
    for chunk, width in enumerate(widths):
        first = chunk == 0
        final = chunk == len(widths) - 1 and whole_group
        taps = taps_x[:, offsets[chunk] : offsets[chunk] + width]
        if first:
            taps = jnp.concatenate([taps, taps_kq], axis=1)
        cols = taps.shape[1]
        operands = [slots, *received[chunk], taps, skip[:, offsets[chunk] : offsets[chunk] + width]]
        if not first:
            left, b_part, inward, outward = shared
            operands += [left, b_part, inward[chunk - 1], outward[chunk - 1], power]
        if final:
            operands += [gain, *totals]
        out = []
        if final:
            out.append(by_source(rows, owned, jnp.bfloat16))
        else:
            out.append(whole(rows, width, jnp.bfloat16))
            out.append(whole(rows, LANES, jnp.float32))
        if first:
            out.append(whole(rows, 2 * STATE, jnp.bfloat16))
            out.append(whole(rows, STATE, jnp.bfloat16))
            for count in (rows, rows + 16 * blocks):
                for size in widths[1:]:
                    out.append(whole(count, 2 * size // HEAD_DIM, jnp.bfloat16))
        scratch = [
            pltpu.VMEM((rows + HALO, cols), jnp.bfloat16),
            pltpu.VMEM((STATE, width), jnp.float32),
        ]
        if final:
            scratch.append(pltpu.VMEM((rows, width), jnp.float32))
        if first:
            scratch.append(pltpu.VMEM((scalar_rows, cols), jnp.bfloat16))
        results = pl.pallas_call(
            functools.partial(mixer_kernel, peers, rows, heads, chunk, widths, whole_group),
            grid=(peers,),
            in_specs=[smem] + [vmem] * (len(operands) - 1),
            out_specs=[spec for spec, _ in out],
            out_shape=[shape for _, shape in out],
            scratch_shapes=scratch,
            compiler_params=params,
            cost_estimate=pl.CostEstimate(
                flops=2 * total_rows * width * 450,
                bytes_accessed=total_rows * (2 * cols + 8 * width),
                transcendentals=total_rows * cols,
            ),
            name=f"mixer{chunk}",
        )(*operands)
        if final:
            return results[0]
        totals.append(results[0])
        power = results[1]
        if first:
            rest = results[4:]
            shared = (results[2], results[3], rest[: len(rest) // 2], rest[len(rest) // 2 :])
    sharers = [list(range(i, i + span)) for i in range(0, peers, span)]
    summed = jnp.sum(power, axis=1, keepdims=True)
    summed = lax.psum(summed, "ctx", axis_index_groups=sharers)
    total = jnp.concatenate(totals, axis=1)
    return (total * lax.rsqrt(summed * (1.0 / GROUP_WIDTH) + EPS) * gain).astype(jnp.bfloat16)


def solution(mesh):
    in_specs = (
        P(("dp", "ctx"), None),
        P(("dp", "ctx"), None),
        P(),
        P(),
        P(("dp", "ctx"), None),
        P(("dp", "ctx"), None),
        P(),
        P(),
    )
    out_specs = P("dp", "ctx")
    return jax.shard_map(
        per_device, mesh=mesh, in_specs=in_specs, out_specs=out_specs, check_vma=False
    )
```

```python
import functools
import math

import jax
import jax.numpy as jnp
import numpy as np
from jax import lax
from jax.experimental import pallas as pl
from jax.experimental.pallas import tpu as pltpu
from jax.sharding import PartitionSpec as P

HEADS = 128
HEAD_DIM = 64
STATE = 128
GROUPS = 8
KW = 4
BLOCK = 128
GROUP_WIDTH = HEADS * HEAD_DIM // GROUPS
EPS = 1e-05
HALO = 16
LANES = 128
SUBLANES = 8
FIELDS = 2
ROUND_ORDER = (0, 1, 2, 4, 3, 5, 6, 7)
STRIP = 64
PACK_VMEM = 58 * 1024 * 1024
VMEM_LIMIT = 32 * 1024 * 1024


def contract(a, b, dims):
    return lax.dot_general(a, b, (dims, ((), ())), preferred_element_type=jnp.float32)


def as_parts(v, count):
    parts = []
    for _ in range(count):
        part = v.astype(jnp.bfloat16)
        parts.append(part)
        v = v - part.astype(jnp.float32)
    return parts


def scalar_units(heads, rows, cols):
    units = []
    for p in range(FIELDS):
        for head in range(0, heads, SUBLANES):
            line, column = divmod(len(units), cols // rows)
            units.append((p, head, min(SUBLANES, heads), line * SUBLANES, column * rows))
    return units


def pack_kernel(peers, span, widths, heads, entries, scalar_rows, *refs):
    refs = list(refs)
    owner_ref = refs.pop(0)
    x_ref = refs.pop(0)
    heading = scalar_rows > 0
    if heading:
        kq_ref, decay_ref, step_ref = refs[:3]
        del refs[:3]
    outs = refs[: len(entries)]
    del refs[: len(entries)]
    if heading:
        raw_scalars, scalars, kq_near = refs[:3]
    sems = refs[-1]
    rows = x_ref.shape[0]
    owned = HEADS * HEAD_DIM // peers
    lead = widths[0] + 2 * STATE
    copies = []
    if heading:
        loads = [
            pltpu.make_async_copy(ref, raw_scalars.at[i], sems.at[2, i])
            for i, ref in enumerate((decay_ref, step_ref))
        ]
        loads.append(pltpu.make_async_copy(kq_ref, kq_near, sems.at[2, 2]))
        for load in loads:
            load.start()
    owners = [owner_ref[code] for code, _ in entries]
    for i, (owner, (_, kind)) in enumerate(zip(owners, entries)):
        pieces = {
            "full": [(0, 0, 0), (1, widths[0], lead)],
            "lead": [(0, 0, 0)],
            "rest": [(1, widths[0], 0)],
        }[kind]
        for index, offset, left in pieces:
            column = pl.multiple_of(owner * owned + offset, LANES)
            copies.append(
                pltpu.make_async_copy(
                    x_ref.at[:, pl.ds(column, widths[index])],
                    outs[i].at[0:rows, left : left + widths[index]],
                    sems.at[index, i],
                )
            )
    for copy in copies:
        copy.start()
    if heading:
        for load in loads:
            load.wait()
        fields = [raw_scalars[0].T, raw_scalars[1].T]
        for p, field in enumerate(fields):
            for owner in range(peers):
                scalars[p, owner] = field[owner * heads : (owner + 1) * heads]
        for i, owner in enumerate(owners):
            outs[i][rows:] = jnp.zeros((scalar_rows, outs[i].shape[1]), jnp.bfloat16)
            for p, head, count, top, left in scalar_units(heads, rows, lead):
                outs[i][rows + top : rows + top + count, left : left + rows] = scalars[
                    p, owner, head : head + count
                ].astype(jnp.bfloat16)
            for j in range(2):
                column = pl.multiple_of((j * GROUPS + owner // span) * STATE, LANES)
                left = widths[0] + j * STATE
                outs[i][0:rows, left : left + STATE] = kq_near[:, pl.ds(column, STATE)]
    for copy in copies:
        copy.wait()


def mixer_kernel(peers, rows, heads, chunk, widths, whole_group, *refs):
    refs = list(refs)

    def take(count):
        taken = refs[:count]
        del refs[:count]
        return taken

    first = chunk == 0
    final = chunk == len(widths) - 1 and whole_group
    later = range(1, len(widths)) if first else ()
    width = widths[chunk]
    (slot_ref,) = take(1)
    parts = take(peers)
    taps_ref, skip_ref = take(2)
    if not first:
        left_ref, b_ref, inward_ref, outward_ref, power_ref = take(5)
    if final:
        (gain_ref,) = take(1)
        earlier = take(chunk)
        (out_ref,) = take(1)
    else:
        total_ref, sums_ref = take(2)
    if first and later:
        left_ref, b_ref = take(2)
        inward_refs = take(len(later))
        outward_refs = take(len(later))
    wide, carry = take(2)
    if final:
        (total_ref,) = take(1)
    if first:
        (scalars,) = take(1)
    blocks = rows // BLOCK
    step = pl.program_id(0)
    scale_rows = rows + 16 * blocks
    base = pl.multiple_of(step * rows, rows)
    scale_base = pl.multiple_of(step * scale_rows, 32)

    @pl.when(step == 0)
    def _():
        carry[...] = jnp.zeros_like(carry)
        wide[rows : rows + HALO] = jnp.zeros((HALO, wide.shape[1]), jnp.bfloat16)

    wide[0:HALO] = wide[rows : rows + HALO]
    slot = slot_ref[step]
    for k in range(peers):

        @pl.when(slot == k)
        def _():
            if first:
                wide[HALO : HALO + rows] = parts[k][0:rows, 0 : wide.shape[1]]
                scalars[...] = parts[k][rows:, 0 : wide.shape[1]]
            else:
                wide[HALO : HALO + rows] = parts[k][0:rows, parts[k].shape[1] - width :]

    def spread(count):
        head_of = lax.broadcasted_iota(jnp.int32, (2 * count, count * HEAD_DIM), 1) // HEAD_DIM
        row = lax.rem(
            lax.broadcasted_iota(jnp.int32, (2 * count, count * HEAD_DIM), 0), count
        )
        return jnp.where(head_of == row, 1.0, 0.0).astype(jnp.bfloat16)

    def activated(top, size, lo, hi):
        rows_out = []
        for r in range(top, top + size, STRIP):
            lanes_out = []
            for lane in range(lo, hi, LANES):
                tap = [taps_ref[k : k + 1, lane : lane + LANES] for k in range(KW)]
                now = wide[r : r + STRIP + HALO, lane : lane + LANES].astype(jnp.float32)[HALO // 2 :]
                before = pltpu.roll(now, 1, 0)
                older = pltpu.roll(tap[0] * before + tap[1] * now, 2, 0)
                summed = (older + (tap[2] * before + tap[3] * now))[HALO // 2 :]
                lanes_out.append(
                    summed * pltpu.reciprocal(1.0 + jnp.exp(-summed), approx=True)
                )
            rows_out.append(jnp.concatenate(lanes_out, axis=1))
        return jnp.concatenate(rows_out, axis=0)

    if first:
        full = width + 2 * STATE
        row = lax.broadcasted_iota(jnp.int32, (rows, rows), 0)
        col = lax.broadcasted_iota(jnp.int32, (rows, rows), 1)
        lower = (row >= col) & (row // BLOCK == col // BLOCK)
        ones = jnp.where(lower, 1.0, 0.0).astype(jnp.bfloat16)
        eye = jnp.where(row == col, 1.0, 0.0).astype(jnp.bfloat16)

        def field(p):
            pieces = [
                scalars[top : top + count, left : left + rows].astype(jnp.float32)
                for q, _, count, top, left in scalar_units(heads, rows, full)
                if q == p
            ]
            return jnp.concatenate(pieces, axis=0).astype(jnp.bfloat16)

        cumul = contract(ones, field(0), ((1,), (1,)))
        steps = contract(eye, field(1), ((1,), (1,)))
        middles = [
            cumul[b * BLOCK + BLOCK // 2 - 1 : b * BLOCK + BLOCK // 2] for b in range(blocks)
        ]
        middle = jnp.concatenate([jnp.broadcast_to(m, (BLOCK, heads)) for m in middles], axis=0)
        inward = as_parts(steps * jnp.exp(middle - cumul), 2)
        outward = as_parts(
            jnp.concatenate(
                [jnp.exp(cumul - middle)]
                + [jnp.broadcast_to(jnp.exp(m), (16, heads)) for m in middles],
                axis=0,
            ),
            2,
        )

        def chosen(halves, index):
            begin = sum(widths[:index]) // HEAD_DIM
            end = begin + widths[index] // HEAD_DIM
            return jnp.concatenate([half[:, begin:end] for half in halves], axis=1)

        bc = activated(0, rows, width, full).astype(jnp.bfloat16)
        b_part, c_part = bc[:, :STATE], bc[:, STATE:]
        scores = contract(c_part, b_part, ((1,), (1,)))
        scores = jnp.where(lower, scores, 0.0).astype(jnp.bfloat16)
        lefts = [
            jnp.concatenate(
                [
                    scores[b * BLOCK : (b + 1) * BLOCK, b * BLOCK : (b + 1) * BLOCK],
                    c_part[b * BLOCK : (b + 1) * BLOCK],
                ],
                axis=1,
            )
            for b in range(blocks)
        ]
        for index in later:
            inward_refs[index - 1][pl.ds(base, rows)] = chosen(inward, index)
            outward_refs[index - 1][pl.ds(scale_base, scale_rows)] = chosen(outward, index)
        if later:
            b_ref[pl.ds(base, rows)] = b_part
            for b in range(blocks):
                left_ref[pl.ds(base + b * BLOCK, BLOCK)] = lefts[b]
        inward = chosen(inward, 0)
        outward = chosen(outward, 0)
    else:
        inward = inward_ref[pl.ds(base, rows)]
        outward = outward_ref[pl.ds(scale_base, scale_rows)]
        b_part = b_ref[pl.ds(base, rows)]
        lefts = [left_ref[pl.ds(base + b * BLOCK, BLOCK)] for b in range(blocks)]

    tile = 2 * LANES if width % (2 * LANES) == 0 else LANES
    expand = spread(width // HEAD_DIM)
    compact = [
        jnp.concatenate(
            [
                inward[b * BLOCK : (b + 1) * BLOCK],
                outward[b * BLOCK : (b + 1) * BLOCK],
                outward[rows + 16 * b : rows + 16 * (b + 1)],
            ],
            axis=0,
        )
        for b in range(blocks)
    ]
    for b in range(blocks):
        top = b * BLOCK
        power = jnp.zeros((BLOCK, LANES), jnp.float32)
        if not first:
            power = power_ref[pl.ds(base + top, BLOCK)]
        for lo in range(0, width, tile):
            hi = lo + tile
            x_conv = activated(top, BLOCK, lo, hi)
            scales = contract(compact[b], expand[:, lo:hi], ((1,), (0,)))
            in_scale = scales[:BLOCK]
            out_scale = scales[BLOCK : 2 * BLOCK]
            mid_scale = scales[2 * BLOCK :]
            scaled = (x_conv * in_scale).astype(jnp.bfloat16)
            held = carry[:, lo:hi] * mid_scale[0:1]
            right = jnp.concatenate([scaled, held.astype(jnp.bfloat16)], axis=0)
            mixed = contract(lefts[b], right, ((1,), (0,)))
            total = mixed * out_scale + skip_ref[0:1, lo:hi] * x_conv
            if final:
                total_ref[top : top + BLOCK, lo:hi] = total
            else:
                total_ref[pl.ds(base + top, BLOCK), lo:hi] = total.astype(jnp.bfloat16)
            squares = total * total
            for lane in range(0, tile, LANES):
                power = power + squares[:, lane : lane + LANES]
            added = contract(b_part[top : top + BLOCK], scaled, ((0,), (0,)))
            carry[:, lo:hi] = (held + added) * out_scale[BLOCK - 1 : BLOCK]
        if final:
            summed = jnp.sum(power, axis=1, keepdims=True)
            norm = lax.rsqrt(summed * (1.0 / GROUP_WIDTH) + EPS)
            column = 0
            for index, size in enumerate(widths):
                if index < chunk:
                    block = earlier[index][pl.ds(base + top, BLOCK)].astype(jnp.float32)
                else:
                    block = total_ref[top : top + BLOCK]
                out_ref[top : top + BLOCK, column : column + size] = (
                    block * norm * gain_ref[0:1, column : column + size]
                ).astype(jnp.bfloat16)
                column += size
        else:
            sums_ref[pl.ds(base + top, BLOCK)] = power


def per_device(inputs, key_query, conv_inputs, conv_kq, step_size, decay_log, skip_gain, norm_gain):
    peers = lax.axis_size("ctx")
    me = lax.axis_index("ctx")
    position = np.arange(peers)
    if peers == len(ROUND_ORDER):
        position = np.argsort(ROUND_ORDER)
    steps = np.arange(peers)
    owner_table = np.argsort(position)[(position[:, None] + steps) % peers].astype(np.int32)
    slot_table = ((position[:, None] - position) % peers).astype(np.int32)
    owners = lax.dynamic_index_in_dim(jnp.asarray(owner_table), me, 0, False)
    slots = lax.dynamic_index_in_dim(jnp.asarray(slot_table), me, 0, False)
    rows = inputs.shape[0]
    owned = HEADS * HEAD_DIM // peers
    heads = HEADS // peers
    span = GROUP_WIDTH // owned
    whole_group = span == 1
    total_rows = peers * rows
    blocks = rows // BLOCK
    tiles = owned // LANES
    last = max(1, tiles // 4)
    widths = [(tiles - last) * LANES, last * LANES]
    offsets = [0, widths[0]]

    smem = pl.BlockSpec(memory_space=pltpu.SMEM)
    hbm = pl.BlockSpec(memory_space=pltpu.HBM)
    vmem = pl.BlockSpec(memory_space=pltpu.VMEM)
    params = pltpu.CompilerParams(vmem_limit_bytes=VMEM_LIMIT)

    def columns(a, first, size):
        return lax.dynamic_slice_in_dim(a, first, size, axis=1)

    lead_cols = widths[0] + 2 * STATE
    scalar_rows = scalar_units(heads, rows, lead_cols)[-1][3] + SUBLANES
    extents = {
        "full": (rows + scalar_rows, lead_cols + widths[1]),
        "lead": (rows + scalar_rows, lead_cols),
        "rest": (rows, widths[1]),
    }

    def pack(entries):
        heading = entries[0][1] != "rest"
        shapes = [jax.ShapeDtypeStruct(extents[kind], jnp.bfloat16) for _, kind in entries]
        operands = [owners, inputs]
        in_specs = [smem, hbm]
        scratch = []
        if heading:
            operands += [key_query, decay_log, step_size]
            in_specs += [hbm] * 3
            scratch.append(pltpu.VMEM((2, rows, HEADS), jnp.float32))
            scratch.append(pltpu.VMEM((FIELDS, peers, heads, rows), jnp.float32))
            scratch.append(pltpu.VMEM(key_query.shape, jnp.bfloat16))
        scratch.append(pltpu.SemaphoreType.DMA((3, max(3, len(entries)))))
        return pl.pallas_call(
            functools.partial(
                pack_kernel,
                peers,
                span,
                widths,
                heads,
                entries,
                scalar_rows if heading else 0,
            ),
            in_specs=in_specs,
            out_specs=[vmem] * len(entries),
            out_shape=shapes,
            scratch_shapes=scratch,
            compiler_params=pltpu.CompilerParams(vmem_limit_bytes=PACK_VMEM),
            cost_estimate=pl.CostEstimate(
                flops=0,
                bytes_accessed=4 * sum(math.prod(shape.shape) for shape in shapes),
                transcendentals=0,
            ),
            name="pack",
        )(*operands)

    def send(message, code, after=()):
        message, _ = lax.optimization_barrier((message, after))
        pairs = [(i, int(owner_table[i, code])) for i in range(peers)]
        return lax.ppermute(message, "ctx", pairs)

    far = sorted(range(2, peers - 1), key=lambda code: abs(code - peers // 2))
    near = [1, peers - 1]
    kinds = [(code, "lead") for code in far] + [(code, "full") for code in near + [0]]
    lead = {code: message for (code, _), message in zip(kinds, pack(kinds))}
    rest = {code: lead[code] for code in near + [0]}
    rest.update(zip(far, pack([(code, "rest") for code in far])))
    for code in far + near:
        lead[code] = send(lead[code], code)
    for code in far:
        rest[code] = send(rest[code], code, [lead[other] for other in far + near])
    for code in near:
        rest[code] = lead[code]
    received = [[parts[code] for code in range(peers)] for parts in (lead, rest)]

    taps_x = columns(conv_inputs, me * owned, owned)
    group = me // span
    taps_kq = jnp.concatenate(
        [
            columns(conv_kq, group * STATE, STATE),
            columns(conv_kq, (GROUPS + group) * STATE, STATE),
        ],
        axis=1,
    )
    skip = jnp.repeat(lax.dynamic_slice_in_dim(skip_gain, me * heads, heads), HEAD_DIM)[None]
    gain = columns(norm_gain[None], me * owned, owned)

    def by_source(count, lanes, dtype):
        spec = pl.BlockSpec((count, lanes), lambda i: (i, 0))
        return spec, jax.ShapeDtypeStruct((peers * count, lanes), dtype)

    def whole(count, lanes, dtype):
        return vmem, jax.ShapeDtypeStruct((peers * count, lanes), dtype)

    totals = []
    power = None
    shared = None
    for chunk, width in enumerate(widths):
        first = chunk == 0
        final = chunk == len(widths) - 1 and whole_group
        taps = taps_x[:, offsets[chunk] : offsets[chunk] + width]
        if first:
            taps = jnp.concatenate([taps, taps_kq], axis=1)
        cols = taps.shape[1]
        operands = [slots, *received[chunk], taps, skip[:, offsets[chunk] : offsets[chunk] + width]]
        if not first:
            left, b_part, inward, outward = shared
            operands += [left, b_part, inward[chunk - 1], outward[chunk - 1], power]
        if final:
            operands += [gain, *totals]
        out = []
        if final:
            out.append(by_source(rows, owned, jnp.bfloat16))
        else:
            out.append(whole(rows, width, jnp.bfloat16))
            out.append(whole(rows, LANES, jnp.float32))
        if first:
            out.append(whole(rows, 2 * STATE, jnp.bfloat16))
            out.append(whole(rows, STATE, jnp.bfloat16))
            for count in (rows, rows + 16 * blocks):
                for size in widths[1:]:
                    out.append(whole(count, 2 * size // HEAD_DIM, jnp.bfloat16))
        scratch = [
            pltpu.VMEM((rows + HALO, cols), jnp.bfloat16),
            pltpu.VMEM((STATE, width), jnp.float32),
        ]
        if final:
            scratch.append(pltpu.VMEM((rows, width), jnp.float32))
        if first:
            scratch.append(pltpu.VMEM((scalar_rows, cols), jnp.bfloat16))
        results = pl.pallas_call(
            functools.partial(mixer_kernel, peers, rows, heads, chunk, widths, whole_group),
            grid=(peers,),
            in_specs=[smem] + [vmem] * (len(operands) - 1),
            out_specs=[spec for spec, _ in out],
            out_shape=[shape for _, shape in out],
            scratch_shapes=scratch,
            compiler_params=params,
            cost_estimate=pl.CostEstimate(
                flops=2 * total_rows * width * 450,
                bytes_accessed=total_rows * (2 * cols + 8 * width),
                transcendentals=total_rows * cols,
            ),
            name=f"mixer{chunk}",
        )(*operands)
        if final:
            return results[0]
        totals.append(results[0])
        power = results[1]
        if first:
            rest = results[4:]
            shared = (results[2], results[3], rest[: len(rest) // 2], rest[len(rest) // 2 :])
    sharers = [list(range(i, i + span)) for i in range(0, peers, span)]
    summed = jnp.sum(power, axis=1, keepdims=True)
    summed = lax.psum(summed, "ctx", axis_index_groups=sharers)
    total = jnp.concatenate(totals, axis=1)
    return (total * lax.rsqrt(summed * (1.0 / GROUP_WIDTH) + EPS) * gain).astype(jnp.bfloat16)


def solution(mesh):
    in_specs = (
        P(("dp", "ctx"), None),
        P(("dp", "ctx"), None),
        P(),
        P(),
        P(("dp", "ctx"), None),
        P(("dp", "ctx"), None),
        P(),
        P(),
    )
    out_specs = P("dp", "ctx")
    return jax.shard_map(
        per_device, mesh=mesh, in_specs=in_specs, out_specs=out_specs, check_vma=False
    )
```

```python
import functools

import jax
import jax.numpy as jnp
from jax import lax
from jax.experimental import pallas as pl
from jax.experimental.pallas import tpu as pltpu
from jax.sharding import PartitionSpec as P

HEADS = 128
HEAD_DIM = 64
STATE = 128
GROUPS = 8
KW = 4
BLOCK = 128
GROUP_WIDTH = HEADS * HEAD_DIM // GROUPS
EPS = 1e-05
HALO = 16
LANES = 128
SUBLANES = 8
FIELDS = 2
STRIP = 64
VMEM_LIMIT = 56 * 1024 * 1024


def contract(a, b, dims):
    return lax.dot_general(a, b, (dims, ((), ())), preferred_element_type=jnp.float32)


def as_parts(v, count):
    parts = []
    for _ in range(count):
        part = v.astype(jnp.bfloat16)
        parts.append(part)
        v = v - part.astype(jnp.float32)
    return parts


def scalar_units(heads, rows, cols):
    units = []
    for p in range(FIELDS):
        for head in range(0, heads, SUBLANES):
            line, column = divmod(len(units), cols // rows)
            units.append((p, head, min(SUBLANES, heads), line * SUBLANES, column * rows))
    return units


def pack_kernel(peers, span, width, heads, codes, *refs):
    owner_ref, x_ref, kq_ref, decay_ref, step_ref = refs[:5]
    outs = refs[5 : 5 + len(codes)]
    raw_scalars, scalars, kq_near, sems = refs[5 + len(codes) :]
    rows = x_ref.shape[0]
    copies = [
        pltpu.make_async_copy(ref, dst, sems.at[1, i])
        for i, (ref, dst) in enumerate(
            ((decay_ref, raw_scalars.at[0]), (step_ref, raw_scalars.at[1]), (kq_ref, kq_near))
        )
    ]
    owners = [owner_ref[code] for code in codes]
    for i, owner in enumerate(owners):
        column = pl.multiple_of(owner * width, LANES)
        copies.append(
            pltpu.make_async_copy(
                x_ref.at[:, pl.ds(column, width)], outs[i].at[0:rows, 0:width], sems.at[0, i]
            )
        )
    for copy in copies:
        copy.start()
    for copy in copies[:3]:
        copy.wait()
    for p in range(FIELDS):
        field = raw_scalars[p].T
        for owner in range(peers):
            scalars[p, owner] = field[owner * heads : (owner + 1) * heads]
    for i, owner in enumerate(owners):
        outs[i][rows:] = jnp.zeros((outs[i].shape[0] - rows, outs[i].shape[1]), jnp.bfloat16)
        for p, head, count, top, left in scalar_units(heads, rows, width + 2 * STATE):
            outs[i][rows + top : rows + top + count, left : left + rows] = scalars[
                p, owner, head : head + count
            ].astype(jnp.bfloat16)
        for j in range(2):
            column = pl.multiple_of((j * GROUPS + owner // span) * STATE, LANES)
            left = width + j * STATE
            outs[i][0:rows, left : left + STATE] = kq_near[:, pl.ds(column, STATE)]
    for copy in copies[3:]:
        copy.wait()


def spread(heads):
    head_of = lax.broadcasted_iota(jnp.int32, (2 * heads, heads * HEAD_DIM), 1) // HEAD_DIM
    row = lax.rem(lax.broadcasted_iota(jnp.int32, (2 * heads, heads * HEAD_DIM), 0), heads)
    return jnp.where(head_of == row, 1.0, 0.0).astype(jnp.bfloat16)


def local_kernel(width, heads, count, chained, *refs):
    source_ref = refs[0]
    parts = refs[1 : 2 + count]
    taps_ref, skip_ref = refs[2 + count : 4 + count]
    refs = refs[4 + count + (4 if chained else 0) :]
    stores, (wide, pre, state, c_out, outward_out, sems) = refs[:4], refs[4:]
    rows = wide.shape[0] - HALO
    blocks = rows // BLOCK
    full = width + 2 * STATE
    row = lax.broadcasted_iota(jnp.int32, (rows, rows), 0)
    col = lax.broadcasted_iota(jnp.int32, (rows, rows), 1)
    lower = (row >= col) & (row // BLOCK == col // BLOCK)
    ones = jnp.where(lower, 1.0, 0.0).astype(jnp.bfloat16)
    eye = jnp.where(row == col, 1.0, 0.0).astype(jnp.bfloat16)
    expand = spread(heads)

    def activated(top, size, lo, hi):
        rows_out = []
        for r in range(top, top + size, STRIP):
            lanes_out = []
            for lane in range(lo, hi, LANES):
                tap = [taps_ref[k : k + 1, lane : lane + LANES] for k in range(KW)]
                now = wide[r : r + STRIP + HALO, lane : lane + LANES].astype(jnp.float32)
                now = now[HALO // 2 :]
                before = pltpu.roll(now, 1, 0)
                older = pltpu.roll(tap[0] * before + tap[1] * now, 2, 0)
                summed = (older + (tap[2] * before + tap[3] * now))[HALO // 2 :]
                lanes_out.append(summed * pltpu.reciprocal(1.0 + jnp.exp(-summed), approx=True))
            rows_out.append(jnp.concatenate(lanes_out, axis=1))
        return jnp.concatenate(rows_out, axis=0)

    for which in range(count):
        source = source_ref[which]
        part, earlier = parts[which], parts[which + 1]
        wide[HALO:] = part[0:rows, 0:full]

        @pl.when(source == 0)
        def _():
            wide[0:HALO] = jnp.zeros((HALO, full), jnp.bfloat16)

        @pl.when(source != 0)
        def _():
            wide[0:HALO] = earlier[rows - HALO : rows, 0:full]

        def field(p):
            pieces = [
                part[rows + top : rows + top + size, left : left + rows].astype(jnp.float32)
                for q, _, size, top, left in scalar_units(heads, rows, full)
                if q == p
            ]
            return jnp.concatenate(pieces, axis=0).astype(jnp.bfloat16)

        cumul = contract(ones, field(0), ((1,), (1,)))
        steps = contract(eye, field(1), ((1,), (1,)))
        middles = [
            cumul[b * BLOCK + BLOCK // 2 - 1 : b * BLOCK + BLOCK // 2] for b in range(blocks)
        ]
        middle = jnp.concatenate([jnp.broadcast_to(m, (BLOCK, heads)) for m in middles], axis=0)
        inward = jnp.concatenate(as_parts(steps * jnp.exp(middle - cumul), 2), axis=1)
        outward = jnp.concatenate(
            as_parts(
                jnp.concatenate(
                    [jnp.exp(cumul - middle)]
                    + [jnp.broadcast_to(jnp.exp(m), (16, heads)) for m in middles],
                    axis=0,
                ),
                2,
            ),
            axis=1,
        )
        bc = activated(0, rows, width, full).astype(jnp.bfloat16)
        b_part, c_part = bc[:, :STATE], bc[:, STATE:]
        scores = contract(c_part, b_part, ((1,), (1,)))
        scores = jnp.where(lower, scores, 0.0).astype(jnp.bfloat16)
        both = jnp.concatenate([inward, outward[:rows]], axis=0)
        tile = min(2 * LANES, width)
        for lo in range(0, width, tile):
            hi = lo + tile
            x_conv = activated(0, rows, lo, hi)
            scales = contract(both, expand[:, lo:hi], ((1,), (0,)))
            scaled = (x_conv * scales[:rows]).astype(jnp.bfloat16)
            intra = contract(scores, scaled, ((1,), (0,)))
            pre[which, :, lo:hi] = (
                intra * scales[rows:] + skip_ref[0:1, lo:hi] * x_conv
            ).astype(jnp.bfloat16)
            for b in range(blocks):
                at = slice(b * BLOCK, (b + 1) * BLOCK)
                state[which, b * STATE : (b + 1) * STATE, lo:hi] = contract(
                    b_part[at], scaled[at], ((0,), (0,))
                )
        c_out[which] = c_part
        outward_out[which] = outward
        for i, (value, store) in enumerate(zip((pre, state, c_out, outward_out), stores)):
            pltpu.make_async_copy(value.at[which], store.at[source], sems.at[i, which]).start()
    for which in range(count):
        source = source_ref[which]
        for i, (value, store) in enumerate(zip((pre, state, c_out, outward_out), stores)):
            pltpu.make_async_copy(value.at[which], store.at[source], sems.at[i, which]).wait()


def carry_kernel(width, heads, whole_group, *refs):
    pre, state, c_part, outward, gain_ref = refs[:5]
    outs, (carry, total_ref) = refs[5:-2], refs[-2:]
    rows = pre.shape[1]

    @pl.when(pl.program_id(0) == 0)
    def _():
        carry[...] = jnp.zeros_like(carry)

    expand = spread(heads)
    tile = min(2 * LANES, width)
    for b in range(rows // BLOCK):
        at = slice(b * BLOCK, (b + 1) * BLOCK)
        compact = jnp.concatenate(
            [outward[0, at], outward[0, rows + 16 * b : rows + 16 * (b + 1)]], axis=0
        )
        power = jnp.zeros((BLOCK, LANES), jnp.float32)
        for lo in range(0, width, tile):
            hi = lo + tile
            scales = contract(compact, expand[:, lo:hi], ((1,), (0,)))
            held = carry[:, lo:hi] * scales[BLOCK : BLOCK + 1]
            inter = contract(c_part[0, at], held.astype(jnp.bfloat16), ((1,), (0,)))
            total = pre[0, at, lo:hi].astype(jnp.float32) + inter * scales[:BLOCK]
            carry[:, lo:hi] = (held + state[0, at, lo:hi]) * scales[BLOCK - 1 : BLOCK]
            total_ref[:, lo:hi] = total
            squares = total * total
            for lane in range(0, tile, LANES):
                power = power + squares[:, lane : lane + LANES]
        if whole_group:
            summed = jnp.sum(power, axis=1, keepdims=True)
            norm = lax.rsqrt(summed * (1.0 / GROUP_WIDTH) + EPS)
            outs[0][at] = (total_ref[...] * norm * gain_ref[...]).astype(jnp.bfloat16)
        else:
            outs[0][at] = total_ref[...]
            outs[1][at] = power


def per_device(inputs, key_query, conv_inputs, conv_kq, step_size, decay_log, skip_gain, norm_gain):
    peers = lax.axis_size("ctx")
    me = lax.axis_index("ctx")
    rows = inputs.shape[0]
    width = HEADS * HEAD_DIM // peers
    heads = HEADS // peers
    span = GROUP_WIDTH // width
    whole_group = span == 1
    blocks = rows // BLOCK
    full = width + 2 * STATE
    scalar_rows = scalar_units(heads, rows, full)[-1][3] + SUBLANES
    scale_rows = rows + 16 * blocks
    cycle = jnp.arange(peers, dtype=jnp.int32)
    owners = lax.rem(me + cycle, peers)
    sources = lax.rem(me + peers - cycle, peers)

    smem = pl.BlockSpec(memory_space=pltpu.SMEM)
    hbm = pl.BlockSpec(memory_space=pltpu.HBM)
    vmem = pl.BlockSpec(memory_space=pltpu.VMEM)
    params = pltpu.CompilerParams(vmem_limit_bytes=VMEM_LIMIT)

    def columns(a, first, size):
        return lax.dynamic_slice_in_dim(a, first, size, axis=1)

    def pack(codes):
        shape = jax.ShapeDtypeStruct((rows + scalar_rows, full), jnp.bfloat16)
        return pl.pallas_call(
            functools.partial(pack_kernel, peers, span, width, heads, codes),
            in_specs=[smem] + [hbm] * 4,
            out_specs=[vmem] * len(codes),
            out_shape=[shape] * len(codes),
            scratch_shapes=[
                pltpu.VMEM((FIELDS, rows, HEADS), jnp.float32),
                pltpu.VMEM((FIELDS, peers, heads, rows), jnp.float32),
                pltpu.VMEM(key_query.shape, jnp.bfloat16),
                pltpu.SemaphoreType.DMA((2, max(3, len(codes)))),
            ],
            compiler_params=params,
            cost_estimate=pl.CostEstimate(
                flops=0, bytes_accessed=4 * len(codes) * rows * full, transcendentals=0
            ),
            name="pack",
        )(owners, inputs, key_query, decay_log, step_size)

    codes = list(range(1, peers)) + [0]
    parts = dict(zip(codes[:2], pack(codes[:2])))
    parts.update(zip(codes[2:], pack(codes[2:])))
    for code in codes[:-1]:
        pairs = [(i, (i + code) % peers) for i in range(peers)]
        parts[code] = lax.ppermute(parts[code], "ctx", pairs)
    parts[peers] = parts[0]

    group = me // span
    taps = jnp.concatenate(
        [
            columns(conv_inputs, me * width, width),
            columns(conv_kq, group * STATE, STATE),
            columns(conv_kq, (GROUPS + group) * STATE, STATE),
        ],
        axis=1,
    )
    skip = jnp.repeat(lax.dynamic_slice_in_dim(skip_gain, me * heads, heads), HEAD_DIM)[None]
    gain = columns(norm_gain[None], me * width, width)

    shapes = [
        ((rows, width), jnp.bfloat16),
        ((blocks * STATE, width), jnp.float32),
        ((rows, STATE), jnp.bfloat16),
        ((scale_rows, 2 * heads), jnp.bfloat16),
    ]
    stores = []
    for first in range(peers - 1):
        count = 2 if first == peers - 2 else 1
        stores = pl.pallas_call(
            functools.partial(local_kernel, width, heads, count, bool(stores)),
            in_specs=[smem] + [vmem] * (count + 3) + [hbm] * len(stores),
            out_specs=[hbm] * 4,
            out_shape=[jax.ShapeDtypeStruct((peers,) + shape, dtype) for shape, dtype in shapes],
            input_output_aliases={4 + count + i: i for i in range(len(stores))},
            scratch_shapes=[pltpu.VMEM((rows + HALO, full), jnp.bfloat16)]
            + [pltpu.VMEM((count,) + shape, dtype) for shape, dtype in shapes]
            + [pltpu.SemaphoreType.DMA((4, count))],
            compiler_params=params,
            cost_estimate=pl.CostEstimate(
                flops=2 * rows * count * width * 450,
                bytes_accessed=count * rows * width * 10,
                transcendentals=count * rows * full,
            ),
            name="local",
        )(
            sources[first : first + count],
            *[parts[first + i] for i in range(count + 1)],
            taps,
            skip,
            *stores,
        )

    out = [((rows, width), jnp.bfloat16 if whole_group else jnp.float32)]
    if not whole_group:
        out.append(((rows, LANES), jnp.float32))
    results = pl.pallas_call(
        functools.partial(carry_kernel, width, heads, whole_group),
        grid=(peers,),
        in_specs=[pl.BlockSpec((1,) + shape, lambda i: (i, 0, 0)) for shape, _ in shapes]
        + [pl.BlockSpec((1, width), lambda i: (0, 0))],
        out_specs=[pl.BlockSpec(shape, lambda i: (i, 0)) for shape, _ in out],
        out_shape=[
            jax.ShapeDtypeStruct((peers * shape[0], shape[1]), dtype) for shape, dtype in out
        ],
        scratch_shapes=[
            pltpu.VMEM((STATE, width), jnp.float32),
            pltpu.VMEM((BLOCK, width), jnp.float32),
        ],
        compiler_params=params,
        cost_estimate=pl.CostEstimate(
            flops=2 * peers * rows * width * 150,
            bytes_accessed=peers * rows * width * 8,
            transcendentals=peers * rows,
        ),
        name="carry",
    )(*stores, gain)
    if whole_group:
        return results[0]
    total, power = results
    sharers = [list(range(i, i + span)) for i in range(0, peers, span)]
    summed = jnp.sum(power, axis=1, keepdims=True)
    summed = lax.psum(summed, "ctx", axis_index_groups=sharers)
    return (total * lax.rsqrt(summed * (1.0 / GROUP_WIDTH) + EPS) * gain).astype(jnp.bfloat16)


def solution(mesh):
    in_specs = (
        P(("dp", "ctx"), None),
        P(("dp", "ctx"), None),
        P(),
        P(),
        P(("dp", "ctx"), None),
        P(("dp", "ctx"), None),
        P(),
        P(),
    )
    out_specs = P("dp", "ctx")
    return jax.shard_map(
        per_device, mesh=mesh, in_specs=in_specs, out_specs=out_specs, check_vma=False
    )
```

```python
import functools
import math

import jax
import jax.numpy as jnp
import numpy as np
from jax import lax
from jax.experimental import pallas as pl
from jax.experimental.pallas import tpu as pltpu
from jax.sharding import PartitionSpec as P

HEADS = 128
HEAD_DIM = 64
STATE = 128
GROUPS = 8
KW = 4
BLOCK = 128
GROUP_WIDTH = HEADS * HEAD_DIM // GROUPS
EPS = 1e-05
HALO = 16
LANES = 128
SUBLANES = 8
FIELDS = 2
ROUND_ORDER = (0, 1, 2, 4, 3, 5, 6, 7)
STRIP = 64
PACK_VMEM = 58 * 1024 * 1024
VMEM_LIMIT = 32 * 1024 * 1024


def contract(a, b, dims):
    return lax.dot_general(a, b, (dims, ((), ())), preferred_element_type=jnp.float32)


def as_parts(v, count):
    parts = []
    for _ in range(count):
        part = v.astype(jnp.bfloat16)
        parts.append(part)
        v = v - part.astype(jnp.float32)
    return parts


def scalar_units(heads, rows, cols):
    units = []
    for p in range(FIELDS):
        for head in range(0, heads, SUBLANES):
            line, column = divmod(len(units), cols // rows)
            units.append((p, head, min(SUBLANES, heads), line * SUBLANES, column * rows))
    return units


def pack_kernel(peers, span, widths, heads, entries, scalar_rows, *refs):
    refs = list(refs)
    owner_ref = refs.pop(0)
    x_ref = refs.pop(0)
    heading = scalar_rows > 0
    if heading:
        kq_ref, decay_ref, step_ref = refs[:3]
        del refs[:3]
    outs = refs[: len(entries)]
    del refs[: len(entries)]
    if heading:
        raw_scalars, scalars, kq_near = refs[:3]
    sems = refs[-1]
    rows = x_ref.shape[0]
    owned = HEADS * HEAD_DIM // peers
    lead = widths[0] + 2 * STATE
    copies = []
    if heading:
        loads = [
            pltpu.make_async_copy(ref, raw_scalars.at[i], sems.at[2, i])
            for i, ref in enumerate((decay_ref, step_ref))
        ]
        loads.append(pltpu.make_async_copy(kq_ref, kq_near, sems.at[2, 2]))
        for load in loads:
            load.start()
    owners = [owner_ref[code] for code, _ in entries]
    for i, (owner, (_, kind)) in enumerate(zip(owners, entries)):
        pieces = {
            "full": [(0, 0, 0), (1, widths[0], lead)],
            "lead": [(0, 0, 0)],
            "rest": [(1, widths[0], 0)],
        }[kind]
        for index, offset, left in pieces:
            column = pl.multiple_of(owner * owned + offset, LANES)
            copies.append(
                pltpu.make_async_copy(
                    x_ref.at[:, pl.ds(column, widths[index])],
                    outs[i].at[0:rows, left : left + widths[index]],
                    sems.at[index, i],
                )
            )
    for copy in copies:
        copy.start()
    if heading:
        for load in loads:
            load.wait()
        fields = [raw_scalars[0].T, raw_scalars[1].T]
        for p, field in enumerate(fields):
            for owner in range(peers):
                scalars[p, owner] = field[owner * heads : (owner + 1) * heads]
        for i, owner in enumerate(owners):
            outs[i][rows:] = jnp.zeros((scalar_rows, outs[i].shape[1]), jnp.bfloat16)
            for p, head, count, top, left in scalar_units(heads, rows, lead):
                outs[i][rows + top : rows + top + count, left : left + rows] = scalars[
                    p, owner, head : head + count
                ].astype(jnp.bfloat16)
            for j in range(2):
                column = pl.multiple_of((j * GROUPS + owner // span) * STATE, LANES)
                left = widths[0] + j * STATE
                outs[i][0:rows, left : left + STATE] = kq_near[:, pl.ds(column, STATE)]
    for copy in copies:
        copy.wait()


def mixer_kernel(peers, rows, heads, chunk, widths, whole_group, *refs):
    refs = list(refs)

    def take(count):
        taken = refs[:count]
        del refs[:count]
        return taken

    first = chunk == 0
    final = chunk == len(widths) - 1 and whole_group
    later = range(1, len(widths)) if first else ()
    width = widths[chunk]
    (slot_ref,) = take(1)
    parts = take(peers)
    taps_ref, skip_ref = take(2)
    if not first:
        left_ref, b_ref, inward_ref, outward_ref, power_ref = take(5)
    if final:
        (gain_ref,) = take(1)
        earlier = take(chunk)
        (out_ref,) = take(1)
    else:
        total_ref, sums_ref = take(2)
    if first and later:
        left_ref, b_ref = take(2)
        inward_refs = take(len(later))
        outward_refs = take(len(later))
    wide, carry, x_ref, scaled_ref, scales, expand = take(6)
    if first:
        scalars, ones, eye = take(3)
    blocks = rows // BLOCK
    step = pl.program_id(0)
    scale_rows = rows + 16 * blocks
    base = pl.multiple_of(step * rows, rows)
    scale_base = pl.multiple_of(step * scale_rows, 32)

    def spread(count):
        head_of = lax.broadcasted_iota(jnp.int32, (2 * count, count * HEAD_DIM), 1) // HEAD_DIM
        row = lax.rem(
            lax.broadcasted_iota(jnp.int32, (2 * count, count * HEAD_DIM), 0), count
        )
        return jnp.where(head_of == row, 1.0, 0.0).astype(jnp.bfloat16)

    @pl.when(step == 0)
    def _():
        carry[...] = jnp.zeros_like(carry)
        expand[...] = spread(width // HEAD_DIM)
        if first:
            row = lax.broadcasted_iota(jnp.int32, (rows, rows), 0)
            col = lax.broadcasted_iota(jnp.int32, (rows, rows), 1)
            lower = (row >= col) & (row // BLOCK == col // BLOCK)
            ones[...] = jnp.where(lower, 1.0, 0.0).astype(jnp.bfloat16)
            eye[...] = jnp.where(row == col, 1.0, 0.0).astype(jnp.bfloat16)
        wide[rows : rows + HALO] = jnp.zeros((HALO, wide.shape[1]), jnp.bfloat16)

    wide[0:HALO] = wide[rows : rows + HALO]
    slot = slot_ref[step]
    for k in range(peers):

        @pl.when(slot == k)
        def _():
            if first:
                wide[HALO : HALO + rows] = parts[k][0:rows, 0 : wide.shape[1]]
                scalars[...] = parts[k][rows:, 0 : wide.shape[1]]
            else:
                wide[HALO : HALO + rows] = parts[k][0:rows, parts[k].shape[1] - width :]

    def activated(r, lane):
        tap = [taps_ref[k : k + 1, lane : lane + LANES] for k in range(KW)]
        now = wide[r : r + STRIP + HALO, lane : lane + LANES].astype(jnp.float32)[HALO // 2 :]
        before = pltpu.roll(now, 1, 0)
        older = pltpu.roll(tap[0] * before + tap[1] * now, 2, 0)
        summed = (older + (tap[2] * before + tap[3] * now))[HALO // 2 :]
        return summed * pltpu.reciprocal(1.0 + jnp.exp(-summed), approx=True)

    if first:
        full = width + 2 * STATE
        def field(p):
            pieces = [
                scalars[top : top + count, left : left + rows].astype(jnp.float32)
                for q, _, count, top, left in scalar_units(heads, rows, full)
                if q == p
            ]
            return jnp.concatenate(pieces, axis=0).astype(jnp.bfloat16)

        cumul = contract(ones[...], field(0), ((1,), (1,)))
        steps = contract(eye[...], field(1), ((1,), (1,)))
        middles = [
            cumul[b * BLOCK + BLOCK // 2 - 1 : b * BLOCK + BLOCK // 2] for b in range(blocks)
        ]
        middle = jnp.concatenate([jnp.broadcast_to(m, (BLOCK, heads)) for m in middles], axis=0)
        inward = as_parts(steps * jnp.exp(middle - cumul), 2)
        outward = as_parts(
            jnp.concatenate(
                [jnp.exp(cumul - middle)]
                + [jnp.broadcast_to(jnp.exp(m), (16, heads)) for m in middles],
                axis=0,
            ),
            2,
        )

        def chosen(halves, index):
            begin = sum(widths[:index]) // HEAD_DIM
            end = begin + widths[index] // HEAD_DIM
            return jnp.concatenate([half[:, begin:end] for half in halves], axis=1)

        b_part, c_part = (
            jnp.concatenate(
                [activated(r, lane) for r in range(0, rows, STRIP)], axis=0
            ).astype(jnp.bfloat16)
            for lane in (width, width + STATE)
        )
        scores = contract(c_part, b_part, ((1,), (1,)))
        scores = jnp.where(ones[...] > 0, scores, 0.0).astype(jnp.bfloat16)
        lefts = [
            jnp.concatenate(
                [
                    scores[b * BLOCK : (b + 1) * BLOCK, b * BLOCK : (b + 1) * BLOCK],
                    c_part[b * BLOCK : (b + 1) * BLOCK],
                ],
                axis=1,
            )
            for b in range(blocks)
        ]
        for index in later:
            inward_refs[index - 1][pl.ds(base, rows)] = chosen(inward, index)
            outward_refs[index - 1][pl.ds(scale_base, scale_rows)] = chosen(outward, index)
        if later:
            b_ref[pl.ds(base, rows)] = b_part
            for b in range(blocks):
                left_ref[pl.ds(base + b * BLOCK, BLOCK)] = lefts[b]
        inward = chosen(inward, 0)
        outward = chosen(outward, 0)
    else:
        inward = inward_ref[pl.ds(base, rows)]
        outward = outward_ref[pl.ds(scale_base, scale_rows)]
        b_part = b_ref[pl.ds(base, rows)]
        lefts = [left_ref[pl.ds(base + b * BLOCK, BLOCK)] for b in range(blocks)]

    scales[...] = contract(
        jnp.concatenate([inward, outward], axis=0), expand[...], ((1,), (0,))
    )
    for lane in range(0, width, LANES):
        at = slice(lane, lane + LANES)
        for r in range(0, rows, STRIP):
            x_conv = activated(r, lane)
            x_ref[r : r + STRIP, at] = x_conv
            scaled_ref[r : r + STRIP, at] = (x_conv * scales[r : r + STRIP, at]).astype(
                jnp.bfloat16
            )
    held = []
    for b in range(blocks):
        at = slice(b * BLOCK, (b + 1) * BLOCK)
        added = contract(b_part[at], scaled_ref[at], ((0,), (0,)))
        middle_row = 2 * rows + 16 * b
        last_row = rows + (b + 1) * BLOCK - 1
        now = carry[...] * scales[middle_row : middle_row + 1]
        held.append(now.astype(jnp.bfloat16))
        carry[...] = (now + added) * scales[last_row : last_row + 1]
    for b in range(blocks):
        at = slice(b * BLOCK, (b + 1) * BLOCK)
        right = jnp.concatenate([scaled_ref[at], held[b]], axis=0)
        total = contract(lefts[b], right, ((1,), (0,)))
        total = total * scales[rows + b * BLOCK : rows + (b + 1) * BLOCK]
        total = total + skip_ref[...] * x_ref[at]
        power = power_ref[pl.ds(base + b * BLOCK, BLOCK)] if not first else None
        for lane in range(0, width, LANES):
            square = total[:, lane : lane + LANES] * total[:, lane : lane + LANES]
            power = square if power is None else power + square
        if final:
            summed = jnp.sum(power, axis=1, keepdims=True)
            norm = lax.rsqrt(summed * (1.0 / GROUP_WIDTH) + EPS)
            column = 0
            for index, size in enumerate(widths):
                if index < chunk:
                    block = earlier[index][pl.ds(base + b * BLOCK, BLOCK)].astype(jnp.float32)
                else:
                    block = total
                out_ref[at, column : column + size] = (
                    block * norm * gain_ref[0:1, column : column + size]
                ).astype(jnp.bfloat16)
                column += size
        else:
            total_ref[pl.ds(base + b * BLOCK, BLOCK)] = total.astype(jnp.bfloat16)
            sums_ref[pl.ds(base + b * BLOCK, BLOCK)] = power


def per_device(inputs, key_query, conv_inputs, conv_kq, step_size, decay_log, skip_gain, norm_gain):
    peers = lax.axis_size("ctx")
    me = lax.axis_index("ctx")
    position = np.arange(peers)
    if peers == len(ROUND_ORDER):
        position = np.argsort(ROUND_ORDER)
    steps = np.arange(peers)
    owner_table = np.argsort(position)[(position[:, None] + steps) % peers].astype(np.int32)
    slot_table = ((position[:, None] - position) % peers).astype(np.int32)
    owners = lax.dynamic_index_in_dim(jnp.asarray(owner_table), me, 0, False)
    slots = lax.dynamic_index_in_dim(jnp.asarray(slot_table), me, 0, False)
    rows = inputs.shape[0]
    owned = HEADS * HEAD_DIM // peers
    heads = HEADS // peers
    span = GROUP_WIDTH // owned
    whole_group = span == 1
    total_rows = peers * rows
    blocks = rows // BLOCK
    tiles = owned // LANES
    last = max(1, tiles // 4)
    widths = [(tiles - last) * LANES, last * LANES]
    offsets = [0, widths[0]]

    smem = pl.BlockSpec(memory_space=pltpu.SMEM)
    hbm = pl.BlockSpec(memory_space=pltpu.HBM)
    vmem = pl.BlockSpec(memory_space=pltpu.VMEM)
    params = pltpu.CompilerParams(vmem_limit_bytes=VMEM_LIMIT)

    def columns(a, first, size):
        return lax.dynamic_slice_in_dim(a, first, size, axis=1)

    lead_cols = widths[0] + 2 * STATE
    scalar_rows = scalar_units(heads, rows, lead_cols)[-1][3] + SUBLANES
    extents = {
        "full": (rows + scalar_rows, lead_cols + widths[1]),
        "lead": (rows + scalar_rows, lead_cols),
        "rest": (rows, widths[1]),
    }

    def pack(entries):
        heading = entries[0][1] != "rest"
        shapes = [jax.ShapeDtypeStruct(extents[kind], jnp.bfloat16) for _, kind in entries]
        operands = [owners, inputs]
        in_specs = [smem, hbm]
        scratch = []
        if heading:
            operands += [key_query, decay_log, step_size]
            in_specs += [hbm] * 3
            scratch.append(pltpu.VMEM((2, rows, HEADS), jnp.float32))
            scratch.append(pltpu.VMEM((FIELDS, peers, heads, rows), jnp.float32))
            scratch.append(pltpu.VMEM(key_query.shape, jnp.bfloat16))
        scratch.append(pltpu.SemaphoreType.DMA((3, max(3, len(entries)))))
        return pl.pallas_call(
            functools.partial(
                pack_kernel,
                peers,
                span,
                widths,
                heads,
                entries,
                scalar_rows if heading else 0,
            ),
            in_specs=in_specs,
            out_specs=[vmem] * len(entries),
            out_shape=shapes,
            scratch_shapes=scratch,
            compiler_params=pltpu.CompilerParams(vmem_limit_bytes=PACK_VMEM),
            cost_estimate=pl.CostEstimate(
                flops=0,
                bytes_accessed=4 * sum(math.prod(shape.shape) for shape in shapes),
                transcendentals=0,
            ),
            name="pack",
        )(*operands)

    def send(message, code, after=()):
        message, _ = lax.optimization_barrier((message, after))
        pairs = [(i, int(owner_table[i, code])) for i in range(peers)]
        return lax.ppermute(message, "ctx", pairs)

    far = sorted(range(2, peers - 1), key=lambda code: abs(code - peers // 2))
    near = [1, peers - 1]
    kinds = [(code, "lead") for code in far] + [(code, "full") for code in near + [0]]
    lead = {code: message for (code, _), message in zip(kinds, pack(kinds))}
    rest = {code: lead[code] for code in near + [0]}
    rest.update(zip(far, pack([(code, "rest") for code in far])))
    for code in far + near:
        lead[code] = send(lead[code], code)
    for code in far:
        rest[code] = send(rest[code], code, [lead[other] for other in far + near])
    for code in near:
        rest[code] = lead[code]
    received = [[parts[code] for code in range(peers)] for parts in (lead, rest)]

    taps_x = columns(conv_inputs, me * owned, owned)
    group = me // span
    taps_kq = jnp.concatenate(
        [
            columns(conv_kq, group * STATE, STATE),
            columns(conv_kq, (GROUPS + group) * STATE, STATE),
        ],
        axis=1,
    )
    skip = jnp.repeat(lax.dynamic_slice_in_dim(skip_gain, me * heads, heads), HEAD_DIM)[None]
    gain = columns(norm_gain[None], me * owned, owned)

    def by_source(count, lanes, dtype):
        spec = pl.BlockSpec((count, lanes), lambda i: (i, 0))
        return spec, jax.ShapeDtypeStruct((peers * count, lanes), dtype)

    def whole(count, lanes, dtype):
        return vmem, jax.ShapeDtypeStruct((peers * count, lanes), dtype)

    totals = []
    power = None
    shared = None
    for chunk, width in enumerate(widths):
        first = chunk == 0
        final = chunk == len(widths) - 1 and whole_group
        taps = taps_x[:, offsets[chunk] : offsets[chunk] + width]
        if first:
            taps = jnp.concatenate([taps, taps_kq], axis=1)
        cols = taps.shape[1]
        operands = [slots, *received[chunk], taps, skip[:, offsets[chunk] : offsets[chunk] + width]]
        if not first:
            left, b_part, inward, outward = shared
            operands += [left, b_part, inward[chunk - 1], outward[chunk - 1], power]
        if final:
            operands += [gain, *totals]
        out = []
        if final:
            out.append(by_source(rows, owned, jnp.bfloat16))
        else:
            out.append(whole(rows, width, jnp.bfloat16))
            out.append(whole(rows, LANES, jnp.float32))
        if first:
            out.append(whole(rows, 2 * STATE, jnp.bfloat16))
            out.append(whole(rows, STATE, jnp.bfloat16))
            for count in (rows, rows + 16 * blocks):
                for size in widths[1:]:
                    out.append(whole(count, 2 * size // HEAD_DIM, jnp.bfloat16))
        scratch = [
            pltpu.VMEM((rows + HALO, cols), jnp.bfloat16),
            pltpu.VMEM((STATE, width), jnp.float32),
            pltpu.VMEM((rows, width), jnp.float32),
            pltpu.VMEM((rows, width), jnp.bfloat16),
            pltpu.VMEM((2 * rows + 16 * blocks, width), jnp.float32),
            pltpu.VMEM((2 * width // HEAD_DIM, width), jnp.bfloat16),
        ]
        if first:
            scratch.append(pltpu.VMEM((scalar_rows, cols), jnp.bfloat16))
            scratch += [pltpu.VMEM((rows, rows), jnp.bfloat16)] * 2
        results = pl.pallas_call(
            functools.partial(mixer_kernel, peers, rows, heads, chunk, widths, whole_group),
            grid=(peers,),
            in_specs=[smem] + [vmem] * (len(operands) - 1),
            out_specs=[spec for spec, _ in out],
            out_shape=[shape for _, shape in out],
            scratch_shapes=scratch,
            compiler_params=params,
            cost_estimate=pl.CostEstimate(
                flops=2 * total_rows * width * 450,
                bytes_accessed=total_rows * (2 * cols + 8 * width),
                transcendentals=total_rows * cols,
            ),
            name=f"mixer{chunk}",
        )(*operands)
        if final:
            return results[0]
        totals.append(results[0])
        power = results[1]
        if first:
            rest = results[4:]
            shared = (results[2], results[3], rest[: len(rest) // 2], rest[len(rest) // 2 :])
    sharers = [list(range(i, i + span)) for i in range(0, peers, span)]
    summed = jnp.sum(power, axis=1, keepdims=True)
    summed = lax.psum(summed, "ctx", axis_index_groups=sharers)
    total = jnp.concatenate(totals, axis=1)
    return (total * lax.rsqrt(summed * (1.0 / GROUP_WIDTH) + EPS) * gain).astype(jnp.bfloat16)


def solution(mesh):
    in_specs = (
        P(("dp", "ctx"), None),
        P(("dp", "ctx"), None),
        P(),
        P(),
        P(("dp", "ctx"), None),
        P(("dp", "ctx"), None),
        P(),
        P(),
    )
    out_specs = P("dp", "ctx")
    return jax.shard_map(
        per_device, mesh=mesh, in_specs=in_specs, out_specs=out_specs, check_vma=False
    )
```

```python
import functools

import jax
import jax.numpy as jnp
from jax import lax
from jax.experimental import pallas as pl
from jax.experimental.pallas import tpu as pltpu
from jax.sharding import PartitionSpec as P

HEADS = 128
HEAD_DIM = 64
STATE = 128
GROUPS = 8
KW = 4
BLOCK = 128
GROUP_WIDTH = HEADS * HEAD_DIM // GROUPS
EPS = 1e-05
HALO = 16
LANES = 128
SUBLANES = 8
FIELDS = 2
STRIP = 64
PAIR = 2
WINDOW = 3
ORDER = (4, 1, 7, 3, 2, 5, 6)
PACK_VMEM = 58 * 1024 * 1024
VMEM_LIMIT = 28 * 1024 * 1024


def contract(a, b, dims):
    return lax.dot_general(a, b, (dims, ((), ())), preferred_element_type=jnp.float32)


def as_parts(v, count):
    parts = []
    for _ in range(count):
        part = v.astype(jnp.bfloat16)
        parts.append(part)
        v = v - part.astype(jnp.float32)
    return parts


def scalar_units(heads, rows, cols):
    units = []
    for p in range(FIELDS):
        for head in range(0, heads, SUBLANES):
            line, column = divmod(len(units), cols // rows)
            units.append((p, head, min(SUBLANES, heads), line * SUBLANES, column * rows))
    return units


def pack_kernel(peers, span, width, heads, codes, *refs):
    owner_ref, x_ref, kq_ref, decay_ref, step_ref = refs[:5]
    outs = refs[5 : 5 + len(codes)]
    raw_scalars, scalars, kq_near, sems = refs[5 + len(codes) :]
    rows = x_ref.shape[0]
    copies = [
        pltpu.make_async_copy(ref, dst, sems.at[1, i])
        for i, (ref, dst) in enumerate(
            ((decay_ref, raw_scalars.at[0]), (step_ref, raw_scalars.at[1]), (kq_ref, kq_near))
        )
    ]
    owners = [owner_ref[code] for code in codes]
    for i, owner in enumerate(owners):
        column = pl.multiple_of(owner * width, LANES)
        copies.append(
            pltpu.make_async_copy(
                x_ref.at[:, pl.ds(column, width)], outs[i].at[0:rows, 0:width], sems.at[0, i]
            )
        )
    for copy in copies:
        copy.start()
    for copy in copies[:3]:
        copy.wait()
    for p in range(FIELDS):
        field = raw_scalars[p].T
        for owner in range(peers):
            scalars[p, owner] = field[owner * heads : (owner + 1) * heads]
    for i, owner in enumerate(owners):
        outs[i][rows:] = jnp.zeros((outs[i].shape[0] - rows, outs[i].shape[1]), jnp.bfloat16)
        for p, head, count, top, left in scalar_units(heads, rows, width + 2 * STATE):
            outs[i][rows + top : rows + top + count, left : left + rows] = scalars[
                p, owner, head : head + count
            ].astype(jnp.bfloat16)
        for j in range(2):
            column = pl.multiple_of((j * GROUPS + owner // span) * STATE, LANES)
            left = width + j * STATE
            outs[i][0:rows, left : left + STATE] = kq_near[:, pl.ds(column, STATE)]
    for copy in copies[3:]:
        copy.wait()


def spread(heads):
    head_of = lax.broadcasted_iota(jnp.int32, (2 * heads, heads * HEAD_DIM), 1) // HEAD_DIM
    row = lax.rem(lax.broadcasted_iota(jnp.int32, (2 * heads, heads * HEAD_DIM), 0), heads)
    return jnp.where(head_of == row, 1.0, 0.0).astype(jnp.bfloat16)


def local_kernel(width, heads, count, chained, *refs):
    source_ref = refs[0]
    parts = refs[1 : 1 + 2 * count]
    taps_ref, skip_ref = refs[1 + 2 * count : 3 + 2 * count]
    refs = refs[3 + 2 * count + (4 if chained else 0) :]
    pre, state, c_out, outward_out = refs[:4]
    wide, x_ref, scaled_ref, scales = refs[4:]
    rows = x_ref.shape[0]
    blocks = rows // BLOCK
    full = width + 2 * STATE
    row = lax.broadcasted_iota(jnp.int32, (rows, rows), 0)
    col = lax.broadcasted_iota(jnp.int32, (rows, rows), 1)
    lower = (row >= col) & (row // BLOCK == col // BLOCK)
    ones = jnp.where(lower, 1.0, 0.0).astype(jnp.bfloat16)
    eye = jnp.where(row == col, 1.0, 0.0).astype(jnp.bfloat16)
    expand = spread(heads)

    for which in range(count):
        source = source_ref[which]
        part, earlier = parts[2 * which : 2 * which + 2]
        wide[HALO:] = part[0:rows, 0:full]
        edge = earlier[rows - HALO : rows, 0:full]
        wide[0:HALO] = jnp.where(source == 0, jnp.zeros_like(edge), edge)

        def activated(r, lane):
            tap = [taps_ref[k : k + 1, lane : lane + LANES] for k in range(KW)]
            now = wide[r : r + STRIP + HALO, lane : lane + LANES].astype(jnp.float32)
            now = now[HALO // 2 :]
            before = pltpu.roll(now, 1, 0)
            older = pltpu.roll(tap[0] * before + tap[1] * now, 2, 0)
            summed = (older + (tap[2] * before + tap[3] * now))[HALO // 2 :]
            return summed * pltpu.reciprocal(1.0 + jnp.exp(-summed), approx=True)

        def field(p):
            pieces = [
                part[rows + top : rows + top + size, left : left + rows].astype(jnp.float32)
                for q, _, size, top, left in scalar_units(heads, rows, full)
                if q == p
            ]
            return jnp.concatenate(pieces, axis=0).astype(jnp.bfloat16)

        cumul = contract(ones, field(0), ((1,), (1,)))
        steps = contract(eye, field(1), ((1,), (1,)))
        middles = [
            cumul[b * BLOCK + BLOCK // 2 - 1 : b * BLOCK + BLOCK // 2] for b in range(blocks)
        ]
        middle = jnp.concatenate([jnp.broadcast_to(m, (BLOCK, heads)) for m in middles], axis=0)
        inward = jnp.concatenate(as_parts(steps * jnp.exp(middle - cumul), 2), axis=1)
        outward = jnp.concatenate(
            as_parts(
                jnp.concatenate(
                    [jnp.exp(cumul - middle)]
                    + [jnp.broadcast_to(jnp.exp(m), (16, heads)) for m in middles],
                    axis=0,
                ),
                2,
            ),
            axis=1,
        )
        outward_out[source] = outward
        scales[...] = contract(
            jnp.concatenate([inward, outward[:rows]], axis=0), expand, ((1,), (0,))
        )
        b_part, c_part = (
            jnp.concatenate(
                [activated(r, lane) for r in range(0, rows, STRIP)], axis=0
            ).astype(jnp.bfloat16)
            for lane in (width, width + STATE)
        )
        c_out[source] = c_part
        scores = contract(c_part, b_part, ((1,), (1,)))
        scores = jnp.where(lower, scores, 0.0).astype(jnp.bfloat16)
        for lane in range(0, width, LANES):
            at = slice(lane, lane + LANES)
            for r in range(0, rows, STRIP):
                x_conv = activated(r, lane)
                x_ref[r : r + STRIP, at] = x_conv
                scaled_ref[r : r + STRIP, at] = (x_conv * scales[r : r + STRIP, at]).astype(
                    jnp.bfloat16
                )
        for b in range(blocks):
            at = slice(b * BLOCK, (b + 1) * BLOCK)
            added = contract(b_part[at], scaled_ref[at], ((0,), (0,)))
            state[source, b * STATE : (b + 1) * STATE] = added.astype(jnp.bfloat16)
        intra = contract(scores, scaled_ref[...], ((1,), (0,)))
        pre[source] = (intra * scales[rows:] + skip_ref[...] * x_ref[...]).astype(jnp.bfloat16)


def carry_kernel(width, heads, whole_group, *refs):
    pre, state, c_part, outward, gain_ref = refs[:5]
    outs, (carry, scales, expand) = refs[5:-3], refs[-3:]
    rows = pre.shape[1]
    blocks = rows // BLOCK
    step = pl.program_id(0)

    @pl.when(step == 0)
    def _():
        carry[...] = jnp.zeros_like(carry)
        expand[...] = spread(heads)

    for half in range(PAIR):
        source = step * PAIR + half
        scales[half] = contract(outward[source], expand[...], ((1,), (0,)))
    held = []
    for half in range(PAIR):
        source = step * PAIR + half
        for b in range(blocks):
            middle_row = rows + 16 * b
            last_row = (b + 1) * BLOCK - 1
            now = carry[...] * scales[half, middle_row : middle_row + 1]
            held.append(now.astype(jnp.bfloat16))
            added = state[source, b * STATE : (b + 1) * STATE].astype(jnp.float32)
            carry[...] = (now + added) * scales[half, last_row : last_row + 1]
    for half in range(PAIR):
        source = step * PAIR + half
        for b in range(blocks):
            at = slice(b * BLOCK, (b + 1) * BLOCK)
            to = slice(half * rows + b * BLOCK, half * rows + (b + 1) * BLOCK)
            inter = contract(c_part[source, at], held[half * blocks + b], ((1,), (0,)))
            total = pre[source, at].astype(jnp.float32) + inter * scales[half, at]
            power = total[:, :LANES] * total[:, :LANES]
            for lane in range(LANES, width, LANES):
                power = power + total[:, lane : lane + LANES] * total[:, lane : lane + LANES]
            if whole_group:
                summed = jnp.sum(power, axis=1, keepdims=True)
                norm = lax.rsqrt(summed * (1.0 / GROUP_WIDTH) + EPS)
                outs[0][to] = (total * norm * gain_ref[...]).astype(jnp.bfloat16)
            else:
                outs[0][to] = total
                outs[1][to] = power


def per_device(inputs, key_query, conv_inputs, conv_kq, step_size, decay_log, skip_gain, norm_gain):
    peers = lax.axis_size("ctx")
    me = lax.axis_index("ctx")
    rows = inputs.shape[0]
    width = HEADS * HEAD_DIM // peers
    heads = HEADS // peers
    span = GROUP_WIDTH // width
    whole_group = span == 1
    blocks = rows // BLOCK
    full = width + 2 * STATE
    scalar_rows = scalar_units(heads, rows, full)[-1][3] + SUBLANES
    scale_rows = rows + 16 * blocks
    cycle = jnp.arange(peers, dtype=jnp.int32)
    owners = lax.rem(me + cycle, peers)
    sources = lax.rem(me + peers - cycle, peers)

    smem = pl.BlockSpec(memory_space=pltpu.SMEM)
    hbm = pl.BlockSpec(memory_space=pltpu.HBM)
    vmem = pl.BlockSpec(memory_space=pltpu.VMEM)
    params = pltpu.CompilerParams(vmem_limit_bytes=VMEM_LIMIT)

    def columns(a, first, size):
        return lax.dynamic_slice_in_dim(a, first, size, axis=1)

    def pack(codes):
        shape = jax.ShapeDtypeStruct((rows + scalar_rows, full), jnp.bfloat16)
        return pl.pallas_call(
            functools.partial(pack_kernel, peers, span, width, heads, codes),
            in_specs=[smem] + [hbm] * 4,
            out_specs=[vmem] * len(codes),
            out_shape=[shape] * len(codes),
            scratch_shapes=[
                pltpu.VMEM((FIELDS, rows, HEADS), jnp.float32),
                pltpu.VMEM((FIELDS, peers, heads, rows), jnp.float32),
                pltpu.VMEM(key_query.shape, jnp.bfloat16),
                pltpu.SemaphoreType.DMA((2, max(3, len(codes)))),
            ],
            compiler_params=pltpu.CompilerParams(vmem_limit_bytes=PACK_VMEM),
            cost_estimate=pl.CostEstimate(
                flops=0, bytes_accessed=4 * len(codes) * rows * full, transcendentals=0
            ),
            name="pack",
        )(owners, inputs, key_query, decay_log, step_size)

    codes = [code for code in ORDER if code < peers]
    codes += [code for code in range(1, peers) if code not in codes]
    parts = dict(zip(codes[:WINDOW], pack(codes[:WINDOW])))
    parts.update(zip(codes[WINDOW:] + [0], pack(codes[WINDOW:] + [0])))
    for i, code in enumerate(codes):
        pairs = [(j, (j + code) % peers) for j in range(peers)]
        message = parts[code]
        if i >= WINDOW:
            message, _ = lax.optimization_barrier((message, parts[codes[i - WINDOW]]))
        parts[code] = lax.ppermute(message, "ctx", pairs)

    group = me // span
    taps = jnp.concatenate(
        [
            columns(conv_inputs, me * width, width),
            columns(conv_kq, group * STATE, STATE),
            columns(conv_kq, (GROUPS + group) * STATE, STATE),
        ],
        axis=1,
    )
    skip = jnp.repeat(lax.dynamic_slice_in_dim(skip_gain, me * heads, heads), HEAD_DIM)[None]
    gain = columns(norm_gain[None], me * width, width)

    shapes = [
        (rows, width),
        (blocks * STATE, width),
        (rows, STATE),
        (scale_rows, 2 * heads),
    ]
    arrived = {0}
    pending = list(range(peers))
    stores = []
    for code in codes:
        arrived.add(code)
        ready = [k for k in pending if {k, (k + 1) % peers} <= arrived]
        pending = [k for k in pending if k not in ready]
        if not ready:
            continue
        count = len(ready)
        operands = []
        for k in ready:
            operands += [parts[k], parts[(k + 1) % peers]]
        stores = pl.pallas_call(
            functools.partial(local_kernel, width, heads, count, bool(stores)),
            in_specs=[smem] + [vmem] * (2 * count + 2 + len(stores)),
            out_specs=[vmem] * 4,
            out_shape=[jax.ShapeDtypeStruct((peers,) + shape, jnp.bfloat16) for shape in shapes],
            input_output_aliases={3 + 2 * count + i: i for i in range(len(stores))},
            scratch_shapes=[
                pltpu.VMEM((rows + HALO, full), jnp.bfloat16),
                pltpu.VMEM((rows, width), jnp.float32),
                pltpu.VMEM((rows, width), jnp.bfloat16),
                pltpu.VMEM((2 * rows, width), jnp.float32),
            ],
            compiler_params=params,
            cost_estimate=pl.CostEstimate(
                flops=2 * rows * count * width * 450,
                bytes_accessed=count * rows * width * 10,
                transcendentals=count * rows * full,
            ),
            name="local",
        )(jnp.stack([sources[k] for k in ready]), *operands, taps, skip, *stores)

    out = [((rows, width), jnp.bfloat16 if whole_group else jnp.float32)]
    if not whole_group:
        out.append(((rows, LANES), jnp.float32))
    results = pl.pallas_call(
        functools.partial(carry_kernel, width, heads, whole_group),
        grid=(peers // PAIR,),
        in_specs=[vmem] * 5,
        out_specs=[pl.BlockSpec((PAIR * shape[0], shape[1]), lambda i: (i, 0)) for shape, _ in out],
        out_shape=[
            jax.ShapeDtypeStruct((peers * shape[0], shape[1]), dtype) for shape, dtype in out
        ],
        scratch_shapes=[
            pltpu.VMEM((STATE, width), jnp.float32),
            pltpu.VMEM((PAIR, scale_rows, width), jnp.float32),
            pltpu.VMEM((2 * heads, width), jnp.bfloat16),
        ],
        compiler_params=params,
        cost_estimate=pl.CostEstimate(
            flops=2 * peers * rows * width * 150,
            bytes_accessed=peers * rows * width * 8,
            transcendentals=peers * rows,
        ),
        name="carry",
    )(*stores, gain)
    if whole_group:
        return results[0]
    total, power = results
    sharers = [list(range(i, i + span)) for i in range(0, peers, span)]
    summed = jnp.sum(power, axis=1, keepdims=True)
    summed = lax.psum(summed, "ctx", axis_index_groups=sharers)
    return (total * lax.rsqrt(summed * (1.0 / GROUP_WIDTH) + EPS) * gain).astype(jnp.bfloat16)


def solution(mesh):
    in_specs = (
        P(("dp", "ctx"), None),
        P(("dp", "ctx"), None),
        P(),
        P(),
        P(("dp", "ctx"), None),
        P(("dp", "ctx"), None),
        P(),
        P(),
    )
    out_specs = P("dp", "ctx")
    return jax.shard_map(
        per_device, mesh=mesh, in_specs=in_specs, out_specs=out_specs, check_vma=False
    )
```

```python
import functools

import jax
import jax.numpy as jnp
from jax import lax
from jax.experimental import pallas as pl
from jax.experimental.pallas import tpu as pltpu
from jax.sharding import PartitionSpec as P

HEADS = 128
HEAD_DIM = 64
STATE = 128
GROUPS = 8
KW = 4
BLOCK = 128
GROUP_WIDTH = HEADS * HEAD_DIM // GROUPS
EPS = 1e-05
HALO = 16
LANES = 128
SUBLANES = 8
FIELDS = 2
STRIP = 64
PAIR = 2
NEAR = 3
PACK_VMEM = 58 * 1024 * 1024
VMEM_LIMIT = 28 * 1024 * 1024


def contract(a, b, dims):
    return lax.dot_general(a, b, (dims, ((), ())), preferred_element_type=jnp.float32)


def as_parts(v, count):
    parts = []
    for _ in range(count):
        part = v.astype(jnp.bfloat16)
        parts.append(part)
        v = v - part.astype(jnp.float32)
    return parts


def scalar_units(heads, rows, cols):
    units = []
    for p in range(FIELDS):
        for head in range(0, heads, SUBLANES):
            line, column = divmod(len(units), cols // rows)
            units.append((p, head, min(SUBLANES, heads), line * SUBLANES, column * rows))
    return units


def pack_kernel(peers, span, width, heads, codes, *refs):
    owner_ref, x_ref, kq_ref, decay_ref, step_ref, rim, taps_x, taps_kq = refs[:8]
    outs = refs[8 : 8 + len(codes)]
    raw_scalars, scalars, kq_near, wide, sems = refs[8 + len(codes) :]
    rows = x_ref.shape[0]
    channels = x_ref.shape[1]
    full = width + 2 * STATE
    copies = [
        pltpu.make_async_copy(ref, dst, sems.at[1, i])
        for i, (ref, dst) in enumerate(
            ((decay_ref, raw_scalars.at[0]), (step_ref, raw_scalars.at[1]), (kq_ref, kq_near))
        )
    ]
    owners = [owner_ref[code] for code in codes]
    for i, owner in enumerate(owners):
        column = pl.multiple_of(owner * width, LANES)
        copies.append(
            pltpu.make_async_copy(
                x_ref.at[:, pl.ds(column, width)],
                wide.at[i, HALO : HALO + rows, 0:width],
                sems.at[0, i],
            )
        )
    for copy in copies:
        copy.start()
    for copy in copies[:3]:
        copy.wait()
    for p in range(FIELDS):
        field = raw_scalars[p].T
        for owner in range(peers):
            scalars[p, owner] = field[owner * heads : (owner + 1) * heads]
    for i, owner in enumerate(owners):
        copies[3 + i].wait()
        column = pl.multiple_of(owner * width, LANES)
        wide[i, HALO - SUBLANES : HALO, 0:width] = rim[:, pl.ds(column, width)]
        for j in range(2):
            column = pl.multiple_of((j * GROUPS + owner // span) * STATE, LANES)
            at = slice(width + j * STATE, width + (j + 1) * STATE)
            wide[i, HALO - SUBLANES : HALO, at] = rim[
                :, pl.ds(pl.multiple_of(channels + column, LANES), STATE)
            ]
            wide[i, HALO:, at] = kq_near[:, pl.ds(column, STATE)]
        outs[i][rows:] = jnp.zeros((outs[i].shape[0] - rows, full), jnp.bfloat16)
        for p, head, count, top, left in scalar_units(heads, rows, full):
            outs[i][rows + top : rows + top + count, left : left + rows] = scalars[
                p, owner, head : head + count
            ].astype(jnp.bfloat16)
        for lane in range(0, full, LANES):
            if lane < width:
                taps_ref, column = taps_x, owner * width + lane
            else:
                part = (lane - width) // STATE
                taps_ref, column = taps_kq, (part * GROUPS + owner // span) * STATE
            column = pl.multiple_of(column, LANES)
            tap = [taps_ref[k : k + 1, pl.ds(column, LANES)] for k in range(KW)]
            for r in range(0, rows, STRIP):
                now = wide[i, r : r + STRIP + HALO, lane : lane + LANES].astype(jnp.float32)
                now = now[HALO // 2 :]
                before = pltpu.roll(now, 1, 0)
                older = pltpu.roll(tap[0] * before + tap[1] * now, 2, 0)
                summed = (older + (tap[2] * before + tap[3] * now))[HALO // 2 :]
                outs[i][r : r + STRIP, lane : lane + LANES] = (
                    summed * pltpu.reciprocal(1.0 + jnp.exp(-summed), approx=True)
                ).astype(jnp.bfloat16)


def spread(heads):
    head_of = lax.broadcasted_iota(jnp.int32, (2 * heads, heads * HEAD_DIM), 1) // HEAD_DIM
    row = lax.rem(lax.broadcasted_iota(jnp.int32, (2 * heads, heads * HEAD_DIM), 0), heads)
    return jnp.where(head_of == row, 1.0, 0.0).astype(jnp.bfloat16)


def local_kernel(width, heads, code, paired, chained, *refs):
    place_ref, part_ref, skip_ref = refs[:3]
    refs = refs[3 + (4 if chained else 0) :]
    pre, state, c_out, outward_out = refs[:4]
    scaled_ref, scales = refs[4:]
    rows = scaled_ref.shape[0]
    blocks = rows // BLOCK
    full = width + 2 * STATE
    row = lax.broadcasted_iota(jnp.int32, (rows, rows), 0)
    col = lax.broadcasted_iota(jnp.int32, (rows, rows), 1)
    lower = (row >= col) & (row // BLOCK == col // BLOCK)
    ones = jnp.where(lower, 1.0, 0.0).astype(jnp.bfloat16)
    eye = jnp.where(row == col, 1.0, 0.0).astype(jnp.bfloat16)
    source = place_ref[code]
    part = part_ref.at[jnp.where(source < place_ref[0], 0, 1)] if paired else part_ref

    def field(p):
        pieces = [
            part[rows + top : rows + top + size, left : left + rows].astype(jnp.float32)
            for q, _, size, top, left in scalar_units(heads, rows, full)
            if q == p
        ]
        return jnp.concatenate(pieces, axis=0).astype(jnp.bfloat16)

    cumul = contract(ones, field(0), ((1,), (1,)))
    steps = contract(eye, field(1), ((1,), (1,)))
    middles = [cumul[b * BLOCK + BLOCK // 2 - 1 : b * BLOCK + BLOCK // 2] for b in range(blocks)]
    middle = jnp.concatenate([jnp.broadcast_to(m, (BLOCK, heads)) for m in middles], axis=0)
    inward = jnp.concatenate(as_parts(steps * jnp.exp(middle - cumul), 2), axis=1)
    outward = jnp.concatenate(
        as_parts(
            jnp.concatenate(
                [jnp.exp(cumul - middle)]
                + [jnp.broadcast_to(jnp.exp(m), (16, heads)) for m in middles],
                axis=0,
            ),
            2,
        ),
        axis=1,
    )
    outward_out[source] = outward
    scales[...] = contract(
        jnp.concatenate([inward, outward[:rows]], axis=0), spread(heads), ((1,), (0,))
    )
    b_part = part[0:rows, width : width + STATE]
    c_part = part[0:rows, width + STATE : full]
    c_out[source] = c_part
    scores = contract(c_part, b_part, ((1,), (1,)))
    scores = jnp.where(lower, scores, 0.0).astype(jnp.bfloat16)
    scaled_ref[...] = (part[0:rows, 0:width].astype(jnp.float32) * scales[:rows]).astype(
        jnp.bfloat16
    )
    for b in range(blocks):
        at = slice(b * BLOCK, (b + 1) * BLOCK)
        added = contract(b_part[at], scaled_ref[at], ((0,), (0,)))
        state[source, b * STATE : (b + 1) * STATE] = added.astype(jnp.bfloat16)
    intra = contract(scores, scaled_ref[...], ((1,), (0,)))
    direct = skip_ref[...] * part[0:rows, 0:width].astype(jnp.float32)
    pre[source] = (intra * scales[rows:] + direct).astype(jnp.bfloat16)


def carry_kernel(width, heads, whole_group, *refs):
    pre, state, c_part, outward, gain_ref = refs[:5]
    outs, (carry, scales, expand) = refs[5:-3], refs[-3:]
    rows = pre.shape[1]
    blocks = rows // BLOCK
    step = pl.program_id(0)

    @pl.when(step == 0)
    def _():
        carry[...] = jnp.zeros_like(carry)
        expand[...] = spread(heads)

    for half in range(PAIR):
        source = step * PAIR + half
        scales[half] = contract(outward[source], expand[...], ((1,), (0,)))
    held = []
    for half in range(PAIR):
        source = step * PAIR + half
        for b in range(blocks):
            middle_row = rows + 16 * b
            last_row = (b + 1) * BLOCK - 1
            now = carry[...] * scales[half, middle_row : middle_row + 1]
            held.append(now.astype(jnp.bfloat16))
            added = state[source, b * STATE : (b + 1) * STATE].astype(jnp.float32)
            carry[...] = (now + added) * scales[half, last_row : last_row + 1]
    for half in range(PAIR):
        source = step * PAIR + half
        for b in range(blocks):
            at = slice(b * BLOCK, (b + 1) * BLOCK)
            to = slice(half * rows + b * BLOCK, half * rows + (b + 1) * BLOCK)
            inter = contract(c_part[source, at], held[half * blocks + b], ((1,), (0,)))
            total = pre[source, at].astype(jnp.float32) + inter * scales[half, at]
            power = total[:, :LANES] * total[:, :LANES]
            for lane in range(LANES, width, LANES):
                power = power + total[:, lane : lane + LANES] * total[:, lane : lane + LANES]
            if whole_group:
                summed = jnp.sum(power, axis=1, keepdims=True)
                norm = lax.rsqrt(summed * (1.0 / GROUP_WIDTH) + EPS)
                outs[0][to] = (total * norm * gain_ref[...]).astype(jnp.bfloat16)
            else:
                outs[0][to] = total
                outs[1][to] = power


def per_device(inputs, key_query, conv_inputs, conv_kq, step_size, decay_log, skip_gain, norm_gain):
    peers = lax.axis_size("ctx")
    me = lax.axis_index("ctx")
    rows = inputs.shape[0]
    width = HEADS * HEAD_DIM // peers
    heads = HEADS // peers
    span = GROUP_WIDTH // width
    whole_group = span == 1
    blocks = rows // BLOCK
    full = width + 2 * STATE
    scalar_rows = scalar_units(heads, rows, full)[-1][3] + SUBLANES
    scale_rows = rows + 16 * blocks
    cycle = jnp.arange(peers, dtype=jnp.int32)
    places = me ^ cycle

    smem = pl.BlockSpec(memory_space=pltpu.SMEM)
    hbm = pl.BlockSpec(memory_space=pltpu.HBM)
    vmem = pl.BlockSpec(memory_space=pltpu.VMEM)
    params = pltpu.CompilerParams(vmem_limit_bytes=VMEM_LIMIT)

    def columns(a, first, size):
        return lax.dynamic_slice_in_dim(a, first, size, axis=1)

    tails = jnp.concatenate([inputs[rows - SUBLANES :], key_query[rows - SUBLANES :]], axis=1)
    rim = lax.ppermute(tails, "ctx", [(i, i + 1) for i in range(peers - 1)])

    def pack(codes, after):
        order, _ = lax.optimization_barrier((places, after))
        shape = jax.ShapeDtypeStruct((rows + scalar_rows, full), jnp.bfloat16)
        return pl.pallas_call(
            functools.partial(pack_kernel, peers, span, width, heads, codes),
            in_specs=[smem] + [hbm] * 4 + [vmem] * 3,
            out_specs=[vmem] * len(codes),
            out_shape=[shape] * len(codes),
            scratch_shapes=[
                pltpu.VMEM((FIELDS, rows, HEADS), jnp.float32),
                pltpu.VMEM((FIELDS, peers, heads, rows), jnp.float32),
                pltpu.VMEM(key_query.shape, jnp.bfloat16),
                pltpu.VMEM((len(codes), rows + HALO, full), jnp.bfloat16),
                pltpu.SemaphoreType.DMA((2, max(3, len(codes)))),
            ],
            compiler_params=pltpu.CompilerParams(vmem_limit_bytes=PACK_VMEM),
            cost_estimate=pl.CostEstimate(
                flops=20 * len(codes) * rows * full,
                bytes_accessed=4 * len(codes) * rows * full,
                transcendentals=len(codes) * rows * full,
            ),
            name="pack",
        )(order, inputs, key_query, decay_log, step_size, rim, conv_inputs, conv_kq)

    far = list(range(peers - 1, NEAR, -1))
    near = list(range(NEAR, 0, -1))
    parts = {}
    packed = ()
    for codes in (far[:2], far[2:], near + [0]):
        packed = pack(codes, packed)
        parts.update(zip(codes, packed))
    for code in far:
        pairs = [(i, i ^ code) for i in range(peers)]
        parts[code] = lax.ppermute(parts[code], "ctx", pairs)
    for code in near:
        couples = [[i, i ^ code] for i in range(peers) if i < i ^ code]
        parts[code] = lax.all_gather(parts[code], "ctx", axis_index_groups=couples)

    skip = jnp.repeat(lax.dynamic_slice_in_dim(skip_gain, me * heads, heads), HEAD_DIM)[None]
    gain = columns(norm_gain[None], me * width, width)

    shapes = [
        (rows, width),
        (blocks * STATE, width),
        (rows, STATE),
        (scale_rows, 2 * heads),
    ]
    stores = []
    for code in [0] + near[::-1] + far:
        stores = pl.pallas_call(
            functools.partial(local_kernel, width, heads, code, code in near, bool(stores)),
            in_specs=[smem] + [vmem] * (2 + len(stores)),
            out_specs=[vmem] * 4,
            out_shape=[jax.ShapeDtypeStruct((peers,) + shape, jnp.bfloat16) for shape in shapes],
            input_output_aliases={3 + i: i for i in range(len(stores))},
            scratch_shapes=[
                pltpu.VMEM((rows, width), jnp.bfloat16),
                pltpu.VMEM((2 * rows, width), jnp.float32),
            ],
            compiler_params=params,
            cost_estimate=pl.CostEstimate(
                flops=2 * rows * width * 450,
                bytes_accessed=rows * width * 10,
                transcendentals=rows * heads,
            ),
            name="local",
        )(places, parts[code], skip, *stores)

    out = [((rows, width), jnp.bfloat16 if whole_group else jnp.float32)]
    if not whole_group:
        out.append(((rows, LANES), jnp.float32))
    results = pl.pallas_call(
        functools.partial(carry_kernel, width, heads, whole_group),
        grid=(peers // PAIR,),
        in_specs=[vmem] * 5,
        out_specs=[pl.BlockSpec((PAIR * shape[0], shape[1]), lambda i: (i, 0)) for shape, _ in out],
        out_shape=[
            jax.ShapeDtypeStruct((peers * shape[0], shape[1]), dtype) for shape, dtype in out
        ],
        scratch_shapes=[
            pltpu.VMEM((STATE, width), jnp.float32),
            pltpu.VMEM((PAIR, scale_rows, width), jnp.float32),
            pltpu.VMEM((2 * heads, width), jnp.bfloat16),
        ],
        compiler_params=params,
        cost_estimate=pl.CostEstimate(
            flops=2 * peers * rows * width * 150,
            bytes_accessed=peers * rows * width * 8,
            transcendentals=peers * rows,
        ),
        name="carry",
    )(*stores, gain)
    if whole_group:
        return results[0]
    total, power = results
    sharers = [list(range(i, i + span)) for i in range(0, peers, span)]
    summed = jnp.sum(power, axis=1, keepdims=True)
    summed = lax.psum(summed, "ctx", axis_index_groups=sharers)
    return (total * lax.rsqrt(summed * (1.0 / GROUP_WIDTH) + EPS) * gain).astype(jnp.bfloat16)


def solution(mesh):
    in_specs = (
        P(("dp", "ctx"), None),
        P(("dp", "ctx"), None),
        P(),
        P(),
        P(("dp", "ctx"), None),
        P(("dp", "ctx"), None),
        P(),
        P(),
    )
    out_specs = P("dp", "ctx")
    return jax.shard_map(
        per_device, mesh=mesh, in_specs=in_specs, out_specs=out_specs, check_vma=False
    )
```

```python
import functools

import jax
import jax.numpy as jnp
from jax import lax
from jax.experimental import pallas as pl
from jax.experimental.pallas import tpu as pltpu
from jax.sharding import PartitionSpec as P

HEADS = 128
HEAD_DIM = 64
STATE = 128
GROUPS = 8
KW = 4
BLOCK = 128
GROUP_WIDTH = HEADS * HEAD_DIM // GROUPS
EPS = 1e-05
HALO = 16
LANES = 128
SUBLANES = 8
FIELDS = 2
STRIP = 64
PAIR = 2
WINDOW = 5
ORDER = (4, 1, 3, 7, 5, 2, 6)
PACK_VMEM = 58 * 1024 * 1024
VMEM_LIMIT = 28 * 1024 * 1024


def contract(a, b, dims):
    return lax.dot_general(a, b, (dims, ((), ())), preferred_element_type=jnp.float32)


def as_parts(v, count):
    parts = []
    for _ in range(count):
        part = v.astype(jnp.bfloat16)
        parts.append(part)
        v = v - part.astype(jnp.float32)
    return parts


def scalar_units(heads, rows, cols):
    units = []
    for p in range(FIELDS):
        for head in range(0, heads, SUBLANES):
            line, column = divmod(len(units), cols // rows)
            units.append((p, head, min(SUBLANES, heads), line * SUBLANES, column * rows))
    return units


def pack_kernel(peers, span, width, heads, codes, *refs):
    owner_ref, x_ref, kq_ref, decay_ref, step_ref = refs[:5]
    outs = refs[5 : 5 + len(codes)]
    raw_scalars, scalars, kq_near, sems = refs[5 + len(codes) :]
    rows = x_ref.shape[0]
    copies = [
        pltpu.make_async_copy(ref, dst, sems.at[1, i])
        for i, (ref, dst) in enumerate(
            ((decay_ref, raw_scalars.at[0]), (step_ref, raw_scalars.at[1]), (kq_ref, kq_near))
        )
    ]
    owners = [owner_ref[code] for code in codes]
    for i, owner in enumerate(owners):
        column = pl.multiple_of(owner * width, LANES)
        copies.append(
            pltpu.make_async_copy(
                x_ref.at[:, pl.ds(column, width)], outs[i].at[0:rows, 0:width], sems.at[0, i]
            )
        )
    for copy in copies:
        copy.start()
    for copy in copies[:3]:
        copy.wait()
    for p in range(FIELDS):
        field = raw_scalars[p].T
        for owner in range(peers):
            scalars[p, owner] = field[owner * heads : (owner + 1) * heads]
    for i, owner in enumerate(owners):
        outs[i][rows:] = jnp.zeros((outs[i].shape[0] - rows, outs[i].shape[1]), jnp.bfloat16)
        for p, head, count, top, left in scalar_units(heads, rows, width + 2 * STATE):
            outs[i][rows + top : rows + top + count, left : left + rows] = scalars[
                p, owner, head : head + count
            ].astype(jnp.bfloat16)
        for j in range(2):
            column = pl.multiple_of((j * GROUPS + owner // span) * STATE, LANES)
            left = width + j * STATE
            outs[i][0:rows, left : left + STATE] = kq_near[:, pl.ds(column, STATE)]
    for copy in copies[3:]:
        copy.wait()


def spread(heads):
    head_of = lax.broadcasted_iota(jnp.int32, (2 * heads, heads * HEAD_DIM), 1) // HEAD_DIM
    row = lax.rem(lax.broadcasted_iota(jnp.int32, (2 * heads, heads * HEAD_DIM), 0), heads)
    return jnp.where(head_of == row, 1.0, 0.0).astype(jnp.bfloat16)


def local_kernel(width, heads, count, chained, *refs):
    source_ref = refs[0]
    parts = refs[1 : 1 + 2 * count]
    taps_ref, skip_ref = refs[1 + 2 * count : 3 + 2 * count]
    refs = refs[3 + 2 * count + (5 if chained else 0) :]
    pre, state, c_out, fade_out, edge_out = refs[:5]
    wide, x_ref, scaled_ref, scales = refs[5:]
    rows = x_ref.shape[0]
    blocks = rows // BLOCK
    full = width + 2 * STATE
    row = lax.broadcasted_iota(jnp.int32, (rows, rows), 0)
    col = lax.broadcasted_iota(jnp.int32, (rows, rows), 1)
    lower = (row >= col) & (row // BLOCK == col // BLOCK)
    ones = jnp.where(lower, 1.0, 0.0).astype(jnp.bfloat16)
    eye = jnp.where(row == col, 1.0, 0.0).astype(jnp.bfloat16)
    expand = spread(heads)

    for which in range(count):
        source = source_ref[which]
        part, earlier = parts[2 * which : 2 * which + 2]
        wide[HALO:] = part[0:rows, 0:full]
        edge = earlier[rows - HALO : rows, 0:full]
        wide[0:HALO] = jnp.where(source == 0, jnp.zeros_like(edge), edge)

        def activated(r, lane):
            tap = [taps_ref[k : k + 1, lane : lane + LANES] for k in range(KW)]
            now = wide[r : r + STRIP + HALO, lane : lane + LANES].astype(jnp.float32)
            now = now[HALO // 2 :]
            before = pltpu.roll(now, 1, 0)
            older = pltpu.roll(tap[0] * before + tap[1] * now, 2, 0)
            summed = (older + (tap[2] * before + tap[3] * now))[HALO // 2 :]
            return summed * pltpu.reciprocal(1.0 + jnp.exp(-summed), approx=True)

        def field(p):
            pieces = [
                part[rows + top : rows + top + size, left : left + rows].astype(jnp.float32)
                for q, _, size, top, left in scalar_units(heads, rows, full)
                if q == p
            ]
            return jnp.concatenate(pieces, axis=0).astype(jnp.bfloat16)

        cumul = contract(ones, field(0), ((1,), (1,)))
        steps = contract(eye, field(1), ((1,), (1,)))
        middles = [
            cumul[b * BLOCK + BLOCK // 2 - 1 : b * BLOCK + BLOCK // 2] for b in range(blocks)
        ]
        middle = jnp.concatenate([jnp.broadcast_to(m, (BLOCK, heads)) for m in middles], axis=0)
        inward = jnp.concatenate(as_parts(steps * jnp.exp(middle - cumul), 2), axis=1)
        outward = jnp.concatenate(
            as_parts(
                jnp.concatenate(
                    [jnp.exp(cumul - middle)]
                    + [jnp.broadcast_to(jnp.exp(m), (16, heads)) for m in middles],
                    axis=0,
                ),
                2,
            ),
            axis=1,
        )
        scales[...] = contract(
            jnp.concatenate([inward, outward], axis=0), expand, ((1,), (0,))
        )
        edges = []
        for b in range(blocks):
            last_row = rows + (b + 1) * BLOCK - 1
            middle_row = 2 * rows + 16 * b
            edges += [scales[middle_row : middle_row + 1], scales[last_row : last_row + 1]]
        edge_out[source, 0 : 2 * blocks] = jnp.concatenate(edges, axis=0)
        fade_out[source] = scales[rows : 2 * rows].astype(jnp.bfloat16)
        b_part, c_part = (
            jnp.concatenate(
                [activated(r, lane) for r in range(0, rows, STRIP)], axis=0
            ).astype(jnp.bfloat16)
            for lane in (width, width + STATE)
        )
        c_out[source] = c_part
        scores = contract(c_part, b_part, ((1,), (1,)))
        scores = jnp.where(lower, scores, 0.0).astype(jnp.bfloat16)
        for lane in range(0, width, LANES):
            at = slice(lane, lane + LANES)
            for r in range(0, rows, STRIP):
                x_conv = activated(r, lane)
                x_ref[r : r + STRIP, at] = x_conv
                scaled_ref[r : r + STRIP, at] = (x_conv * scales[r : r + STRIP, at]).astype(
                    jnp.bfloat16
                )
        for b in range(blocks):
            at = slice(b * BLOCK, (b + 1) * BLOCK)
            added = contract(b_part[at], scaled_ref[at], ((0,), (0,)))
            state[source, b * STATE : (b + 1) * STATE] = added.astype(jnp.bfloat16)
        intra = contract(scores, scaled_ref[...], ((1,), (0,)))
        pre[source] = (intra * scales[rows : 2 * rows] + skip_ref[...] * x_ref[...]).astype(jnp.bfloat16)


def carry_kernel(width, whole_group, *refs):
    pre, state, c_part, fade, edge, gain_ref = refs[:6]
    outs, carry = refs[6:-1], refs[-1]
    rows = pre.shape[1]
    blocks = rows // BLOCK
    step = pl.program_id(0)

    @pl.when(step == 0)
    def _():
        carry[...] = jnp.zeros_like(carry)

    held = []
    for half in range(PAIR):
        source = step * PAIR + half
        for b in range(blocks):
            now = carry[...] * edge[source, 2 * b : 2 * b + 1]
            held.append(now.astype(jnp.bfloat16))
            added = state[source, b * STATE : (b + 1) * STATE].astype(jnp.float32)
            carry[...] = (now + added) * edge[source, 2 * b + 1 : 2 * b + 2]
    for half in range(PAIR):
        source = step * PAIR + half
        for b in range(blocks):
            at = slice(b * BLOCK, (b + 1) * BLOCK)
            to = slice(half * rows + b * BLOCK, half * rows + (b + 1) * BLOCK)
            inter = contract(c_part[source, at], held[half * blocks + b], ((1,), (0,)))
            total = pre[source, at].astype(jnp.float32) + inter * fade[source, at].astype(
                jnp.float32
            )
            power = total[:, :LANES] * total[:, :LANES]
            for lane in range(LANES, width, LANES):
                power = power + total[:, lane : lane + LANES] * total[:, lane : lane + LANES]
            if whole_group:
                summed = jnp.sum(power, axis=1, keepdims=True)
                norm = lax.rsqrt(summed * (1.0 / GROUP_WIDTH) + EPS)
                outs[0][to] = (total * norm * gain_ref[...]).astype(jnp.bfloat16)
            else:
                outs[0][to] = total
                outs[1][to] = power


def per_device(inputs, key_query, conv_inputs, conv_kq, step_size, decay_log, skip_gain, norm_gain):
    peers = lax.axis_size("ctx")
    me = lax.axis_index("ctx")
    rows = inputs.shape[0]
    width = HEADS * HEAD_DIM // peers
    heads = HEADS // peers
    span = GROUP_WIDTH // width
    whole_group = span == 1
    blocks = rows // BLOCK
    full = width + 2 * STATE
    scalar_rows = scalar_units(heads, rows, full)[-1][3] + SUBLANES
    scale_rows = rows + 16 * blocks
    cycle = jnp.arange(peers, dtype=jnp.int32)
    owners = lax.rem(me + cycle, peers)
    sources = lax.rem(me + peers - cycle, peers)

    smem = pl.BlockSpec(memory_space=pltpu.SMEM)
    hbm = pl.BlockSpec(memory_space=pltpu.HBM)
    vmem = pl.BlockSpec(memory_space=pltpu.VMEM)
    params = pltpu.CompilerParams(vmem_limit_bytes=VMEM_LIMIT)

    def columns(a, first, size):
        return lax.dynamic_slice_in_dim(a, first, size, axis=1)

    def pack(codes):
        shape = jax.ShapeDtypeStruct((rows + scalar_rows, full), jnp.bfloat16)
        return pl.pallas_call(
            functools.partial(pack_kernel, peers, span, width, heads, codes),
            in_specs=[smem] + [hbm] * 4,
            out_specs=[vmem] * len(codes),
            out_shape=[shape] * len(codes),
            scratch_shapes=[
                pltpu.VMEM((FIELDS, rows, HEADS), jnp.float32),
                pltpu.VMEM((FIELDS, peers, heads, rows), jnp.float32),
                pltpu.VMEM(key_query.shape, jnp.bfloat16),
                pltpu.SemaphoreType.DMA((2, max(3, len(codes)))),
            ],
            compiler_params=pltpu.CompilerParams(vmem_limit_bytes=PACK_VMEM),
            cost_estimate=pl.CostEstimate(
                flops=0, bytes_accessed=4 * len(codes) * rows * full, transcendentals=0
            ),
            name="pack",
        )(owners, inputs, key_query, decay_log, step_size)

    codes = [code for code in ORDER if code < peers]
    codes += [code for code in range(1, peers) if code not in codes]
    parts = dict(zip(codes[:WINDOW], pack(codes[:WINDOW])))
    parts.update(zip(codes[WINDOW:] + [0], pack(codes[WINDOW:] + [0])))
    for i, code in enumerate(codes):
        pairs = [(j, (j + code) % peers) for j in range(peers)]
        message = parts[code]
        if i >= WINDOW:
            message, _ = lax.optimization_barrier((message, parts[codes[i - WINDOW]]))
        parts[code] = lax.ppermute(message, "ctx", pairs)

    group = me // span
    taps = jnp.concatenate(
        [
            columns(conv_inputs, me * width, width),
            columns(conv_kq, group * STATE, STATE),
            columns(conv_kq, (GROUPS + group) * STATE, STATE),
        ],
        axis=1,
    )
    skip = jnp.repeat(lax.dynamic_slice_in_dim(skip_gain, me * heads, heads), HEAD_DIM)[None]
    gain = columns(norm_gain[None], me * width, width)

    shapes = [
        ((rows, width), jnp.bfloat16),
        ((blocks * STATE, width), jnp.bfloat16),
        ((rows, STATE), jnp.bfloat16),
        ((rows, width), jnp.bfloat16),
        ((2 * blocks, width), jnp.float32),
    ]
    arrived = {0}
    pending = list(range(peers))
    stores = []
    for code in codes:
        arrived.add(code)
        ready = [k for k in pending if {k, (k + 1) % peers} <= arrived]
        pending = [k for k in pending if k not in ready]
        if not ready:
            continue
        count = len(ready)
        operands = []
        for k in ready:
            operands += [parts[k], parts[(k + 1) % peers]]
        stores = pl.pallas_call(
            functools.partial(local_kernel, width, heads, count, bool(stores)),
            in_specs=[smem] + [vmem] * (2 * count + 2 + len(stores)),
            out_specs=[vmem] * len(shapes),
            out_shape=[jax.ShapeDtypeStruct((peers,) + shape, dtype) for shape, dtype in shapes],
            input_output_aliases={3 + 2 * count + i: i for i in range(len(stores))},
            scratch_shapes=[
                pltpu.VMEM((rows + HALO, full), jnp.bfloat16),
                pltpu.VMEM((rows, width), jnp.float32),
                pltpu.VMEM((rows, width), jnp.bfloat16),
                pltpu.VMEM((rows + scale_rows, width), jnp.float32),
            ],
            compiler_params=params,
            cost_estimate=pl.CostEstimate(
                flops=2 * rows * count * width * 450,
                bytes_accessed=count * rows * width * 10,
                transcendentals=count * rows * full,
            ),
            name="local",
        )(jnp.stack([sources[k] for k in ready]), *operands, taps, skip, *stores)

    out = [((rows, width), jnp.bfloat16 if whole_group else jnp.float32)]
    if not whole_group:
        out.append(((rows, LANES), jnp.float32))
    results = pl.pallas_call(
        functools.partial(carry_kernel, width, whole_group),
        grid=(peers // PAIR,),
        in_specs=[vmem] * (len(shapes) + 1),
        out_specs=[pl.BlockSpec((PAIR * shape[0], shape[1]), lambda i: (i, 0)) for shape, _ in out],
        out_shape=[
            jax.ShapeDtypeStruct((peers * shape[0], shape[1]), dtype) for shape, dtype in out
        ],
        scratch_shapes=[
            pltpu.VMEM((STATE, width), jnp.float32),
        ],
        compiler_params=params,
        cost_estimate=pl.CostEstimate(
            flops=2 * peers * rows * width * 150,
            bytes_accessed=peers * rows * width * 8,
            transcendentals=peers * rows,
        ),
        name="carry",
    )(*stores, gain)
    if whole_group:
        return results[0]
    total, power = results
    sharers = [list(range(i, i + span)) for i in range(0, peers, span)]
    summed = jnp.sum(power, axis=1, keepdims=True)
    summed = lax.psum(summed, "ctx", axis_index_groups=sharers)
    return (total * lax.rsqrt(summed * (1.0 / GROUP_WIDTH) + EPS) * gain).astype(jnp.bfloat16)


def solution(mesh):
    in_specs = (
        P(("dp", "ctx"), None),
        P(("dp", "ctx"), None),
        P(),
        P(),
        P(("dp", "ctx"), None),
        P(("dp", "ctx"), None),
        P(),
        P(),
    )
    out_specs = P("dp", "ctx")
    return jax.shard_map(
        per_device, mesh=mesh, in_specs=in_specs, out_specs=out_specs, check_vma=False
    )
```

```python
import functools

import jax
import jax.numpy as jnp
from jax import lax
from jax.experimental import pallas as pl
from jax.experimental.pallas import tpu as pltpu
from jax.sharding import PartitionSpec as P

HEADS = 128
HEAD_DIM = 64
STATE = 128
GROUPS = 8
KW = 4
BLOCK = 128
GROUP_WIDTH = HEADS * HEAD_DIM // GROUPS
EPS = 1e-05
HALO = 16
LANES = 128
SUBLANES = 8
FIELDS = 2
STRIP = 64
PAIR = 2
WINDOW = 5
ORDER = (1, 7, 4, 2, 6, 3, 5)
PACK_VMEM = 58 * 1024 * 1024
VMEM_LIMIT = 28 * 1024 * 1024


def contract(a, b, dims):
    return lax.dot_general(a, b, (dims, ((), ())), preferred_element_type=jnp.float32)


def as_parts(v, count):
    parts = []
    for _ in range(count):
        part = v.astype(jnp.bfloat16)
        parts.append(part)
        v = v - part.astype(jnp.float32)
    return parts


def scalar_units(heads, rows, cols):
    units = []
    for p in range(FIELDS):
        for head in range(0, heads, SUBLANES):
            line, column = divmod(len(units), cols // rows)
            units.append((p, head, min(SUBLANES, heads), line * SUBLANES, column * rows))
    return units


def pack_kernel(peers, span, width, heads, codes, *refs):
    owner_ref, x_ref, kq_ref, decay_ref, step_ref = refs[:5]
    outs = refs[5 : 5 + len(codes)]
    raw_scalars, scalars, kq_near, sems = refs[5 + len(codes) :]
    rows = x_ref.shape[0]
    copies = [
        pltpu.make_async_copy(ref, dst, sems.at[1, i])
        for i, (ref, dst) in enumerate(
            ((decay_ref, raw_scalars.at[0]), (step_ref, raw_scalars.at[1]), (kq_ref, kq_near))
        )
    ]
    owners = [owner_ref[code] for code in codes]
    for i, owner in enumerate(owners):
        column = pl.multiple_of(owner * width, LANES)
        copies.append(
            pltpu.make_async_copy(
                x_ref.at[:, pl.ds(column, width)], outs[i].at[0:rows, 0:width], sems.at[0, i]
            )
        )
    for copy in copies:
        copy.start()
    for copy in copies[:3]:
        copy.wait()
    for p in range(FIELDS):
        field = raw_scalars[p].T
        for owner in range(peers):
            scalars[p, owner] = field[owner * heads : (owner + 1) * heads]
    for i, owner in enumerate(owners):
        outs[i][rows:] = jnp.zeros((outs[i].shape[0] - rows, outs[i].shape[1]), jnp.bfloat16)
        for p, head, count, top, left in scalar_units(heads, rows, width + 2 * STATE):
            outs[i][rows + top : rows + top + count, left : left + rows] = scalars[
                p, owner, head : head + count
            ].astype(jnp.bfloat16)
        for j in range(2):
            column = pl.multiple_of((j * GROUPS + owner // span) * STATE, LANES)
            left = width + j * STATE
            outs[i][0:rows, left : left + STATE] = kq_near[:, pl.ds(column, STATE)]
    for copy in copies[3:]:
        copy.wait()


def spread(heads):
    head_of = lax.broadcasted_iota(jnp.int32, (2 * heads, heads * HEAD_DIM), 1) // HEAD_DIM
    row = lax.rem(lax.broadcasted_iota(jnp.int32, (2 * heads, heads * HEAD_DIM), 0), heads)
    return jnp.where(head_of == row, 1.0, 0.0).astype(jnp.bfloat16)


def local_kernel(width, heads, count, chained, *refs):
    source_ref = refs[0]
    parts = refs[1 : 1 + 2 * count]
    taps_ref, skip_ref = refs[1 + 2 * count : 3 + 2 * count]
    refs = refs[3 + 2 * count + (5 if chained else 0) :]
    pre, state, c_out, fade_out, edge_out = refs[:5]
    wide, x_ref, scaled_ref, scales = refs[5:]
    rows = x_ref.shape[0]
    blocks = rows // BLOCK
    full = width + 2 * STATE
    row = lax.broadcasted_iota(jnp.int32, (rows, rows), 0)
    col = lax.broadcasted_iota(jnp.int32, (rows, rows), 1)
    lower = (row >= col) & (row // BLOCK == col // BLOCK)
    ones = jnp.where(lower, 1.0, 0.0).astype(jnp.bfloat16)
    eye = jnp.where(row == col, 1.0, 0.0).astype(jnp.bfloat16)
    expand = spread(heads)

    for which in range(count):
        source = source_ref[which]
        part, earlier = parts[2 * which : 2 * which + 2]
        wide[HALO:] = part[0:rows, 0:full]
        edge = earlier[rows - HALO : rows, 0:full]
        wide[0:HALO] = jnp.where(source == 0, jnp.zeros_like(edge), edge)

        def activated(r, lane):
            tap = [taps_ref[k : k + 1, lane : lane + LANES] for k in range(KW)]
            now = wide[r : r + STRIP + HALO, lane : lane + LANES].astype(jnp.float32)
            now = now[HALO // 2 :]
            before = pltpu.roll(now, 1, 0)
            older = pltpu.roll(tap[0] * before + tap[1] * now, 2, 0)
            summed = (older + (tap[2] * before + tap[3] * now))[HALO // 2 :]
            return summed * pltpu.reciprocal(1.0 + jnp.exp(-summed), approx=True)

        def field(p):
            pieces = [
                part[rows + top : rows + top + size, left : left + rows].astype(jnp.float32)
                for q, _, size, top, left in scalar_units(heads, rows, full)
                if q == p
            ]
            return jnp.concatenate(pieces, axis=0).astype(jnp.bfloat16)

        cumul = contract(ones, field(0), ((1,), (1,)))
        steps = contract(eye, field(1), ((1,), (1,)))
        middles = [
            cumul[b * BLOCK + BLOCK // 2 - 1 : b * BLOCK + BLOCK // 2] for b in range(blocks)
        ]
        middle = jnp.concatenate([jnp.broadcast_to(m, (BLOCK, heads)) for m in middles], axis=0)
        inward = jnp.concatenate(as_parts(steps * jnp.exp(middle - cumul), 2), axis=1)
        outward = jnp.concatenate(
            as_parts(
                jnp.concatenate(
                    [jnp.exp(cumul - middle)]
                    + [jnp.broadcast_to(jnp.exp(m), (16, heads)) for m in middles],
                    axis=0,
                ),
                2,
            ),
            axis=1,
        )
        scales[...] = contract(
            jnp.concatenate([inward, outward], axis=0), expand, ((1,), (0,))
        )
        edges = []
        for b in range(blocks):
            last_row = rows + (b + 1) * BLOCK - 1
            middle_row = 2 * rows + 16 * b
            edges += [scales[middle_row : middle_row + 1], scales[last_row : last_row + 1]]
        edge_out[source, 0 : 2 * blocks] = jnp.concatenate(edges, axis=0)
        fade_out[source] = scales[rows : 2 * rows].astype(jnp.bfloat16)
        b_part, c_part = (
            jnp.concatenate(
                [activated(r, lane) for r in range(0, rows, STRIP)], axis=0
            ).astype(jnp.bfloat16)
            for lane in (width, width + STATE)
        )
        c_out[source] = c_part
        scores = contract(c_part, b_part, ((1,), (1,)))
        scores = jnp.where(lower, scores, 0.0).astype(jnp.bfloat16)
        for lane in range(0, width, LANES):
            at = slice(lane, lane + LANES)
            for r in range(0, rows, STRIP):
                x_conv = activated(r, lane)
                x_ref[r : r + STRIP, at] = x_conv
                scaled_ref[r : r + STRIP, at] = (x_conv * scales[r : r + STRIP, at]).astype(
                    jnp.bfloat16
                )
        for b in range(blocks):
            at = slice(b * BLOCK, (b + 1) * BLOCK)
            added = contract(b_part[at], scaled_ref[at], ((0,), (0,)))
            state[source, b * STATE : (b + 1) * STATE] = added.astype(jnp.bfloat16)
        intra = contract(scores, scaled_ref[...], ((1,), (0,)))
        pre[source] = (intra * scales[rows : 2 * rows] + skip_ref[...] * x_ref[...]).astype(jnp.bfloat16)


def carry_kernel(width, whole_group, *refs):
    pre, state, c_part, fade, edge, gain_ref = refs[:6]
    outs, carry = refs[6:-1], refs[-1]
    rows = pre.shape[1]
    blocks = rows // BLOCK
    step = pl.program_id(0)

    @pl.when(step == 0)
    def _():
        carry[...] = jnp.zeros_like(carry)

    held = []
    for half in range(PAIR):
        source = step * PAIR + half
        for b in range(blocks):
            now = carry[...] * edge[source, 2 * b : 2 * b + 1]
            held.append(now.astype(jnp.bfloat16))
            added = state[source, b * STATE : (b + 1) * STATE].astype(jnp.float32)
            carry[...] = (now + added) * edge[source, 2 * b + 1 : 2 * b + 2]
    for half in range(PAIR):
        source = step * PAIR + half
        for b in range(blocks):
            at = slice(b * BLOCK, (b + 1) * BLOCK)
            to = slice(half * rows + b * BLOCK, half * rows + (b + 1) * BLOCK)
            inter = contract(c_part[source, at], held[half * blocks + b], ((1,), (0,)))
            total = pre[source, at].astype(jnp.float32) + inter * fade[source, at].astype(
                jnp.float32
            )
            power = total[:, :LANES] * total[:, :LANES]
            for lane in range(LANES, width, LANES):
                power = power + total[:, lane : lane + LANES] * total[:, lane : lane + LANES]
            if whole_group:
                summed = jnp.sum(power, axis=1, keepdims=True)
                norm = lax.rsqrt(summed * (1.0 / GROUP_WIDTH) + EPS)
                outs[0][to] = (total * norm * gain_ref[...]).astype(jnp.bfloat16)
            else:
                outs[0][to] = total
                outs[1][to] = power


def per_device(inputs, key_query, conv_inputs, conv_kq, step_size, decay_log, skip_gain, norm_gain):
    peers = lax.axis_size("ctx")
    me = lax.axis_index("ctx")
    rows = inputs.shape[0]
    width = HEADS * HEAD_DIM // peers
    heads = HEADS // peers
    span = GROUP_WIDTH // width
    whole_group = span == 1
    blocks = rows // BLOCK
    full = width + 2 * STATE
    scalar_rows = scalar_units(heads, rows, full)[-1][3] + SUBLANES
    scale_rows = rows + 16 * blocks
    cycle = jnp.arange(peers, dtype=jnp.int32)
    owners = lax.rem(me + cycle, peers)
    sources = lax.rem(me + peers - cycle, peers)

    smem = pl.BlockSpec(memory_space=pltpu.SMEM)
    hbm = pl.BlockSpec(memory_space=pltpu.HBM)
    vmem = pl.BlockSpec(memory_space=pltpu.VMEM)
    params = pltpu.CompilerParams(vmem_limit_bytes=VMEM_LIMIT)

    def columns(a, first, size):
        return lax.dynamic_slice_in_dim(a, first, size, axis=1)

    def pack(codes):
        shape = jax.ShapeDtypeStruct((rows + scalar_rows, full), jnp.bfloat16)
        return pl.pallas_call(
            functools.partial(pack_kernel, peers, span, width, heads, codes),
            in_specs=[smem] + [hbm] * 4,
            out_specs=[vmem] * len(codes),
            out_shape=[shape] * len(codes),
            scratch_shapes=[
                pltpu.VMEM((FIELDS, rows, HEADS), jnp.float32),
                pltpu.VMEM((FIELDS, peers, heads, rows), jnp.float32),
                pltpu.VMEM(key_query.shape, jnp.bfloat16),
                pltpu.SemaphoreType.DMA((2, max(3, len(codes)))),
            ],
            compiler_params=pltpu.CompilerParams(vmem_limit_bytes=PACK_VMEM),
            cost_estimate=pl.CostEstimate(
                flops=0, bytes_accessed=4 * len(codes) * rows * full, transcendentals=0
            ),
            name="pack",
        )(owners, inputs, key_query, decay_log, step_size)

    codes = [code for code in ORDER if code < peers]
    codes += [code for code in range(1, peers) if code not in codes]
    parts = dict(zip(codes[:WINDOW], pack(codes[:WINDOW])))
    parts.update(zip(codes[WINDOW:] + [0], pack(codes[WINDOW:] + [0])))
    for i, code in enumerate(codes):
        pairs = [(j, (j + code) % peers) for j in range(peers)]
        message = parts[code]
        if i >= WINDOW:
            message, _ = lax.optimization_barrier((message, parts[codes[i - WINDOW]]))
        parts[code] = lax.ppermute(message, "ctx", pairs)

    group = me // span
    taps = jnp.concatenate(
        [
            columns(conv_inputs, me * width, width),
            columns(conv_kq, group * STATE, STATE),
            columns(conv_kq, (GROUPS + group) * STATE, STATE),
        ],
        axis=1,
    )
    skip = jnp.repeat(lax.dynamic_slice_in_dim(skip_gain, me * heads, heads), HEAD_DIM)[None]
    gain = columns(norm_gain[None], me * width, width)

    shapes = [
        ((rows, width), jnp.bfloat16),
        ((blocks * STATE, width), jnp.bfloat16),
        ((rows, STATE), jnp.bfloat16),
        ((rows, width), jnp.bfloat16),
        ((2 * blocks, width), jnp.float32),
    ]
    arrived = {0}
    pending = list(range(peers))
    stores = []
    for code in codes:
        arrived.add(code)
        ready = [k for k in pending if {k, (k + 1) % peers} <= arrived]
        pending = [k for k in pending if k not in ready]
        if not ready:
            continue
        count = len(ready)
        operands = []
        for k in ready:
            operands += [parts[k], parts[(k + 1) % peers]]
        stores = pl.pallas_call(
            functools.partial(local_kernel, width, heads, count, bool(stores)),
            in_specs=[smem] + [vmem] * (2 * count + 2 + len(stores)),
            out_specs=[vmem] * len(shapes),
            out_shape=[jax.ShapeDtypeStruct((peers,) + shape, dtype) for shape, dtype in shapes],
            input_output_aliases={3 + 2 * count + i: i for i in range(len(stores))},
            scratch_shapes=[
                pltpu.VMEM((rows + HALO, full), jnp.bfloat16),
                pltpu.VMEM((rows, width), jnp.float32),
                pltpu.VMEM((rows, width), jnp.bfloat16),
                pltpu.VMEM((rows + scale_rows, width), jnp.float32),
            ],
            compiler_params=params,
            cost_estimate=pl.CostEstimate(
                flops=2 * rows * count * width * 450,
                bytes_accessed=count * rows * width * 10,
                transcendentals=count * rows * full,
            ),
            name="local",
        )(jnp.stack([sources[k] for k in ready]), *operands, taps, skip, *stores)

    out = [((rows, width), jnp.bfloat16 if whole_group else jnp.float32)]
    if not whole_group:
        out.append(((rows, LANES), jnp.float32))
    results = pl.pallas_call(
        functools.partial(carry_kernel, width, whole_group),
        grid=(peers // PAIR,),
        in_specs=[vmem] * (len(shapes) + 1),
        out_specs=[pl.BlockSpec((PAIR * shape[0], shape[1]), lambda i: (i, 0)) for shape, _ in out],
        out_shape=[
            jax.ShapeDtypeStruct((peers * shape[0], shape[1]), dtype) for shape, dtype in out
        ],
        scratch_shapes=[
            pltpu.VMEM((STATE, width), jnp.float32),
        ],
        compiler_params=params,
        cost_estimate=pl.CostEstimate(
            flops=2 * peers * rows * width * 150,
            bytes_accessed=peers * rows * width * 8,
            transcendentals=peers * rows,
        ),
        name="carry",
    )(*stores, gain)
    if whole_group:
        return results[0]
    total, power = results
    sharers = [list(range(i, i + span)) for i in range(0, peers, span)]
    summed = jnp.sum(power, axis=1, keepdims=True)
    summed = lax.psum(summed, "ctx", axis_index_groups=sharers)
    return (total * lax.rsqrt(summed * (1.0 / GROUP_WIDTH) + EPS) * gain).astype(jnp.bfloat16)


def solution(mesh):
    in_specs = (
        P(("dp", "ctx"), None),
        P(("dp", "ctx"), None),
        P(),
        P(),
        P(("dp", "ctx"), None),
        P(("dp", "ctx"), None),
        P(),
        P(),
    )
    out_specs = P("dp", "ctx")
    return jax.shard_map(
        per_device, mesh=mesh, in_specs=in_specs, out_specs=out_specs, check_vma=False
    )
```

```python
import functools

import jax
import jax.numpy as jnp
from jax import lax
from jax.experimental import pallas as pl
from jax.experimental.pallas import tpu as pltpu
from jax.sharding import PartitionSpec as P

HEADS = 128
HEAD_DIM = 64
STATE = 128
GROUPS = 8
KW = 4
BLOCK = 128
GROUP_WIDTH = HEADS * HEAD_DIM // GROUPS
EPS = 1e-05
HALO = 16
LANES = 128
SUBLANES = 8
FIELDS = 2
STRIP = 64
PAIR = 2
WINDOW = 5
ORDER = (1, 7, 4, 2, 6, 3, 5)
PACK_VMEM = 50 * 1024 * 1024
VMEM_LIMIT = 28 * 1024 * 1024


def contract(a, b, dims):
    return lax.dot_general(a, b, (dims, ((), ())), preferred_element_type=jnp.float32)


def as_parts(v, count):
    parts = []
    for _ in range(count):
        part = v.astype(jnp.bfloat16)
        parts.append(part)
        v = v - part.astype(jnp.float32)
    return parts


def scalar_units(heads, rows, cols):
    units = []
    for p in range(FIELDS):
        for head in range(0, heads, SUBLANES):
            line, column = divmod(len(units), cols // rows)
            units.append((p, head, min(SUBLANES, heads), line * SUBLANES, column * rows))
    return units


def pack_kernel(peers, span, width, heads, codes, *refs):
    owner_ref, x_ref, kq_ref, decay_ref, step_ref = refs[:5]
    outs = refs[5 : 5 + len(codes)]
    scalars, sems = refs[5 + len(codes) :]
    rows = x_ref.shape[0]
    copies = []
    owners = [owner_ref[code] for code in codes]
    for i, owner in enumerate(owners):
        column = pl.multiple_of(owner * width, LANES)
        copies.append(
            pltpu.make_async_copy(
                x_ref.at[:, pl.ds(column, width)], outs[i].at[0:rows, 0:width], sems.at[i]
            )
        )
    for copy in copies:
        copy.start()
    for p, ref in enumerate((decay_ref, step_ref)):
        field = ref[...].T
        for owner in range(peers):
            scalars[p, owner] = field[owner * heads : (owner + 1) * heads]
    for i, owner in enumerate(owners):
        outs[i][rows:] = jnp.zeros((outs[i].shape[0] - rows, outs[i].shape[1]), jnp.bfloat16)
        for p, head, count, top, left in scalar_units(heads, rows, width + 2 * STATE):
            outs[i][rows + top : rows + top + count, left : left + rows] = scalars[
                p, owner, head : head + count
            ].astype(jnp.bfloat16)
        for j in range(2):
            column = pl.multiple_of((j * GROUPS + owner // span) * STATE, LANES)
            left = width + j * STATE
            outs[i][0:rows, left : left + STATE] = kq_ref[:, pl.ds(column, STATE)]
    for copy in copies:
        copy.wait()


def spread(heads):
    head_of = lax.broadcasted_iota(jnp.int32, (2 * heads, heads * HEAD_DIM), 1) // HEAD_DIM
    row = lax.rem(lax.broadcasted_iota(jnp.int32, (2 * heads, heads * HEAD_DIM), 0), heads)
    return jnp.where(head_of == row, 1.0, 0.0).astype(jnp.bfloat16)


def local_kernel(width, heads, count, chained, *refs):
    source_ref = refs[0]
    parts = refs[1 : 1 + 2 * count]
    taps_ref, skip_ref = refs[1 + 2 * count : 3 + 2 * count]
    refs = refs[3 + 2 * count + (5 if chained else 0) :]
    pre, state, c_out, fade_out, edge_out = refs[:5]
    wide, x_ref, scaled_ref, scales = refs[5:]
    rows = x_ref.shape[0]
    blocks = rows // BLOCK
    full = width + 2 * STATE
    row = lax.broadcasted_iota(jnp.int32, (rows, rows), 0)
    col = lax.broadcasted_iota(jnp.int32, (rows, rows), 1)
    lower = (row >= col) & (row // BLOCK == col // BLOCK)
    ones = jnp.where(lower, 1.0, 0.0).astype(jnp.bfloat16)
    eye = jnp.where(row == col, 1.0, 0.0).astype(jnp.bfloat16)
    expand = spread(heads)

    for which in range(count):
        source = source_ref[which]
        part, earlier = parts[2 * which : 2 * which + 2]
        wide[HALO:] = part[0:rows, 0:full]
        edge = earlier[rows - HALO : rows, 0:full]
        wide[0:HALO] = jnp.where(source == 0, jnp.zeros_like(edge), edge)

        def activated(r, lane):
            tap = [taps_ref[k : k + 1, lane : lane + LANES] for k in range(KW)]
            now = wide[r : r + STRIP + HALO, lane : lane + LANES].astype(jnp.float32)
            now = now[HALO // 2 :]
            before = pltpu.roll(now, 1, 0)
            older = pltpu.roll(tap[0] * before + tap[1] * now, 2, 0)
            summed = (older + (tap[2] * before + tap[3] * now))[HALO // 2 :]
            return summed * pltpu.reciprocal(1.0 + jnp.exp(-summed), approx=True)

        def field(p):
            pieces = [
                part[rows + top : rows + top + size, left : left + rows].astype(jnp.float32)
                for q, _, size, top, left in scalar_units(heads, rows, full)
                if q == p
            ]
            return jnp.concatenate(pieces, axis=0).astype(jnp.bfloat16)

        cumul = contract(ones, field(0), ((1,), (1,)))
        steps = contract(eye, field(1), ((1,), (1,)))
        middles = [
            cumul[b * BLOCK + BLOCK // 2 - 1 : b * BLOCK + BLOCK // 2] for b in range(blocks)
        ]
        middle = jnp.concatenate([jnp.broadcast_to(m, (BLOCK, heads)) for m in middles], axis=0)
        inward = jnp.concatenate(as_parts(steps * jnp.exp(middle - cumul), 2), axis=1)
        outward = jnp.concatenate(
            as_parts(
                jnp.concatenate(
                    [jnp.exp(cumul - middle)]
                    + [jnp.broadcast_to(jnp.exp(m), (16, heads)) for m in middles],
                    axis=0,
                ),
                2,
            ),
            axis=1,
        )
        scales[...] = contract(
            jnp.concatenate([inward, outward], axis=0), expand, ((1,), (0,))
        )
        edges = []
        for b in range(blocks):
            last_row = rows + (b + 1) * BLOCK - 1
            middle_row = 2 * rows + 16 * b
            edges += [scales[middle_row : middle_row + 1], scales[last_row : last_row + 1]]
        edge_out[source, 0 : 2 * blocks] = jnp.concatenate(edges, axis=0)
        fade_out[source] = scales[rows : 2 * rows].astype(jnp.bfloat16)
        b_part, c_part = (
            jnp.concatenate(
                [activated(r, lane) for r in range(0, rows, STRIP)], axis=0
            ).astype(jnp.bfloat16)
            for lane in (width, width + STATE)
        )
        c_out[source] = c_part
        scores = contract(c_part, b_part, ((1,), (1,)))
        scores = jnp.where(lower, scores, 0.0).astype(jnp.bfloat16)
        for lane in range(0, width, LANES):
            at = slice(lane, lane + LANES)
            for r in range(0, rows, STRIP):
                x_conv = activated(r, lane)
                x_ref[r : r + STRIP, at] = x_conv
                scaled_ref[r : r + STRIP, at] = (x_conv * scales[r : r + STRIP, at]).astype(
                    jnp.bfloat16
                )
        for b in range(blocks):
            at = slice(b * BLOCK, (b + 1) * BLOCK)
            added = contract(b_part[at], scaled_ref[at], ((0,), (0,)))
            state[source, b * STATE : (b + 1) * STATE] = added.astype(jnp.bfloat16)
        intra = contract(scores, scaled_ref[...], ((1,), (0,)))
        pre[source] = (intra * scales[rows : 2 * rows] + skip_ref[...] * x_ref[...]).astype(jnp.bfloat16)


def carry_kernel(width, whole_group, *refs):
    pre, state, c_part, fade, edge, gain_ref = refs[:6]
    outs, carry = refs[6:-1], refs[-1]
    rows = pre.shape[1]
    blocks = rows // BLOCK
    step = pl.program_id(0)

    @pl.when(step == 0)
    def _():
        carry[...] = jnp.zeros_like(carry)

    held = []
    for half in range(PAIR):
        source = step * PAIR + half
        for b in range(blocks):
            now = carry[...] * edge[source, 2 * b : 2 * b + 1]
            held.append(now.astype(jnp.bfloat16))
            added = state[source, b * STATE : (b + 1) * STATE].astype(jnp.float32)
            carry[...] = (now + added) * edge[source, 2 * b + 1 : 2 * b + 2]
    for half in range(PAIR):
        source = step * PAIR + half
        for b in range(blocks):
            at = slice(b * BLOCK, (b + 1) * BLOCK)
            to = slice(half * rows + b * BLOCK, half * rows + (b + 1) * BLOCK)
            inter = contract(c_part[source, at], held[half * blocks + b], ((1,), (0,)))
            total = pre[source, at].astype(jnp.float32) + inter * fade[source, at].astype(
                jnp.float32
            )
            power = total[:, :LANES] * total[:, :LANES]
            for lane in range(LANES, width, LANES):
                power = power + total[:, lane : lane + LANES] * total[:, lane : lane + LANES]
            if whole_group:
                summed = jnp.sum(power, axis=1, keepdims=True)
                norm = lax.rsqrt(summed * (1.0 / GROUP_WIDTH) + EPS)
                outs[0][to] = (total * norm * gain_ref[...]).astype(jnp.bfloat16)
            else:
                outs[0][to] = total
                outs[1][to] = power


def per_device(inputs, key_query, conv_inputs, conv_kq, step_size, decay_log, skip_gain, norm_gain):
    peers = lax.axis_size("ctx")
    me = lax.axis_index("ctx")
    rows = inputs.shape[0]
    width = HEADS * HEAD_DIM // peers
    heads = HEADS // peers
    span = GROUP_WIDTH // width
    whole_group = span == 1
    blocks = rows // BLOCK
    full = width + 2 * STATE
    scalar_rows = scalar_units(heads, rows, full)[-1][3] + SUBLANES
    scale_rows = rows + 16 * blocks
    cycle = jnp.arange(peers, dtype=jnp.int32)
    owners = lax.rem(me + cycle, peers)
    sources = lax.rem(me + peers - cycle, peers)

    smem = pl.BlockSpec(memory_space=pltpu.SMEM)
    hbm = pl.BlockSpec(memory_space=pltpu.HBM)
    vmem = pl.BlockSpec(memory_space=pltpu.VMEM)
    params = pltpu.CompilerParams(vmem_limit_bytes=VMEM_LIMIT)

    def columns(a, first, size):
        return lax.dynamic_slice_in_dim(a, first, size, axis=1)

    def pack(codes):
        shape = jax.ShapeDtypeStruct((rows + scalar_rows, full), jnp.bfloat16)
        return pl.pallas_call(
            functools.partial(pack_kernel, peers, span, width, heads, codes),
            in_specs=[smem, hbm] + [vmem] * 3,
            out_specs=[vmem] * len(codes),
            out_shape=[shape] * len(codes),
            scratch_shapes=[
                pltpu.VMEM((FIELDS, peers, heads, rows), jnp.float32),
                pltpu.SemaphoreType.DMA((len(codes),)),
            ],
            compiler_params=pltpu.CompilerParams(vmem_limit_bytes=PACK_VMEM),
            cost_estimate=pl.CostEstimate(
                flops=0, bytes_accessed=4 * len(codes) * rows * full, transcendentals=0
            ),
            name="pack",
        )(owners, inputs, key_query, decay_log, step_size)

    codes = [code for code in ORDER if code < peers]
    codes += [code for code in range(1, peers) if code not in codes]
    parts = dict(zip(codes[:WINDOW], pack(codes[:WINDOW])))
    parts.update(zip(codes[WINDOW:] + [0], pack(codes[WINDOW:] + [0])))
    for i, code in enumerate(codes):
        pairs = [(j, (j + code) % peers) for j in range(peers)]
        message = parts[code]
        if i >= WINDOW:
            message, _ = lax.optimization_barrier((message, parts[codes[i - WINDOW]]))
        parts[code] = lax.ppermute(message, "ctx", pairs)

    group = me // span
    taps = jnp.concatenate(
        [
            columns(conv_inputs, me * width, width),
            columns(conv_kq, group * STATE, STATE),
            columns(conv_kq, (GROUPS + group) * STATE, STATE),
        ],
        axis=1,
    )
    skip = jnp.repeat(lax.dynamic_slice_in_dim(skip_gain, me * heads, heads), HEAD_DIM)[None]
    gain = columns(norm_gain[None], me * width, width)

    shapes = [
        ((rows, width), jnp.bfloat16),
        ((blocks * STATE, width), jnp.bfloat16),
        ((rows, STATE), jnp.bfloat16),
        ((rows, width), jnp.bfloat16),
        ((2 * blocks, width), jnp.float32),
    ]
    arrived = {0}
    pending = list(range(peers))
    stores = []
    for code in codes:
        arrived.add(code)
        ready = [k for k in pending if {k, (k + 1) % peers} <= arrived]
        pending = [k for k in pending if k not in ready]
        if not ready:
            continue
        count = len(ready)
        operands = []
        for k in ready:
            operands += [parts[k], parts[(k + 1) % peers]]
        stores = pl.pallas_call(
            functools.partial(local_kernel, width, heads, count, bool(stores)),
            in_specs=[smem] + [vmem] * (2 * count + 2 + len(stores)),
            out_specs=[vmem] * len(shapes),
            out_shape=[jax.ShapeDtypeStruct((peers,) + shape, dtype) for shape, dtype in shapes],
            input_output_aliases={3 + 2 * count + i: i for i in range(len(stores))},
            scratch_shapes=[
                pltpu.VMEM((rows + HALO, full), jnp.bfloat16),
                pltpu.VMEM((rows, width), jnp.float32),
                pltpu.VMEM((rows, width), jnp.bfloat16),
                pltpu.VMEM((rows + scale_rows, width), jnp.float32),
            ],
            compiler_params=params,
            cost_estimate=pl.CostEstimate(
                flops=2 * rows * count * width * 450,
                bytes_accessed=count * rows * width * 10,
                transcendentals=count * rows * full,
            ),
            name="local",
        )(jnp.stack([sources[k] for k in ready]), *operands, taps, skip, *stores)

    out = [((rows, width), jnp.bfloat16 if whole_group else jnp.float32)]
    if not whole_group:
        out.append(((rows, LANES), jnp.float32))
    results = pl.pallas_call(
        functools.partial(carry_kernel, width, whole_group),
        grid=(peers // PAIR,),
        in_specs=[vmem] * (len(shapes) + 1),
        out_specs=[pl.BlockSpec((PAIR * shape[0], shape[1]), lambda i: (i, 0)) for shape, _ in out],
        out_shape=[
            jax.ShapeDtypeStruct((peers * shape[0], shape[1]), dtype) for shape, dtype in out
        ],
        scratch_shapes=[
            pltpu.VMEM((STATE, width), jnp.float32),
        ],
        compiler_params=params,
        cost_estimate=pl.CostEstimate(
            flops=2 * peers * rows * width * 150,
            bytes_accessed=peers * rows * width * 8,
            transcendentals=peers * rows,
        ),
        name="carry",
    )(*stores, gain)
    if whole_group:
        return results[0]
    total, power = results
    sharers = [list(range(i, i + span)) for i in range(0, peers, span)]
    summed = jnp.sum(power, axis=1, keepdims=True)
    summed = lax.psum(summed, "ctx", axis_index_groups=sharers)
    return (total * lax.rsqrt(summed * (1.0 / GROUP_WIDTH) + EPS) * gain).astype(jnp.bfloat16)


def solution(mesh):
    in_specs = (
        P(("dp", "ctx"), None),
        P(("dp", "ctx"), None),
        P(),
        P(),
        P(("dp", "ctx"), None),
        P(("dp", "ctx"), None),
        P(),
        P(),
    )
    out_specs = P("dp", "ctx")
    return jax.shard_map(
        per_device, mesh=mesh, in_specs=in_specs, out_specs=out_specs, check_vma=False
    )
```

```python
import functools

import jax
import jax.numpy as jnp
from jax import lax
from jax.experimental import pallas as pl
from jax.experimental.pallas import tpu as pltpu
from jax.sharding import PartitionSpec as P

HEADS = 128
HEAD_DIM = 64
STATE = 128
GROUPS = 8
KW = 4
BLOCK = 128
GROUP_WIDTH = HEADS * HEAD_DIM // GROUPS
EPS = 1e-05
HALO = 16
LANES = 128
SUBLANES = 8
FIELDS = 2
STRIP = 64
PAIR = 2
WINDOW = 5
ORDER = (2, 6, 4, 3, 5, 1, 7)
ARRIVAL = (2, 6, 1, 7, 4, 3, 5)
PACK_VMEM = 58 * 1024 * 1024
VMEM_LIMIT = 28 * 1024 * 1024


def contract(a, b, dims):
    return lax.dot_general(a, b, (dims, ((), ())), preferred_element_type=jnp.float32)


def as_parts(v, count):
    parts = []
    for _ in range(count):
        part = v.astype(jnp.bfloat16)
        parts.append(part)
        v = v - part.astype(jnp.float32)
    return parts


def scalar_units(heads, rows, cols):
    units = []
    for p in range(FIELDS):
        for head in range(0, heads, SUBLANES):
            line, column = divmod(len(units), cols // rows)
            units.append((p, head, min(SUBLANES, heads), line * SUBLANES, column * rows))
    return units


def pack_kernel(peers, span, width, heads, codes, *refs):
    owner_ref, x_ref, kq_ref, decay_ref, step_ref = refs[:5]
    outs = refs[5 : 5 + len(codes)]
    raw_scalars, scalars, kq_near, sems = refs[5 + len(codes) :]
    rows = x_ref.shape[0]
    copies = [
        pltpu.make_async_copy(ref, dst, sems.at[1, i])
        for i, (ref, dst) in enumerate(
            ((decay_ref, raw_scalars.at[0]), (step_ref, raw_scalars.at[1]), (kq_ref, kq_near))
        )
    ]
    owners = [owner_ref[code] for code in codes]
    for i, owner in enumerate(owners):
        column = pl.multiple_of(owner * width, LANES)
        copies.append(
            pltpu.make_async_copy(
                x_ref.at[:, pl.ds(column, width)], outs[i].at[0:rows, 0:width], sems.at[0, i]
            )
        )
    for copy in copies:
        copy.start()
    for copy in copies[:3]:
        copy.wait()
    for p in range(FIELDS):
        field = raw_scalars[p].T
        for owner in range(peers):
            scalars[p, owner] = field[owner * heads : (owner + 1) * heads]
    for i, owner in enumerate(owners):
        outs[i][rows:] = jnp.zeros((outs[i].shape[0] - rows, outs[i].shape[1]), jnp.bfloat16)
        for p, head, count, top, left in scalar_units(heads, rows, width + 2 * STATE):
            outs[i][rows + top : rows + top + count, left : left + rows] = scalars[
                p, owner, head : head + count
            ].astype(jnp.bfloat16)
        for j in range(2):
            column = pl.multiple_of((j * GROUPS + owner // span) * STATE, LANES)
            left = width + j * STATE
            outs[i][0:rows, left : left + STATE] = kq_near[:, pl.ds(column, STATE)]
    for copy in copies[3:]:
        copy.wait()


def spread(heads):
    head_of = lax.broadcasted_iota(jnp.int32, (2 * heads, heads * HEAD_DIM), 1) // HEAD_DIM
    row = lax.rem(lax.broadcasted_iota(jnp.int32, (2 * heads, heads * HEAD_DIM), 0), heads)
    return jnp.where(head_of == row, 1.0, 0.0).astype(jnp.bfloat16)


def local_kernel(width, heads, count, chained, *refs):
    source_ref = refs[0]
    parts = refs[1 : 1 + 2 * count]
    taps_ref, skip_ref = refs[1 + 2 * count : 3 + 2 * count]
    refs = refs[3 + 2 * count + (5 if chained else 0) :]
    pre, state, c_out, fade_out, edge_out = refs[:5]
    wide, x_ref, scaled_ref, scales = refs[5:]
    rows = x_ref.shape[0]
    blocks = rows // BLOCK
    full = width + 2 * STATE
    row = lax.broadcasted_iota(jnp.int32, (rows, rows), 0)
    col = lax.broadcasted_iota(jnp.int32, (rows, rows), 1)
    lower = (row >= col) & (row // BLOCK == col // BLOCK)
    ones = jnp.where(lower, 1.0, 0.0).astype(jnp.bfloat16)
    eye = jnp.where(row == col, 1.0, 0.0).astype(jnp.bfloat16)
    expand = spread(heads)

    for which in range(count):
        source = source_ref[which]
        part, earlier = parts[2 * which : 2 * which + 2]
        wide[HALO:] = part[0:rows, 0:full]
        edge = earlier[rows - HALO : rows, 0:full]
        wide[0:HALO] = jnp.where(source == 0, jnp.zeros_like(edge), edge)

        def activated(r, lane):
            tap = [taps_ref[k : k + 1, lane : lane + LANES] for k in range(KW)]
            now = wide[r : r + STRIP + HALO, lane : lane + LANES].astype(jnp.float32)
            now = now[HALO // 2 :]
            before = pltpu.roll(now, 1, 0)
            older = pltpu.roll(tap[0] * before + tap[1] * now, 2, 0)
            summed = (older + (tap[2] * before + tap[3] * now))[HALO // 2 :]
            return summed * pltpu.reciprocal(1.0 + jnp.exp(-summed), approx=True)

        def field(p):
            pieces = [
                part[rows + top : rows + top + size, left : left + rows].astype(jnp.float32)
                for q, _, size, top, left in scalar_units(heads, rows, full)
                if q == p
            ]
            return jnp.concatenate(pieces, axis=0).astype(jnp.bfloat16)

        cumul = contract(ones, field(0), ((1,), (1,)))
        steps = contract(eye, field(1), ((1,), (1,)))
        middles = [
            cumul[b * BLOCK + BLOCK // 2 - 1 : b * BLOCK + BLOCK // 2] for b in range(blocks)
        ]
        middle = jnp.concatenate([jnp.broadcast_to(m, (BLOCK, heads)) for m in middles], axis=0)
        inward = jnp.concatenate(as_parts(steps * jnp.exp(middle - cumul), 2), axis=1)
        outward = jnp.concatenate(
            as_parts(
                jnp.concatenate(
                    [jnp.exp(cumul - middle)]
                    + [jnp.broadcast_to(jnp.exp(m), (16, heads)) for m in middles],
                    axis=0,
                ),
                2,
            ),
            axis=1,
        )
        scales[...] = contract(
            jnp.concatenate([inward, outward], axis=0), expand, ((1,), (0,))
        )
        edges = []
        for b in range(blocks):
            last_row = rows + (b + 1) * BLOCK - 1
            middle_row = 2 * rows + 16 * b
            edges += [scales[middle_row : middle_row + 1], scales[last_row : last_row + 1]]
        edge_out[source, 0 : 2 * blocks] = jnp.concatenate(edges, axis=0)
        fade_out[source] = scales[rows : 2 * rows].astype(jnp.bfloat16)
        b_part, c_part = (
            jnp.concatenate(
                [activated(r, lane) for r in range(0, rows, STRIP)], axis=0
            ).astype(jnp.bfloat16)
            for lane in (width, width + STATE)
        )
        c_out[source] = c_part
        scores = contract(c_part, b_part, ((1,), (1,)))
        scores = jnp.where(lower, scores, 0.0).astype(jnp.bfloat16)
        for lane in range(0, width, LANES):
            at = slice(lane, lane + LANES)
            for r in range(0, rows, STRIP):
                x_conv = activated(r, lane)
                x_ref[r : r + STRIP, at] = x_conv
                scaled_ref[r : r + STRIP, at] = (x_conv * scales[r : r + STRIP, at]).astype(
                    jnp.bfloat16
                )
        for b in range(blocks):
            at = slice(b * BLOCK, (b + 1) * BLOCK)
            added = contract(b_part[at], scaled_ref[at], ((0,), (0,)))
            state[source, b * STATE : (b + 1) * STATE] = added.astype(jnp.bfloat16)
        intra = contract(scores, scaled_ref[...], ((1,), (0,)))
        pre[source] = (intra * scales[rows : 2 * rows] + skip_ref[...] * x_ref[...]).astype(jnp.bfloat16)


def carry_kernel(width, whole_group, *refs):
    pre, state, c_part, fade, edge, gain_ref = refs[:6]
    outs, carry = refs[6:-1], refs[-1]
    rows = pre.shape[1]
    blocks = rows // BLOCK
    step = pl.program_id(0)

    @pl.when(step == 0)
    def _():
        carry[...] = jnp.zeros_like(carry)

    held = []
    for half in range(PAIR):
        source = step * PAIR + half
        for b in range(blocks):
            now = carry[...] * edge[source, 2 * b : 2 * b + 1]
            held.append(now.astype(jnp.bfloat16))
            added = state[source, b * STATE : (b + 1) * STATE].astype(jnp.float32)
            carry[...] = (now + added) * edge[source, 2 * b + 1 : 2 * b + 2]
    for half in range(PAIR):
        source = step * PAIR + half
        for b in range(blocks):
            at = slice(b * BLOCK, (b + 1) * BLOCK)
            to = slice(half * rows + b * BLOCK, half * rows + (b + 1) * BLOCK)
            inter = contract(c_part[source, at], held[half * blocks + b], ((1,), (0,)))
            total = pre[source, at].astype(jnp.float32) + inter * fade[source, at].astype(
                jnp.float32
            )
            power = total[:, :LANES] * total[:, :LANES]
            for lane in range(LANES, width, LANES):
                power = power + total[:, lane : lane + LANES] * total[:, lane : lane + LANES]
            if whole_group:
                summed = jnp.sum(power, axis=1, keepdims=True)
                norm = lax.rsqrt(summed * (1.0 / GROUP_WIDTH) + EPS)
                outs[0][to] = (total * norm * gain_ref[...]).astype(jnp.bfloat16)
            else:
                outs[0][to] = total
                outs[1][to] = power


def per_device(inputs, key_query, conv_inputs, conv_kq, step_size, decay_log, skip_gain, norm_gain):
    peers = lax.axis_size("ctx")
    me = lax.axis_index("ctx")
    rows = inputs.shape[0]
    width = HEADS * HEAD_DIM // peers
    heads = HEADS // peers
    span = GROUP_WIDTH // width
    whole_group = span == 1
    blocks = rows // BLOCK
    full = width + 2 * STATE
    scalar_rows = scalar_units(heads, rows, full)[-1][3] + SUBLANES
    scale_rows = rows + 16 * blocks
    cycle = jnp.arange(peers, dtype=jnp.int32)
    owners = lax.rem(me + cycle, peers)
    sources = lax.rem(me + peers - cycle, peers)

    smem = pl.BlockSpec(memory_space=pltpu.SMEM)
    hbm = pl.BlockSpec(memory_space=pltpu.HBM)
    vmem = pl.BlockSpec(memory_space=pltpu.VMEM)
    params = pltpu.CompilerParams(vmem_limit_bytes=VMEM_LIMIT)

    def columns(a, first, size):
        return lax.dynamic_slice_in_dim(a, first, size, axis=1)

    def pack(codes):
        shape = jax.ShapeDtypeStruct((rows + scalar_rows, full), jnp.bfloat16)
        return pl.pallas_call(
            functools.partial(pack_kernel, peers, span, width, heads, codes),
            in_specs=[smem] + [hbm] * 4,
            out_specs=[vmem] * len(codes),
            out_shape=[shape] * len(codes),
            scratch_shapes=[
                pltpu.VMEM((FIELDS, rows, HEADS), jnp.float32),
                pltpu.VMEM((FIELDS, peers, heads, rows), jnp.float32),
                pltpu.VMEM(key_query.shape, jnp.bfloat16),
                pltpu.SemaphoreType.DMA((2, max(3, len(codes)))),
            ],
            compiler_params=pltpu.CompilerParams(vmem_limit_bytes=PACK_VMEM),
            cost_estimate=pl.CostEstimate(
                flops=0, bytes_accessed=4 * len(codes) * rows * full, transcendentals=0
            ),
            name="pack",
        )(owners, inputs, key_query, decay_log, step_size)

    codes = [code for code in ORDER if code < peers]
    codes += [code for code in range(1, peers) if code not in codes]
    parts = dict(zip(codes[:WINDOW], pack(codes[:WINDOW])))
    parts.update(zip(codes[WINDOW:] + [0], pack(codes[WINDOW:] + [0])))
    for i, code in enumerate(codes):
        pairs = [(j, (j + code) % peers) for j in range(peers)]
        message = parts[code]
        if i >= WINDOW:
            message, _ = lax.optimization_barrier((message, parts[codes[i - WINDOW]]))
        parts[code] = lax.ppermute(message, "ctx", pairs)

    group = me // span
    taps = jnp.concatenate(
        [
            columns(conv_inputs, me * width, width),
            columns(conv_kq, group * STATE, STATE),
            columns(conv_kq, (GROUPS + group) * STATE, STATE),
        ],
        axis=1,
    )
    skip = jnp.repeat(lax.dynamic_slice_in_dim(skip_gain, me * heads, heads), HEAD_DIM)[None]
    gain = columns(norm_gain[None], me * width, width)

    shapes = [
        ((rows, width), jnp.bfloat16),
        ((blocks * STATE, width), jnp.bfloat16),
        ((rows, STATE), jnp.bfloat16),
        ((rows, width), jnp.bfloat16),
        ((2 * blocks, width), jnp.float32),
    ]
    codes_after = tuple(code for code in codes if code not in ARRIVAL)
    arrived = {0}
    pending = list(range(peers))
    stores = []
    for code in sorted(codes, key=lambda code: (ARRIVAL + codes_after).index(code)):
        arrived.add(code)
        ready = [k for k in pending if {k, (k + 1) % peers} <= arrived]
        pending = [k for k in pending if k not in ready]
        if not ready:
            continue
        count = len(ready)
        operands = []
        for k in ready:
            operands += [parts[k], parts[(k + 1) % peers]]
        stores = pl.pallas_call(
            functools.partial(local_kernel, width, heads, count, bool(stores)),
            in_specs=[smem] + [vmem] * (2 * count + 2 + len(stores)),
            out_specs=[vmem] * len(shapes),
            out_shape=[jax.ShapeDtypeStruct((peers,) + shape, dtype) for shape, dtype in shapes],
            input_output_aliases={3 + 2 * count + i: i for i in range(len(stores))},
            scratch_shapes=[
                pltpu.VMEM((rows + HALO, full), jnp.bfloat16),
                pltpu.VMEM((rows, width), jnp.float32),
                pltpu.VMEM((rows, width), jnp.bfloat16),
                pltpu.VMEM((rows + scale_rows, width), jnp.float32),
            ],
            compiler_params=params,
            cost_estimate=pl.CostEstimate(
                flops=2 * rows * count * width * 450,
                bytes_accessed=count * rows * width * 10,
                transcendentals=count * rows * full,
            ),
            name="local",
        )(jnp.stack([sources[k] for k in ready]), *operands, taps, skip, *stores)

    out = [((rows, width), jnp.bfloat16 if whole_group else jnp.float32)]
    if not whole_group:
        out.append(((rows, LANES), jnp.float32))
    results = pl.pallas_call(
        functools.partial(carry_kernel, width, whole_group),
        grid=(peers // PAIR,),
        in_specs=[vmem] * (len(shapes) + 1),
        out_specs=[pl.BlockSpec((PAIR * shape[0], shape[1]), lambda i: (i, 0)) for shape, _ in out],
        out_shape=[
            jax.ShapeDtypeStruct((peers * shape[0], shape[1]), dtype) for shape, dtype in out
        ],
        scratch_shapes=[
            pltpu.VMEM((STATE, width), jnp.float32),
        ],
        compiler_params=params,
        cost_estimate=pl.CostEstimate(
            flops=2 * peers * rows * width * 150,
            bytes_accessed=peers * rows * width * 8,
            transcendentals=peers * rows,
        ),
        name="carry",
    )(*stores, gain)
    if whole_group:
        return results[0]
    total, power = results
    sharers = [list(range(i, i + span)) for i in range(0, peers, span)]
    summed = jnp.sum(power, axis=1, keepdims=True)
    summed = lax.psum(summed, "ctx", axis_index_groups=sharers)
    return (total * lax.rsqrt(summed * (1.0 / GROUP_WIDTH) + EPS) * gain).astype(jnp.bfloat16)


def solution(mesh):
    in_specs = (
        P(("dp", "ctx"), None),
        P(("dp", "ctx"), None),
        P(),
        P(),
        P(("dp", "ctx"), None),
        P(("dp", "ctx"), None),
        P(),
        P(),
    )
    out_specs = P("dp", "ctx")
    return jax.shard_map(
        per_device, mesh=mesh, in_specs=in_specs, out_specs=out_specs, check_vma=False
    )
```

```python
import functools

import jax
import jax.numpy as jnp
from jax import lax
from jax.experimental import pallas as pl
from jax.experimental.pallas import tpu as pltpu
from jax.sharding import PartitionSpec as P

HEADS = 128
HEAD_DIM = 64
STATE = 128
GROUPS = 8
KW = 4
BLOCK = 128
GROUP_WIDTH = HEADS * HEAD_DIM // GROUPS
EPS = 1e-05
HALO = 16
LANES = 128
SUBLANES = 8
FIELDS = 2
STRIP = 64
PAIR = 2
WINDOW = 5
ORDER = (1, 7, 4, 3, 5, 2, 6)
ARRIVAL = (1, 7, 2, 6, 4, 3, 5)
PACK_VMEM = 58 * 1024 * 1024
VMEM_LIMIT = 28 * 1024 * 1024


def contract(a, b, dims):
    return lax.dot_general(a, b, (dims, ((), ())), preferred_element_type=jnp.float32)


def as_parts(v, count):
    parts = []
    for _ in range(count):
        part = v.astype(jnp.bfloat16)
        parts.append(part)
        v = v - part.astype(jnp.float32)
    return parts


def scalar_units(heads, rows, cols):
    units = []
    for p in range(FIELDS):
        for head in range(0, heads, SUBLANES):
            line, column = divmod(len(units), cols // rows)
            units.append((p, head, min(SUBLANES, heads), line * SUBLANES, column * rows))
    return units


def pack_kernel(peers, span, width, heads, codes, *refs):
    owner_ref, x_ref, kq_ref, decay_ref, step_ref = refs[:5]
    outs = refs[5 : 5 + len(codes)]
    raw_scalars, scalars, kq_near, sems = refs[5 + len(codes) :]
    rows = x_ref.shape[0]
    copies = [
        pltpu.make_async_copy(ref, dst, sems.at[1, i])
        for i, (ref, dst) in enumerate(
            ((decay_ref, raw_scalars.at[0]), (step_ref, raw_scalars.at[1]), (kq_ref, kq_near))
        )
    ]
    owners = [owner_ref[code] for code in codes]
    for i, owner in enumerate(owners):
        column = pl.multiple_of(owner * width, LANES)
        copies.append(
            pltpu.make_async_copy(
                x_ref.at[:, pl.ds(column, width)], outs[i].at[0:rows, 0:width], sems.at[0, i]
            )
        )
    for copy in copies:
        copy.start()
    for copy in copies[:3]:
        copy.wait()
    for p in range(FIELDS):
        field = raw_scalars[p].T
        for owner in range(peers):
            scalars[p, owner] = field[owner * heads : (owner + 1) * heads]
    for i, owner in enumerate(owners):
        outs[i][rows:] = jnp.zeros((outs[i].shape[0] - rows, outs[i].shape[1]), jnp.bfloat16)
        for p, head, count, top, left in scalar_units(heads, rows, width + 2 * STATE):
            outs[i][rows + top : rows + top + count, left : left + rows] = scalars[
                p, owner, head : head + count
            ].astype(jnp.bfloat16)
        for j in range(2):
            column = pl.multiple_of((j * GROUPS + owner // span) * STATE, LANES)
            left = width + j * STATE
            outs[i][0:rows, left : left + STATE] = kq_near[:, pl.ds(column, STATE)]
    for copy in copies[3:]:
        copy.wait()


def spread(heads):
    head_of = lax.broadcasted_iota(jnp.int32, (2 * heads, heads * HEAD_DIM), 1) // HEAD_DIM
    row = lax.rem(lax.broadcasted_iota(jnp.int32, (2 * heads, heads * HEAD_DIM), 0), heads)
    return jnp.where(head_of == row, 1.0, 0.0).astype(jnp.bfloat16)


def local_kernel(width, heads, count, chained, *refs):
    source_ref = refs[0]
    parts = refs[1 : 1 + 2 * count]
    taps_ref, skip_ref = refs[1 + 2 * count : 3 + 2 * count]
    refs = refs[3 + 2 * count + (5 if chained else 0) :]
    pre, state, c_out, fade_out, edge_out = refs[:5]
    wide, x_ref, scaled_ref, scales = refs[5:]
    rows = x_ref.shape[0]
    blocks = rows // BLOCK
    full = width + 2 * STATE
    row = lax.broadcasted_iota(jnp.int32, (rows, rows), 0)
    col = lax.broadcasted_iota(jnp.int32, (rows, rows), 1)
    lower = (row >= col) & (row // BLOCK == col // BLOCK)
    ones = jnp.where(lower, 1.0, 0.0).astype(jnp.bfloat16)
    eye = jnp.where(row == col, 1.0, 0.0).astype(jnp.bfloat16)
    expand = spread(heads)

    for which in range(count):
        source = source_ref[which]
        part, earlier = parts[2 * which : 2 * which + 2]
        wide[HALO:] = part[0:rows, 0:full]
        edge = earlier[rows - HALO : rows, 0:full]
        wide[0:HALO] = jnp.where(source == 0, jnp.zeros_like(edge), edge)

        def activated(r, lane):
            tap = [taps_ref[k : k + 1, lane : lane + LANES] for k in range(KW)]
            now = wide[r : r + STRIP + HALO, lane : lane + LANES].astype(jnp.float32)
            now = now[HALO // 2 :]
            before = pltpu.roll(now, 1, 0)
            older = pltpu.roll(tap[0] * before + tap[1] * now, 2, 0)
            summed = (older + (tap[2] * before + tap[3] * now))[HALO // 2 :]
            return summed * pltpu.reciprocal(1.0 + jnp.exp(-summed), approx=True)

        def field(p):
            pieces = [
                part[rows + top : rows + top + size, left : left + rows].astype(jnp.float32)
                for q, _, size, top, left in scalar_units(heads, rows, full)
                if q == p
            ]
            return jnp.concatenate(pieces, axis=0).astype(jnp.bfloat16)

        cumul = contract(ones, field(0), ((1,), (1,)))
        steps = contract(eye, field(1), ((1,), (1,)))
        middles = [
            cumul[b * BLOCK + BLOCK // 2 - 1 : b * BLOCK + BLOCK // 2] for b in range(blocks)
        ]
        middle = jnp.concatenate([jnp.broadcast_to(m, (BLOCK, heads)) for m in middles], axis=0)
        inward = jnp.concatenate(as_parts(steps * jnp.exp(middle - cumul), 2), axis=1)
        outward = jnp.concatenate(
            as_parts(
                jnp.concatenate(
                    [jnp.exp(cumul - middle)]
                    + [jnp.broadcast_to(jnp.exp(m), (16, heads)) for m in middles],
                    axis=0,
                ),
                2,
            ),
            axis=1,
        )
        scales[...] = contract(
            jnp.concatenate([inward, outward], axis=0), expand, ((1,), (0,))
        )
        edges = []
        for b in range(blocks):
            last_row = rows + (b + 1) * BLOCK - 1
            middle_row = 2 * rows + 16 * b
            edges += [scales[middle_row : middle_row + 1], scales[last_row : last_row + 1]]
        edge_out[source, 0 : 2 * blocks] = jnp.concatenate(edges, axis=0)
        fade_out[source] = scales[rows : 2 * rows].astype(jnp.bfloat16)
        b_part, c_part = (
            jnp.concatenate(
                [activated(r, lane) for r in range(0, rows, STRIP)], axis=0
            ).astype(jnp.bfloat16)
            for lane in (width, width + STATE)
        )
        c_out[source] = c_part
        scores = contract(c_part, b_part, ((1,), (1,)))
        scores = jnp.where(lower, scores, 0.0).astype(jnp.bfloat16)
        for lane in range(0, width, LANES):
            at = slice(lane, lane + LANES)
            for r in range(0, rows, STRIP):
                x_conv = activated(r, lane)
                x_ref[r : r + STRIP, at] = x_conv
                scaled_ref[r : r + STRIP, at] = (x_conv * scales[r : r + STRIP, at]).astype(
                    jnp.bfloat16
                )
        for b in range(blocks):
            at = slice(b * BLOCK, (b + 1) * BLOCK)
            added = contract(b_part[at], scaled_ref[at], ((0,), (0,)))
            state[source, b * STATE : (b + 1) * STATE] = added.astype(jnp.bfloat16)
        intra = contract(scores, scaled_ref[...], ((1,), (0,)))
        pre[source] = (intra * scales[rows : 2 * rows] + skip_ref[...] * x_ref[...]).astype(jnp.bfloat16)


def carry_kernel(width, whole_group, *refs):
    pre, state, c_part, fade, edge, gain_ref = refs[:6]
    outs, carry = refs[6:-1], refs[-1]
    rows = pre.shape[1]
    blocks = rows // BLOCK
    step = pl.program_id(0)

    @pl.when(step == 0)
    def _():
        carry[...] = jnp.zeros_like(carry)

    held = []
    for half in range(PAIR):
        source = step * PAIR + half
        for b in range(blocks):
            now = carry[...] * edge[source, 2 * b : 2 * b + 1]
            held.append(now.astype(jnp.bfloat16))
            added = state[source, b * STATE : (b + 1) * STATE].astype(jnp.float32)
            carry[...] = (now + added) * edge[source, 2 * b + 1 : 2 * b + 2]
    for half in range(PAIR):
        source = step * PAIR + half
        for b in range(blocks):
            at = slice(b * BLOCK, (b + 1) * BLOCK)
            to = slice(half * rows + b * BLOCK, half * rows + (b + 1) * BLOCK)
            inter = contract(c_part[source, at], held[half * blocks + b], ((1,), (0,)))
            total = pre[source, at].astype(jnp.float32) + inter * fade[source, at].astype(
                jnp.float32
            )
            power = total[:, :LANES] * total[:, :LANES]
            for lane in range(LANES, width, LANES):
                power = power + total[:, lane : lane + LANES] * total[:, lane : lane + LANES]
            if whole_group:
                summed = jnp.sum(power, axis=1, keepdims=True)
                norm = lax.rsqrt(summed * (1.0 / GROUP_WIDTH) + EPS)
                outs[0][to] = (total * norm * gain_ref[...]).astype(jnp.bfloat16)
            else:
                outs[0][to] = total
                outs[1][to] = power


def per_device(inputs, key_query, conv_inputs, conv_kq, step_size, decay_log, skip_gain, norm_gain):
    peers = lax.axis_size("ctx")
    me = lax.axis_index("ctx")
    rows = inputs.shape[0]
    width = HEADS * HEAD_DIM // peers
    heads = HEADS // peers
    span = GROUP_WIDTH // width
    whole_group = span == 1
    blocks = rows // BLOCK
    full = width + 2 * STATE
    scalar_rows = scalar_units(heads, rows, full)[-1][3] + SUBLANES
    scale_rows = rows + 16 * blocks
    cycle = jnp.arange(peers, dtype=jnp.int32)
    owners = lax.rem(me + cycle, peers)
    sources = lax.rem(me + peers - cycle, peers)

    smem = pl.BlockSpec(memory_space=pltpu.SMEM)
    hbm = pl.BlockSpec(memory_space=pltpu.HBM)
    vmem = pl.BlockSpec(memory_space=pltpu.VMEM)
    params = pltpu.CompilerParams(vmem_limit_bytes=VMEM_LIMIT)

    def columns(a, first, size):
        return lax.dynamic_slice_in_dim(a, first, size, axis=1)

    def pack(codes):
        shape = jax.ShapeDtypeStruct((rows + scalar_rows, full), jnp.bfloat16)
        return pl.pallas_call(
            functools.partial(pack_kernel, peers, span, width, heads, codes),
            in_specs=[smem] + [hbm] * 4,
            out_specs=[vmem] * len(codes),
            out_shape=[shape] * len(codes),
            scratch_shapes=[
                pltpu.VMEM((FIELDS, rows, HEADS), jnp.float32),
                pltpu.VMEM((FIELDS, peers, heads, rows), jnp.float32),
                pltpu.VMEM(key_query.shape, jnp.bfloat16),
                pltpu.SemaphoreType.DMA((2, max(3, len(codes)))),
            ],
            compiler_params=pltpu.CompilerParams(vmem_limit_bytes=PACK_VMEM),
            cost_estimate=pl.CostEstimate(
                flops=0, bytes_accessed=4 * len(codes) * rows * full, transcendentals=0
            ),
            name="pack",
        )(owners, inputs, key_query, decay_log, step_size)

    codes = [code for code in ORDER if code < peers]
    codes += [code for code in range(1, peers) if code not in codes]
    parts = dict(zip(codes[:WINDOW], pack(codes[:WINDOW])))
    parts.update(zip(codes[WINDOW:] + [0], pack(codes[WINDOW:] + [0])))
    for i, code in enumerate(codes):
        pairs = [(j, (j + code) % peers) for j in range(peers)]
        message = parts[code]
        if i >= WINDOW:
            message, _ = lax.optimization_barrier((message, parts[codes[i - WINDOW]]))
        parts[code] = lax.ppermute(message, "ctx", pairs)

    group = me // span
    taps = jnp.concatenate(
        [
            columns(conv_inputs, me * width, width),
            columns(conv_kq, group * STATE, STATE),
            columns(conv_kq, (GROUPS + group) * STATE, STATE),
        ],
        axis=1,
    )
    skip = jnp.repeat(lax.dynamic_slice_in_dim(skip_gain, me * heads, heads), HEAD_DIM)[None]
    gain = columns(norm_gain[None], me * width, width)

    shapes = [
        ((rows, width), jnp.bfloat16),
        ((blocks * STATE, width), jnp.bfloat16),
        ((rows, STATE), jnp.bfloat16),
        ((rows, width), jnp.bfloat16),
        ((2 * blocks, width), jnp.float32),
    ]
    codes_after = tuple(code for code in codes if code not in ARRIVAL)
    arrived = {0}
    pending = list(range(peers))
    stores = []
    for code in sorted(codes, key=lambda code: (ARRIVAL + codes_after).index(code)):
        arrived.add(code)
        ready = [k for k in pending if {k, (k + 1) % peers} <= arrived]
        pending = [k for k in pending if k not in ready]
        if not ready:
            continue
        count = len(ready)
        operands = []
        for k in ready:
            operands += [parts[k], parts[(k + 1) % peers]]
        stores = pl.pallas_call(
            functools.partial(local_kernel, width, heads, count, bool(stores)),
            in_specs=[smem] + [vmem] * (2 * count + 2 + len(stores)),
            out_specs=[vmem] * len(shapes),
            out_shape=[jax.ShapeDtypeStruct((peers,) + shape, dtype) for shape, dtype in shapes],
            input_output_aliases={3 + 2 * count + i: i for i in range(len(stores))},
            scratch_shapes=[
                pltpu.VMEM((rows + HALO, full), jnp.bfloat16),
                pltpu.VMEM((rows, width), jnp.float32),
                pltpu.VMEM((rows, width), jnp.bfloat16),
                pltpu.VMEM((rows + scale_rows, width), jnp.float32),
            ],
            compiler_params=params,
            cost_estimate=pl.CostEstimate(
                flops=2 * rows * count * width * 450,
                bytes_accessed=count * rows * width * 10,
                transcendentals=count * rows * full,
            ),
            name="local",
        )(jnp.stack([sources[k] for k in ready]), *operands, taps, skip, *stores)

    out = [((rows, width), jnp.bfloat16 if whole_group else jnp.float32)]
    if not whole_group:
        out.append(((rows, LANES), jnp.float32))
    results = pl.pallas_call(
        functools.partial(carry_kernel, width, whole_group),
        grid=(peers // PAIR,),
        in_specs=[vmem] * (len(shapes) + 1),
        out_specs=[pl.BlockSpec((PAIR * shape[0], shape[1]), lambda i: (i, 0)) for shape, _ in out],
        out_shape=[
            jax.ShapeDtypeStruct((peers * shape[0], shape[1]), dtype) for shape, dtype in out
        ],
        scratch_shapes=[
            pltpu.VMEM((STATE, width), jnp.float32),
        ],
        compiler_params=params,
        cost_estimate=pl.CostEstimate(
            flops=2 * peers * rows * width * 150,
            bytes_accessed=peers * rows * width * 8,
            transcendentals=peers * rows,
        ),
        name="carry",
    )(*stores, gain)
    if whole_group:
        return results[0]
    total, power = results
    sharers = [list(range(i, i + span)) for i in range(0, peers, span)]
    summed = jnp.sum(power, axis=1, keepdims=True)
    summed = lax.psum(summed, "ctx", axis_index_groups=sharers)
    return (total * lax.rsqrt(summed * (1.0 / GROUP_WIDTH) + EPS) * gain).astype(jnp.bfloat16)


def solution(mesh):
    in_specs = (
        P(("dp", "ctx"), None),
        P(("dp", "ctx"), None),
        P(),
        P(),
        P(("dp", "ctx"), None),
        P(("dp", "ctx"), None),
        P(),
        P(),
    )
    out_specs = P("dp", "ctx")
    return jax.shard_map(
        per_device, mesh=mesh, in_specs=in_specs, out_specs=out_specs, check_vma=False
    )
```

```python
import functools

import jax
import jax.numpy as jnp
from jax import lax
from jax.experimental import pallas as pl
from jax.experimental.pallas import tpu as pltpu
from jax.sharding import PartitionSpec as P

HEADS = 128
HEAD_DIM = 64
STATE = 128
GROUPS = 8
KW = 4
BLOCK = 128
GROUP_WIDTH = HEADS * HEAD_DIM // GROUPS
EPS = 1e-05
HALO = 16
LANES = 128
SUBLANES = 8
FIELDS = 2
STRIP = 64
PAIR = 2
PACK_VMEM = 58 * 1024 * 1024
VMEM_LIMIT = 28 * 1024 * 1024


def contract(a, b, dims):
    return lax.dot_general(a, b, (dims, ((), ())), preferred_element_type=jnp.float32)


def as_parts(v, count):
    parts = []
    for _ in range(count):
        part = v.astype(jnp.bfloat16)
        parts.append(part)
        v = v - part.astype(jnp.float32)
    return parts


def scalar_units(heads, rows, cols):
    units = []
    for p in range(FIELDS):
        for head in range(0, heads, SUBLANES):
            line, column = divmod(len(units), cols // rows)
            units.append((p, head, min(SUBLANES, heads), line * SUBLANES, column * rows))
    return units


def pack_kernel(peers, span, width, heads, codes, *refs):
    owner_ref, x_ref, kq_ref, decay_ref, step_ref = refs[:5]
    outs = refs[5 : 5 + len(codes)]
    raw_scalars, scalars, kq_near, sems = refs[5 + len(codes) :]
    rows = x_ref.shape[0]
    copies = [
        pltpu.make_async_copy(ref, dst, sems.at[1, i])
        for i, (ref, dst) in enumerate(
            ((decay_ref, raw_scalars.at[0]), (step_ref, raw_scalars.at[1]), (kq_ref, kq_near))
        )
    ]
    owners = [owner_ref[code] for code in codes]
    for i, owner in enumerate(owners):
        column = pl.multiple_of(owner * width, LANES)
        copies.append(
            pltpu.make_async_copy(
                x_ref.at[:, pl.ds(column, width)], outs[i].at[0:rows, 0:width], sems.at[0, i]
            )
        )
    for copy in copies:
        copy.start()
    for copy in copies[:3]:
        copy.wait()
    for p in range(FIELDS):
        field = raw_scalars[p].T
        for owner in range(peers):
            scalars[p, owner] = field[owner * heads : (owner + 1) * heads]
    for i, owner in enumerate(owners):
        outs[i][rows:] = jnp.zeros((outs[i].shape[0] - rows, outs[i].shape[1]), jnp.bfloat16)
        for p, head, count, top, left in scalar_units(heads, rows, width + 2 * STATE):
            outs[i][rows + top : rows + top + count, left : left + rows] = scalars[
                p, owner, head : head + count
            ].astype(jnp.bfloat16)
        for j in range(2):
            column = pl.multiple_of((j * GROUPS + owner // span) * STATE, LANES)
            left = width + j * STATE
            outs[i][0:rows, left : left + STATE] = kq_near[:, pl.ds(column, STATE)]
    for copy in copies[3:]:
        copy.wait()


def spread(heads):
    head_of = lax.broadcasted_iota(jnp.int32, (2 * heads, heads * HEAD_DIM), 1) // HEAD_DIM
    row = lax.rem(lax.broadcasted_iota(jnp.int32, (2 * heads, heads * HEAD_DIM), 0), heads)
    return jnp.where(head_of == row, 1.0, 0.0).astype(jnp.bfloat16)


def local_kernel(width, heads, count, chained, *refs):
    source_ref = refs[0]
    parts = refs[1 : 1 + 2 * count]
    taps_ref, skip_ref = refs[1 + 2 * count : 3 + 2 * count]
    refs = refs[3 + 2 * count + (5 if chained else 0) :]
    pre, state, c_out, fade_out, edge_out = refs[:5]
    wide, x_ref, scaled_ref, scales = refs[5:]
    rows = x_ref.shape[0]
    blocks = rows // BLOCK
    full = width + 2 * STATE
    row = lax.broadcasted_iota(jnp.int32, (rows, rows), 0)
    col = lax.broadcasted_iota(jnp.int32, (rows, rows), 1)
    lower = (row >= col) & (row // BLOCK == col // BLOCK)
    ones = jnp.where(lower, 1.0, 0.0).astype(jnp.bfloat16)
    eye = jnp.where(row == col, 1.0, 0.0).astype(jnp.bfloat16)
    expand = spread(heads)

    for which in range(count):
        source = source_ref[which]
        part, earlier = parts[2 * which : 2 * which + 2]
        wide[HALO:] = part[0:rows, 0:full]
        edge = earlier[rows - HALO : rows, 0:full]
        wide[0:HALO] = jnp.where(source == 0, jnp.zeros_like(edge), edge)

        def activated(r, lane):
            tap = [taps_ref[k : k + 1, lane : lane + LANES] for k in range(KW)]
            now = wide[r : r + STRIP + HALO, lane : lane + LANES].astype(jnp.float32)
            now = now[HALO // 2 :]
            before = pltpu.roll(now, 1, 0)
            older = pltpu.roll(tap[0] * before + tap[1] * now, 2, 0)
            summed = (older + (tap[2] * before + tap[3] * now))[HALO // 2 :]
            return summed * pltpu.reciprocal(1.0 + jnp.exp(-summed), approx=True)

        def field(p):
            pieces = [
                part[rows + top : rows + top + size, left : left + rows].astype(jnp.float32)
                for q, _, size, top, left in scalar_units(heads, rows, full)
                if q == p
            ]
            return jnp.concatenate(pieces, axis=0).astype(jnp.bfloat16)

        cumul = contract(ones, field(0), ((1,), (1,)))
        steps = contract(eye, field(1), ((1,), (1,)))
        middles = [
            cumul[b * BLOCK + BLOCK // 2 - 1 : b * BLOCK + BLOCK // 2] for b in range(blocks)
        ]
        middle = jnp.concatenate([jnp.broadcast_to(m, (BLOCK, heads)) for m in middles], axis=0)
        inward = jnp.concatenate(as_parts(steps * jnp.exp(middle - cumul), 2), axis=1)
        outward = jnp.concatenate(
            as_parts(
                jnp.concatenate(
                    [jnp.exp(cumul - middle)]
                    + [jnp.broadcast_to(jnp.exp(m), (16, heads)) for m in middles],
                    axis=0,
                ),
                2,
            ),
            axis=1,
        )
        scales[...] = contract(
            jnp.concatenate([inward, outward], axis=0), expand, ((1,), (0,))
        )
        edges = []
        for b in range(blocks):
            last_row = rows + (b + 1) * BLOCK - 1
            middle_row = 2 * rows + 16 * b
            edges += [scales[middle_row : middle_row + 1], scales[last_row : last_row + 1]]
        edge_out[source, 0 : 2 * blocks] = jnp.concatenate(edges, axis=0)
        fade_out[source] = scales[rows : 2 * rows].astype(jnp.bfloat16)
        b_part, c_part = (
            jnp.concatenate(
                [activated(r, lane) for r in range(0, rows, STRIP)], axis=0
            ).astype(jnp.bfloat16)
            for lane in (width, width + STATE)
        )
        c_out[source] = c_part
        scores = contract(c_part, b_part, ((1,), (1,)))
        scores = jnp.where(lower, scores, 0.0).astype(jnp.bfloat16)
        for lane in range(0, width, LANES):
            at = slice(lane, lane + LANES)
            for r in range(0, rows, STRIP):
                x_conv = activated(r, lane)
                x_ref[r : r + STRIP, at] = x_conv
                scaled_ref[r : r + STRIP, at] = (x_conv * scales[r : r + STRIP, at]).astype(
                    jnp.bfloat16
                )
        for b in range(blocks):
            at = slice(b * BLOCK, (b + 1) * BLOCK)
            added = contract(b_part[at], scaled_ref[at], ((0,), (0,)))
            state[source, b * STATE : (b + 1) * STATE] = added.astype(jnp.bfloat16)
        intra = contract(scores, scaled_ref[...], ((1,), (0,)))
        pre[source] = (intra * scales[rows : 2 * rows] + skip_ref[...] * x_ref[...]).astype(jnp.bfloat16)


def carry_kernel(width, whole_group, *refs):
    pre, state, c_part, fade, edge, gain_ref = refs[:6]
    outs, carry = refs[6:-1], refs[-1]
    rows = pre.shape[1]
    blocks = rows // BLOCK
    step = pl.program_id(0)

    @pl.when(step == 0)
    def _():
        carry[...] = jnp.zeros_like(carry)

    held = []
    for half in range(PAIR):
        source = step * PAIR + half
        for b in range(blocks):
            now = carry[...] * edge[source, 2 * b : 2 * b + 1]
            held.append(now.astype(jnp.bfloat16))
            added = state[source, b * STATE : (b + 1) * STATE].astype(jnp.float32)
            carry[...] = (now + added) * edge[source, 2 * b + 1 : 2 * b + 2]
    for half in range(PAIR):
        source = step * PAIR + half
        for b in range(blocks):
            at = slice(b * BLOCK, (b + 1) * BLOCK)
            to = slice(half * rows + b * BLOCK, half * rows + (b + 1) * BLOCK)
            inter = contract(c_part[source, at], held[half * blocks + b], ((1,), (0,)))
            total = pre[source, at].astype(jnp.float32) + inter * fade[source, at].astype(
                jnp.float32
            )
            power = total[:, :LANES] * total[:, :LANES]
            for lane in range(LANES, width, LANES):
                power = power + total[:, lane : lane + LANES] * total[:, lane : lane + LANES]
            if whole_group:
                summed = jnp.sum(power, axis=1, keepdims=True)
                norm = lax.rsqrt(summed * (1.0 / GROUP_WIDTH) + EPS)
                outs[0][to] = (total * norm * gain_ref[...]).astype(jnp.bfloat16)
            else:
                outs[0][to] = total
                outs[1][to] = power


def per_device(inputs, key_query, conv_inputs, conv_kq, step_size, decay_log, skip_gain, norm_gain):
    peers = lax.axis_size("ctx")
    me = lax.axis_index("ctx")
    rows = inputs.shape[0]
    width = HEADS * HEAD_DIM // peers
    heads = HEADS // peers
    span = GROUP_WIDTH // width
    whole_group = span == 1
    blocks = rows // BLOCK
    full = width + 2 * STATE
    scalar_rows = scalar_units(heads, rows, full)[-1][3] + SUBLANES
    scale_rows = rows + 16 * blocks
    cycle = jnp.arange(peers, dtype=jnp.int32)
    odd = me % 2 == 1
    owners = lax.rem(me + cycle, peers)
    turned = lax.rem(me + peers - cycle, peers)
    owners = jnp.where(odd & ((cycle == 1) | (cycle == peers - 1)), turned, owners)
    sources = lax.rem(me + peers - cycle, peers)

    smem = pl.BlockSpec(memory_space=pltpu.SMEM)
    hbm = pl.BlockSpec(memory_space=pltpu.HBM)
    vmem = pl.BlockSpec(memory_space=pltpu.VMEM)
    params = pltpu.CompilerParams(vmem_limit_bytes=VMEM_LIMIT)

    def columns(a, first, size):
        return lax.dynamic_slice_in_dim(a, first, size, axis=1)

    def pack(codes):
        shape = jax.ShapeDtypeStruct((rows + scalar_rows, full), jnp.bfloat16)
        return pl.pallas_call(
            functools.partial(pack_kernel, peers, span, width, heads, codes),
            in_specs=[smem] + [hbm] * 4,
            out_specs=[vmem] * len(codes),
            out_shape=[shape] * len(codes),
            scratch_shapes=[
                pltpu.VMEM((FIELDS, rows, HEADS), jnp.float32),
                pltpu.VMEM((FIELDS, peers, heads, rows), jnp.float32),
                pltpu.VMEM(key_query.shape, jnp.bfloat16),
                pltpu.SemaphoreType.DMA((2, max(3, len(codes)))),
            ],
            compiler_params=pltpu.CompilerParams(vmem_limit_bytes=PACK_VMEM),
            cost_estimate=pl.CostEstimate(
                flops=0, bytes_accessed=4 * len(codes) * rows * full, transcendentals=0
            ),
            name="pack",
        )(owners, inputs, key_query, decay_log, step_size)

    shifts = list(range(2, peers - 1))
    codes = shifts + [1, peers - 1, 0]
    parts = dict(zip(codes, pack(codes)))
    for code in shifts:
        pairs = [(i, (i + code) % peers) for i in range(peers)]
        parts[code] = lax.ppermute(parts[code], "ctx", pairs)
    siblings = [[i, i + 1] for i in range(0, peers, 2)]
    neighbours = [[i, (i + 1) % peers] for i in range(1, peers, 2)]
    inner = lax.all_gather(parts[1], "ctx", axis_index_groups=siblings)
    outer = lax.all_gather(parts[peers - 1], "ctx", axis_index_groups=neighbours)
    parts[1] = jnp.where(odd, inner[0], outer[0])
    parts[peers - 1] = jnp.where(odd, outer[1], inner[1])

    group = me // span
    taps = jnp.concatenate(
        [
            columns(conv_inputs, me * width, width),
            columns(conv_kq, group * STATE, STATE),
            columns(conv_kq, (GROUPS + group) * STATE, STATE),
        ],
        axis=1,
    )
    skip = jnp.repeat(lax.dynamic_slice_in_dim(skip_gain, me * heads, heads), HEAD_DIM)[None]
    gain = columns(norm_gain[None], me * width, width)

    shapes = [
        ((rows, width), jnp.bfloat16),
        ((blocks * STATE, width), jnp.bfloat16),
        ((rows, STATE), jnp.bfloat16),
        ((rows, width), jnp.bfloat16),
        ((2 * blocks, width), jnp.float32),
    ]
    arrived = {0}
    pending = list(range(peers))
    stores = []
    for code in sorted(range(1, peers), key=lambda code: -abs(code - peers // 2)):
        arrived.add(code)
        ready = [k for k in pending if {k, (k + 1) % peers} <= arrived]
        pending = [k for k in pending if k not in ready]
        if not ready:
            continue
        count = len(ready)
        operands = []
        for k in ready:
            operands += [parts[k], parts[(k + 1) % peers]]
        stores = pl.pallas_call(
            functools.partial(local_kernel, width, heads, count, bool(stores)),
            in_specs=[smem] + [vmem] * (2 * count + 2 + len(stores)),
            out_specs=[vmem] * len(shapes),
            out_shape=[jax.ShapeDtypeStruct((peers,) + shape, dtype) for shape, dtype in shapes],
            input_output_aliases={3 + 2 * count + i: i for i in range(len(stores))},
            scratch_shapes=[
                pltpu.VMEM((rows + HALO, full), jnp.bfloat16),
                pltpu.VMEM((rows, width), jnp.float32),
                pltpu.VMEM((rows, width), jnp.bfloat16),
                pltpu.VMEM((rows + scale_rows, width), jnp.float32),
            ],
            compiler_params=params,
            cost_estimate=pl.CostEstimate(
                flops=2 * rows * count * width * 450,
                bytes_accessed=count * rows * width * 10,
                transcendentals=count * rows * full,
            ),
            name="local",
        )(jnp.stack([sources[k] for k in ready]), *operands, taps, skip, *stores)

    out = [((rows, width), jnp.bfloat16 if whole_group else jnp.float32)]
    if not whole_group:
        out.append(((rows, LANES), jnp.float32))
    results = pl.pallas_call(
        functools.partial(carry_kernel, width, whole_group),
        grid=(peers // PAIR,),
        in_specs=[vmem] * (len(shapes) + 1),
        out_specs=[pl.BlockSpec((PAIR * shape[0], shape[1]), lambda i: (i, 0)) for shape, _ in out],
        out_shape=[
            jax.ShapeDtypeStruct((peers * shape[0], shape[1]), dtype) for shape, dtype in out
        ],
        scratch_shapes=[
            pltpu.VMEM((STATE, width), jnp.float32),
        ],
        compiler_params=params,
        cost_estimate=pl.CostEstimate(
            flops=2 * peers * rows * width * 150,
            bytes_accessed=peers * rows * width * 8,
            transcendentals=peers * rows,
        ),
        name="carry",
    )(*stores, gain)
    if whole_group:
        return results[0]
    total, power = results
    sharers = [list(range(i, i + span)) for i in range(0, peers, span)]
    summed = jnp.sum(power, axis=1, keepdims=True)
    summed = lax.psum(summed, "ctx", axis_index_groups=sharers)
    return (total * lax.rsqrt(summed * (1.0 / GROUP_WIDTH) + EPS) * gain).astype(jnp.bfloat16)


def solution(mesh):
    in_specs = (
        P(("dp", "ctx"), None),
        P(("dp", "ctx"), None),
        P(),
        P(),
        P(("dp", "ctx"), None),
        P(("dp", "ctx"), None),
        P(),
        P(),
    )
    out_specs = P("dp", "ctx")
    return jax.shard_map(
        per_device, mesh=mesh, in_specs=in_specs, out_specs=out_specs, check_vma=False
    )
```

```python
import functools

import jax
import jax.numpy as jnp
from jax import lax
from jax.experimental import pallas as pl
from jax.experimental.pallas import tpu as pltpu
from jax.sharding import PartitionSpec as P

HEADS = 128
HEAD_DIM = 64
STATE = 128
GROUPS = 8
KW = 4
BLOCK = 128
GROUP_WIDTH = HEADS * HEAD_DIM // GROUPS
EPS = 1e-05
HALO = 16
LANES = 128
SUBLANES = 8
FIELDS = 2
STRIP = 64
PAIR = 2
WINDOW = 5
ORDER = (1, 7, 4, 3, 5, 2, 6)
ARRIVAL = (1, 7, 2, 6, 4, 3, 5)
PACK_VMEM = 58 * 1024 * 1024
VMEM_LIMIT = 28 * 1024 * 1024


def contract(a, b, dims):
    return lax.dot_general(a, b, (dims, ((), ())), preferred_element_type=jnp.float32)


def as_parts(v, count):
    parts = []
    for _ in range(count):
        part = v.astype(jnp.bfloat16)
        parts.append(part)
        v = v - part.astype(jnp.float32)
    return parts


def scalar_units(heads, rows, cols):
    units = []
    for p in range(FIELDS):
        for head in range(0, heads, SUBLANES):
            line, column = divmod(len(units), cols // rows)
            units.append((p, head, min(SUBLANES, heads), line * SUBLANES, column * rows))
    return units


def pack_kernel(peers, span, width, heads, codes, *refs):
    owner_ref, x_ref, kq_ref, decay_ref, step_ref = refs[:5]
    outs = refs[5 : 5 + len(codes)]
    raw_scalars, scalars, kq_near, sems = refs[5 + len(codes) :]
    rows = x_ref.shape[0]
    copies = [
        pltpu.make_async_copy(ref, dst, sems.at[1, i])
        for i, (ref, dst) in enumerate(
            ((decay_ref, raw_scalars.at[0]), (step_ref, raw_scalars.at[1]), (kq_ref, kq_near))
        )
    ]
    owners = [owner_ref[code] for code in codes]
    for i, owner in enumerate(owners):
        column = pl.multiple_of(owner * width, LANES)
        copies.append(
            pltpu.make_async_copy(
                x_ref.at[:, pl.ds(column, width)], outs[i].at[0:rows, 0:width], sems.at[0, i]
            )
        )
    for copy in copies:
        copy.start()
    for copy in copies[:3]:
        copy.wait()
    for p in range(FIELDS):
        field = raw_scalars[p].T
        for owner in range(peers):
            scalars[p, owner] = field[owner * heads : (owner + 1) * heads]
    for i, owner in enumerate(owners):
        outs[i][rows:] = jnp.zeros((outs[i].shape[0] - rows, outs[i].shape[1]), jnp.bfloat16)
        for p, head, count, top, left in scalar_units(heads, rows, width + 2 * STATE):
            outs[i][rows + top : rows + top + count, left : left + rows] = scalars[
                p, owner, head : head + count
            ].astype(jnp.bfloat16)
        for j in range(2):
            column = pl.multiple_of((j * GROUPS + owner // span) * STATE, LANES)
            left = width + j * STATE
            outs[i][0:rows, left : left + STATE] = kq_near[:, pl.ds(column, STATE)]
    for copy in copies[3:]:
        copy.wait()


def spread(heads):
    head_of = lax.broadcasted_iota(jnp.int32, (2 * heads, heads * HEAD_DIM), 1) // HEAD_DIM
    row = lax.rem(lax.broadcasted_iota(jnp.int32, (2 * heads, heads * HEAD_DIM), 0), heads)
    return jnp.where(head_of == row, 1.0, 0.0).astype(jnp.bfloat16)


def local_kernel(width, heads, count, chained, *refs):
    source_ref = refs[0]
    parts = refs[1 : 1 + 2 * count]
    taps_ref, skip_ref = refs[1 + 2 * count : 3 + 2 * count]
    refs = refs[3 + 2 * count + (5 if chained else 0) :]
    pre, state, c_out, fade_out, edge_out = refs[:5]
    wide, x_ref, scaled_ref, scales = refs[5:]
    rows = x_ref.shape[0]
    blocks = rows // BLOCK
    full = width + 2 * STATE
    row = lax.broadcasted_iota(jnp.int32, (rows, rows), 0)
    col = lax.broadcasted_iota(jnp.int32, (rows, rows), 1)
    lower = (row >= col) & (row // BLOCK == col // BLOCK)
    ones = jnp.where(lower, 1.0, 0.0).astype(jnp.bfloat16)
    eye = jnp.where(row == col, 1.0, 0.0).astype(jnp.bfloat16)
    expand = spread(heads)

    for which in range(count):
        source = source_ref[which]
        part, earlier = parts[2 * which : 2 * which + 2]
        wide[HALO:] = part[0:rows, 0:full]
        edge = earlier[rows - HALO : rows, 0:full]
        wide[0:HALO] = jnp.where(source == 0, jnp.zeros_like(edge), edge)

        def activated(r, lane):
            tap = [taps_ref[k : k + 1, lane : lane + LANES] for k in range(KW)]
            now = wide[r : r + STRIP + HALO, lane : lane + LANES].astype(jnp.float32)
            now = now[HALO // 2 :]
            before = pltpu.roll(now, 1, 0)
            older = pltpu.roll(tap[0] * before + tap[1] * now, 2, 0)
            summed = (older + (tap[2] * before + tap[3] * now))[HALO // 2 :]
            return summed * pltpu.reciprocal(1.0 + jnp.exp(-summed), approx=True)

        def field(p):
            pieces = [
                part[rows + top : rows + top + size, left : left + rows].astype(jnp.float32)
                for q, _, size, top, left in scalar_units(heads, rows, full)
                if q == p
            ]
            return jnp.concatenate(pieces, axis=0).astype(jnp.bfloat16)

        cumul = contract(ones, field(0), ((1,), (1,)))
        steps = contract(eye, field(1), ((1,), (1,)))
        middles = [
            cumul[b * BLOCK + BLOCK // 2 - 1 : b * BLOCK + BLOCK // 2] for b in range(blocks)
        ]
        middle = jnp.concatenate([jnp.broadcast_to(m, (BLOCK, heads)) for m in middles], axis=0)
        inward = jnp.concatenate(as_parts(steps * jnp.exp(middle - cumul), 2), axis=1)
        outward = jnp.concatenate(
            as_parts(
                jnp.concatenate(
                    [jnp.exp(cumul - middle)]
                    + [jnp.broadcast_to(jnp.exp(m), (16, heads)) for m in middles],
                    axis=0,
                ),
                2,
            ),
            axis=1,
        )
        scales[...] = contract(
            jnp.concatenate([inward, outward], axis=0), expand, ((1,), (0,))
        )
        edges = []
        for b in range(blocks):
            last_row = rows + (b + 1) * BLOCK - 1
            middle_row = 2 * rows + 16 * b
            edges += [scales[middle_row : middle_row + 1], scales[last_row : last_row + 1]]
        edge_out[source, 0 : 2 * blocks] = jnp.concatenate(edges, axis=0)
        fade_out[source] = scales[rows : 2 * rows].astype(jnp.bfloat16)
        b_part, c_part = (
            jnp.concatenate(
                [activated(r, lane) for r in range(0, rows, STRIP)], axis=0
            ).astype(jnp.bfloat16)
            for lane in (width, width + STATE)
        )
        c_out[source] = c_part
        scores = contract(c_part, b_part, ((1,), (1,)))
        scores = jnp.where(lower, scores, 0.0).astype(jnp.bfloat16)
        for lane in range(0, width, LANES):
            at = slice(lane, lane + LANES)
            for r in range(0, rows, STRIP):
                x_conv = activated(r, lane)
                x_ref[r : r + STRIP, at] = x_conv
                scaled_ref[r : r + STRIP, at] = (x_conv * scales[r : r + STRIP, at]).astype(
                    jnp.bfloat16
                )
        for b in range(blocks):
            at = slice(b * BLOCK, (b + 1) * BLOCK)
            added = contract(b_part[at], scaled_ref[at], ((0,), (0,)))
            state[source, b * STATE : (b + 1) * STATE] = added.astype(jnp.bfloat16)
        intra = contract(scores, scaled_ref[...], ((1,), (0,)))
        pre[source] = (intra * scales[rows : 2 * rows] + skip_ref[...] * x_ref[...]).astype(jnp.bfloat16)


def carry_kernel(width, whole_group, *refs):
    pre, state, c_part, fade, edge, gain_ref = refs[:6]
    outs, carry = refs[6:-1], refs[-1]
    rows = pre.shape[1]
    blocks = rows // BLOCK
    step = pl.program_id(0)

    @pl.when(step == 0)
    def _():
        carry[...] = jnp.zeros_like(carry)

    held = []
    for half in range(PAIR):
        source = step * PAIR + half
        for b in range(blocks):
            now = carry[...] * edge[source, 2 * b : 2 * b + 1]
            held.append(now.astype(jnp.bfloat16))
            added = state[source, b * STATE : (b + 1) * STATE].astype(jnp.float32)
            carry[...] = (now + added) * edge[source, 2 * b + 1 : 2 * b + 2]
    for half in range(PAIR):
        source = step * PAIR + half
        for b in range(blocks):
            at = slice(b * BLOCK, (b + 1) * BLOCK)
            to = slice(half * rows + b * BLOCK, half * rows + (b + 1) * BLOCK)
            inter = contract(c_part[source, at], held[half * blocks + b], ((1,), (0,)))
            total = pre[source, at].astype(jnp.float32) + inter * fade[source, at].astype(
                jnp.float32
            )
            power = total[:, :LANES] * total[:, :LANES]
            for lane in range(LANES, width, LANES):
                power = power + total[:, lane : lane + LANES] * total[:, lane : lane + LANES]
            if whole_group:
                summed = jnp.sum(power, axis=1, keepdims=True)
                norm = lax.rsqrt(summed * (1.0 / GROUP_WIDTH) + EPS)
                outs[0][to] = (total * norm * gain_ref[...]).astype(jnp.bfloat16)
            else:
                outs[0][to] = total
                outs[1][to] = power


def per_device(inputs, key_query, conv_inputs, conv_kq, step_size, decay_log, skip_gain, norm_gain):
    peers = lax.axis_size("ctx")
    me = lax.axis_index("ctx")
    rows = inputs.shape[0]
    width = HEADS * HEAD_DIM // peers
    heads = HEADS // peers
    span = GROUP_WIDTH // width
    whole_group = span == 1
    blocks = rows // BLOCK
    full = width + 2 * STATE
    scalar_rows = scalar_units(heads, rows, full)[-1][3] + SUBLANES
    scale_rows = rows + 16 * blocks
    cycle = jnp.arange(peers, dtype=jnp.int32)
    owners = lax.rem(me + cycle, peers)
    sources = lax.rem(me + peers - cycle, peers)

    smem = pl.BlockSpec(memory_space=pltpu.SMEM)
    hbm = pl.BlockSpec(memory_space=pltpu.HBM)
    vmem = pl.BlockSpec(memory_space=pltpu.VMEM)
    params = pltpu.CompilerParams(vmem_limit_bytes=VMEM_LIMIT)

    def columns(a, first, size):
        return lax.dynamic_slice_in_dim(a, first, size, axis=1)

    def pack(codes):
        shape = jax.ShapeDtypeStruct((rows + scalar_rows, full), jnp.bfloat16)
        return pl.pallas_call(
            functools.partial(pack_kernel, peers, span, width, heads, codes),
            in_specs=[smem] + [hbm] * 4,
            out_specs=[vmem] * len(codes),
            out_shape=[shape] * len(codes),
            scratch_shapes=[
                pltpu.VMEM((FIELDS, rows, HEADS), jnp.float32),
                pltpu.VMEM((FIELDS, peers, heads, rows), jnp.float32),
                pltpu.VMEM(key_query.shape, jnp.bfloat16),
                pltpu.SemaphoreType.DMA((2, max(3, len(codes)))),
            ],
            compiler_params=pltpu.CompilerParams(vmem_limit_bytes=PACK_VMEM),
            cost_estimate=pl.CostEstimate(
                flops=0, bytes_accessed=4 * len(codes) * rows * full, transcendentals=0
            ),
            name="pack",
        )(owners, inputs, key_query, decay_log, step_size)

    codes = [code for code in ORDER if code < peers]
    codes += [code for code in range(1, peers) if code not in codes]
    parts = dict(zip(codes[:2], pack(codes[:2])))
    parts.update(zip(codes[2:] + [0], pack(codes[2:] + [0])))
    for i, code in enumerate(codes):
        pairs = [(j, (j + code) % peers) for j in range(peers)]
        message = parts[code]
        if i >= WINDOW:
            message, _ = lax.optimization_barrier((message, parts[codes[i - WINDOW]]))
        parts[code] = lax.ppermute(message, "ctx", pairs)

    group = me // span
    taps = jnp.concatenate(
        [
            columns(conv_inputs, me * width, width),
            columns(conv_kq, group * STATE, STATE),
            columns(conv_kq, (GROUPS + group) * STATE, STATE),
        ],
        axis=1,
    )
    skip = jnp.repeat(lax.dynamic_slice_in_dim(skip_gain, me * heads, heads), HEAD_DIM)[None]
    gain = columns(norm_gain[None], me * width, width)

    shapes = [
        ((rows, width), jnp.bfloat16),
        ((blocks * STATE, width), jnp.bfloat16),
        ((rows, STATE), jnp.bfloat16),
        ((rows, width), jnp.bfloat16),
        ((2 * blocks, width), jnp.float32),
    ]
    codes_after = tuple(code for code in codes if code not in ARRIVAL)
    arrived = {0}
    pending = list(range(peers))
    stores = []
    for code in sorted(codes, key=lambda code: (ARRIVAL + codes_after).index(code)):
        arrived.add(code)
        ready = [k for k in pending if {k, (k + 1) % peers} <= arrived]
        pending = [k for k in pending if k not in ready]
        if not ready:
            continue
        count = len(ready)
        operands = []
        for k in ready:
            operands += [parts[k], parts[(k + 1) % peers]]
        stores = pl.pallas_call(
            functools.partial(local_kernel, width, heads, count, bool(stores)),
            in_specs=[smem] + [vmem] * (2 * count + 2 + len(stores)),
            out_specs=[vmem] * len(shapes),
            out_shape=[jax.ShapeDtypeStruct((peers,) + shape, dtype) for shape, dtype in shapes],
            input_output_aliases={3 + 2 * count + i: i for i in range(len(stores))},
            scratch_shapes=[
                pltpu.VMEM((rows + HALO, full), jnp.bfloat16),
                pltpu.VMEM((rows, width), jnp.float32),
                pltpu.VMEM((rows, width), jnp.bfloat16),
                pltpu.VMEM((rows + scale_rows, width), jnp.float32),
            ],
            compiler_params=params,
            cost_estimate=pl.CostEstimate(
                flops=2 * rows * count * width * 450,
                bytes_accessed=count * rows * width * 10,
                transcendentals=count * rows * full,
            ),
            name="local",
        )(jnp.stack([sources[k] for k in ready]), *operands, taps, skip, *stores)

    out = [((rows, width), jnp.bfloat16 if whole_group else jnp.float32)]
    if not whole_group:
        out.append(((rows, LANES), jnp.float32))
    results = pl.pallas_call(
        functools.partial(carry_kernel, width, whole_group),
        grid=(peers // PAIR,),
        in_specs=[vmem] * (len(shapes) + 1),
        out_specs=[pl.BlockSpec((PAIR * shape[0], shape[1]), lambda i: (i, 0)) for shape, _ in out],
        out_shape=[
            jax.ShapeDtypeStruct((peers * shape[0], shape[1]), dtype) for shape, dtype in out
        ],
        scratch_shapes=[
            pltpu.VMEM((STATE, width), jnp.float32),
        ],
        compiler_params=params,
        cost_estimate=pl.CostEstimate(
            flops=2 * peers * rows * width * 150,
            bytes_accessed=peers * rows * width * 8,
            transcendentals=peers * rows,
        ),
        name="carry",
    )(*stores, gain)
    if whole_group:
        return results[0]
    total, power = results
    sharers = [list(range(i, i + span)) for i in range(0, peers, span)]
    summed = jnp.sum(power, axis=1, keepdims=True)
    summed = lax.psum(summed, "ctx", axis_index_groups=sharers)
    return (total * lax.rsqrt(summed * (1.0 / GROUP_WIDTH) + EPS) * gain).astype(jnp.bfloat16)


def solution(mesh):
    in_specs = (
        P(("dp", "ctx"), None),
        P(("dp", "ctx"), None),
        P(),
        P(),
        P(("dp", "ctx"), None),
        P(("dp", "ctx"), None),
        P(),
        P(),
    )
    out_specs = P("dp", "ctx")
    return jax.shard_map(
        per_device, mesh=mesh, in_specs=in_specs, out_specs=out_specs, check_vma=False
    )
```

```python
import functools

import jax
import jax.numpy as jnp
from jax import lax
from jax.experimental import pallas as pl
from jax.experimental.pallas import tpu as pltpu
from jax.sharding import PartitionSpec as P

HEADS = 128
HEAD_DIM = 64
STATE = 128
GROUPS = 8
KW = 4
BLOCK = 128
GROUP_WIDTH = HEADS * HEAD_DIM // GROUPS
EPS = 1e-05
HALO = 16
LANES = 128
SUBLANES = 8
FIELDS = 2
STRIP = 64
PAIR = 2
WINDOW = 5
ORDER = (1, 7, 4, 2, 6, 3, 5)
PACK_VMEM = 58 * 1024 * 1024
VMEM_LIMIT = 28 * 1024 * 1024


def contract(a, b, dims):
    return lax.dot_general(a, b, (dims, ((), ())), preferred_element_type=jnp.float32)


def as_parts(v, count):
    parts = []
    for _ in range(count):
        part = v.astype(jnp.bfloat16)
        parts.append(part)
        v = v - part.astype(jnp.float32)
    return parts


def scalar_units(heads, rows, cols):
    units = []
    for p in range(FIELDS):
        for head in range(0, heads, SUBLANES):
            line, column = divmod(len(units), cols // rows)
            units.append((p, head, min(SUBLANES, heads), line * SUBLANES, column * rows))
    return units


def pack_kernel(peers, span, width, heads, codes, *refs):
    owner_ref, x_ref, kq_ref, decay_ref, step_ref = refs[:5]
    outs = refs[5 : 5 + len(codes)]
    raw_scalars, scalars, kq_near, sems = refs[5 + len(codes) :]
    rows = x_ref.shape[0]
    copies = [
        pltpu.make_async_copy(ref, dst, sems.at[1, i])
        for i, (ref, dst) in enumerate(
            ((decay_ref, raw_scalars.at[0]), (step_ref, raw_scalars.at[1]), (kq_ref, kq_near))
        )
    ]
    owners = [owner_ref[code] for code in codes]
    for i, owner in enumerate(owners):
        column = pl.multiple_of(owner * width, LANES)
        copies.append(
            pltpu.make_async_copy(
                x_ref.at[:, pl.ds(column, width)], outs[i].at[0:rows, 0:width], sems.at[0, i]
            )
        )
    for copy in copies:
        copy.start()
    for copy in copies[:3]:
        copy.wait()
    for p in range(FIELDS):
        field = raw_scalars[p].T
        for owner in range(peers):
            scalars[p, owner] = field[owner * heads : (owner + 1) * heads]
    for i, owner in enumerate(owners):
        outs[i][rows:] = jnp.zeros((outs[i].shape[0] - rows, outs[i].shape[1]), jnp.bfloat16)
        for p, head, count, top, left in scalar_units(heads, rows, width + 2 * STATE):
            outs[i][rows + top : rows + top + count, left : left + rows] = scalars[
                p, owner, head : head + count
            ].astype(jnp.bfloat16)
        for j in range(2):
            column = pl.multiple_of((j * GROUPS + owner // span) * STATE, LANES)
            left = width + j * STATE
            outs[i][0:rows, left : left + STATE] = kq_near[:, pl.ds(column, STATE)]
    for copy in copies[3:]:
        copy.wait()


def spread(heads):
    head_of = lax.broadcasted_iota(jnp.int32, (2 * heads, heads * HEAD_DIM), 1) // HEAD_DIM
    row = lax.rem(lax.broadcasted_iota(jnp.int32, (2 * heads, heads * HEAD_DIM), 0), heads)
    return jnp.where(head_of == row, 1.0, 0.0).astype(jnp.bfloat16)


def local_kernel(width, heads, count, chained, *refs):
    source_ref = refs[0]
    parts = refs[1 : 1 + 2 * count]
    taps_ref, skip_ref = refs[1 + 2 * count : 3 + 2 * count]
    refs = refs[3 + 2 * count + (5 if chained else 0) :]
    pre, state, c_out, fade_out, edge_out = refs[:5]
    wide, x_ref, scaled_ref, scales = refs[5:]
    rows = x_ref.shape[0]
    blocks = rows // BLOCK
    full = width + 2 * STATE
    row = lax.broadcasted_iota(jnp.int32, (rows, rows), 0)
    col = lax.broadcasted_iota(jnp.int32, (rows, rows), 1)
    lower = (row >= col) & (row // BLOCK == col // BLOCK)
    ones = jnp.where(lower, 1.0, 0.0).astype(jnp.bfloat16)
    eye = jnp.where(row == col, 1.0, 0.0).astype(jnp.bfloat16)
    expand = spread(heads)

    for which in range(count):
        source = source_ref[which]
        part, earlier = parts[2 * which : 2 * which + 2]
        wide[HALO:] = part[0:rows, 0:full]
        edge = earlier[rows - HALO : rows, 0:full]
        wide[0:HALO] = jnp.where(source == 0, jnp.zeros_like(edge), edge)

        def activated(r, lane):
            tap = [taps_ref[k : k + 1, lane : lane + LANES] for k in range(KW)]
            now = wide[r : r + STRIP + HALO, lane : lane + LANES].astype(jnp.float32)
            now = now[HALO // 2 :]
            before = pltpu.roll(now, 1, 0)
            older = pltpu.roll(tap[0] * before + tap[1] * now, 2, 0)
            summed = (older + (tap[2] * before + tap[3] * now))[HALO // 2 :]
            return summed * pltpu.reciprocal(1.0 + jnp.exp(-summed), approx=True)

        def field(p):
            pieces = [
                part[rows + top : rows + top + size, left : left + rows].astype(jnp.float32)
                for q, _, size, top, left in scalar_units(heads, rows, full)
                if q == p
            ]
            return jnp.concatenate(pieces, axis=0).astype(jnp.bfloat16)

        cumul = contract(ones, field(0), ((1,), (1,)))
        steps = contract(eye, field(1), ((1,), (1,)))
        middles = [
            cumul[b * BLOCK + BLOCK // 2 - 1 : b * BLOCK + BLOCK // 2] for b in range(blocks)
        ]
        middle = jnp.concatenate([jnp.broadcast_to(m, (BLOCK, heads)) for m in middles], axis=0)
        inward = jnp.concatenate(as_parts(steps * jnp.exp(middle - cumul), 2), axis=1)
        outward = jnp.concatenate(
            as_parts(
                jnp.concatenate(
                    [jnp.exp(cumul - middle)]
                    + [jnp.broadcast_to(jnp.exp(m), (16, heads)) for m in middles],
                    axis=0,
                ),
                2,
            ),
            axis=1,
        )
        scales[...] = contract(
            jnp.concatenate([inward, outward], axis=0), expand, ((1,), (0,))
        )
        edges = []
        for b in range(blocks):
            last_row = rows + (b + 1) * BLOCK - 1
            middle_row = 2 * rows + 16 * b
            edges += [scales[middle_row : middle_row + 1], scales[last_row : last_row + 1]]
        edge_out[source, 0 : 2 * blocks] = jnp.concatenate(edges, axis=0)
        fade_out[source] = scales[rows : 2 * rows].astype(jnp.bfloat16)
        b_part, c_part = (
            jnp.concatenate(
                [activated(r, lane) for r in range(0, rows, STRIP)], axis=0
            ).astype(jnp.bfloat16)
            for lane in (width, width + STATE)
        )
        c_out[source] = c_part
        scores = contract(c_part, b_part, ((1,), (1,)))
        scores = jnp.where(lower, scores, 0.0).astype(jnp.bfloat16)
        for lane in range(0, width, LANES):
            at = slice(lane, lane + LANES)
            for r in range(0, rows, STRIP):
                x_conv = activated(r, lane)
                x_ref[r : r + STRIP, at] = x_conv
                scaled_ref[r : r + STRIP, at] = (x_conv * scales[r : r + STRIP, at]).astype(
                    jnp.bfloat16
                )
        for b in range(blocks):
            at = slice(b * BLOCK, (b + 1) * BLOCK)
            added = contract(b_part[at], scaled_ref[at], ((0,), (0,)))
            state[source, b * STATE : (b + 1) * STATE] = added.astype(jnp.bfloat16)
        intra = contract(scores, scaled_ref[...], ((1,), (0,)))
        pre[source] = (intra * scales[rows : 2 * rows] + skip_ref[...] * x_ref[...]).astype(jnp.bfloat16)


def carry_kernel(width, whole_group, *refs):
    pre, state, c_part, fade, edge, gain_ref = refs[:6]
    outs, carry = refs[6:-1], refs[-1]
    rows = pre.shape[1]
    blocks = rows // BLOCK
    step = pl.program_id(0)

    @pl.when(step == 0)
    def _():
        carry[...] = jnp.zeros_like(carry)

    held = []
    for half in range(PAIR):
        source = step * PAIR + half
        for b in range(blocks):
            now = carry[...] * edge[source, 2 * b : 2 * b + 1]
            held.append(now.astype(jnp.bfloat16))
            added = state[source, b * STATE : (b + 1) * STATE].astype(jnp.float32)
            carry[...] = (now + added) * edge[source, 2 * b + 1 : 2 * b + 2]
    for half in range(PAIR):
        source = step * PAIR + half
        for b in range(blocks):
            at = slice(b * BLOCK, (b + 1) * BLOCK)
            to = slice(half * rows + b * BLOCK, half * rows + (b + 1) * BLOCK)
            inter = contract(c_part[source, at], held[half * blocks + b], ((1,), (0,)))
            total = pre[source, at].astype(jnp.float32) + inter * fade[source, at].astype(
                jnp.float32
            )
            power = total[:, :LANES] * total[:, :LANES]
            for lane in range(LANES, width, LANES):
                power = power + total[:, lane : lane + LANES] * total[:, lane : lane + LANES]
            if whole_group:
                summed = jnp.sum(power, axis=1, keepdims=True)
                norm = lax.rsqrt(summed * (1.0 / GROUP_WIDTH) + EPS)
                outs[0][to] = (total * norm * gain_ref[...]).astype(jnp.bfloat16)
            else:
                outs[0][to] = total
                outs[1][to] = power


def per_device(inputs, key_query, conv_inputs, conv_kq, step_size, decay_log, skip_gain, norm_gain):
    peers = lax.axis_size("ctx")
    me = lax.axis_index("ctx")
    rows = inputs.shape[0]
    width = HEADS * HEAD_DIM // peers
    heads = HEADS // peers
    span = GROUP_WIDTH // width
    whole_group = span == 1
    blocks = rows // BLOCK
    full = width + 2 * STATE
    scalar_rows = scalar_units(heads, rows, full)[-1][3] + SUBLANES
    scale_rows = rows + 16 * blocks
    cycle = jnp.arange(peers, dtype=jnp.int32)
    owners = lax.rem(me + cycle, peers)
    sources = lax.rem(me + peers - cycle, peers)

    smem = pl.BlockSpec(memory_space=pltpu.SMEM)
    hbm = pl.BlockSpec(memory_space=pltpu.HBM)
    vmem = pl.BlockSpec(memory_space=pltpu.VMEM)
    params = pltpu.CompilerParams(vmem_limit_bytes=VMEM_LIMIT)

    def columns(a, first, size):
        return lax.dynamic_slice_in_dim(a, first, size, axis=1)

    def pack(codes):
        shape = jax.ShapeDtypeStruct((rows + scalar_rows, full), jnp.bfloat16)
        return pl.pallas_call(
            functools.partial(pack_kernel, peers, span, width, heads, codes),
            in_specs=[smem] + [hbm] * 4,
            out_specs=[vmem] * len(codes),
            out_shape=[shape] * len(codes),
            scratch_shapes=[
                pltpu.VMEM((FIELDS, rows, HEADS), jnp.float32),
                pltpu.VMEM((FIELDS, peers, heads, rows), jnp.float32),
                pltpu.VMEM(key_query.shape, jnp.bfloat16),
                pltpu.SemaphoreType.DMA((2, max(3, len(codes)))),
            ],
            compiler_params=pltpu.CompilerParams(vmem_limit_bytes=PACK_VMEM),
            cost_estimate=pl.CostEstimate(
                flops=0, bytes_accessed=4 * len(codes) * rows * full, transcendentals=0
            ),
            name="pack",
        )(owners, inputs, key_query, decay_log, step_size)

    codes = [code for code in ORDER if code < peers]
    codes += [code for code in range(1, peers) if code not in codes]
    parts = dict(zip(codes[:2], pack(codes[:2])))
    parts.update(zip(codes[2:] + [0], pack(codes[2:] + [0])))
    for i, code in enumerate(codes):
        pairs = [(j, (j + code) % peers) for j in range(peers)]
        message = parts[code]
        if i >= WINDOW:
            message, _ = lax.optimization_barrier((message, parts[codes[i - WINDOW]]))
        parts[code] = lax.ppermute(message, "ctx", pairs)

    group = me // span
    taps = jnp.concatenate(
        [
            columns(conv_inputs, me * width, width),
            columns(conv_kq, group * STATE, STATE),
            columns(conv_kq, (GROUPS + group) * STATE, STATE),
        ],
        axis=1,
    )
    skip = jnp.repeat(lax.dynamic_slice_in_dim(skip_gain, me * heads, heads), HEAD_DIM)[None]
    gain = columns(norm_gain[None], me * width, width)

    shapes = [
        ((rows, width), jnp.bfloat16),
        ((blocks * STATE, width), jnp.bfloat16),
        ((rows, STATE), jnp.bfloat16),
        ((rows, width), jnp.bfloat16),
        ((2 * blocks, width), jnp.float32),
    ]
    arrived = {0}
    pending = list(range(peers))
    stores = []
    for code in codes:
        arrived.add(code)
        ready = [k for k in pending if {k, (k + 1) % peers} <= arrived]
        pending = [k for k in pending if k not in ready]
        if not ready:
            continue
        count = len(ready)
        operands = []
        for k in ready:
            operands += [parts[k], parts[(k + 1) % peers]]
        stores = pl.pallas_call(
            functools.partial(local_kernel, width, heads, count, bool(stores)),
            in_specs=[smem] + [vmem] * (2 * count + 2 + len(stores)),
            out_specs=[vmem] * len(shapes),
            out_shape=[jax.ShapeDtypeStruct((peers,) + shape, dtype) for shape, dtype in shapes],
            input_output_aliases={3 + 2 * count + i: i for i in range(len(stores))},
            scratch_shapes=[
                pltpu.VMEM((rows + HALO, full), jnp.bfloat16),
                pltpu.VMEM((rows, width), jnp.float32),
                pltpu.VMEM((rows, width), jnp.bfloat16),
                pltpu.VMEM((rows + scale_rows, width), jnp.float32),
            ],
            compiler_params=params,
            cost_estimate=pl.CostEstimate(
                flops=2 * rows * count * width * 450,
                bytes_accessed=count * rows * width * 10,
                transcendentals=count * rows * full,
            ),
            name="local",
        )(jnp.stack([sources[k] for k in ready]), *operands, taps, skip, *stores)

    out = [((rows, width), jnp.bfloat16 if whole_group else jnp.float32)]
    if not whole_group:
        out.append(((rows, LANES), jnp.float32))
    results = pl.pallas_call(
        functools.partial(carry_kernel, width, whole_group),
        grid=(peers // PAIR,),
        in_specs=[vmem] * (len(shapes) + 1),
        out_specs=[pl.BlockSpec((PAIR * shape[0], shape[1]), lambda i: (i, 0)) for shape, _ in out],
        out_shape=[
            jax.ShapeDtypeStruct((peers * shape[0], shape[1]), dtype) for shape, dtype in out
        ],
        scratch_shapes=[
            pltpu.VMEM((STATE, width), jnp.float32),
        ],
        compiler_params=params,
        cost_estimate=pl.CostEstimate(
            flops=2 * peers * rows * width * 150,
            bytes_accessed=peers * rows * width * 8,
            transcendentals=peers * rows,
        ),
        name="carry",
    )(*stores, gain)
    if whole_group:
        return results[0]
    total, power = results
    sharers = [list(range(i, i + span)) for i in range(0, peers, span)]
    summed = jnp.sum(power, axis=1, keepdims=True)
    summed = lax.psum(summed, "ctx", axis_index_groups=sharers)
    return (total * lax.rsqrt(summed * (1.0 / GROUP_WIDTH) + EPS) * gain).astype(jnp.bfloat16)


def solution(mesh):
    in_specs = (
        P(("dp", "ctx"), None),
        P(("dp", "ctx"), None),
        P(),
        P(),
        P(("dp", "ctx"), None),
        P(("dp", "ctx"), None),
        P(),
        P(),
    )
    out_specs = P("dp", "ctx")
    return jax.shard_map(
        per_device, mesh=mesh, in_specs=in_specs, out_specs=out_specs, check_vma=False
    )
```

```python
import functools

import jax
import jax.numpy as jnp
from jax import lax
from jax.experimental import pallas as pl
from jax.experimental.pallas import tpu as pltpu
from jax.sharding import PartitionSpec as P

HEADS = 128
HEAD_DIM = 64
STATE = 128
GROUPS = 8
KW = 4
BLOCK = 128
GROUP_WIDTH = HEADS * HEAD_DIM // GROUPS
EPS = 1e-05
HALO = 16
LANES = 128
SUBLANES = 8
FIELDS = 2
STRIP = 64
PAIR = 2
WINDOW = 5
ORDER = (1, 7, 4, 2, 6, 5, 3)
PACK_VMEM = 58 * 1024 * 1024
VMEM_LIMIT = 28 * 1024 * 1024


def contract(a, b, dims):
    return lax.dot_general(a, b, (dims, ((), ())), preferred_element_type=jnp.float32)


def as_parts(v, count):
    parts = []
    for _ in range(count):
        part = v.astype(jnp.bfloat16)
        parts.append(part)
        v = v - part.astype(jnp.float32)
    return parts


def scalar_units(heads, rows, cols):
    units = []
    for p in range(FIELDS):
        for head in range(0, heads, SUBLANES):
            line, column = divmod(len(units), cols // rows)
            units.append((p, head, min(SUBLANES, heads), line * SUBLANES, column * rows))
    return units


def pack_kernel(peers, span, width, heads, codes, *refs):
    owner_ref, x_ref, kq_ref, decay_ref, step_ref = refs[:5]
    outs = refs[5 : 5 + len(codes)]
    raw_scalars, scalars, kq_near, sems = refs[5 + len(codes) :]
    rows = x_ref.shape[0]
    copies = [
        pltpu.make_async_copy(ref, dst, sems.at[1, i])
        for i, (ref, dst) in enumerate(
            ((decay_ref, raw_scalars.at[0]), (step_ref, raw_scalars.at[1]), (kq_ref, kq_near))
        )
    ]
    owners = [owner_ref[code] for code in codes]
    for i, owner in enumerate(owners):
        column = pl.multiple_of(owner * width, LANES)
        copies.append(
            pltpu.make_async_copy(
                x_ref.at[:, pl.ds(column, width)], outs[i].at[0:rows, 0:width], sems.at[0, i]
            )
        )
    for copy in copies:
        copy.start()
    for copy in copies[:3]:
        copy.wait()
    for p in range(FIELDS):
        field = raw_scalars[p].T
        for owner in range(peers):
            scalars[p, owner] = field[owner * heads : (owner + 1) * heads]
    for i, owner in enumerate(owners):
        outs[i][rows:] = jnp.zeros((outs[i].shape[0] - rows, outs[i].shape[1]), jnp.bfloat16)
        for p, head, count, top, left in scalar_units(heads, rows, width + 2 * STATE):
            outs[i][rows + top : rows + top + count, left : left + rows] = scalars[
                p, owner, head : head + count
            ].astype(jnp.bfloat16)
        for j in range(2):
            column = pl.multiple_of((j * GROUPS + owner // span) * STATE, LANES)
            left = width + j * STATE
            outs[i][0:rows, left : left + STATE] = kq_near[:, pl.ds(column, STATE)]
    for copy in copies[3:]:
        copy.wait()


def spread(heads):
    head_of = lax.broadcasted_iota(jnp.int32, (2 * heads, heads * HEAD_DIM), 1) // HEAD_DIM
    row = lax.rem(lax.broadcasted_iota(jnp.int32, (2 * heads, heads * HEAD_DIM), 0), heads)
    return jnp.where(head_of == row, 1.0, 0.0).astype(jnp.bfloat16)


def local_kernel(width, heads, count, chained, *refs):
    source_ref = refs[0]
    parts = refs[1 : 1 + 2 * count]
    taps_ref, skip_ref = refs[1 + 2 * count : 3 + 2 * count]
    refs = refs[3 + 2 * count + (5 if chained else 0) :]
    pre, state, c_out, fade_out, edge_out = refs[:5]
    wide, x_ref, scaled_ref, scales = refs[5:]
    rows = x_ref.shape[0]
    blocks = rows // BLOCK
    full = width + 2 * STATE
    row = lax.broadcasted_iota(jnp.int32, (rows, rows), 0)
    col = lax.broadcasted_iota(jnp.int32, (rows, rows), 1)
    lower = (row >= col) & (row // BLOCK == col // BLOCK)
    ones = jnp.where(lower, 1.0, 0.0).astype(jnp.bfloat16)
    eye = jnp.where(row == col, 1.0, 0.0).astype(jnp.bfloat16)
    expand = spread(heads)

    for which in range(count):
        source = source_ref[which]
        part, earlier = parts[2 * which : 2 * which + 2]
        wide[HALO:] = part[0:rows, 0:full]
        edge = earlier[rows - HALO : rows, 0:full]
        wide[0:HALO] = jnp.where(source == 0, jnp.zeros_like(edge), edge)

        def activated(r, lane):
            tap = [taps_ref[k : k + 1, lane : lane + LANES] for k in range(KW)]
            now = wide[r : r + STRIP + HALO, lane : lane + LANES].astype(jnp.float32)
            now = now[HALO // 2 :]
            before = pltpu.roll(now, 1, 0)
            older = pltpu.roll(tap[0] * before + tap[1] * now, 2, 0)
            summed = (older + (tap[2] * before + tap[3] * now))[HALO // 2 :]
            return summed * pltpu.reciprocal(1.0 + jnp.exp(-summed), approx=True)

        def field(p):
            pieces = [
                part[rows + top : rows + top + size, left : left + rows].astype(jnp.float32)
                for q, _, size, top, left in scalar_units(heads, rows, full)
                if q == p
            ]
            return jnp.concatenate(pieces, axis=0).astype(jnp.bfloat16)

        cumul = contract(ones, field(0), ((1,), (1,)))
        steps = contract(eye, field(1), ((1,), (1,)))
        middles = [
            cumul[b * BLOCK + BLOCK // 2 - 1 : b * BLOCK + BLOCK // 2] for b in range(blocks)
        ]
        middle = jnp.concatenate([jnp.broadcast_to(m, (BLOCK, heads)) for m in middles], axis=0)
        inward = jnp.concatenate(as_parts(steps * jnp.exp(middle - cumul), 2), axis=1)
        outward = jnp.concatenate(
            as_parts(
                jnp.concatenate(
                    [jnp.exp(cumul - middle)]
                    + [jnp.broadcast_to(jnp.exp(m), (16, heads)) for m in middles],
                    axis=0,
                ),
                2,
            ),
            axis=1,
        )
        scales[...] = contract(
            jnp.concatenate([inward, outward], axis=0), expand, ((1,), (0,))
        )
        edges = []
        for b in range(blocks):
            last_row = rows + (b + 1) * BLOCK - 1
            middle_row = 2 * rows + 16 * b
            edges += [scales[middle_row : middle_row + 1], scales[last_row : last_row + 1]]
        edge_out[source, 0 : 2 * blocks] = jnp.concatenate(edges, axis=0)
        fade_out[source] = scales[rows : 2 * rows].astype(jnp.bfloat16)
        b_part, c_part = (
            jnp.concatenate(
                [activated(r, lane) for r in range(0, rows, STRIP)], axis=0
            ).astype(jnp.bfloat16)
            for lane in (width, width + STATE)
        )
        c_out[source] = c_part
        scores = contract(c_part, b_part, ((1,), (1,)))
        scores = jnp.where(lower, scores, 0.0).astype(jnp.bfloat16)
        for lane in range(0, width, LANES):
            at = slice(lane, lane + LANES)
            for r in range(0, rows, STRIP):
                x_conv = activated(r, lane)
                x_ref[r : r + STRIP, at] = x_conv
                scaled_ref[r : r + STRIP, at] = (x_conv * scales[r : r + STRIP, at]).astype(
                    jnp.bfloat16
                )
        for b in range(blocks):
            at = slice(b * BLOCK, (b + 1) * BLOCK)
            added = contract(b_part[at], scaled_ref[at], ((0,), (0,)))
            state[source, b * STATE : (b + 1) * STATE] = added.astype(jnp.bfloat16)
        intra = contract(scores, scaled_ref[...], ((1,), (0,)))
        pre[source] = (intra * scales[rows : 2 * rows] + skip_ref[...] * x_ref[...]).astype(jnp.bfloat16)


def carry_kernel(width, whole_group, *refs):
    pre, state, c_part, fade, edge, gain_ref = refs[:6]
    outs, carry = refs[6:-1], refs[-1]
    rows = pre.shape[1]
    blocks = rows // BLOCK
    step = pl.program_id(0)

    @pl.when(step == 0)
    def _():
        carry[...] = jnp.zeros_like(carry)

    held = []
    for half in range(PAIR):
        source = step * PAIR + half
        for b in range(blocks):
            now = carry[...] * edge[source, 2 * b : 2 * b + 1]
            held.append(now.astype(jnp.bfloat16))
            added = state[source, b * STATE : (b + 1) * STATE].astype(jnp.float32)
            carry[...] = (now + added) * edge[source, 2 * b + 1 : 2 * b + 2]
    for half in range(PAIR):
        source = step * PAIR + half
        for b in range(blocks):
            at = slice(b * BLOCK, (b + 1) * BLOCK)
            to = slice(half * rows + b * BLOCK, half * rows + (b + 1) * BLOCK)
            inter = contract(c_part[source, at], held[half * blocks + b], ((1,), (0,)))
            total = pre[source, at].astype(jnp.float32) + inter * fade[source, at].astype(
                jnp.float32
            )
            power = total[:, :LANES] * total[:, :LANES]
            for lane in range(LANES, width, LANES):
                power = power + total[:, lane : lane + LANES] * total[:, lane : lane + LANES]
            if whole_group:
                summed = jnp.sum(power, axis=1, keepdims=True)
                norm = lax.rsqrt(summed * (1.0 / GROUP_WIDTH) + EPS)
                outs[0][to] = (total * norm * gain_ref[...]).astype(jnp.bfloat16)
            else:
                outs[0][to] = total
                outs[1][to] = power


def per_device(inputs, key_query, conv_inputs, conv_kq, step_size, decay_log, skip_gain, norm_gain):
    peers = lax.axis_size("ctx")
    me = lax.axis_index("ctx")
    rows = inputs.shape[0]
    width = HEADS * HEAD_DIM // peers
    heads = HEADS // peers
    span = GROUP_WIDTH // width
    whole_group = span == 1
    blocks = rows // BLOCK
    full = width + 2 * STATE
    scalar_rows = scalar_units(heads, rows, full)[-1][3] + SUBLANES
    scale_rows = rows + 16 * blocks
    cycle = jnp.arange(peers, dtype=jnp.int32)
    owners = lax.rem(me + cycle, peers)
    sources = lax.rem(me + peers - cycle, peers)

    smem = pl.BlockSpec(memory_space=pltpu.SMEM)
    hbm = pl.BlockSpec(memory_space=pltpu.HBM)
    vmem = pl.BlockSpec(memory_space=pltpu.VMEM)
    params = pltpu.CompilerParams(vmem_limit_bytes=VMEM_LIMIT)

    def columns(a, first, size):
        return lax.dynamic_slice_in_dim(a, first, size, axis=1)

    def pack(codes):
        shape = jax.ShapeDtypeStruct((rows + scalar_rows, full), jnp.bfloat16)
        return pl.pallas_call(
            functools.partial(pack_kernel, peers, span, width, heads, codes),
            in_specs=[smem] + [hbm] * 4,
            out_specs=[vmem] * len(codes),
            out_shape=[shape] * len(codes),
            scratch_shapes=[
                pltpu.VMEM((FIELDS, rows, HEADS), jnp.float32),
                pltpu.VMEM((FIELDS, peers, heads, rows), jnp.float32),
                pltpu.VMEM(key_query.shape, jnp.bfloat16),
                pltpu.SemaphoreType.DMA((2, max(3, len(codes)))),
            ],
            compiler_params=pltpu.CompilerParams(vmem_limit_bytes=PACK_VMEM),
            cost_estimate=pl.CostEstimate(
                flops=0, bytes_accessed=4 * len(codes) * rows * full, transcendentals=0
            ),
            name="pack",
        )(owners, inputs, key_query, decay_log, step_size)

    codes = [code for code in ORDER if code < peers]
    codes += [code for code in range(1, peers) if code not in codes]
    parts = dict(zip(codes[:2], pack(codes[:2])))
    parts.update(zip(codes[2:] + [0], pack(codes[2:] + [0])))
    for i, code in enumerate(codes):
        pairs = [(j, (j + code) % peers) for j in range(peers)]
        message = parts[code]
        if i >= WINDOW:
            message, _ = lax.optimization_barrier((message, parts[codes[i - WINDOW]]))
        parts[code] = lax.ppermute(message, "ctx", pairs)

    group = me // span
    taps = jnp.concatenate(
        [
            columns(conv_inputs, me * width, width),
            columns(conv_kq, group * STATE, STATE),
            columns(conv_kq, (GROUPS + group) * STATE, STATE),
        ],
        axis=1,
    )
    skip = jnp.repeat(lax.dynamic_slice_in_dim(skip_gain, me * heads, heads), HEAD_DIM)[None]
    gain = columns(norm_gain[None], me * width, width)

    shapes = [
        ((rows, width), jnp.bfloat16),
        ((blocks * STATE, width), jnp.bfloat16),
        ((rows, STATE), jnp.bfloat16),
        ((rows, width), jnp.bfloat16),
        ((2 * blocks, width), jnp.float32),
    ]
    arrived = {0}
    pending = list(range(peers))
    stores = []
    for code in codes:
        arrived.add(code)
        ready = [k for k in pending if {k, (k + 1) % peers} <= arrived]
        pending = [k for k in pending if k not in ready]
        if not ready:
            continue
        count = len(ready)
        operands = []
        for k in ready:
            operands += [parts[k], parts[(k + 1) % peers]]
        stores = pl.pallas_call(
            functools.partial(local_kernel, width, heads, count, bool(stores)),
            in_specs=[smem] + [vmem] * (2 * count + 2 + len(stores)),
            out_specs=[vmem] * len(shapes),
            out_shape=[jax.ShapeDtypeStruct((peers,) + shape, dtype) for shape, dtype in shapes],
            input_output_aliases={3 + 2 * count + i: i for i in range(len(stores))},
            scratch_shapes=[
                pltpu.VMEM((rows + HALO, full), jnp.bfloat16),
                pltpu.VMEM((rows, width), jnp.float32),
                pltpu.VMEM((rows, width), jnp.bfloat16),
                pltpu.VMEM((rows + scale_rows, width), jnp.float32),
            ],
            compiler_params=params,
            cost_estimate=pl.CostEstimate(
                flops=2 * rows * count * width * 450,
                bytes_accessed=count * rows * width * 10,
                transcendentals=count * rows * full,
            ),
            name="local",
        )(jnp.stack([sources[k] for k in ready]), *operands, taps, skip, *stores)

    out = [((rows, width), jnp.bfloat16 if whole_group else jnp.float32)]
    if not whole_group:
        out.append(((rows, LANES), jnp.float32))
    results = pl.pallas_call(
        functools.partial(carry_kernel, width, whole_group),
        grid=(peers // PAIR,),
        in_specs=[vmem] * (len(shapes) + 1),
        out_specs=[pl.BlockSpec((PAIR * shape[0], shape[1]), lambda i: (i, 0)) for shape, _ in out],
        out_shape=[
            jax.ShapeDtypeStruct((peers * shape[0], shape[1]), dtype) for shape, dtype in out
        ],
        scratch_shapes=[
            pltpu.VMEM((STATE, width), jnp.float32),
        ],
        compiler_params=params,
        cost_estimate=pl.CostEstimate(
            flops=2 * peers * rows * width * 150,
            bytes_accessed=peers * rows * width * 8,
            transcendentals=peers * rows,
        ),
        name="carry",
    )(*stores, gain)
    if whole_group:
        return results[0]
    total, power = results
    sharers = [list(range(i, i + span)) for i in range(0, peers, span)]
    summed = jnp.sum(power, axis=1, keepdims=True)
    summed = lax.psum(summed, "ctx", axis_index_groups=sharers)
    return (total * lax.rsqrt(summed * (1.0 / GROUP_WIDTH) + EPS) * gain).astype(jnp.bfloat16)


def solution(mesh):
    in_specs = (
        P(("dp", "ctx"), None),
        P(("dp", "ctx"), None),
        P(),
        P(),
        P(("dp", "ctx"), None),
        P(("dp", "ctx"), None),
        P(),
        P(),
    )
    out_specs = P("dp", "ctx")
    return jax.shard_map(
        per_device, mesh=mesh, in_specs=in_specs, out_specs=out_specs, check_vma=False
    )
```
